32 devices in a mesh: rep: 8 (over z, y), shard: 4 (over x, core).
Axes of the slice: x: 2, y: 2, z: 4, core: 2. Of those that a mesh axis runs over, the one named last changes fastest.
Arguments:
- tokens: bfloat16 [8192, 1024], P(('rep', 'shard')), may hold values from -6 to 6
- segment_ids: int32 [8, 1024], P('rep'), may hold values from 0 to 4, as said below
- ln1_gain: bfloat16 [1024], P('shard'), may hold values from 0.099609375 to 1.8984375
- w_qkv: bfloat16 [1024, 3072], P('shard'), may hold values from -0.1875 to 0.1875
- w_out: bfloat16 [1024, 1024], P('shard'), may hold values from -1.5 to 1.5
- ln2_gain: bfloat16 [1024], P('shard'), may hold values from 0.099609375 to 1.8984375
- w_in: bfloat16 [1024, 5248], P('shard'), may hold values from -0.1875 to 0.1875
- w_down: bfloat16 [2624, 1024], P('shard'), may hold values from -0.125 to 0.125
- cotangent: bfloat16 [8192, 1024], P(('rep', 'shard')), may hold values from -6 to 6
Outputs:
- activations: bfloat16 [8192, 1024], P(('rep', 'shard'))
- input_grad: float32 [8192, 1024], P(('rep', 'shard'))
- ln1_grad: float32 [1024], P('shard')
- qkv_grad: float32 [1024, 3072], P('shard')
- out_grad: float32 [1024, 1024], P('shard')
- ln2_grad: float32 [1024], P('shard')
- in_grad: float32 [1024, 5248], P('shard')
- down_grad: float32 [2624, 1024], P('shard')
The draws below stay inside these ranges and needn't reach their ends.
Inputs may be any that keep to these rules, and one draw needn't show every extreme that they name: `segment_ids`: along each packed sequence the numbers never fall; one document covers every position from some position under 256 to some position at or over 1024 - 255; the other documents lie before or after it.
All inputs are finite; a program needn't handle non-finite values.
Results may differ from the reference program's by a relative error of at most 0.018.
Values may be sent and summed in bfloat16 or wider, within the bound.
No kernel may reach another device: no remote copies, remote signals or barrier semaphores. Data moves between devices by JAX's collectives and lax.ppermute only.
A program may use at most 192 MiB of HBM per device.

```python
import math
import jax
import jax.numpy as jnp
from jax import lax

D = 1024
HEADS = 16
HEAD_DIM = 64
FF = 2624
HALF = 64
SEQ = 1024
TOK_DEV = 256
TOKENS = 8192
QBLOCK = 512
N_REP = 8


def draw_segment_ids(key, part):
    key = jax.random.fold_in(key, 7)
    key_one, key_two, key_three, key_four = jax.random.split(key, 4)
    long_start = jax.random.randint(key_one, (N_REP, 1), 2, TOK_DEV)
    first_cut = jax.random.randint(key_two, (N_REP, 1), 1, long_start)
    long_end = SEQ - jax.random.randint(key_three, (N_REP, 1), 2, TOK_DEV - 1)
    last_cut = jax.random.randint(key_four, (N_REP, 1), long_end + 1, SEQ)
    positions = jnp.arange(SEQ, dtype=jnp.int32)[None, :]
    result = (positions >= first_cut).astype(jnp.int32) + (positions >= long_start).astype(jnp.int32) + (positions >= long_end).astype(jnp.int32) + (positions >= last_cut).astype(jnp.int32)
    return result.astype(jnp.int32)


def level_of(stream_key, shape, shards, least, largest):
    level, own = 1.0, jax.random.fold_in(stream_key, 6)
    for position, shards_of in shards:
        draws = jnp.exp(jax.random.uniform(jax.random.fold_in(own, position), (shards_of,), jnp.float32, least / len(shards), largest / len(shards)))
        level = level * jnp.repeat(draws, shape[position] // shards_of).reshape([-1 if axis == position else 1 for axis in range(len(shape))])
    return level


def normal_values(stream_key, shape, spread, bound, cuts=(), held_as=jnp.bfloat16):
    array = spread * jax.random.normal(stream_key, shape, jnp.float32)
    if cuts:
        array = array * level_of(stream_key, shape, cuts, -0.22, 0.18)
    return jnp.clip(array, -bound, bound).astype(held_as)


def setup_inputs(seed: int = 0) -> dict:
    splits = jax.random.split(jax.random.key(seed), 10)
    tokens = normal_values(splits[0], (TOKENS, D), 1.0, 6.0, ((0, 32),))
    segment_ids = draw_segment_ids(jax.random.fold_in(splits[9], 71), 0)
    ln1_gain = jnp.clip(1.0 + 0.18 * jax.random.normal(splits[2], (D,), jnp.float32), 0.099609375, 1.8984375).astype(jnp.bfloat16)
    w_qkv = normal_values(splits[3], (D, 3 * D), D ** -0.5, 0.1875, ((0, 4),))
    w_out = normal_values(splits[4], (D, D), (max(D // 64, 1)) ** -0.5, 1.5, ((0, 4),))
    ln2_gain = jnp.clip(1.0 + 0.18 * jax.random.normal(splits[5], (D,), jnp.float32), 0.099609375, 1.8984375).astype(jnp.bfloat16)
    w_in = normal_values(splits[6], (D, 2 * FF), D ** -0.5, 0.1875, ((0, 4),))
    w_down = normal_values(splits[7], (FF, D), FF ** -0.5, 0.125, ((0, 4),))
    cotangent = normal_values(splits[8], (TOKENS, D), 1.0, 6.0, ((0, 32),))
    return dict(tokens=tokens, segment_ids=segment_ids, ln1_gain=ln1_gain, w_qkv=w_qkv, w_out=w_out, ln2_gain=ln2_gain, w_in=w_in, w_down=w_down, cotangent=cotangent)


norm_epsilon = 1e-05
rope_base = 10000.0
masked_score = -1e+30

@jax.custom_vjp
def low(v):
    return lax.optimization_barrier(v.astype(jnp.bfloat16)).astype(jnp.float32)

@jax.custom_vjp
def low_back(v):
    return v

def low_keep(v):
    return (low(v), None)

def low_pass(kept, grad):
    return (grad,)

def back_keep(v):
    return (v, None)

def back_low(kept, grad):
    return (low(grad),)
low.defvjp(low_keep, low_pass)
low_back.defvjp(back_keep, back_low)

def matmul(left, right):
    return jnp.dot(left, right, precision=lax.Precision.HIGHEST)

def layer_norm(values, gain):
    centred = values - lax.optimization_barrier(jnp.mean(values, axis=-1, keepdims=True))
    variance = lax.optimization_barrier(jnp.mean(centred * centred, axis=-1, keepdims=True))
    return centred * lax.rsqrt(variance + norm_epsilon) * gain

def rotate(values, positions):
    half_dim = HEAD_DIM // 2
    frequency = jnp.exp(-math.log(rope_base) * 2.0 * jnp.arange(half_dim, dtype=jnp.float32) / HEAD_DIM)
    angles = positions.astype(jnp.float32)[:, None] * frequency[None, :]
    cosine_table = jnp.cos(angles)[:, None, :]
    sine_table = jnp.sin(angles)[:, None, :]
    front_half = values[..., :half_dim]
    back_half = values[..., half_dim:]
    return jnp.concatenate([front_half * cosine_table - back_half * sine_table, back_half * cosine_table + front_half * sine_table], axis=-1)

def sequence_layer(activations, seq_ids, first_norm_gain, qkv_weight, out_weight, second_norm_gain, in_weight, down_weight):
    positions = jnp.arange(SEQ, dtype=jnp.int32)
    first_normalized = low(layer_norm(activations, first_norm_gain))
    qkv = low_back(matmul(first_normalized, qkv_weight))
    queries = low(rotate(qkv[:, :D].reshape(SEQ, HEADS, HEAD_DIM), positions))
    keys = low(rotate(qkv[:, D:2 * D].reshape(SEQ, HEADS, HEAD_DIM), positions))
    values = low(qkv[:, 2 * D:].reshape(SEQ, HEADS, HEAD_DIM))
    key_pad = jnp.pad(keys, ((HALF, HALF), (0, 0), (0, 0)))
    value_pad = jnp.pad(values, ((HALF, HALF), (0, 0), (0, 0)))
    id_pad = jnp.pad(seq_ids, (HALF, HALF), constant_values=-1)
    score_scale = 1.0 / math.sqrt(HEAD_DIM)

    def block(row_start):
        query_block = lax.dynamic_slice_in_dim(queries, row_start, QBLOCK)
        key_block = lax.dynamic_slice_in_dim(key_pad, row_start, QBLOCK + 2 * HALF)
        value_block = lax.dynamic_slice_in_dim(value_pad, row_start, QBLOCK + 2 * HALF)
        query_ids = lax.dynamic_slice_in_dim(seq_ids, row_start, QBLOCK)
        key_ids = lax.dynamic_slice_in_dim(id_pad, row_start, QBLOCK + 2 * HALF)
        query_pos = row_start + jnp.arange(QBLOCK, dtype=jnp.int32)
        key_pos = row_start - HALF + jnp.arange(QBLOCK + 2 * HALF, dtype=jnp.int32)
        allowed = (query_ids[:, None] == key_ids[None, :]) & (jnp.abs(query_pos[:, None] - key_pos[None, :]) <= HALF)
        scores = jnp.einsum('qhd,khd->hqk', query_block, key_block, precision=lax.Precision.HIGHEST) * score_scale
        scores = low_back(scores)
        scores = jnp.where(allowed[None, :, :], scores, masked_score)
        probs = low(jax.nn.softmax(scores, axis=-1))
        return jnp.einsum('hqk,khd->qhd', probs, value_block, precision=lax.Precision.HIGHEST)
    starts = jnp.arange(0, SEQ, QBLOCK, dtype=jnp.int32)
    attended = lax.map(jax.checkpoint(block), starts).reshape(SEQ, D)
    attended = low_back(low(attended))
    first_hidden_state = activations + low_back(matmul(attended, out_weight))
    second_normalized = low(layer_norm(first_hidden_state, second_norm_gain))
    up_proj = low_back(matmul(second_normalized, in_weight))
    act = low(jax.nn.gelu(up_proj[:, :FF], approximate=False) * up_proj[:, FF:])
    return first_hidden_state + low_back(matmul(act, down_weight))

def reference(tokens, segment_ids, ln1_gain, w_qkv, w_out, ln2_gain, w_in, w_down, cotangent):

    def forward(layer_inputs, first_norm_gain, qkv_weight, out_weight, second_norm_gain, in_weight, down_weight):

        def run_sequence(packed):
            return sequence_layer(packed[0], packed[1], first_norm_gain, qkv_weight, out_weight, second_norm_gain, in_weight, down_weight)
        results = lax.map(run_sequence, (layer_inputs.reshape(N_REP, SEQ, D), segment_ids))
        return results.reshape(TOKENS, D)
    floats = (tokens.astype(jnp.float32), ln1_gain.astype(jnp.float32), w_qkv.astype(jnp.float32), w_out.astype(jnp.float32), ln2_gain.astype(jnp.float32), w_in.astype(jnp.float32), w_down.astype(jnp.float32))
    result, pullback = jax.vjp(forward, *floats)
    grads = pullback(cotangent.astype(jnp.float32))
    return (result.astype(jnp.bfloat16), grads[0], grads[1], grads[2], grads[3], grads[4], grads[5], grads[6])
```

```python
import math

import jax
import jax.numpy as jnp
from jax import lax
from jax.experimental import pallas as pl
from jax.experimental.pallas import tpu as pltpu
from jax.sharding import PartitionSpec as P

HEADS = 16
HEAD_DIM = 64
FF = 2624
HALF = 64
QB = 128

norm_epsilon = 1e-05
rope_base = 10000.0
masked_score = -1e30

F32 = jnp.float32
BF16 = jnp.bfloat16


def bit_of(axis, bit):
    return (lax.axis_index(axis) >> bit) & 1


def swap(x, axis, bit):
    size = lax.axis_size(axis)
    return lax.ppermute(x, axis, [(i, i ^ (1 << bit)) for i in range(size)])


def bits_of(axis):
    return lax.axis_size(axis).bit_length() - 1


def pick(x, index, dim):
    return lax.dynamic_index_in_dim(x, index, dim, keepdims=False)


def pair(mine, other, bit, dim):
    return jnp.where(bit == 0, jnp.stack([mine, other], dim), jnp.stack([other, mine], dim))


def gather_blocks(x, axis):
    count = bits_of(axis)
    shape = x.shape
    for step, bit in enumerate(reversed(range(count))):
        x = pair(x, swap(x, axis, bit), bit_of(axis, bit), step)
    return x.reshape((1 << count,) + shape)


def scatter_sum(x, axis):
    count = bits_of(axis)
    x = x.reshape((2,) * count + x.shape[1:])
    for bit in range(count):
        dim = count - 1 - bit
        b = bit_of(axis, bit)
        got = swap(pick(x, 1 - b, dim).astype(BF16), axis, bit)
        x = pick(x, b, dim).astype(F32) + got.astype(F32)
    return x


def all_to_all_blocks(x, axis):
    count = bits_of(axis)
    shape = x.shape
    x = x.reshape((2,) * count + shape[1:])
    for dim, bit in enumerate(reversed(range(count))):
        b = bit_of(axis, bit)
        got = swap(pick(x, 1 - b, dim), axis, bit)
        x = pair(pick(x, b, dim), got, b, dim)
    return x.reshape(shape)


def replica_scatter(x, order):
    left = list(reversed(range(bits_of("rep"))))
    x = x.reshape((2,) * len(left) + x.shape[1:])
    for bit in order:
        dim = left.index(bit)
        b = bit_of("rep", bit)
        got = swap(pick(x, 1 - b, dim), "rep", bit)
        x = (pick(x, b, dim).astype(F32) + got.astype(F32)).astype(BF16)
        left.remove(bit)
    return x


def replica_gather(x, order):
    shape = x.shape
    have = []
    for bit in reversed(order):
        have = sorted(have + [bit], reverse=True)
        x = pair(x, swap(x, "rep", bit), bit_of("rep", bit), have.index(bit))
    return x.reshape((1 << len(order),) + shape)


def partner(x):
    width = x.shape[-1]
    lane = lax.broadcasted_iota(jnp.int32, x.shape, 1)
    front = (lane % HEAD_DIM) < HEAD_DIM // 2
    return jnp.where(
        front,
        pltpu.roll(x, width - HEAD_DIM // 2, 1),
        pltpu.roll(x, HEAD_DIM // 2, 1),
    )


def head_masks(heads, width):
    lane = lax.broadcasted_iota(jnp.int32, (QB, width), 1) // HEAD_DIM
    return [lane == h for h in range(heads)]


def stack_heads(x, masks):
    x = x.astype(F32)
    return jnp.concatenate([jnp.where(m, x, 0.0) for m in masks], axis=0).astype(BF16)


def merge_heads(x, masks):
    total = None
    for h, m in enumerate(masks):
        part = jnp.where(m, x[h * QB : (h + 1) * QB], 0.0)
        total = part if total is None else total + part
    return total


def window_bias(ids_q, ids_k):
    row = lax.broadcasted_iota(jnp.int32, (QB, QB + 2 * HALF), 0)
    col = lax.broadcasted_iota(jnp.int32, (QB, QB + 2 * HALF), 1)
    ids_q = jnp.concatenate([ids_q] * ((QB + 2 * HALF) // 128), axis=1)
    allowed = (col >= row) & (col <= row + 2 * HALF) & (ids_q == ids_k)
    return jnp.where(allowed, 0.0, masked_score)


def block_probs(stacked_q, keys, bias, heads):
    scores = lax.dot_general(
        stacked_q, keys, (((1,), (1,)), ((), ())), preferred_element_type=F32
    )
    rows, cols = scores.shape
    scores = (scores.reshape(heads, QB, cols) + bias[None]).reshape(rows, cols)
    weights = jnp.exp(scores - jnp.max(scores, axis=-1, keepdims=True))
    return weights * (1.0 / jnp.sum(weights, axis=-1, keepdims=True))


def attention_kernel(
    heads, width, qkv_ref, cos_ref, sin_ref, idq_ref, idk_ref, q_ref, k_ref, v_ref, out_ref
):
    seq = qkv_ref.shape[0]
    edge = jnp.zeros((HALF, width), BF16)
    for ref in (k_ref, v_ref):
        ref[0:HALF, :] = edge
        ref[seq + HALF : seq + 2 * HALF, :] = edge

    def prepare(i, carry):
        rows = pl.ds(pl.multiple_of(i * QB, QB), QB)
        shifted = pl.ds(pl.multiple_of(i * QB + HALF, HALF), QB)
        cos, sin = cos_ref[rows, :], sin_ref[rows, :]
        q = qkv_ref[rows, 0:width]
        k = qkv_ref[rows, width : 2 * width]
        rotated = (q * cos + partner(q) * sin).astype(BF16)
        q_ref[rows, :] = (rotated.astype(F32) * (1.0 / math.sqrt(HEAD_DIM))).astype(BF16)
        k_ref[shifted, :] = (k * cos + partner(k) * sin).astype(BF16)
        v_ref[shifted, :] = qkv_ref[rows, 2 * width : 3 * width].astype(BF16)
        return carry

    lax.fori_loop(0, seq // QB, prepare, 0)
    masks = head_masks(heads, width)

    def attend(i, carry):
        rows = pl.ds(pl.multiple_of(i * QB, QB), QB)
        window = pl.ds(pl.multiple_of(i * QB, QB), QB + 2 * HALF)
        bias = window_bias(idq_ref[rows, :], idk_ref[0:1, window])
        probs = block_probs(stack_heads(q_ref[rows, :], masks), k_ref[window, :], bias, heads)
        mixed = jnp.dot(probs.astype(BF16), v_ref[window, :], preferred_element_type=F32)
        out_ref[rows, :] = merge_heads(mixed, masks).astype(BF16)
        return carry

    lax.fori_loop(0, seq // QB, attend, 0)


def attention_back_kernel(
    heads, width, q_ref, k_ref, v_ref, da_ref, cos_ref, sin_ref, idq_ref, idk_ref, out_ref, dk, dv
):
    seq = q_ref.shape[0]
    dk[...] = jnp.zeros_like(dk)
    dv[...] = jnp.zeros_like(dv)
    masks = head_masks(heads, width)

    def back(i, carry):
        rows = pl.ds(pl.multiple_of(i * QB, QB), QB)
        window = pl.ds(pl.multiple_of(i * QB, QB), QB + 2 * HALF)
        bias = window_bias(idq_ref[rows, :], idk_ref[0:1, window])
        queries = stack_heads(q_ref[rows, :], masks)
        keys = k_ref[window, :]
        probs = block_probs(queries, keys, bias, heads)
        grads = stack_heads(da_ref[rows, :], masks)
        dprobs = lax.dot_general(
            grads, v_ref[window, :], (((1,), (1,)), ((), ())), preferred_element_type=F32
        )
        delta = jnp.sum(probs * dprobs, axis=-1, keepdims=True)
        dscores = (probs * (dprobs - delta)).astype(BF16)
        dq = merge_heads(jnp.dot(dscores, keys, preferred_element_type=F32), masks)
        dq = dq * (1.0 / math.sqrt(HEAD_DIM))
        cos, sin = cos_ref[rows, :], sin_ref[rows, :]
        out_ref[rows, 0:width] = (dq * cos - partner(dq) * sin).astype(BF16)
        dk[window, :] += lax.dot_general(
            dscores, queries, (((0,), (0,)), ((), ())), preferred_element_type=F32
        )
        dv[window, :] += lax.dot_general(
            probs.astype(BF16), grads, (((0,), (0,)), ((), ())), preferred_element_type=F32
        )
        return carry

    lax.fori_loop(0, seq // QB, back, 0)

    def finish(i, carry):
        rows = pl.ds(pl.multiple_of(i * QB, QB), QB)
        shifted = pl.ds(pl.multiple_of(i * QB + HALF, HALF), QB)
        cos, sin = cos_ref[rows, :], sin_ref[rows, :]
        g = dk[shifted, :]
        out_ref[rows, width : 2 * width] = (g * cos - partner(g) * sin).astype(BF16)
        out_ref[rows, 2 * width : 3 * width] = dv[shifted, :].astype(BF16)
        return carry

    lax.fori_loop(0, seq // QB, finish, 0)


def attention(qkv, tables, heads, width):
    seq = qkv.shape[0]
    shape = jax.ShapeDtypeStruct
    return pl.pallas_call(
        lambda *refs: attention_kernel(heads, width, *refs),
        out_shape=(
            shape((seq, width), BF16),
            shape((seq + 2 * HALF, width), BF16),
            shape((seq + 2 * HALF, width), BF16),
            shape((seq, width), BF16),
        ),
        compiler_params=pltpu.CompilerParams(vmem_limit_bytes=40 << 20),
        name="attention",
    )(qkv, *tables)


def attention_back(queries, keys, values, grads, tables, heads, width):
    seq = queries.shape[0]
    return pl.pallas_call(
        lambda *refs: attention_back_kernel(heads, width, *refs),
        out_shape=jax.ShapeDtypeStruct((seq, 3 * width), BF16),
        scratch_shapes=[pltpu.VMEM((seq + 2 * HALF, width), F32)] * 2,
        compiler_params=pltpu.CompilerParams(vmem_limit_bytes=40 << 20),
        name="attention_back",
    )(queries, keys, values, grads, *tables)


def layer_norm(values):
    centred = values - jnp.mean(values, axis=-1, keepdims=True)
    scale = lax.rsqrt(jnp.mean(centred * centred, axis=-1, keepdims=True) + norm_epsilon)
    return centred * scale, scale


def norm_backward(grad_hat, normed, scale):
    return (
        grad_hat
        - jnp.mean(grad_hat, axis=-1, keepdims=True)
        - normed * jnp.mean(grad_hat * normed, axis=-1, keepdims=True)
    ) * scale


def geglu(gate_part, linear_part):
    return jax.nn.gelu(gate_part, approximate=False) * linear_part


def dot(a, b, dims):
    return lax.dot_general(a, b, (dims, ((), ())), preferred_element_type=F32)


def shards(tokens, segment_ids, ln1_gain, w_qkv, w_out, ln2_gain, w_in, w_down, cotangent):
    n = lax.axis_size("shard")
    replicas = lax.axis_size("rep")
    me = lax.axis_index("shard")
    rows, model = tokens.shape
    seq = rows * n
    part = model // n
    ff = w_down.shape[0]
    heads = HEADS // n
    head_cols = heads * HEAD_DIM
    width = max(128, head_cols)

    gains = jnp.concatenate([ln1_gain, ln2_gain])
    gains = jnp.pad(gains, (0, model - 2 * part))[None]
    gains = jnp.pad(gains, ((0, 15), (0, 0)))
    first = gather_blocks(jnp.concatenate([tokens, gains]), "shard")
    all_tokens = first[:, :rows].reshape(seq, model)
    gain1 = first[:, rows, :part].reshape(model).astype(F32)
    gain2 = first[:, rows, part : 2 * part].reshape(model).astype(F32)

    qkv_to = w_qkv.reshape(part, 3, n, head_cols).transpose(2, 0, 1, 3)
    qkv_w = all_to_all_blocks(qkv_to.reshape(n, part, 3 * head_cols), "shard")
    qkv_w = qkv_w.reshape(model, 3 * head_cols)
    if width != head_cols:
        qkv_w = qkv_w.reshape(model, 3, head_cols)
        qkv_w = jnp.pad(qkv_w, ((0, 0), (0, 0), (0, width - head_cols)))
        qkv_w = qkv_w.reshape(model, 3 * width)
    out_w = gather_blocks(w_out, "shard").reshape(model, model)
    in_to = w_in.reshape(part, 2, n, ff).transpose(2, 0, 1, 3).reshape(n, part, 2 * ff)
    in_w = all_to_all_blocks(in_to, "shard").reshape(model, 2 * ff)
    cot = gather_blocks(cotangent, "shard").reshape(seq, model)

    lane = jnp.arange(width, dtype=jnp.int32) % HEAD_DIM
    half = HEAD_DIM // 2
    frequency = jnp.exp(
        -math.log(rope_base) * 2.0 * (lane % half).astype(F32) / HEAD_DIM
    )
    angles = jnp.arange(seq, dtype=F32)[:, None] * frequency[None, :]
    sign = jnp.where(lane < half, -1.0, 1.0)
    ids = segment_ids[0]
    tables = (
        jnp.cos(angles),
        jnp.sin(angles) * sign[None, :],
        jnp.broadcast_to(ids[:, None], (seq, 128)),
        jnp.pad(ids, (HALF, HALF), constant_values=-1)[None],
    )

    hat1, _ = layer_norm(all_tokens.astype(F32))
    normed1 = (hat1 * gain1).astype(BF16)
    qkv = dot(normed1, qkv_w, ((1,), (0,)))
    queries, keys, values, attended = attention(qkv, tables, heads, width)
    everyone = gather_blocks(attended[:, :head_cols], "shard")
    everyone = everyone.transpose(1, 0, 2).reshape(seq, model)
    hidden = all_tokens.astype(F32) + dot(everyone, out_w, ((1,), (0,)))
    hat2, scale2 = layer_norm(hidden)
    normed2 = (hat2 * gain2).astype(BF16)
    up = dot(normed2, in_w, ((1,), (0,)))
    act, geglu_pull = jax.vjp(geglu, up[:, :ff], up[:, ff:])
    act = act.astype(BF16)
    mlp = dot(act, w_down, ((1,), (0,)))
    mlp = scatter_sum(mlp.astype(BF16).reshape(n, rows, model), "shard")
    own = me * rows
    output = (lax.dynamic_slice_in_dim(hidden, own, rows) + mlp).astype(BF16)

    dact = dot(cot, w_down, ((1,), (1,)))
    dgate, dlin = geglu_pull(dact)
    dup = jnp.concatenate([dgate, dlin], axis=1).astype(BF16)
    dnormed2 = dot(dup, in_w, ((1,), (1,))).astype(BF16)
    dnormed2 = scatter_sum(dnormed2.reshape(n, rows, model), "shard")
    own_hat2 = lax.dynamic_slice_in_dim(hat2, own, rows)
    own_scale2 = lax.dynamic_slice_in_dim(scale2, own, rows)
    ln2_part = jnp.sum(dnormed2 * own_hat2, axis=0)
    dhidden = cotangent.astype(F32) + norm_backward(dnormed2 * gain2, own_hat2, own_scale2)
    dproj = gather_blocks(dhidden.astype(BF16), "shard").reshape(seq, model)
    down_grad = dot(act, cot, ((0,), (0,))).astype(BF16)
    in_grad = dot(normed2, dup, ((0,), (0,))).astype(BF16)

    out_grad = dot(attended[:, :head_cols], dproj, ((0,), (0,))).astype(BF16)
    dattended = dot(dproj, w_out, ((1,), (1,))).astype(BF16)
    if width != head_cols:
        dattended = jnp.pad(dattended, ((0, 0), (0, width - head_cols)))
    dqkv = attention_back(queries, keys, values, dattended, tables, heads, width)
    qkv_grad = dot(normed1, dqkv, ((0,), (0,))).astype(BF16)
    dnormed1 = dot(dqkv, qkv_w, ((1,), (1,))).astype(BF16)
    dnormed1 = scatter_sum(dnormed1.reshape(n, rows, model), "shard")
    own_hat1, own_scale1 = layer_norm(tokens.astype(F32))
    ln1_part = jnp.sum(dnormed1 * own_hat1, axis=0)
    input_grad = dhidden + norm_backward(dnormed1 * gain1, own_hat1, own_scale1)

    near = list(range(bits_of("rep")))
    far = near[1:] + near[:1]
    chunk = part // replicas

    def columns_total(grad, cols):
        grad = grad.reshape(n, replicas, chunk, cols).transpose(1, 0, 2, 3)
        grad = all_to_all_blocks(replica_scatter(grad, near), "shard")
        return replica_gather(grad, near).transpose(0, 2, 1, 3).reshape(part, n, cols)

    in_total = columns_total(in_grad, 2 * ff).reshape(part, n, 2, ff)
    in_total = in_total.transpose(0, 2, 1, 3).reshape(part, 2 * n * ff).astype(F32)

    def rows_total(grad):
        height, cols = grad.shape
        grad = grad.reshape(height, replicas, cols // replicas).transpose(1, 0, 2)
        grad = replica_gather(replica_scatter(grad, far), far)
        return grad.transpose(1, 0, 2).reshape(height, cols).astype(F32)

    down_total = rows_total(down_grad)
    out_total = rows_total(out_grad)
    if width != head_cols:
        qkv_grad = qkv_grad.reshape(model, 3, width)[:, :, :head_cols].reshape(model, 3 * head_cols)
    qkv_total = columns_total(qkv_grad, 3 * head_cols).reshape(part, n, 3, head_cols)
    qkv_total = qkv_total.transpose(0, 2, 1, 3).reshape(part, 3 * model).astype(F32)
    gain_parts = lax.psum(jnp.stack([ln1_part, ln2_part]), ("rep", "shard"))
    gain_parts = lax.dynamic_slice_in_dim(gain_parts, me * part, part, axis=1)
    return (
        output,
        input_grad,
        gain_parts[0],
        qkv_total,
        out_total,
        gain_parts[1],
        in_total,
        down_total,
    )


def solution(mesh):
    return jax.shard_map(
        shards,
        mesh=mesh,
        in_specs=(
            P(("rep", "shard"), None),
            P("rep", None),
            P("shard"),
            P("shard", None),
            P("shard", None),
            P("shard"),
            P("shard", None),
            P("shard", None),
            P(("rep", "shard"), None),
        ),
        out_specs=(
            P(("rep", "shard"), None),
            P(("rep", "shard"), None),
            P("shard"),
            P("shard", None),
            P("shard", None),
            P("shard"),
            P("shard", None),
            P("shard", None),
        ),
        check_vma=False,
    )
```

```python
import functools
import math

import jax
import jax.numpy as jnp
from jax import lax
from jax.experimental import pallas as pl
from jax.experimental.pallas import tpu as pltpu
from jax.sharding import PartitionSpec as P

HEADS = 16
HEAD_DIM = 64
HALF = 64
QB = 128
LANES = 128
EXTRA = 16

norm_epsilon = 1e-05
rope_base = 10000.0
masked_score = -1e30

F32 = jnp.float32
BF16 = jnp.bfloat16
VMEM_LIMIT = 52 << 20


def bits_of(axis):
    return lax.axis_size(axis).bit_length() - 1


def bit_of(axis, bit):
    return (lax.axis_index(axis) >> bit) & 1


def swap(x, axis, bit):
    size = lax.axis_size(axis)
    return lax.ppermute(x, axis, [(i, i ^ (1 << bit)) for i in range(size)])


def gather_list(x, axis):
    blocks = {0: x}
    for bit in reversed(range(bits_of(axis))):
        for j in list(blocks):
            blocks[j | 1 << bit] = swap(blocks[j], axis, bit)
    return [blocks[j] for j in range(len(blocks))]


def scatter_sum_list(blocks, axis):
    blocks = dict(enumerate(blocks))
    for bit in range(bits_of(axis)):
        for j in [j for j in blocks if j >> bit & 1]:
            got = swap(blocks.pop(j).astype(BF16), axis, bit)
            k = j ^ (1 << bit)
            blocks[k] = blocks[k].astype(F32) + got.astype(F32)
    return blocks[0]


def half_by_replica(x, dim, bit):
    shape = x.shape
    x = x.reshape(shape[:dim] + (2, shape[dim] // 2) + shape[dim + 1 :])
    return lax.dynamic_index_in_dim(x, bit_of("rep", bit), dim, keepdims=False)


def gather_weight(x, rep_bit):
    top = bits_of("shard") - 1
    got = swap(half_by_replica(x, 0, rep_bit), "shard", top)
    pieces = [(0, None, x), (1 << top, 0, got), (1 << top, 1, swap(got, "rep", rep_bit))]
    for bit in reversed(range(top)):
        pieces += [(j | 1 << bit, h, swap(a, "shard", bit)) for j, h, a in pieces]
    return pieces


def split_weight(x, rep_bit):
    me = lax.axis_index("shard")
    top = bits_of("shard") - 1

    def part_for(a, bit):
        start = ((me & (a.shape[0] - 1)) >> bit ^ 1) << bit
        return lax.dynamic_slice_in_dim(a, start, 1 << bit)

    got = swap(half_by_replica(part_for(x, top), 1, rep_bit), "shard", top)
    pieces = [(0, None, x), (1 << top, 0, got), (1 << top, 1, swap(got, "rep", rep_bit))]
    for bit in reversed(range(top)):
        pieces += [(j | 1 << bit, h, swap(part_for(a, bit), "shard", bit)) for j, h, a in pieces]
    return pieces


def replica_reduce(keep, send, order):
    for step, bit in enumerate(order):
        got = swap(send, "rep", bit)

        def total(a, b):
            return (keep[a:b].astype(F32) + got[a:b].astype(F32)).astype(BF16)

        size = keep.shape[0]
        if size == 1:
            return total(0, 1)[0]
        keep, send = total(0, size // 2), total(size // 2, size)


def replica_spread(x, order):
    now = x[None]
    for bit in reversed(order[1:]):
        now = jnp.concatenate([now, swap(now, "rep", bit)])
    return now, swap(now, "rep", order[0])


def turn(x, n):
    pieces = {0: x}
    for bit in reversed(range(n.bit_length() - 1)):
        for j in list(pieces):
            half = pieces[j].shape[0] // 2
            pieces[j | 1 << bit] = swap(pieces[j][half:], "shard", bit)
            pieces[j] = pieces[j][:half]
    return jnp.concatenate([pieces[j] for j in range(n)])


def slot_mask(slot, order):
    count = len(order)
    return sum(((slot >> (count - 1 - i)) & 1) << bit for i, bit in enumerate(order))


def slot_of(mask, order):
    count = len(order)
    return sum(((mask >> bit) & 1) << (count - 1 - i) for i, bit in enumerate(order))


def dot(a, b, dims):
    return lax.dot_general(a, b, (dims, ((), ())), preferred_element_type=F32)


def normalise(values):
    centred = values - jnp.mean(values, axis=-1, keepdims=True)
    scale = lax.rsqrt(jnp.mean(centred * centred, axis=-1, keepdims=True) + norm_epsilon)
    return centred * scale, scale


def weight_copies(pieces, refs, target, me, sems, rep, rep_bit, by_owner, rows):
    copies = []
    for i, ((j, half, shape), ref) in enumerate(zip(pieces, refs)):
        start = (me ^ j if by_owner else j) * rows
        count = rows
        if half is not None:
            count = rows // 2
            start = start + (((rep >> rep_bit) & 1) ^ half) * count
        source = ref.at[me & (shape[0] - 1)] if len(shape) == 3 else ref
        place = target.at[pl.ds(pl.multiple_of(start, count), count), :]
        copies.append(pltpu.make_async_copy(source, place, sems.at[i]))
    return copies


def partner(x):
    width = x.shape[-1]
    lane = lax.broadcasted_iota(jnp.int32, x.shape, 1)
    front = (lane % HEAD_DIM) < HEAD_DIM // 2
    return jnp.where(
        front,
        pltpu.roll(x, width - HEAD_DIM // 2, 1),
        pltpu.roll(x, HEAD_DIM // 2, 1),
    )


def head_masks(heads, width):
    lane = lax.broadcasted_iota(jnp.int32, (QB, width), 1) // HEAD_DIM
    return [lane == h for h in range(heads)]


def stack_heads(x, masks):
    x = x.astype(F32)
    return jnp.concatenate([jnp.where(m, x, 0.0) for m in masks], axis=0).astype(BF16)


def merge_heads(x, masks):
    total = None
    for h, m in enumerate(masks):
        part = jnp.where(m, x[h * QB : (h + 1) * QB], 0.0)
        total = part if total is None else total + part
    return total


def window_bias(ids_q, ids_k):
    row = lax.broadcasted_iota(jnp.int32, (QB, QB + 2 * HALF), 0)
    col = lax.broadcasted_iota(jnp.int32, (QB, QB + 2 * HALF), 1)
    ids_q = jnp.concatenate([ids_q] * ((QB + 2 * HALF) // LANES), axis=1)
    allowed = (col >= row) & (col <= row + 2 * HALF) & (ids_q == ids_k)
    return jnp.where(allowed, 0.0, masked_score)


def block_probs(stacked_q, keys, bias, heads):
    scores = dot(stacked_q, keys, ((1,), (1,)))
    rows, cols = scores.shape
    scores = (scores.reshape(heads, QB, cols) + bias[None]).reshape(rows, cols)
    weights = jnp.exp(scores - jnp.max(scores, axis=-1, keepdims=True))
    return weights * (1.0 / jnp.sum(weights, axis=-1, keepdims=True))


def column_chunk(ref, chunk, cols):
    if cols >= LANES:
        return ref[:, pl.ds(pl.multiple_of(chunk * cols, cols), cols)]
    per = LANES // cols
    tile = ref[:, pl.ds(pl.multiple_of(chunk // per * LANES, LANES), LANES)]
    result = tile
    for k in range(1, per):
        result = jnp.where(chunk % per == k, pltpu.roll(tile, LANES - k * cols, 1), result)
    return result


def row_chunk(ref, chunk, rows, start):
    if rows % 8 == 0:
        return ref[pl.ds(pl.multiple_of(chunk * rows, rows), rows), start : start + LANES]
    per = 8 // rows
    tile = ref[pl.ds(pl.multiple_of(chunk // per * 8, 8), 8), start : start + LANES]
    result = tile[:rows]
    for k in range(1, per):
        result = jnp.where(chunk % per == k, tile[k * rows : (k + 1) * rows], result)
    return result


def attention_kernel(
    pieces, rep_bit, n, heads, place_ref, gain_ref, cos_ref, sin_ref, idq_ref, idk_ref, *refs
):
    tok_refs, refs = refs[:n], refs[n:]
    piece_refs, refs = refs[: len(pieces)], refs[len(pieces) :]
    q_ref, k_ref, v_ref, out_ref, normed_ref, w_ref, sems = refs
    seq, width = q_ref.shape
    rows = seq // n
    me, rep = place_ref[0], place_ref[1]
    copies = weight_copies(
        pieces, piece_refs, w_ref, me, sems, rep, rep_bit, True, w_ref.shape[0] // n
    )
    for c in copies:
        c.start()
    edge = jnp.zeros((HALF, width), BF16)
    for ref in (k_ref, v_ref):
        ref[0:HALF, :] = edge
        ref[seq + HALF : seq + 2 * HALF, :] = edge
    for c in copies:
        c.wait()
    gain = gain_ref[0:1, :]
    for j in range(n):
        start = (me ^ j) * rows
        at = pl.ds(pl.multiple_of(start, rows), rows)
        shifted = pl.ds(pl.multiple_of(start + HALF, HALF), rows)
        hat, _ = normalise(tok_refs[j][...].astype(F32))
        normed = (hat * gain).astype(BF16)
        normed_ref[at, :] = normed
        qkv = jnp.dot(normed, w_ref[...], preferred_element_type=F32)
        cos, sin = cos_ref[at, :], sin_ref[at, :]
        q, k = qkv[:, 0:width], qkv[:, width : 2 * width]
        rotated = (q * cos + partner(q) * sin).astype(BF16)
        q_ref[at, :] = (rotated.astype(F32) * (1.0 / math.sqrt(HEAD_DIM))).astype(BF16)
        k_ref[shifted, :] = (k * cos + partner(k) * sin).astype(BF16)
        v_ref[shifted, :] = qkv[:, 2 * width : 3 * width].astype(BF16)
    masks = head_masks(heads, width)

    def attend(i, carry):
        at = pl.ds(pl.multiple_of(i * QB, QB), QB)
        window = pl.ds(pl.multiple_of(i * QB, QB), QB + 2 * HALF)
        bias = window_bias(idq_ref[at, :], idk_ref[0:1, window])
        probs = block_probs(stack_heads(q_ref[at, :], masks), k_ref[window, :], bias, heads)
        mixed = jnp.dot(probs.astype(BF16), v_ref[window, :], preferred_element_type=F32)
        out_ref[at, :] = merge_heads(mixed, masks).astype(BF16)
        return carry

    lax.fori_loop(0, seq // QB, attend, 0)


def feed_forward_kernel(out_pieces, in_pieces, out_bit, in_bit, n, place_ref, gain_ref, *refs):
    tok_refs, refs = refs[:n], refs[n:]
    cot_refs, refs = refs[:n], refs[n:]
    att_refs, refs = refs[:n], refs[n:]
    out_refs, refs = refs[: len(out_pieces)], refs[len(out_pieces) :]
    in_refs, refs = refs[: len(in_pieces)], refs[len(in_pieces) :]
    down_ref, hidden_out, normed_out, act_out, dup_out, ln_out, *refs = refs
    mlp_outs, refs = refs[:n], refs[n:]
    dnormed_outs, refs = refs[:n], refs[n:]
    tok, cot, att, w_out, w_in, w_down, hidden_own, normed, act, dup, mlp, dnormed = refs[:12]
    out_sems, in_sems, att_sems, tok_sems, cot_sems, down_sem, sems = refs[12:]
    me, rep = place_ref[0], place_ref[1]
    rows, model = tok_refs[0].shape
    padded = w_down.shape[0]
    given = down_ref.shape[0]
    if given != padded:
        w_down[given:padded, :] = jnp.zeros((padded - given, model), BF16)
    down_copy = pltpu.make_async_copy(down_ref, w_down.at[0:given, :], down_sem)
    copy = pltpu.make_async_copy
    att_copies = [copy(att_refs[j], att.at[j], att_sems.at[j]) for j in range(n)]
    tok_copies = [copy(tok_refs[j], tok.at[j], tok_sems.at[j]) for j in range(n)]
    cot_copies = [copy(cot_refs[j], cot.at[j], cot_sems.at[j]) for j in range(n)]
    part = model // n
    out_copies = weight_copies(out_pieces, out_refs, w_out, me, out_sems, rep, out_bit, False, part)
    in_copies = weight_copies(in_pieces, in_refs, w_in, me, in_sems, rep, in_bit, True, part)
    for c in att_copies + tok_copies[:1] + out_copies + in_copies + [down_copy]:
        c.start()
    for c in cot_copies[:1] + tok_copies[1:] + cot_copies[1:]:
        c.start()
    for c in att_copies + out_copies:
        c.wait()
    gain = gain_ref[1:2, :]
    ln_sum = jnp.zeros((1, model), F32)
    sent = []
    for j in range(n):
        at = pl.ds(pl.multiple_of((me ^ j) * rows, rows), rows)
        here = slice(j * rows, (j + 1) * rows)
        tok_copies[j].wait()
        hidden = tok[j].astype(F32)
        for i in range(n):
            hidden = hidden + jnp.dot(
                att[i, at, :], w_out[i * part : (i + 1) * part, :], preferred_element_type=F32
            )
        if j == 0:
            hidden_own[...] = hidden
        hat, _ = normalise(hidden)
        low = (hat * gain).astype(BF16)
        normed[here, :] = low
        if j == 0:
            for c in in_copies + [down_copy]:
                c.wait()
        up = jnp.dot(low, w_in[...], preferred_element_type=F32)
        gate, lin = up[:, :padded], up[:, padded:]
        phi = 0.5 + 0.5 * lax.erf(gate * (1.0 / math.sqrt(2.0)))
        gelu = gate * phi
        slope = phi + gate * jnp.exp(gate * gate * -0.5) * (1.0 / math.sqrt(2.0 * math.pi))
        act_low = (gelu * lin).astype(BF16)
        act[here, :] = act_low
        cot_copies[j].wait()
        dact = dot(cot[j], w_down[...], ((1,), (1,)))
        dup[here, :padded] = (dact * lin * slope).astype(BF16)
        dup[here, padded:] = (dact * gelu).astype(BF16)
        dlow = dot(dup[here, :], w_in[...], ((1,), (1,)))
        ln_sum = ln_sum + jnp.sum(dlow * hat, axis=0, keepdims=True)
        dnormed[j] = dlow.astype(BF16)
        mlp[j] = jnp.dot(act_low, w_down[...], preferred_element_type=F32).astype(BF16)
        sent += [
            copy(dnormed.at[j], dnormed_outs[j], sems.at[5 * j]),
            copy(mlp.at[j], mlp_outs[j], sems.at[5 * j + 1]),
            copy(normed.at[here, :], normed_out.at[here, :], sems.at[5 * j + 2]),
            copy(act.at[here, :], act_out.at[here, :], sems.at[5 * j + 3]),
            copy(dup.at[here, :], dup_out.at[here, :], sems.at[5 * j + 4]),
        ]
        for c in sent[-5:]:
            c.start()
    ln_out[...] = ln_sum
    sent.append(copy(hidden_own, hidden_out, sems.at[5 * n]))
    sent[-1].start()
    for c in sent:
        c.wait()


def store_slots(keep_ref, send_ref, rep, order, write):
    half = keep_ref.shape[0]
    for slot in range(2 * half):
        target = keep_ref if slot < half else send_ref
        write(target, slot % half, rep ^ slot_mask(slot, order))


def up_tiles(ff):
    return 2 * (ff // LANES) + 1


def weight_gradient_kernel(n, ff, near, far, place_ref, normed, dup, act, *refs):
    cot_refs, refs = refs[:n], refs[n:]
    in_keep, in_send, down_keep, down_send, in_sum, down_sum = refs
    me, rep = place_ref[0], place_ref[1]
    rows, model = cot_refs[0].shape
    part = model // n
    padded = act.shape[1]
    chunk = in_keep.shape[2]
    tiles = up_tiles(ff)
    whole, rest = ff // LANES, ff % LANES
    cols = model // (2 * in_keep.shape[0])
    total = None
    for j in range(n):
        term = dot(act[j * rows : (j + 1) * rows, :], cot_refs[j][...], ((0,), (0,)))
        total = term if total is None else total + term
    down_sum[...] = total

    def write_down(target, slot, c):
        target[slot] = column_chunk(down_sum, c, cols)[:ff].astype(BF16)

    store_slots(down_keep, down_send, rep, far, write_down)
    for owner in range(n):
        block = dot(normed[:, owner * part : (owner + 1) * part], dup[...], ((0,), (0,)))
        in_sum[:, : 2 * padded] = block
        first = block[:, whole * LANES : (whole + 1) * LANES]
        second = block[:, padded + whole * LANES : padded + (whole + 1) * LANES]
        lane = lax.broadcasted_iota(jnp.int32, first.shape, 1)
        both = jnp.where(lane < rest, first, pltpu.roll(second, rest, 1))
        in_sum[:, 2 * padded :] = both
        base = (me ^ owner) * tiles
        starts = [t * LANES for t in range(whole)] + [padded + t * LANES for t in range(whole)]
        starts.append(2 * padded)

        def write_in(target, slot, c):
            for t, s in enumerate(starts):
                target[slot, base + t] = row_chunk(in_sum, c, chunk, s).astype(BF16)

        store_slots(in_keep, in_send, rep, near, write_in)


def attention_back_kernel(n, heads, near, far, place_ref, *refs):
    dproj_refs, refs = refs[:n], refs[n:]
    w_out, att, q_ref, k_ref, v_ref, cos_ref, sin_ref, idq_ref, idk_ref, *refs = refs
    normed, w_qkv, gain_ref, ln2_ref, *refs = refs
    qkv_keep, qkv_send, out_keep, out_send, *refs = refs
    dnormed_refs, refs = refs[:n], refs[n:]
    da, dqkv, dk, dv, qkv_sum, out_sum = refs
    me, rep = place_ref[0], place_ref[1]
    seq, width = q_ref.shape
    rows, model = dproj_refs[0].shape
    part = model // n
    dk[...] = jnp.zeros_like(dk)
    dv[...] = jnp.zeros_like(dv)
    head_cols = heads * HEAD_DIM
    total = None
    for j in range(n):
        at = pl.ds(pl.multiple_of((me ^ j) * rows, rows), rows)
        dproj = dproj_refs[j][...]
        da[at, 0:head_cols] = dot(dproj, w_out[...], ((1,), (1,))).astype(BF16)
        term = dot(att[at, :], dproj, ((0,), (0,)))
        total = term if total is None else total + term
    if head_cols != width:
        da[:, head_cols:] = jnp.zeros((seq, width - head_cols), BF16)
    out_sum[0:part, :] = total[0:part]
    masks = head_masks(heads, width)

    def back(i, carry):
        at = pl.ds(pl.multiple_of(i * QB, QB), QB)
        window = pl.ds(pl.multiple_of(i * QB, QB), QB + 2 * HALF)
        bias = window_bias(idq_ref[at, :], idk_ref[0:1, window])
        queries = stack_heads(q_ref[at, :], masks)
        keys = k_ref[window, :]
        probs = block_probs(queries, keys, bias, heads)
        grads = stack_heads(da[at, :], masks)
        dprobs = dot(grads, v_ref[window, :], ((1,), (1,)))
        delta = jnp.sum(probs * dprobs, axis=-1, keepdims=True)
        dscores = (probs * (dprobs - delta)).astype(BF16)
        dq = merge_heads(jnp.dot(dscores, keys, preferred_element_type=F32), masks)
        dq = dq * (1.0 / math.sqrt(HEAD_DIM))
        cos, sin = cos_ref[at, :], sin_ref[at, :]
        dqkv[at, 0:width] = (dq * cos - partner(dq) * sin).astype(BF16)
        dk[window, :] += dot(dscores, queries, ((0,), (0,)))
        dv[window, :] += dot(probs.astype(BF16), grads, ((0,), (0,)))
        return carry

    lax.fori_loop(0, seq // QB, back, 0)

    def finish(i, carry):
        at = pl.ds(pl.multiple_of(i * QB, QB), QB)
        shifted = pl.ds(pl.multiple_of(i * QB + HALF, HALF), QB)
        cos, sin = cos_ref[at, :], sin_ref[at, :]
        g = dk[shifted, :]
        dqkv[at, width : 2 * width] = (g * cos - partner(g) * sin).astype(BF16)
        dqkv[at, 2 * width : 3 * width] = dv[shifted, :].astype(BF16)
        return carry

    lax.fori_loop(0, seq // QB, finish, 0)

    ln_sum = jnp.zeros((1, model), F32)
    for j in range(n):
        at = pl.ds(pl.multiple_of((me ^ j) * rows, rows), rows)
        dlow = dot(dqkv[at, :], w_qkv[...], ((1,), (1,)))
        ln_sum = ln_sum + jnp.sum(dlow * normed[at, :].astype(F32), axis=0, keepdims=True)
        dnormed_refs[j][...] = dlow.astype(BF16)
    pad = jnp.zeros((EXTRA - 2, model), F32)
    out_sum[part:, :] = jnp.concatenate([ln_sum / gain_ref[0:1, :], ln2_ref[...], pad])
    cols = model // (2 * out_keep.shape[0])

    def write_out(target, slot, c):
        target[slot] = column_chunk(out_sum, c, cols).astype(BF16)

    store_slots(out_keep, out_send, rep, far, write_out)
    chunk = qkv_keep.shape[2]
    tiles = 3 * width // LANES
    for owner in range(n):
        qkv_sum[...] = dot(normed[:, owner * part : (owner + 1) * part], dqkv[...], ((0,), (0,)))
        base = (me ^ owner) * tiles

        def write_qkv(target, slot, c):
            for t in range(tiles):
                target[slot, base + t] = row_chunk(qkv_sum, c, chunk, t * LANES).astype(BF16)

        store_slots(qkv_keep, qkv_send, rep, near, write_qkv)


def place_piece(canvas, piece, offset, valid):
    shift = offset % LANES
    height, size = piece.shape
    count = -(-(shift + valid) // LANES)
    if count * LANES > size:
        piece = jnp.concatenate([piece, jnp.zeros((height, count * LANES - size), F32)], axis=1)
    if shift:
        piece = pltpu.roll(piece, shift, 1)
    lane = lax.broadcasted_iota(jnp.int32, (height, LANES), 1)
    for t in range(count):
        tile = piece[:, t * LANES : (t + 1) * LANES]
        low, high = shift - t * LANES, shift + valid - t * LANES
        if low > 0 or high < LANES:
            tile = jnp.where((lane >= low) & (lane < high), tile, 0.0)
        index = offset // LANES + t
        canvas[index] = tile if index not in canvas else canvas[index] + tile


def columns_out_kernel(n, ff, head_cols, width, order, place_ref, now_ref, got_ref, out_ref):
    me, rep = place_ref[0], place_ref[1]
    half = now_ref.shape[0]
    slot = slot_of(rep ^ pl.program_id(0), order)
    tiles = now_ref.shape[1] // n
    at = slot & (half - 1)
    canvas = {}
    for owner in range(n):
        base = (me ^ owner) * tiles

        def tile(t):
            value = jnp.where(slot < half, now_ref[at, base + t], got_ref[at, base + t])
            return value.astype(F32)

        if ff:
            whole, rest = ff // LANES, ff % LANES
            last = tile(2 * whole)
            gate = jnp.concatenate([tile(t) for t in range(whole)] + [last], axis=1)
            last = pltpu.roll(last, LANES - rest, 1)
            lin = jnp.concatenate([tile(whole + t) for t in range(whole)] + [last], axis=1)
            place_piece(canvas, gate, owner * ff, ff)
            place_piece(canvas, lin, (n + owner) * ff, ff)
        else:
            per = width // LANES
            for b in range(3):
                piece = jnp.concatenate([tile(b * per + t) for t in range(per)], axis=1)
                place_piece(canvas, piece, (b * n + owner) * head_cols, head_cols)
    for index, value in canvas.items():
        out_ref[:, index * LANES : (index + 1) * LANES] = value


def columns_out(place, pair, n, model, cols, order, ff=0, head_cols=0, width=0):
    now, got = pair
    chunk = now.shape[2]
    full = pl.BlockSpec(now.shape, lambda i: (0, 0, 0, 0))
    return pl.pallas_call(
        functools.partial(columns_out_kernel, n, ff, head_cols, width, order),
        grid=(2 * now.shape[0],),
        in_specs=[pl.BlockSpec(memory_space=pltpu.SMEM), full, full],
        out_specs=pl.BlockSpec((None, chunk, cols), lambda i: (i, 0, 0)),
        out_shape=jax.ShapeDtypeStruct((2 * now.shape[0], chunk, cols), F32),
        compiler_params=pltpu.CompilerParams(vmem_limit_bytes=32 << 20),
        name="columns_out",
    )(place, now, got).reshape(model // n, cols)


def rows_out_kernel(order, cols, place_ref, now_ref, got_ref, out_ref):
    rep = place_ref[1]
    half = now_ref.shape[0]

    def chunk(c):
        slot = slot_of(rep ^ c, order)
        at = slot & (half - 1)
        return jnp.where(slot < half, now_ref[at], got_ref[at]).astype(F32)

    if cols >= LANES:
        for c in range(2 * half):
            out_ref[:, c * cols : (c + 1) * cols] = chunk(c)
    else:
        per = LANES // cols
        lane = lax.broadcasted_iota(jnp.int32, out_ref.shape[:1] + (LANES,), 1) // cols
        for t in range(2 * half // per):
            value = chunk(per * t)
            for k in range(1, per):
                value = jnp.where(lane == k, pltpu.roll(chunk(per * t + k), k * cols, 1), value)
            out_ref[:, t * LANES : (t + 1) * LANES] = value


def rows_out(place, pair, model, order):
    now, got = pair
    return pl.pallas_call(
        functools.partial(rows_out_kernel, order, model // (2 * now.shape[0])),
        in_specs=[
            pl.BlockSpec(memory_space=pltpu.SMEM),
            pl.BlockSpec(memory_space=pltpu.VMEM),
            pl.BlockSpec(memory_space=pltpu.VMEM),
        ],
        out_shape=jax.ShapeDtypeStruct((now.shape[1], model), F32),
        compiler_params=pltpu.CompilerParams(vmem_limit_bytes=32 << 20),
        name="rows_out",
    )(place, now, got)


SMEM_SPEC = pl.BlockSpec(memory_space=pltpu.SMEM)
VMEM_SPEC = pl.BlockSpec(memory_space=pltpu.VMEM)
ANY_SPEC = pl.BlockSpec(memory_space=pl.ANY)


def norm_backward(grad_hat, normed, scale):
    return (
        grad_hat
        - jnp.mean(grad_hat, axis=-1, keepdims=True)
        - normed * jnp.mean(grad_hat * normed, axis=-1, keepdims=True)
    ) * scale


def after(value, *earlier):
    return lax.optimization_barrier((value,) + earlier)[0]


def shards(tokens, segment_ids, ln1_gain, w_qkv, w_out, ln2_gain, w_in, w_down, cotangent):
    n = lax.axis_size("shard")
    replicas = lax.axis_size("rep")
    me = lax.axis_index("shard")
    place = jnp.stack([me, lax.axis_index("rep")]).astype(jnp.int32)
    rows, model = tokens.shape
    seq = rows * n
    part = model // n
    ff = w_down.shape[0]
    heads = HEADS // n
    head_cols = heads * HEAD_DIM
    width = max(LANES, head_cols)
    padded = -(-ff // LANES) * LANES
    near = list(range(bits_of("rep")))
    far = near[1:] + near[:1]
    shape = jax.ShapeDtypeStruct
    params = pltpu.CompilerParams(vmem_limit_bytes=VMEM_LIMIT)

    toks = gather_list(tokens, "shard")
    gains = gather_list(jnp.stack([ln1_gain, ln2_gain]), "shard")
    gains = jnp.stack(gains)[me ^ jnp.arange(n)].transpose(1, 0, 2).reshape(2, model).astype(F32)

    qkv_to = w_qkv.reshape(part, 3, n, head_cols).transpose(2, 0, 1, 3)
    qkv_to = jnp.pad(qkv_to, ((0, 0), (0, 0), (0, 0), (0, width - head_cols)))
    qkv_pieces = split_weight(qkv_to.reshape(n, part, 3 * width), 0)
    in_to = w_in.reshape(part, 2, n, ff).transpose(2, 0, 1, 3)
    in_to = jnp.pad(in_to, ((0, 0), (0, 0), (0, 0), (0, padded - ff)))
    first_done = [a for j, _, a in qkv_pieces if j == n // 2] + [toks[n // 2]]
    out_pieces = gather_weight(after(w_out, *first_done), 0)
    in_pieces = split_weight(after(in_to.reshape(n, part, 2 * padded), *first_done), 1)
    later = [a for j, h, a in in_pieces if j == n // 2 and h == 0]
    cots = gather_list(after(cotangent, *later), "shard")

    lane = jnp.arange(width, dtype=jnp.int32) % HEAD_DIM
    half = HEAD_DIM // 2
    frequency = jnp.exp(-math.log(rope_base) * 2.0 * (lane % half).astype(F32) / HEAD_DIM)
    angles = jnp.arange(seq, dtype=F32)[:, None] * frequency[None, :]
    sign = jnp.where(lane < half, -1.0, 1.0)
    ids = segment_ids[0]
    tables = (
        jnp.cos(angles),
        jnp.sin(angles) * sign[None, :],
        jnp.broadcast_to(ids[:, None], (seq, LANES)),
        jnp.pad(ids, (HALF, HALF), constant_values=-1)[None],
    )

    def about(pieces):
        return [(j, h, a.shape) for j, h, a in pieces]

    queries, keys, values, attended, normed1, qkv_w = pl.pallas_call(
        functools.partial(attention_kernel, about(qkv_pieces), 0, n, heads),
        in_specs=[SMEM_SPEC] + [VMEM_SPEC] * (5 + n) + [ANY_SPEC] * len(qkv_pieces),
        out_shape=(
            shape((seq, width), BF16),
            shape((seq + 2 * HALF, width), BF16),
            shape((seq + 2 * HALF, width), BF16),
            shape((seq, width), BF16),
            shape((seq, model), BF16),
            shape((model, 3 * width), BF16),
        ),
        scratch_shapes=[pltpu.SemaphoreType.DMA((len(qkv_pieces),))],
        compiler_params=params,
        name="attention",
    )(place, gains, *tables, *toks, *[a for _, _, a in qkv_pieces])

    atts = gather_list(attended[:, :head_cols], "shard")
    blocks = [shape((rows, model), BF16)] * n
    hidden, normed2, act, dup, ln2_part, *mixed = pl.pallas_call(
        functools.partial(
            feed_forward_kernel, about(out_pieces), about(in_pieces), 0, 1, n
        ),
        in_specs=[SMEM_SPEC, VMEM_SPEC]
        + [ANY_SPEC] * (3 * n + len(out_pieces) + len(in_pieces) + 1),
        out_specs=[ANY_SPEC] * 4 + [VMEM_SPEC] + [ANY_SPEC] * (2 * n),
        out_shape=[
            shape((rows, model), F32),
            shape((seq, model), BF16),
            shape((seq, padded), BF16),
            shape((seq, 2 * padded), BF16),
            shape((1, model), F32),
        ]
        + blocks * 2,
        scratch_shapes=[
            pltpu.VMEM((n, rows, model), BF16),
            pltpu.VMEM((n, rows, model), BF16),
            pltpu.VMEM((n, seq, head_cols), BF16),
            pltpu.VMEM((model, model), BF16),
            pltpu.VMEM((model, 2 * padded), BF16),
            pltpu.VMEM((padded, model), BF16),
            pltpu.VMEM((rows, model), F32),
            pltpu.VMEM((seq, model), BF16),
            pltpu.VMEM((seq, padded), BF16),
            pltpu.VMEM((seq, 2 * padded), BF16),
            pltpu.VMEM((n, rows, model), BF16),
            pltpu.VMEM((n, rows, model), BF16),
            pltpu.SemaphoreType.DMA((len(out_pieces),)),
            pltpu.SemaphoreType.DMA((len(in_pieces),)),
            pltpu.SemaphoreType.DMA((n,)),
            pltpu.SemaphoreType.DMA((n,)),
            pltpu.SemaphoreType.DMA((n,)),
            pltpu.SemaphoreType.DMA,
            pltpu.SemaphoreType.DMA((5 * n + 1,)),
        ],
        compiler_params=params,
        name="feed_forward",
    )(
        place,
        gains,
        *toks,
        *cots,
        *atts,
        *[a for _, _, a in out_pieces],
        *[a for _, _, a in in_pieces],
        jnp.pad(w_down, ((0, -ff % 16), (0, 0))),
    )
    mlp_blocks, dnormed2_blocks = mixed[:n], mixed[n:]

    dnormed2 = scatter_sum_list(dnormed2_blocks, "shard")
    hat2, scale2 = normalise(hidden)
    dhidden = cotangent.astype(F32) + norm_backward(dnormed2 * gains[1], hat2, scale2)
    dprojs = gather_list(dhidden.astype(BF16), "shard")

    slots = replicas // 2
    chunk = part // replicas
    lanes = max(LANES, model // replicas)
    tiles = up_tiles(ff)
    in_shape = shape((slots, n * tiles, chunk, LANES), BF16)
    down_shape = shape((slots, ff, lanes), BF16)
    in_keep, in_send, down_keep, down_send = pl.pallas_call(
        functools.partial(weight_gradient_kernel, n, ff, near, far),
        in_specs=[SMEM_SPEC] + [VMEM_SPEC] * (3 + n),
        out_shape=(in_shape, in_shape, down_shape, down_shape),
        scratch_shapes=[
            pltpu.VMEM((part, 2 * padded + LANES), F32),
            pltpu.VMEM((padded, model), F32),
        ],
        compiler_params=params,
        name="weight_gradient",
    )(place, normed2, dup, act, *cots)

    mlp = scatter_sum_list(mlp_blocks, "shard")
    output = (hidden + mlp).astype(BF16)

    qkv_tiles = 3 * width // LANES
    qkv_shape = shape((slots, n * qkv_tiles, chunk, LANES), BF16)
    out_shape = shape((slots, part + EXTRA, lanes), BF16)
    qkv_keep, qkv_send, out_keep, out_send, *dnormed1_blocks = pl.pallas_call(
        functools.partial(attention_back_kernel, n, heads, near, far),
        in_specs=[SMEM_SPEC] + [VMEM_SPEC] * (n + 13),
        out_shape=[qkv_shape, qkv_shape, out_shape, out_shape] + blocks,
        scratch_shapes=[
            pltpu.VMEM((seq, width), BF16),
            pltpu.VMEM((seq, 3 * width), BF16),
            pltpu.VMEM((seq + 2 * HALF, width), F32),
            pltpu.VMEM((seq + 2 * HALF, width), F32),
            pltpu.VMEM((part, 3 * width), F32),
            pltpu.VMEM((part + EXTRA, model), F32),
        ],
        compiler_params=params,
        name="attention_back",
    )(
        place,
        *dprojs,
        w_out,
        attended,
        queries,
        keys,
        values,
        *tables,
        normed1,
        qkv_w,
        gains,
        ln2_part,
    )

    dnormed1 = scatter_sum_list(dnormed1_blocks, "shard")
    hat1, scale1 = normalise(tokens.astype(F32))
    input_grad = dhidden + norm_backward(dnormed1 * gains[0], hat1, scale1)

    def columns_pair(keep, send, tiles):
        share = replica_reduce(keep, send, near)
        share = turn(share.reshape(n, tiles, chunk, LANES), n)
        return replica_spread(share.reshape(n * tiles, chunk, LANES), near)

    in_pair = columns_pair(in_keep, in_send, tiles)
    down_pair = replica_spread(replica_reduce(down_keep, down_send, far), far)
    out_share = replica_reduce(out_keep, out_send, far)
    ln_share = out_share[part:]
    for bit in range(bits_of("shard")):
        ln_share = (ln_share.astype(F32) + swap(ln_share, "shard", bit).astype(F32)).astype(BF16)
    out_pair = replica_spread(jnp.concatenate([out_share[:part], ln_share]), far)
    qkv_pair = columns_pair(qkv_keep, qkv_send, qkv_tiles)

    in_total = columns_out(place, in_pair, n, model, 2 * n * ff, near, ff=ff)
    down_total = rows_out(place, down_pair, model, far)
    qkv_total = columns_out(
        place, qkv_pair, n, model, 3 * model, near, head_cols=head_cols, width=width
    )
    out_total = rows_out(place, out_pair, model, far)
    ln_own = lax.dynamic_slice_in_dim(out_total[part : part + 2], me * part, part, axis=1)
    return (
        output,
        input_grad,
        ln_own[0],
        qkv_total,
        out_total[:part],
        ln_own[1],
        in_total,
        down_total,
    )


def solution(mesh):
    return jax.shard_map(
        shards,
        mesh=mesh,
        in_specs=(
            P(("rep", "shard"), None),
            P("rep", None),
            P("shard"),
            P("shard", None),
            P("shard", None),
            P("shard"),
            P("shard", None),
            P("shard", None),
            P(("rep", "shard"), None),
        ),
        out_specs=(
            P(("rep", "shard"), None),
            P(("rep", "shard"), None),
            P("shard"),
            P("shard", None),
            P("shard", None),
            P("shard"),
            P("shard", None),
            P("shard", None),
        ),
        check_vma=False,
    )
```

```python
import functools
import math

import jax
import jax.numpy as jnp
from jax import lax
from jax.experimental import pallas as pl
from jax.experimental.pallas import tpu as pltpu
from jax.sharding import PartitionSpec as P

HEADS = 16
HEAD_DIM = 64
HALF = 64
QB = 128
LANES = 128

norm_epsilon = 1e-05
rope_base = 10000.0
masked_score = -1e30

F32 = jnp.float32
BF16 = jnp.bfloat16
VMEM_LIMIT = 52 << 20


def bits_of(axis):
    return lax.axis_size(axis).bit_length() - 1


def bit_of(axis, bit):
    return (lax.axis_index(axis) >> bit) & 1


def swap(x, axis, bit):
    size = lax.axis_size(axis)
    return lax.ppermute(x, axis, [(i, i ^ (1 << bit)) for i in range(size)])


def gather_list(x, axis):
    blocks = {0: x}
    for bit in reversed(range(bits_of(axis))):
        for j in list(blocks):
            blocks[j | 1 << bit] = swap(blocks[j], axis, bit)
    return [blocks[j] for j in range(len(blocks))]


def scatter_bits(blocks, axis, bits):
    blocks = dict(blocks)
    for bit in bits:
        for j in [j for j in blocks if j >> bit & 1]:
            got = swap(blocks.pop(j).astype(BF16), axis, bit)
            k = j ^ (1 << bit)
            blocks[k] = blocks[k].astype(F32) + got.astype(F32)
    return blocks


def scatter_sum_list(blocks, axis):
    return scatter_bits(enumerate(blocks), axis, range(bits_of(axis)))[0]


def half_by_replica(x, dim, bit):
    shape = x.shape
    x = x.reshape(shape[:dim] + (2, shape[dim] // 2) + shape[dim + 1 :])
    return lax.dynamic_index_in_dim(x, bit_of("rep", bit), dim, keepdims=False)


def gather_weight(x, rep_bit):
    top = bits_of("shard") - 1
    got = swap(half_by_replica(x, 0, rep_bit), "shard", top)
    pieces = [(0, None, x), (1 << top, 0, got), (1 << top, 1, swap(got, "rep", rep_bit))]
    for bit in reversed(range(top)):
        pieces += [(j | 1 << bit, h, swap(a, "shard", bit)) for j, h, a in pieces]
    return pieces


def split_weight(x, rep_bit):
    me = lax.axis_index("shard")
    top = bits_of("shard") - 1

    def part_for(a, bit):
        start = ((me & (a.shape[0] - 1)) >> bit ^ 1) << bit
        return lax.dynamic_slice_in_dim(a, start, 1 << bit)

    got = swap(half_by_replica(part_for(x, top), 1, rep_bit), "shard", top)
    pieces = [(0, None, x), (1 << top, 0, got), (1 << top, 1, swap(got, "rep", rep_bit))]
    for bit in reversed(range(top)):
        pieces += [(j | 1 << bit, h, swap(part_for(a, bit), "shard", bit)) for j, h, a in pieces]
    return pieces


def replica_reduce(keep, send, order, gates=()):
    for step, bit in enumerate(order):
        got = swap(send, "rep", bit)
        if step < len(gates):
            got = after(got, gates[step])

        def total(a, b):
            return (keep[a:b].astype(F32) + got[a:b].astype(F32)).astype(BF16)

        size = keep.shape[0]
        if size == 1:
            return total(0, 1)[0]
        keep, send = total(0, size // 2), total(size // 2, size)


def replica_spread(x, order):
    now = x[None]
    for bit in reversed(order[1:]):
        now = jnp.concatenate([now, swap(now, "rep", bit)])
    return now, swap(now, "rep", order[0])


def turn(x, n):
    pieces = {0: x}
    for bit in reversed(range(n.bit_length() - 1)):
        for j in list(pieces):
            half = pieces[j].shape[0] // 2
            pieces[j | 1 << bit] = swap(pieces[j][half:], "shard", bit)
            pieces[j] = pieces[j][:half]
    return jnp.concatenate([pieces[j] for j in range(n)])


def slot_mask(slot, order):
    count = len(order)
    return sum(((slot >> (count - 1 - i)) & 1) << bit for i, bit in enumerate(order))


def slot_of(mask, order):
    count = len(order)
    return sum(((mask >> bit) & 1) << (count - 1 - i) for i, bit in enumerate(order))


def dot(a, b, dims):
    return lax.dot_general(a, b, (dims, ((), ())), preferred_element_type=F32)


def normalise(values):
    centred = values - jnp.mean(values, axis=-1, keepdims=True)
    scale = lax.rsqrt(jnp.mean(centred * centred, axis=-1, keepdims=True) + norm_epsilon)
    return centred * scale, scale


def weight_copies(pieces, refs, target, me, sems, rep, rep_bit, by_owner, rows):
    copies = []
    for i, ((j, half, shape), ref) in enumerate(zip(pieces, refs)):
        start = (me ^ j if by_owner else j) * rows
        count = rows
        if half is not None:
            count = rows // 2
            start = start + (((rep >> rep_bit) & 1) ^ half) * count
        source = ref.at[me & (shape[0] - 1)] if len(shape) == 3 else ref
        place = target.at[pl.ds(pl.multiple_of(start, count), count), :]
        copies.append(pltpu.make_async_copy(source, place, sems.at[i]))
    return copies


def partner(x):
    width = x.shape[-1]
    lane = lax.broadcasted_iota(jnp.int32, x.shape, 1)
    front = (lane % HEAD_DIM) < HEAD_DIM // 2
    return jnp.where(
        front,
        pltpu.roll(x, width - HEAD_DIM // 2, 1),
        pltpu.roll(x, HEAD_DIM // 2, 1),
    )


def head_masks(heads, width):
    lane = lax.broadcasted_iota(jnp.int32, (QB, width), 1) // HEAD_DIM
    return [lane == h for h in range(heads)]


def stack_heads(x, masks):
    x = x.astype(F32)
    return jnp.concatenate([jnp.where(m, x, 0.0) for m in masks], axis=0).astype(BF16)


def merge_heads(x, masks):
    total = None
    for h, m in enumerate(masks):
        part = jnp.where(m, x[h * QB : (h + 1) * QB], 0.0)
        total = part if total is None else total + part
    return total


def window_bias(ids_q, ids_k):
    row = lax.broadcasted_iota(jnp.int32, (QB, QB + 2 * HALF), 0)
    col = lax.broadcasted_iota(jnp.int32, (QB, QB + 2 * HALF), 1)
    ids_q = jnp.concatenate([ids_q] * ((QB + 2 * HALF) // LANES), axis=1)
    allowed = (col >= row) & (col <= row + 2 * HALF) & (ids_q == ids_k)
    return jnp.where(allowed, 0.0, masked_score)


def block_probs(stacked_q, keys, bias, heads):
    scores = dot(stacked_q, keys, ((1,), (1,)))
    rows, cols = scores.shape
    scores = (scores.reshape(heads, QB, cols) + bias[None]).reshape(rows, cols)
    weights = jnp.exp(scores - jnp.max(scores, axis=-1, keepdims=True))
    return weights * (1.0 / jnp.sum(weights, axis=-1, keepdims=True))


def column_chunk(ref, chunk, cols):
    if cols >= LANES:
        return ref[:, pl.ds(pl.multiple_of(chunk * cols, cols), cols)]
    per = LANES // cols
    tile = ref[:, pl.ds(pl.multiple_of(chunk // per * LANES, LANES), LANES)]
    result = tile
    for k in range(1, per):
        result = jnp.where(chunk % per == k, pltpu.roll(tile, LANES - k * cols, 1), result)
    return result


def row_chunk(ref, chunk, rows, start):
    if rows % 8 == 0:
        return ref[pl.ds(pl.multiple_of(chunk * rows, rows), rows), start : start + LANES]
    per = 8 // rows
    tile = ref[pl.ds(pl.multiple_of(chunk // per * 8, 8), 8), start : start + LANES]
    result = tile[:rows]
    for k in range(1, per):
        result = jnp.where(chunk % per == k, tile[k * rows : (k + 1) * rows], result)
    return result


def take_columns(ref, offset, valid, size):
    begin = offset // LANES * LANES
    end = -(-(offset + valid) // LANES) * LANES
    x = ref[:, begin:end].astype(F32)
    if offset != begin:
        x = pltpu.roll(x, end - offset, 1)
    x = x[:, :size]
    if valid != size:
        lane = lax.broadcasted_iota(jnp.int32, x.shape, 1)
        x = jnp.where(lane < valid, x, 0.0)
    return x


def split_kernel(n, blocks, valid, size, gain_ref, w_ref, out_ref):
    gain = gain_ref[...]
    for owner in range(n):
        for b in range(blocks):
            x = take_columns(w_ref, (b * n + owner) * valid, valid, size)
            out_ref[owner, :, b * size : (b + 1) * size] = (x * gain).astype(BF16)


def split_columns(w, gain, n, blocks, valid, size):
    rows, cols = w.shape
    step = min(rows, 64)
    return pl.pallas_call(
        functools.partial(split_kernel, n, blocks, valid, size),
        grid=(rows // step,),
        in_specs=[
            pl.BlockSpec((step, 1), lambda i: (i, 0)),
            pl.BlockSpec((step, cols), lambda i: (i, 0)),
        ],
        out_specs=pl.BlockSpec((n, step, blocks * size), lambda i: (0, i, 0)),
        out_shape=jax.ShapeDtypeStruct((n, rows, blocks * size), BF16),
        compiler_params=pltpu.CompilerParams(vmem_limit_bytes=24 << 20),
        name="split_columns",
    )(gain, w)


def attention_kernel(
    pieces, rep_bit, n, heads, place_ref, cos_ref, sin_ref, idq_ref, idk_ref, *refs
):
    tok_refs, refs = refs[:n], refs[n:]
    piece_refs, refs = refs[: len(pieces)], refs[len(pieces) :]
    q_ref, k_ref, v_ref, out_ref, normed_ref, w_ref, sems = refs
    seq, width = q_ref.shape
    rows = seq // n
    me, rep = place_ref[0], place_ref[1]
    copies = weight_copies(
        pieces, piece_refs, w_ref, me, sems, rep, rep_bit, True, w_ref.shape[0] // n
    )
    for c in copies:
        c.start()
    edge = jnp.zeros((HALF, width), BF16)
    for ref in (k_ref, v_ref):
        ref[0:HALF, :] = edge
        ref[seq + HALF : seq + 2 * HALF, :] = edge
    for c in copies:
        c.wait()
    for j in range(n):
        start = (me ^ j) * rows
        at = pl.ds(pl.multiple_of(start, rows), rows)
        shifted = pl.ds(pl.multiple_of(start + HALF, HALF), rows)
        hat, _ = normalise(tok_refs[j][...].astype(F32))
        normed = hat.astype(BF16)
        normed_ref[at, :] = normed
        qkv = jnp.dot(normed, w_ref[...], preferred_element_type=F32)
        cos, sin = cos_ref[at, :], sin_ref[at, :]
        q, k = qkv[:, 0:width], qkv[:, width : 2 * width]
        rotated = (q * cos + partner(q) * sin).astype(BF16)
        q_ref[at, :] = (rotated.astype(F32) * (1.0 / math.sqrt(HEAD_DIM))).astype(BF16)
        k_ref[shifted, :] = (k * cos + partner(k) * sin).astype(BF16)
        v_ref[shifted, :] = qkv[:, 2 * width : 3 * width].astype(BF16)
    masks = head_masks(heads, width)

    def attend(i, carry):
        at = pl.ds(pl.multiple_of(i * QB, QB), QB)
        window = pl.ds(pl.multiple_of(i * QB, QB), QB + 2 * HALF)
        bias = window_bias(idq_ref[at, :], idk_ref[0:1, window])
        probs = block_probs(stack_heads(q_ref[at, :], masks), k_ref[window, :], bias, heads)
        mixed = jnp.dot(probs.astype(BF16), v_ref[window, :], preferred_element_type=F32)
        out_ref[at, :] = merge_heads(mixed, masks).astype(BF16)
        return carry

    lax.fori_loop(0, seq // QB, attend, 0)


def feed_forward_kernel(out_pieces, in_pieces, out_bit, in_bit, n, place_ref, *refs):
    tok_refs, refs = refs[:n], refs[n:]
    cot_refs, refs = refs[:n], refs[n:]
    att_refs, refs = refs[:n], refs[n:]
    out_refs, refs = refs[: len(out_pieces)], refs[len(out_pieces) :]
    in_refs, refs = refs[: len(in_pieces)], refs[len(in_pieces) :]
    down_ref, hidden_out, normed_out, act_out, dup_out, *refs = refs
    dnormed_outs, refs = refs[:n], refs[n:]
    tok, cot, att, w_out, w_in, w_down, hidden_own, normed, act, dup, dnormed = refs[:11]
    out_sems, in_sems, att_sems, tok_sems, cot_sems, down_sem, sems = refs[11:]
    me, rep = place_ref[0], place_ref[1]
    rows, model = tok_refs[0].shape
    padded = w_down.shape[0]
    given = down_ref.shape[0]
    if given != padded:
        w_down[given:padded, :] = jnp.zeros((padded - given, model), BF16)
    down_copy = pltpu.make_async_copy(down_ref, w_down.at[0:given, :], down_sem)
    copy = pltpu.make_async_copy
    att_copies = [copy(att_refs[j], att.at[j], att_sems.at[j]) for j in range(n)]
    tok_copies = [copy(tok_refs[j], tok.at[j], tok_sems.at[j]) for j in range(n)]
    cot_copies = [copy(cot_refs[j], cot.at[j], cot_sems.at[j]) for j in range(n)]
    part = model // n
    out_copies = weight_copies(out_pieces, out_refs, w_out, me, out_sems, rep, out_bit, False, part)
    in_copies = weight_copies(in_pieces, in_refs, w_in, me, in_sems, rep, in_bit, True, part)
    for c in att_copies + tok_copies[:1] + out_copies + in_copies + [down_copy]:
        c.start()
    for c in cot_copies[:1] + tok_copies[1:] + cot_copies[1:]:
        c.start()
    for c in att_copies + out_copies:
        c.wait()
    sent = []
    for j in range(n):
        at = pl.ds(pl.multiple_of((me ^ j) * rows, rows), rows)
        here = slice(j * rows, (j + 1) * rows)
        tok_copies[j].wait()
        hidden = tok[j].astype(F32)
        for i in range(n):
            hidden = hidden + jnp.dot(
                att[i, at, :], w_out[i * part : (i + 1) * part, :], preferred_element_type=F32
            )
        if j == 0:
            hidden_own[...] = hidden
        hat, _ = normalise(hidden)
        low = hat.astype(BF16)
        normed[here, :] = low
        if j == 0:
            for c in in_copies + [down_copy]:
                c.wait()
        up = jnp.dot(low, w_in[...], preferred_element_type=F32)
        gate, lin = up[:, :padded], up[:, padded:]
        phi = 0.5 + 0.5 * lax.erf(gate * (1.0 / math.sqrt(2.0)))
        gelu = gate * phi
        slope = phi + gate * jnp.exp(gate * gate * -0.5) * (1.0 / math.sqrt(2.0 * math.pi))
        act_low = (gelu * lin).astype(BF16)
        act[here, :] = act_low
        cot_copies[j].wait()
        dact = dot(cot[j], w_down[...], ((1,), (1,)))
        dup[here, :padded] = (dact * lin * slope).astype(BF16)
        dup[here, padded:] = (dact * gelu).astype(BF16)
        dnormed[j] = dot(dup[here, :], w_in[...], ((1,), (1,))).astype(BF16)
        sent += [
            copy(dnormed.at[j], dnormed_outs[j], sems.at[4 * j]),
            copy(normed.at[here, :], normed_out.at[here, :], sems.at[4 * j + 1]),
            copy(act.at[here, :], act_out.at[here, :], sems.at[4 * j + 2]),
            copy(dup.at[here, :], dup_out.at[here, :], sems.at[4 * j + 3]),
        ]
        for c in sent[-4:]:
            c.start()
    sent.append(copy(hidden_own, hidden_out, sems.at[4 * n]))
    sent[-1].start()
    for c in sent:
        c.wait()


def store_slots(keep_ref, send_ref, rep, order, write):
    half = keep_ref.shape[0]
    for slot in range(2 * half):
        target = keep_ref if slot < half else send_ref
        write(target, slot % half, rep ^ slot_mask(slot, order))


def up_tiles(ff):
    return 2 * (ff // LANES) + 1


def down_kernel(n, ff, far, place_ref, act, w_down, *refs):
    cot_refs, refs = refs[:n], refs[n:]
    keep, send, *refs = refs
    mlp_refs, refs = refs[:n], refs[n:]
    (down_sum,) = refs
    rows, model = cot_refs[0].shape
    cols = model // (2 * keep.shape[0])
    total = None
    for j in range(n):
        term = dot(act[j * rows : (j + 1) * rows, :], cot_refs[j][...], ((0,), (0,)))
        total = term if total is None else total + term
    down_sum[...] = total

    def write(target, slot, c):
        target[slot] = column_chunk(down_sum, c, cols)[:ff].astype(BF16)

    store_slots(keep, send, place_ref[1], far, write)
    given = w_down.shape[0]
    for j in range(n):
        low = act[j * rows : (j + 1) * rows, 0:given]
        mlp_refs[j][...] = jnp.dot(low, w_down[...], preferred_element_type=F32).astype(BF16)


def in_kernel(n, ff, near, place_ref, normed, dup, keep, send, in_sum):
    me, rep = place_ref[0], place_ref[1]
    part = normed.shape[1] // n
    padded = dup.shape[1] // 2
    chunk = keep.shape[2]
    tiles = up_tiles(ff)
    whole, rest = ff // LANES, ff % LANES
    for owner in range(n):
        block = dot(normed[:, owner * part : (owner + 1) * part], dup[...], ((0,), (0,)))
        in_sum[:, : 2 * padded] = block
        first = block[:, whole * LANES : (whole + 1) * LANES]
        second = block[:, padded + whole * LANES : padded + (whole + 1) * LANES]
        lane = lax.broadcasted_iota(jnp.int32, first.shape, 1)
        both = jnp.where(lane < rest, first, pltpu.roll(second, rest, 1))
        in_sum[:, 2 * padded :] = both
        base = (me ^ owner) * tiles
        starts = [t * LANES for t in range(whole)] + [padded + t * LANES for t in range(whole)]
        starts.append(2 * padded)

        def write(target, slot, c):
            for t, s in enumerate(starts):
                target[slot, base + t] = row_chunk(in_sum, c, chunk, s).astype(BF16)

        store_slots(keep, send, rep, near, write)


def add_kernel(a_ref, b_ref, c_ref, d_ref, mine_ref, other_ref):
    mine_ref[...] = a_ref[...].astype(F32) + b_ref[...].astype(F32)
    other_ref[...] = (c_ref[...].astype(F32) + d_ref[...].astype(F32)).astype(BF16)


def norm_back_kernel(mine, got, hidden, cotangent, dhidden, dproj):
    hat, scale = normalise(hidden[...])
    e = mine[...] + got[...].astype(F32)
    value = cotangent[...].astype(F32) + norm_backward(e, hat, scale)
    dhidden[...] = value
    dproj[...] = value.astype(BF16)


def attention_back_kernel(n, heads, far, place_ref, *refs):
    dproj_refs, refs = refs[:n], refs[n:]
    w_out, att, q_ref, k_ref, v_ref, cos_ref, sin_ref, idq_ref, idk_ref, *refs = refs
    dqkv, out_keep, out_send, da, dk, dv, out_sum = refs
    me, rep = place_ref[0], place_ref[1]
    seq, width = q_ref.shape
    rows, model = dproj_refs[0].shape
    part = model // n
    dk[...] = jnp.zeros_like(dk)
    dv[...] = jnp.zeros_like(dv)
    head_cols = heads * HEAD_DIM
    total = None
    for j in range(n):
        at = pl.ds(pl.multiple_of((me ^ j) * rows, rows), rows)
        dproj = dproj_refs[j][...]
        da[at, 0:head_cols] = dot(dproj, w_out[...], ((1,), (1,))).astype(BF16)
        term = dot(att[at, :], dproj, ((0,), (0,)))
        total = term if total is None else total + term
    if head_cols != width:
        da[:, head_cols:] = jnp.zeros((seq, width - head_cols), BF16)
    out_sum[...] = total[0:part]
    cols = model // (2 * out_keep.shape[0])

    def write_out(target, slot, c):
        target[slot] = column_chunk(out_sum, c, cols).astype(BF16)

    store_slots(out_keep, out_send, rep, far, write_out)
    masks = head_masks(heads, width)

    def back(i, carry):
        at = pl.ds(pl.multiple_of(i * QB, QB), QB)
        window = pl.ds(pl.multiple_of(i * QB, QB), QB + 2 * HALF)
        bias = window_bias(idq_ref[at, :], idk_ref[0:1, window])
        queries = stack_heads(q_ref[at, :], masks)
        keys = k_ref[window, :]
        probs = block_probs(queries, keys, bias, heads)
        grads = stack_heads(da[at, :], masks)
        dprobs = dot(grads, v_ref[window, :], ((1,), (1,)))
        delta = jnp.sum(probs * dprobs, axis=-1, keepdims=True)
        dscores = (probs * (dprobs - delta)).astype(BF16)
        dq = merge_heads(jnp.dot(dscores, keys, preferred_element_type=F32), masks)
        dq = dq * (1.0 / math.sqrt(HEAD_DIM))
        cos, sin = cos_ref[at, :], sin_ref[at, :]
        dqkv[at, 0:width] = (dq * cos - partner(dq) * sin).astype(BF16)
        dk[window, :] += dot(dscores, queries, ((0,), (0,)))
        dv[window, :] += dot(probs.astype(BF16), grads, ((0,), (0,)))
        return carry

    lax.fori_loop(0, seq // QB, back, 0)

    def finish(i, carry):
        at = pl.ds(pl.multiple_of(i * QB, QB), QB)
        shifted = pl.ds(pl.multiple_of(i * QB + HALF, HALF), QB)
        cos, sin = cos_ref[at, :], sin_ref[at, :]
        g = dk[shifted, :]
        dqkv[at, width : 2 * width] = (g * cos - partner(g) * sin).astype(BF16)
        dqkv[at, 2 * width : 3 * width] = dv[shifted, :].astype(BF16)
        return carry

    lax.fori_loop(0, seq // QB, finish, 0)


def qkv_kernel(n, near, place_ref, normed, dqkv, keep, send, qkv_sum):
    me, rep = place_ref[0], place_ref[1]
    part = normed.shape[1] // n
    chunk = keep.shape[2]
    tiles = dqkv.shape[1] // LANES
    for owner in range(n):
        qkv_sum[...] = dot(normed[:, owner * part : (owner + 1) * part], dqkv[...], ((0,), (0,)))
        base = (me ^ owner) * tiles

        def write(target, slot, c):
            for t in range(tiles):
                target[slot, base + t] = row_chunk(qkv_sum, c, chunk, t * LANES).astype(BF16)

        store_slots(keep, send, rep, near, write)


def project_back_kernel(n, place_ref, dqkv, w_qkv, *out_refs):
    rows = out_refs[0].shape[0]
    for j in range(n):
        at = pl.ds(pl.multiple_of((place_ref[0] ^ j) * rows, rows), rows)
        out_refs[j][...] = dot(dqkv[at, :], w_qkv[...], ((1,), (1,))).astype(BF16)


def place_piece(canvas, piece, offset, valid):
    shift = offset % LANES
    height, size = piece.shape
    count = -(-(shift + valid) // LANES)
    if count * LANES > size:
        piece = jnp.concatenate([piece, jnp.zeros((height, count * LANES - size), F32)], axis=1)
    if shift:
        piece = pltpu.roll(piece, shift, 1)
    lane = lax.broadcasted_iota(jnp.int32, (height, LANES), 1)
    for t in range(count):
        tile = piece[:, t * LANES : (t + 1) * LANES]
        low, high = shift - t * LANES, shift + valid - t * LANES
        if low > 0 or high < LANES:
            tile = jnp.where((lane >= low) & (lane < high), tile, 0.0)
        index = offset // LANES + t
        canvas[index] = tile if index not in canvas else canvas[index] + tile


def columns_out_kernel(
    n, ff, head_cols, width, order, count, place_ref, gain_ref, w_ref, *refs
):
    me, rep = place_ref[0], place_ref[1]
    *parts, out_ref, ln_ref = refs
    tiles = count // n
    if len(parts) == 1:

        def read(index):
            return parts[0][index]

    else:
        half = parts[0].shape[0]
        slot = slot_of(rep ^ pl.program_id(0), order)
        at = slot & (half - 1)

        def read(index):
            return jnp.where(slot < half, parts[0][at, index], parts[1][at, index])

    canvas = {}
    for owner in range(n):
        base = (me ^ owner) * tiles

        def tile(t):
            return read(base + t).astype(F32)

        if ff:
            whole, rest = ff // LANES, ff % LANES
            last = tile(2 * whole)
            gate = jnp.concatenate([tile(t) for t in range(whole)] + [last], axis=1)
            last = pltpu.roll(last, LANES - rest, 1)
            lin = jnp.concatenate([tile(whole + t) for t in range(whole)] + [last], axis=1)
            place_piece(canvas, gate, owner * ff, ff)
            place_piece(canvas, lin, (n + owner) * ff, ff)
        else:
            per = width // LANES
            for b in range(3):
                piece = jnp.concatenate([tile(b * per + t) for t in range(per)], axis=1)
                place_piece(canvas, piece, (b * n + owner) * head_cols, head_cols)
    gain = gain_ref[...]
    total = None
    for index, value in canvas.items():
        at = slice(index * LANES, (index + 1) * LANES)
        term = value * w_ref[:, at].astype(F32)
        total = term if total is None else total + term
        out_ref[:, at] = value * gain
    ln_ref[...] = jnp.sum(total, axis=1, keepdims=True)


def columns_out(place, parts, weight, gain, n, tiles, order, ff=0, head_cols=0, width=0):
    now, got = parts
    chunk = now.shape[2]
    part, cols = weight.shape
    count = part // chunk
    if got is None:
        parts = [now]
        part_specs = [pl.BlockSpec((None, tiles, chunk, LANES), lambda i: (i, 0, 0, 0))]
    else:
        part_specs = [pl.BlockSpec(now.shape, lambda i: (0, 0, 0, 0))] * 2
    total, ln = pl.pallas_call(
        functools.partial(columns_out_kernel, n, ff, head_cols, width, order, tiles),
        grid=(count,),
        in_specs=[
            pl.BlockSpec(memory_space=pltpu.SMEM),
            pl.BlockSpec((None, chunk, 1), lambda i: (i, 0, 0)),
            pl.BlockSpec((None, chunk, cols), lambda i: (i, 0, 0)),
            *part_specs,
        ],
        out_specs=[
            pl.BlockSpec((None, chunk, cols), lambda i: (i, 0, 0)),
            pl.BlockSpec((None, chunk, 1), lambda i: (i, 0, 0)),
        ],
        out_shape=[
            jax.ShapeDtypeStruct((count, chunk, cols), F32),
            jax.ShapeDtypeStruct((count, chunk, 1), F32),
        ],
        compiler_params=pltpu.CompilerParams(vmem_limit_bytes=32 << 20),
        name="columns_out",
    )(place, gain.reshape(count, chunk, 1), weight.reshape(count, chunk, cols), *parts)
    return total.reshape(part, cols), ln.reshape(part)


def rows_out_kernel(order, cols, place_ref, *refs):
    *parts, out_ref = refs
    rep = place_ref[1]

    def chunk(c):
        if len(parts) == 1:
            return parts[0][c].astype(F32)
        half = parts[0].shape[0]
        slot = slot_of(rep ^ c, order)
        at = slot & (half - 1)
        return jnp.where(slot < half, parts[0][at], parts[1][at]).astype(F32)

    count = out_ref.shape[1] // cols
    if cols >= LANES:
        for c in range(count):
            out_ref[:, c * cols : (c + 1) * cols] = chunk(c)
    else:
        per = LANES // cols
        lane = lax.broadcasted_iota(jnp.int32, out_ref.shape[:1] + (LANES,), 1) // cols
        for t in range(count // per):
            value = chunk(per * t)
            for k in range(1, per):
                value = jnp.where(lane == k, pltpu.roll(chunk(per * t + k), k * cols, 1), value)
            out_ref[:, t * LANES : (t + 1) * LANES] = value


def rows_out(place, parts, model, order):
    now, got = parts
    count = now.shape[0]
    if got is None:
        parts = [now]
    else:
        count = 2 * count
    return pl.pallas_call(
        functools.partial(rows_out_kernel, order, model // count),
        in_specs=[pl.BlockSpec(memory_space=pltpu.SMEM)]
        + [pl.BlockSpec(memory_space=pltpu.VMEM)] * len(parts),
        out_shape=jax.ShapeDtypeStruct((now.shape[1], model), F32),
        compiler_params=pltpu.CompilerParams(vmem_limit_bytes=32 << 20),
        name="rows_out",
    )(place, *parts)


def ordered(kernel, first, count):
    def body(*refs):
        kernel(*refs[:first], *refs[first + count :])

    return body


def work(flops):
    return pl.CostEstimate(flops=int(flops), bytes_accessed=1 << 22, transcendentals=0)


SMEM_SPEC = pl.BlockSpec(memory_space=pltpu.SMEM)
VMEM_SPEC = pl.BlockSpec(memory_space=pltpu.VMEM)
ANY_SPEC = pl.BlockSpec(memory_space=pl.ANY)


def norm_backward(grad_hat, normed, scale):
    return (
        grad_hat
        - jnp.mean(grad_hat, axis=-1, keepdims=True)
        - normed * jnp.mean(grad_hat * normed, axis=-1, keepdims=True)
    ) * scale


def after(value, *earlier):
    return lax.optimization_barrier((value,) + earlier)[0]


def shards(tokens, segment_ids, ln1_gain, w_qkv, w_out, ln2_gain, w_in, w_down, cotangent):
    n = lax.axis_size("shard")
    replicas = lax.axis_size("rep")
    me = lax.axis_index("shard")
    place = jnp.stack([me, lax.axis_index("rep")]).astype(jnp.int32)
    rows, model = tokens.shape
    seq = rows * n
    part = model // n
    ff = w_down.shape[0]
    heads = HEADS // n
    head_cols = heads * HEAD_DIM
    width = max(LANES, head_cols)
    padded = -(-ff // LANES) * LANES
    near = list(range(bits_of("rep")))
    far = near[1:2] + near[:1] + near[2:]
    shape = jax.ShapeDtypeStruct
    params = pltpu.CompilerParams(vmem_limit_bytes=VMEM_LIMIT)

    gain1 = ln1_gain.astype(F32)[:, None]
    gain2 = ln2_gain.astype(F32)[:, None]
    qkv_to = split_columns(w_qkv, gain1, n, 3, head_cols, width)
    in_to = split_columns(w_in, gain2, n, 2, ff, padded)
    qkv_pieces = split_weight(qkv_to, 0)

    def fetched(pieces):
        return [a for j, h, a in pieces if j == n // 2 and h == 0]

    toks = gather_list(after(tokens, *fetched(qkv_pieces)), "shard")
    out_pieces = gather_weight(after(w_out, toks[n // 2]), 0)
    in_pieces = split_weight(after(in_to, toks[n // 2]), 1)
    cots = gather_list(after(cotangent, *fetched(in_pieces)), "shard")

    lane = jnp.arange(width, dtype=jnp.int32) % HEAD_DIM
    half = HEAD_DIM // 2
    frequency = jnp.exp(-math.log(rope_base) * 2.0 * (lane % half).astype(F32) / HEAD_DIM)
    angles = jnp.arange(seq, dtype=F32)[:, None] * frequency[None, :]
    sign = jnp.where(lane < half, -1.0, 1.0)
    ids = segment_ids[0]
    tables = (
        jnp.cos(angles),
        jnp.sin(angles) * sign[None, :],
        jnp.broadcast_to(ids[:, None], (seq, LANES)),
        jnp.pad(ids, (HALF, HALF), constant_values=-1)[None],
    )

    def about(pieces):
        return [(j, h, a.shape) for j, h, a in pieces]

    queries, keys, values, attended, normed1, qkv_w = pl.pallas_call(
        functools.partial(attention_kernel, about(qkv_pieces), 0, n, heads),
        in_specs=[SMEM_SPEC] + [VMEM_SPEC] * (4 + n) + [ANY_SPEC] * len(qkv_pieces),
        out_shape=(
            shape((seq, width), BF16),
            shape((seq + 2 * HALF, width), BF16),
            shape((seq + 2 * HALF, width), BF16),
            shape((seq, width), BF16),
            shape((seq, model), BF16),
            shape((model, 3 * width), BF16),
        ),
        scratch_shapes=[pltpu.SemaphoreType.DMA((len(qkv_pieces),))],
        compiler_params=params,
        cost_estimate=work(40 * seq * model * width),
        name="attention",
    )(place, *tables, *toks, *[a for _, _, a in qkv_pieces])

    atts = gather_list(attended[:, :head_cols], "shard")
    blocks = [shape((rows, model), BF16)] * n
    hidden, normed2, act, dup, *dnormed2_blocks = pl.pallas_call(
        functools.partial(
            feed_forward_kernel, about(out_pieces), about(in_pieces), 0, 1, n
        ),
        in_specs=[SMEM_SPEC]
        + [ANY_SPEC] * (3 * n + len(out_pieces) + len(in_pieces) + 1),
        out_specs=[ANY_SPEC] * (4 + n),
        out_shape=[
            shape((rows, model), F32),
            shape((seq, model), BF16),
            shape((seq, padded), BF16),
            shape((seq, 2 * padded), BF16),
        ]
        + blocks,
        scratch_shapes=[
            pltpu.VMEM((n, rows, model), BF16),
            pltpu.VMEM((n, rows, model), BF16),
            pltpu.VMEM((n, seq, head_cols), BF16),
            pltpu.VMEM((model, model), BF16),
            pltpu.VMEM((model, 2 * padded), BF16),
            pltpu.VMEM((padded, model), BF16),
            pltpu.VMEM((rows, model), F32),
            pltpu.VMEM((seq, model), BF16),
            pltpu.VMEM((seq, padded), BF16),
            pltpu.VMEM((seq, 2 * padded), BF16),
            pltpu.VMEM((n, rows, model), BF16),
            pltpu.SemaphoreType.DMA((len(out_pieces),)),
            pltpu.SemaphoreType.DMA((len(in_pieces),)),
            pltpu.SemaphoreType.DMA((n,)),
            pltpu.SemaphoreType.DMA((n,)),
            pltpu.SemaphoreType.DMA((n,)),
            pltpu.SemaphoreType.DMA,
            pltpu.SemaphoreType.DMA((4 * n + 1,)),
        ],
        compiler_params=params,
        cost_estimate=work(26 * seq * model * padded),
        name="feed_forward",
    )(
        place,
        *toks,
        *cots,
        *atts,
        *[a for _, _, a in out_pieces],
        *[a for _, _, a in in_pieces],
        jnp.pad(w_down, ((0, -ff % 16), (0, 0))),
    )
    slots = replicas // 2
    chunk = part // replicas
    lanes = max(LANES, model // replicas)
    tiles = up_tiles(ff)
    in_shape = shape((slots, n * tiles, chunk, LANES), BF16)
    down_shape = shape((slots, ff, lanes), BF16)

    in_keep, in_send = pl.pallas_call(
        functools.partial(in_kernel, n, ff, near),
        in_specs=[SMEM_SPEC] + [VMEM_SPEC] * 2,
        out_shape=[in_shape, in_shape],
        scratch_shapes=[pltpu.VMEM((part, 2 * padded + LANES), F32)],
        compiler_params=params,
        cost_estimate=work(8 * seq * model * padded),
        name="in_gradient",
    )(place, normed2, dup)

    top = bits_of("shard") - 1
    sums = scatter_bits(enumerate(dnormed2_blocks), "shard", range(top - 1))
    low, high = 1 << (top - 1), 1 << top
    mine, other = pl.pallas_call(
        ordered(add_kernel, 4, 1),
        in_specs=[VMEM_SPEC] * 4 + [ANY_SPEC],
        out_shape=[shape((rows, model), F32), shape((rows, model), BF16)],
        compiler_params=pltpu.CompilerParams(vmem_limit_bytes=16 << 20),
        name="near_sum",
    )(
        sums[0],
        swap(sums[low].astype(BF16), "shard", top - 1),
        sums[high],
        swap(sums[low | high].astype(BF16), "shard", top - 1),
        in_keep,
    )
    down_keep, down_send, *mlp_blocks = pl.pallas_call(
        ordered(functools.partial(down_kernel, n, ff, far), 3 + n, 1),
        in_specs=[SMEM_SPEC] + [VMEM_SPEC] * (2 + n) + [ANY_SPEC],
        out_shape=[down_shape, down_shape] + blocks,
        scratch_shapes=[pltpu.VMEM((padded, model), F32)],
        compiler_params=params,
        cost_estimate=work(8 * seq * model * padded),
        name="down_gradient",
    )(place, act, jnp.pad(w_down, ((0, -ff % 16), (0, 0))), *cots, other)
    dhidden, dproj = pl.pallas_call(
        ordered(norm_back_kernel, 4, 1),
        in_specs=[VMEM_SPEC] * 4 + [ANY_SPEC],
        out_shape=[shape((rows, model), F32), shape((rows, model), BF16)],
        compiler_params=pltpu.CompilerParams(vmem_limit_bytes=24 << 20),
        name="norm_back",
    )(mine, swap(other, "shard", top), hidden, cotangent, down_keep)
    dprojs = gather_list(dproj, "shard")

    out_shape = shape((slots, part, lanes), BF16)
    dqkv, out_keep, out_send = pl.pallas_call(
        functools.partial(attention_back_kernel, n, heads, far),
        in_specs=[SMEM_SPEC] + [VMEM_SPEC] * (n + 9),
        out_shape=[shape((seq, 3 * width), BF16), out_shape, out_shape],
        scratch_shapes=[
            pltpu.VMEM((seq, width), BF16),
            pltpu.VMEM((seq + 2 * HALF, width), F32),
            pltpu.VMEM((seq + 2 * HALF, width), F32),
            pltpu.VMEM((part, model), F32),
        ],
        compiler_params=params,
        cost_estimate=work(40 * seq * model * width),
        name="attention_back",
    )(place, *dprojs, w_out, attended, queries, keys, values, *tables)

    mlp_blocks = [after(b, dprojs[n // 2]) for b in mlp_blocks]
    mlp = scatter_sum_list(mlp_blocks, "shard")
    output = (hidden + mlp).astype(BF16)

    qkv_tiles = 3 * width // LANES
    qkv_shape = shape((slots, n * qkv_tiles, chunk, LANES), BF16)
    qkv_keep, qkv_send = pl.pallas_call(
        functools.partial(qkv_kernel, n, near),
        in_specs=[SMEM_SPEC] + [VMEM_SPEC] * 2,
        out_shape=[qkv_shape, qkv_shape],
        scratch_shapes=[pltpu.VMEM((part, 3 * width), F32)],
        compiler_params=params,
        cost_estimate=work(12 * seq * model * width),
        name="qkv_gradient",
    )(place, normed1, dqkv)
    dnormed1_blocks = pl.pallas_call(
        ordered(functools.partial(project_back_kernel, n), 3, 1),
        in_specs=[SMEM_SPEC] + [VMEM_SPEC] * 2 + [ANY_SPEC],
        out_shape=blocks,
        compiler_params=params,
        cost_estimate=work(6 * seq * model * width),
        name="project_back",
    )(place, dqkv, qkv_w, qkv_keep)
    dnormed1 = scatter_sum_list(dnormed1_blocks, "shard")
    hat1, scale1 = normalise(tokens.astype(F32))
    input_grad = dhidden + norm_backward(dnormed1, hat1, scale1)

    def turned(share, tiles):
        return turn(share.reshape(n, tiles, chunk, LANES), n).reshape(n * tiles, chunk, LANES)

    in_share = turned(replica_reduce(in_keep, in_send, near, [dproj, dqkv]), tiles)
    down_share = replica_reduce(down_keep, down_send, far, [dproj, dqkv])
    down_share = jnp.pad(down_share, ((0, -ff % chunk), (0, 0))).reshape(-1, chunk, LANES)
    both = lax.all_gather(jnp.concatenate([in_share, down_share]), "rep", axis=0)
    down_all = both[:, n * tiles :].reshape(replicas, -1, LANES)[:, :ff]

    out_pair = replica_spread(replica_reduce(out_keep, out_send, far), far)
    qkv_share = turned(replica_reduce(qkv_keep, qkv_send, near), qkv_tiles)
    qkv_pair = replica_spread(qkv_share, near)

    in_total, ln2_total = columns_out(place, (both, None), w_in, gain2, n, n * tiles, near, ff=ff)
    down_total = rows_out(place, (down_all, None), model, far)
    out_total = rows_out(place, out_pair, model, far)
    qkv_total, ln1_total = columns_out(
        place,
        qkv_pair,
        w_qkv,
        gain1,
        n,
        n * qkv_tiles,
        near,
        head_cols=head_cols,
        width=width,
    )
    return (
        output,
        input_grad,
        ln1_total,
        qkv_total,
        out_total,
        ln2_total,
        in_total,
        down_total,
    )


def solution(mesh):
    return jax.shard_map(
        shards,
        mesh=mesh,
        in_specs=(
            P(("rep", "shard"), None),
            P("rep", None),
            P("shard"),
            P("shard", None),
            P("shard", None),
            P("shard"),
            P("shard", None),
            P("shard", None),
            P(("rep", "shard"), None),
        ),
        out_specs=(
            P(("rep", "shard"), None),
            P(("rep", "shard"), None),
            P("shard"),
            P("shard", None),
            P("shard", None),
            P("shard"),
            P("shard", None),
            P("shard", None),
        ),
        check_vma=False,
    )
```

```python
import functools
import math

import jax
import jax.numpy as jnp
from jax import lax
from jax.experimental import pallas as pl
from jax.experimental.pallas import tpu as pltpu
from jax.sharding import PartitionSpec as P

HEADS = 16
HEAD_DIM = 64
HALF = 64
QB = 128
LANES = 128

norm_epsilon = 1e-05
rope_base = 10000.0
masked_score = -1e30

F32 = jnp.float32
BF16 = jnp.bfloat16
VMEM_LIMIT = 52 << 20


def bits_of(axis):
    return lax.axis_size(axis).bit_length() - 1


def bit_of(axis, bit):
    return (lax.axis_index(axis) >> bit) & 1


def swap(x, axis, bit):
    size = lax.axis_size(axis)
    return lax.ppermute(x, axis, [(i, i ^ (1 << bit)) for i in range(size)])


def gather_list(x, axis):
    blocks = {0: x}
    for bit in reversed(range(bits_of(axis))):
        for j in list(blocks):
            blocks[j | 1 << bit] = swap(blocks[j], axis, bit)
    return [blocks[j] for j in range(len(blocks))]


def scatter_bits(blocks, axis, bits):
    blocks = dict(blocks)
    for bit in bits:
        for j in [j for j in blocks if j >> bit & 1]:
            got = swap(blocks.pop(j).astype(BF16), axis, bit)
            k = j ^ (1 << bit)
            blocks[k] = blocks[k].astype(F32) + got.astype(F32)
    return blocks


def scatter_sum_list(blocks, axis):
    return scatter_bits(enumerate(blocks), axis, range(bits_of(axis)))[0]


def parity():
    return bit_of("rep", 0) ^ bit_of("rep", 1)


def half_by_replica(x, dim):
    shape = x.shape
    x = x.reshape(shape[:dim] + (2, shape[dim] // 2) + shape[dim + 1 :])
    return lax.dynamic_index_in_dim(x, parity(), dim, keepdims=False)


def fetch_far(send, dim, top, gate):
    got = swap(half_by_replica(send, dim), "shard", top)
    kept = got if gate is None else after(got, gate())
    first, second = jnp.split(kept, 2, axis=dim)
    return [
        (1 << top, 0, got),
        (1 << top, 1, swap(first, "rep", 0)),
        (1 << top, 2, swap(second, "rep", 1)),
    ]


def gather_weight(x, gate=None):
    top = bits_of("shard") - 1
    pieces = [(0, None, x)] + fetch_far(x, 0, top, gate)
    for bit in reversed(range(top)):
        pieces += [(j | 1 << bit, h, swap(a, "shard", bit)) for j, h, a in pieces]
    return pieces


def split_weight(x, gate=None):
    me = lax.axis_index("shard")
    top = bits_of("shard") - 1

    def part_for(a, bit):
        start = ((me & (a.shape[0] - 1)) >> bit ^ 1) << bit
        return lax.dynamic_slice_in_dim(a, start, 1 << bit)

    pieces = [(0, None, x)] + fetch_far(part_for(x, top), 1, top, gate)
    for bit in reversed(range(top)):
        pieces += [(j | 1 << bit, h, swap(part_for(a, bit), "shard", bit)) for j, h, a in pieces]
    return pieces


def replica_reduce(keep, send, order, gates=()):
    for step, bit in enumerate(order):
        got = swap(send, "rep", bit)
        if step < len(gates):
            got = after(got, gates[step])

        def total(a, b):
            return (keep[a:b].astype(F32) + got[a:b].astype(F32)).astype(BF16)

        size = keep.shape[0]
        if size == 1:
            return total(0, 1)[0]
        keep, send = total(0, size // 2), total(size // 2, size)


def replica_spread(x, order):
    now = x[None]
    for bit in reversed(order[1:]):
        now = jnp.concatenate([now, swap(now, "rep", bit)])
    return now, swap(now, "rep", order[0])


def turn(x, n):
    pieces = {0: x}
    for bit in reversed(range(n.bit_length() - 1)):
        for j in list(pieces):
            half = pieces[j].shape[0] // 2
            pieces[j | 1 << bit] = swap(pieces[j][half:], "shard", bit)
            pieces[j] = pieces[j][:half]
    return jnp.concatenate([pieces[j] for j in range(n)])


def slot_mask(slot, order):
    count = len(order)
    return sum(((slot >> (count - 1 - i)) & 1) << bit for i, bit in enumerate(order))


def slot_of(mask, order):
    count = len(order)
    return sum(((mask >> bit) & 1) << (count - 1 - i) for i, bit in enumerate(order))


def dot(a, b, dims):
    return lax.dot_general(a, b, (dims, ((), ())), preferred_element_type=F32)


def normalise(values):
    centred = values - jnp.mean(values, axis=-1, keepdims=True)
    scale = lax.rsqrt(jnp.mean(centred * centred, axis=-1, keepdims=True) + norm_epsilon)
    return centred * scale, scale


def weight_copies(pieces, refs, target, me, sems, rep, by_owner, rows):
    copies = []
    for i, ((j, half, shape), ref) in enumerate(zip(pieces, refs)):
        start = (me ^ j if by_owner else j) * rows
        count = rows
        if half is not None:
            own = (rep ^ (rep >> 1)) & 1
            count = rows // 2 if half == 0 else rows // 4
            start = start + (own if half == 0 else 1 - own) * (rows // 2)
            start = start + (rows // 4 if half == 2 else 0)
        source = ref.at[me & (shape[0] - 1)] if len(shape) == 3 else ref
        place = target.at[pl.ds(pl.multiple_of(start, count), count), :]
        copies.append(pltpu.make_async_copy(source, place, sems.at[i]))
    return copies


def partner(x):
    width = x.shape[-1]
    lane = lax.broadcasted_iota(jnp.int32, x.shape, 1)
    front = (lane % HEAD_DIM) < HEAD_DIM // 2
    return jnp.where(
        front,
        pltpu.roll(x, width - HEAD_DIM // 2, 1),
        pltpu.roll(x, HEAD_DIM // 2, 1),
    )


def head_masks(heads, width):
    lane = lax.broadcasted_iota(jnp.int32, (QB, width), 1) // HEAD_DIM
    return [lane == h for h in range(heads)]


def stack_heads(x, masks):
    x = x.astype(F32)
    return jnp.concatenate([jnp.where(m, x, 0.0) for m in masks], axis=0).astype(BF16)


def merge_heads(x, masks):
    total = None
    for h, m in enumerate(masks):
        part = jnp.where(m, x[h * QB : (h + 1) * QB], 0.0)
        total = part if total is None else total + part
    return total


def window_bias(ids_q, ids_k):
    row = lax.broadcasted_iota(jnp.int32, (QB, QB + 2 * HALF), 0)
    col = lax.broadcasted_iota(jnp.int32, (QB, QB + 2 * HALF), 1)
    ids_q = jnp.concatenate([ids_q] * ((QB + 2 * HALF) // LANES), axis=1)
    allowed = (col >= row) & (col <= row + 2 * HALF) & (ids_q == ids_k)
    return jnp.where(allowed, 0.0, masked_score)


def block_probs(stacked_q, keys, bias, heads):
    scores = dot(stacked_q, keys, ((1,), (1,)))
    rows, cols = scores.shape
    scores = (scores.reshape(heads, QB, cols) + bias[None]).reshape(rows, cols)
    weights = jnp.exp(scores - jnp.max(scores, axis=-1, keepdims=True))
    return weights * (1.0 / jnp.sum(weights, axis=-1, keepdims=True))


def column_chunk(ref, chunk, cols):
    if cols >= LANES:
        return ref[:, pl.ds(pl.multiple_of(chunk * cols, cols), cols)]
    per = LANES // cols
    tile = ref[:, pl.ds(pl.multiple_of(chunk // per * LANES, LANES), LANES)]
    result = tile
    for k in range(1, per):
        result = jnp.where(chunk % per == k, pltpu.roll(tile, LANES - k * cols, 1), result)
    return result


def row_chunk(ref, chunk, rows, start):
    if rows % 8 == 0:
        return ref[pl.ds(pl.multiple_of(chunk * rows, rows), rows), start : start + LANES]
    per = 8 // rows
    tile = ref[pl.ds(pl.multiple_of(chunk // per * 8, 8), 8), start : start + LANES]
    result = tile[:rows]
    for k in range(1, per):
        result = jnp.where(chunk % per == k, tile[k * rows : (k + 1) * rows], result)
    return result


def take_columns(ref, offset, valid, size):
    begin = offset // LANES * LANES
    end = -(-(offset + valid) // LANES) * LANES
    x = ref[:, begin:end].astype(F32)
    if offset != begin:
        x = pltpu.roll(x, end - offset, 1)
    x = x[:, :size]
    if valid != size:
        lane = lax.broadcasted_iota(jnp.int32, x.shape, 1)
        x = jnp.where(lane < valid, x, 0.0)
    return x


def split_kernel(n, blocks, valid, size, gain_ref, w_ref, out_ref):
    gain = gain_ref[...]
    for owner in range(n):
        for b in range(blocks):
            x = take_columns(w_ref, (b * n + owner) * valid, valid, size)
            out_ref[owner, :, b * size : (b + 1) * size] = (x * gain).astype(BF16)


def split_columns(w, gain, n, blocks, valid, size):
    rows, cols = w.shape
    step = min(rows, 64)
    return pl.pallas_call(
        functools.partial(split_kernel, n, blocks, valid, size),
        grid=(rows // step,),
        in_specs=[
            pl.BlockSpec((step, 1), lambda i: (i, 0)),
            pl.BlockSpec((step, cols), lambda i: (i, 0)),
        ],
        out_specs=pl.BlockSpec((n, step, blocks * size), lambda i: (0, i, 0)),
        out_shape=jax.ShapeDtypeStruct((n, rows, blocks * size), BF16),
        compiler_params=pltpu.CompilerParams(vmem_limit_bytes=24 << 20),
        name="split_columns",
    )(gain, w)


def attention_kernel(
    pieces, n, heads, place_ref, cos_ref, sin_ref, idq_ref, idk_ref, *refs
):
    tok_refs, refs = refs[:n], refs[n:]
    piece_refs, refs = refs[: len(pieces)], refs[len(pieces) :]
    q_ref, k_ref, v_ref, out_ref, normed_ref, w_ref, sems = refs
    seq, width = q_ref.shape
    rows = seq // n
    me, rep = place_ref[0], place_ref[1]
    copies = weight_copies(
        pieces, piece_refs, w_ref, me, sems, rep, True, w_ref.shape[0] // n
    )
    for c in copies:
        c.start()
    edge = jnp.zeros((HALF, width), BF16)
    for ref in (k_ref, v_ref):
        ref[0:HALF, :] = edge
        ref[seq + HALF : seq + 2 * HALF, :] = edge
    for c in copies:
        c.wait()
    for j in range(n):
        start = (me ^ j) * rows
        at = pl.ds(pl.multiple_of(start, rows), rows)
        shifted = pl.ds(pl.multiple_of(start + HALF, HALF), rows)
        hat, _ = normalise(tok_refs[j][...].astype(F32))
        normed = hat.astype(BF16)
        normed_ref[at, :] = normed
        qkv = jnp.dot(normed, w_ref[...], preferred_element_type=F32)
        cos, sin = cos_ref[at, :], sin_ref[at, :]
        q, k = qkv[:, 0:width], qkv[:, width : 2 * width]
        rotated = (q * cos + partner(q) * sin).astype(BF16)
        q_ref[at, :] = (rotated.astype(F32) * (1.0 / math.sqrt(HEAD_DIM))).astype(BF16)
        k_ref[shifted, :] = (k * cos + partner(k) * sin).astype(BF16)
        v_ref[shifted, :] = qkv[:, 2 * width : 3 * width].astype(BF16)
    masks = head_masks(heads, width)

    def attend(i, carry):
        at = pl.ds(pl.multiple_of(i * QB, QB), QB)
        window = pl.ds(pl.multiple_of(i * QB, QB), QB + 2 * HALF)
        bias = window_bias(idq_ref[at, :], idk_ref[0:1, window])
        probs = block_probs(stack_heads(q_ref[at, :], masks), k_ref[window, :], bias, heads)
        mixed = jnp.dot(probs.astype(BF16), v_ref[window, :], preferred_element_type=F32)
        out_ref[at, :] = merge_heads(mixed, masks).astype(BF16)
        return carry

    lax.fori_loop(0, seq // QB, attend, 0)


def up_kernel(out_pieces, in_pieces, n, place_ref, *refs):
    tok_refs, refs = refs[:n], refs[n:]
    att_refs, refs = refs[:n], refs[n:]
    out_refs, refs = refs[: len(out_pieces)], refs[len(out_pieces) :]
    in_refs, refs = refs[: len(in_pieces)], refs[len(in_pieces) :]
    hidden_out, normed_out, up_out, in_out, *refs = refs
    tok, att, w_out, w_in, hidden_own, normed, up, *refs = refs
    out_sems, in_sems, att_sems, tok_sems, sems = refs
    me, rep = place_ref[0], place_ref[1]
    rows, model = tok_refs[0].shape
    copy = pltpu.make_async_copy
    att_copies = [copy(att_refs[j], att.at[j], att_sems.at[j]) for j in range(n)]
    tok_copies = [copy(tok_refs[j], tok.at[j], tok_sems.at[j]) for j in range(n)]
    part = model // n
    out_copies = weight_copies(out_pieces, out_refs, w_out, me, out_sems, rep, False, part)
    in_copies = weight_copies(in_pieces, in_refs, w_in, me, in_sems, rep, True, part)
    for c in att_copies + tok_copies[:1] + out_copies + in_copies + tok_copies[1:]:
        c.start()
    for c in att_copies + out_copies:
        c.wait()
    sent = []
    for j in range(n):
        at = pl.ds(pl.multiple_of((me ^ j) * rows, rows), rows)
        here = slice(j * rows, (j + 1) * rows)
        tok_copies[j].wait()
        hidden = tok[j].astype(F32)
        for i in range(n):
            hidden = hidden + jnp.dot(
                att[i, at, :], w_out[i * part : (i + 1) * part, :], preferred_element_type=F32
            )
        if j == 0:
            hidden_own[...] = hidden
            sent.append(copy(hidden_own, hidden_out, sems.at[2 * n]))
            sent[-1].start()
        hat, _ = normalise(hidden)
        low = hat.astype(BF16)
        normed[here, :] = low
        if j == 0:
            for c in in_copies:
                c.wait()
            sent.append(copy(w_in, in_out, sems.at[2 * n + 1]))
            sent[-1].start()
        up[here, :] = jnp.dot(low, w_in[...], preferred_element_type=F32)
        sent += [
            copy(normed.at[here, :], normed_out.at[here, :], sems.at[2 * j]),
            copy(up.at[here, :], up_out.at[here, :], sems.at[2 * j + 1]),
        ]
        for c in sent[-2:]:
            c.start()
    for c in sent:
        c.wait()


def dup_kernel(n, up_ref, w_in_ref, down_ref, *refs):
    cot_refs, refs = refs[:n], refs[n:]
    act_out, dup_out, *refs = refs
    dnormed_outs, refs = refs[:n], refs[n:]
    up, cot, w_in, w_down, act, dup, dnormed, in_sem, down_sem, up_sems, cot_sems, sems = refs
    rows, model = cot_refs[0].shape
    padded = w_down.shape[0]
    given = down_ref.shape[0]
    if given != padded:
        w_down[given:padded, :] = jnp.zeros((padded - given, model), BF16)
    copy = pltpu.make_async_copy
    down_copy = copy(down_ref, w_down.at[0:given, :], down_sem)
    in_copy = copy(w_in_ref, w_in, in_sem)
    cot_copies = [copy(cot_refs[j], cot.at[j], cot_sems.at[j]) for j in range(n)]
    up_copies = []
    for j in range(n):
        here = slice(j * rows, (j + 1) * rows)
        up_copies.append(copy(up_ref.at[here, :], up.at[here, :], up_sems.at[j]))
    for c in [up_copies[0], cot_copies[0], down_copy, in_copy]:
        c.start()
    for c in up_copies[1:] + cot_copies[1:]:
        c.start()
    sent = []
    for j in range(n):
        here = slice(j * rows, (j + 1) * rows)
        up_copies[j].wait()
        gate, lin = up[here, :padded], up[here, padded:]
        phi = 0.5 + 0.5 * lax.erf(gate * (1.0 / math.sqrt(2.0)))
        gelu = gate * phi
        slope = phi + gate * jnp.exp(gate * gate * -0.5) * (1.0 / math.sqrt(2.0 * math.pi))
        act[here, :] = (gelu * lin).astype(BF16)
        cot_copies[j].wait()
        if j == 0:
            down_copy.wait()
        dact = dot(cot[j], w_down[...], ((1,), (1,)))
        dup[here, :padded] = (dact * lin * slope).astype(BF16)
        dup[here, padded:] = (dact * gelu).astype(BF16)
        if j == 0:
            in_copy.wait()
        dnormed[j] = dot(dup[here, :], w_in[...], ((1,), (1,))).astype(BF16)
        sent += [
            copy(dnormed.at[j], dnormed_outs[j], sems.at[3 * j]),
            copy(act.at[here, :], act_out.at[here, :], sems.at[3 * j + 1]),
            copy(dup.at[here, :], dup_out.at[here, :], sems.at[3 * j + 2]),
        ]
        for c in sent[-3:]:
            c.start()
    for c in sent:
        c.wait()


def store_slots(keep_ref, send_ref, rep, order, write):
    half = keep_ref.shape[0]
    for slot in range(2 * half):
        target = keep_ref if slot < half else send_ref
        write(target, slot % half, rep ^ slot_mask(slot, order))


def up_tiles(ff):
    return 2 * (ff // LANES) + 1


def down_kernel(n, ff, far, place_ref, act, w_down, *refs):
    cot_refs, refs = refs[:n], refs[n:]
    keep, send, *refs = refs
    mlp_refs, refs = refs[:n], refs[n:]
    (down_sum,) = refs
    rows, model = cot_refs[0].shape
    cols = model // (2 * keep.shape[0])
    total = None
    for j in range(n):
        term = dot(act[j * rows : (j + 1) * rows, :], cot_refs[j][...], ((0,), (0,)))
        total = term if total is None else total + term
    down_sum[...] = total

    def write(target, slot, c):
        target[slot] = column_chunk(down_sum, c, cols)[:ff].astype(BF16)

    store_slots(keep, send, place_ref[1], far, write)
    given = w_down.shape[0]
    for j in range(n):
        low = act[j * rows : (j + 1) * rows, 0:given]
        mlp_refs[j][...] = jnp.dot(low, w_down[...], preferred_element_type=F32).astype(BF16)


def in_kernel(n, ff, counts, orders, place_ref, normed, dup, *refs):
    flows, in_sum = refs[:-1], refs[-1]
    me, rep = place_ref[0], place_ref[1]
    part = normed.shape[1] // n
    padded = dup.shape[1] // 2
    whole, rest = ff // LANES, ff % LANES
    starts = [t * LANES for t in range(whole)] + [padded + t * LANES for t in range(whole)]
    starts.append(2 * padded)
    for owner in range(n):
        block = dot(normed[:, owner * part : (owner + 1) * part], dup[...], ((0,), (0,)))
        in_sum[:, : 2 * padded] = block
        first = block[:, whole * LANES : (whole + 1) * LANES]
        second = block[:, padded + whole * LANES : padded + (whole + 1) * LANES]
        lane = lax.broadcasted_iota(jnp.int32, first.shape, 1)
        in_sum[:, 2 * padded :] = jnp.where(lane < rest, first, pltpu.roll(second, rest, 1))
        begin = 0
        for f, (count, order) in enumerate(zip(counts, orders)):
            keep, send = flows[2 * f], flows[2 * f + 1]
            chunk = keep.shape[2]

            def write(target, slot, c):
                for t in range(count):
                    value = row_chunk(in_sum, c, chunk, starts[begin + t])
                    target[slot, (me ^ owner) * count + t] = value.astype(BF16)

            store_slots(keep, send, rep, order, write)
            begin += count


def add_kernel(a_ref, b_ref, c_ref, d_ref, mine_ref, other_ref):
    mine_ref[...] = a_ref[...].astype(F32) + b_ref[...].astype(F32)
    other_ref[...] = (c_ref[...].astype(F32) + d_ref[...].astype(F32)).astype(BF16)


def norm_back_kernel(mine, got, hidden, cotangent, dhidden, dproj):
    hat, scale = normalise(hidden[...])
    e = mine[...] + got[...].astype(F32)
    value = cotangent[...].astype(F32) + norm_backward(e, hat, scale)
    dhidden[...] = value
    dproj[...] = value.astype(BF16)


def attention_back_kernel(n, heads, far, place_ref, *refs):
    dproj_refs, refs = refs[:n], refs[n:]
    w_out, att, q_ref, k_ref, v_ref, cos_ref, sin_ref, idq_ref, idk_ref, *refs = refs
    dqkv, out_keep, out_send, da, dk, dv, out_sum = refs
    me, rep = place_ref[0], place_ref[1]
    seq, width = q_ref.shape
    rows, model = dproj_refs[0].shape
    part = model // n
    dk[...] = jnp.zeros_like(dk)
    dv[...] = jnp.zeros_like(dv)
    head_cols = heads * HEAD_DIM
    total = None
    for j in range(n):
        at = pl.ds(pl.multiple_of((me ^ j) * rows, rows), rows)
        dproj = dproj_refs[j][...]
        da[at, 0:head_cols] = dot(dproj, w_out[...], ((1,), (1,))).astype(BF16)
        term = dot(att[at, :], dproj, ((0,), (0,)))
        total = term if total is None else total + term
    if head_cols != width:
        da[:, head_cols:] = jnp.zeros((seq, width - head_cols), BF16)
    out_sum[...] = total[0:part]
    cols = model // (2 * out_keep.shape[0])

    def write_out(target, slot, c):
        target[slot] = column_chunk(out_sum, c, cols).astype(BF16)

    store_slots(out_keep, out_send, rep, far, write_out)
    masks = head_masks(heads, width)

    def back(i, carry):
        at = pl.ds(pl.multiple_of(i * QB, QB), QB)
        window = pl.ds(pl.multiple_of(i * QB, QB), QB + 2 * HALF)
        bias = window_bias(idq_ref[at, :], idk_ref[0:1, window])
        queries = stack_heads(q_ref[at, :], masks)
        keys = k_ref[window, :]
        probs = block_probs(queries, keys, bias, heads)
        grads = stack_heads(da[at, :], masks)
        dprobs = dot(grads, v_ref[window, :], ((1,), (1,)))
        delta = jnp.sum(probs * dprobs, axis=-1, keepdims=True)
        dscores = (probs * (dprobs - delta)).astype(BF16)
        dq = merge_heads(jnp.dot(dscores, keys, preferred_element_type=F32), masks)
        dq = dq * (1.0 / math.sqrt(HEAD_DIM))
        cos, sin = cos_ref[at, :], sin_ref[at, :]
        dqkv[at, 0:width] = (dq * cos - partner(dq) * sin).astype(BF16)
        dk[window, :] += dot(dscores, queries, ((0,), (0,)))
        dv[window, :] += dot(probs.astype(BF16), grads, ((0,), (0,)))
        return carry

    lax.fori_loop(0, seq // QB, back, 0)

    def finish(i, carry):
        at = pl.ds(pl.multiple_of(i * QB, QB), QB)
        shifted = pl.ds(pl.multiple_of(i * QB + HALF, HALF), QB)
        cos, sin = cos_ref[at, :], sin_ref[at, :]
        g = dk[shifted, :]
        dqkv[at, width : 2 * width] = (g * cos - partner(g) * sin).astype(BF16)
        dqkv[at, 2 * width : 3 * width] = dv[shifted, :].astype(BF16)
        return carry

    lax.fori_loop(0, seq // QB, finish, 0)


def qkv_kernel(n, near, place_ref, normed, dqkv, keep, send, qkv_sum):
    me, rep = place_ref[0], place_ref[1]
    part = normed.shape[1] // n
    chunk = keep.shape[2]
    tiles = dqkv.shape[1] // LANES
    for owner in range(n):
        qkv_sum[...] = dot(normed[:, owner * part : (owner + 1) * part], dqkv[...], ((0,), (0,)))
        base = (me ^ owner) * tiles

        def write(target, slot, c):
            for t in range(tiles):
                target[slot, base + t] = row_chunk(qkv_sum, c, chunk, t * LANES).astype(BF16)

        store_slots(keep, send, rep, near, write)


def project_back_kernel(n, place_ref, dqkv, w_qkv, *out_refs):
    rows = out_refs[0].shape[0]
    for j in range(n):
        at = pl.ds(pl.multiple_of((place_ref[0] ^ j) * rows, rows), rows)
        out_refs[j][...] = dot(dqkv[at, :], w_qkv[...], ((1,), (1,))).astype(BF16)


def place_piece(canvas, piece, offset, valid):
    shift = offset % LANES
    height, size = piece.shape
    count = -(-(shift + valid) // LANES)
    if count * LANES > size:
        piece = jnp.concatenate([piece, jnp.zeros((height, count * LANES - size), F32)], axis=1)
    if shift:
        piece = pltpu.roll(piece, shift, 1)
    lane = lax.broadcasted_iota(jnp.int32, (height, LANES), 1)
    for t in range(count):
        tile = piece[:, t * LANES : (t + 1) * LANES]
        low, high = shift - t * LANES, shift + valid - t * LANES
        if low > 0 or high < LANES:
            tile = jnp.where((lane >= low) & (lane < high), tile, 0.0)
        index = offset // LANES + t
        canvas[index] = tile if index not in canvas else canvas[index] + tile


def columns_out_kernel(n, ff, head_cols, width, counts, orders, place_ref, gain_ref, w_ref, *refs):
    me, rep = place_ref[0], place_ref[1]
    *parts, out_ref, ln_ref = refs
    half = parts[0].shape[0]
    slots = [slot_of(rep ^ pl.program_id(0), order) for order in orders]

    def read(owner, t):
        f = 0
        while t >= counts[f]:
            t -= counts[f]
            f += 1
        slot, index = slots[f], (me ^ owner) * counts[f] + t
        at = slot & (half - 1)
        now, got = parts[2 * f][at, index], parts[2 * f + 1][at, index]
        return jnp.where(slot < half, now, got).astype(F32)

    canvas = {}
    for owner in range(n):
        tile = functools.partial(read, owner)

        if ff:
            whole, rest = ff // LANES, ff % LANES
            last = tile(2 * whole)
            gate = jnp.concatenate([tile(t) for t in range(whole)] + [last], axis=1)
            last = pltpu.roll(last, LANES - rest, 1)
            lin = jnp.concatenate([tile(whole + t) for t in range(whole)] + [last], axis=1)
            place_piece(canvas, gate, owner * ff, ff)
            place_piece(canvas, lin, (n + owner) * ff, ff)
        else:
            per = width // LANES
            for b in range(3):
                piece = jnp.concatenate([tile(b * per + t) for t in range(per)], axis=1)
                place_piece(canvas, piece, (b * n + owner) * head_cols, head_cols)
    gain = gain_ref[...]
    total = None
    for index, value in canvas.items():
        at = slice(index * LANES, (index + 1) * LANES)
        term = value * w_ref[:, at].astype(F32)
        total = term if total is None else total + term
        out_ref[:, at] = value * gain
    ln_ref[...] = jnp.sum(total, axis=1, keepdims=True)


def columns_out(place, pairs, counts, orders, weight, gain, n, ff=0, head_cols=0, width=0):
    parts = [a for pair in pairs for a in pair]
    chunk = parts[0].shape[2]
    part, cols = weight.shape
    count = part // chunk
    part_specs = [pl.BlockSpec(a.shape, lambda i: (0, 0, 0, 0)) for a in parts]
    total, ln = pl.pallas_call(
        functools.partial(columns_out_kernel, n, ff, head_cols, width, counts, orders),
        grid=(count,),
        in_specs=[
            pl.BlockSpec(memory_space=pltpu.SMEM),
            pl.BlockSpec((None, chunk, 1), lambda i: (i, 0, 0)),
            pl.BlockSpec((None, chunk, cols), lambda i: (i, 0, 0)),
            *part_specs,
        ],
        out_specs=[
            pl.BlockSpec((None, chunk, cols), lambda i: (i, 0, 0)),
            pl.BlockSpec((None, chunk, 1), lambda i: (i, 0, 0)),
        ],
        out_shape=[
            jax.ShapeDtypeStruct((count, chunk, cols), F32),
            jax.ShapeDtypeStruct((count, chunk, 1), F32),
        ],
        compiler_params=pltpu.CompilerParams(vmem_limit_bytes=32 << 20),
        name="columns_out",
    )(place, gain.reshape(count, chunk, 1), weight.reshape(count, chunk, cols), *parts)
    return total.reshape(part, cols), ln.reshape(part)


def rows_out_kernel(order, cols, place_ref, *refs):
    *parts, out_ref = refs
    rep = place_ref[1]

    def chunk(c):
        if len(parts) == 1:
            return parts[0][c].astype(F32)
        half = parts[0].shape[0]
        slot = slot_of(rep ^ c, order)
        at = slot & (half - 1)
        return jnp.where(slot < half, parts[0][at], parts[1][at]).astype(F32)

    count = out_ref.shape[1] // cols
    if cols >= LANES:
        for c in range(count):
            out_ref[:, c * cols : (c + 1) * cols] = chunk(c)
    else:
        per = LANES // cols
        lane = lax.broadcasted_iota(jnp.int32, out_ref.shape[:1] + (LANES,), 1) // cols
        for t in range(count // per):
            value = chunk(per * t)
            for k in range(1, per):
                value = jnp.where(lane == k, pltpu.roll(chunk(per * t + k), k * cols, 1), value)
            out_ref[:, t * LANES : (t + 1) * LANES] = value


def rows_out(place, parts, model, order):
    now, got = parts
    count = now.shape[0]
    if got is None:
        parts = [now]
    else:
        count = 2 * count
    return pl.pallas_call(
        functools.partial(rows_out_kernel, order, model // count),
        in_specs=[pl.BlockSpec(memory_space=pltpu.SMEM)]
        + [pl.BlockSpec(memory_space=pltpu.VMEM)] * len(parts),
        out_shape=jax.ShapeDtypeStruct((now.shape[1], model), F32),
        compiler_params=pltpu.CompilerParams(vmem_limit_bytes=32 << 20),
        name="rows_out",
    )(place, *parts)


def ordered(kernel, first, count):
    def body(*refs):
        kernel(*refs[:first], *refs[first + count :])

    return body


def work(flops):
    return pl.CostEstimate(flops=int(flops), bytes_accessed=1 << 22, transcendentals=0)


SMEM_SPEC = pl.BlockSpec(memory_space=pltpu.SMEM)
VMEM_SPEC = pl.BlockSpec(memory_space=pltpu.VMEM)
ANY_SPEC = pl.BlockSpec(memory_space=pl.ANY)


def norm_backward(grad_hat, normed, scale):
    return (
        grad_hat
        - jnp.mean(grad_hat, axis=-1, keepdims=True)
        - normed * jnp.mean(grad_hat * normed, axis=-1, keepdims=True)
    ) * scale


def after(value, *earlier):
    return lax.optimization_barrier((value,) + earlier)[0]


def shards(tokens, segment_ids, ln1_gain, w_qkv, w_out, ln2_gain, w_in, w_down, cotangent):
    n = lax.axis_size("shard")
    replicas = lax.axis_size("rep")
    me = lax.axis_index("shard")
    place = jnp.stack([me, lax.axis_index("rep")]).astype(jnp.int32)
    rows, model = tokens.shape
    seq = rows * n
    part = model // n
    ff = w_down.shape[0]
    heads = HEADS // n
    head_cols = heads * HEAD_DIM
    width = max(LANES, head_cols)
    padded = -(-ff // LANES) * LANES
    near = list(range(bits_of("rep")))
    far = near[1:2] + near[:1] + near[2:]
    shape = jax.ShapeDtypeStruct
    params = pltpu.CompilerParams(vmem_limit_bytes=VMEM_LIMIT)

    gain1 = ln1_gain.astype(F32)[:, None]
    gain2 = ln2_gain.astype(F32)[:, None]
    qkv_to = split_columns(w_qkv, gain1, n, 3, head_cols, width)
    in_to = split_columns(w_in, gain2, n, 2, ff, padded)
    qkv_pieces = split_weight(qkv_to)

    toks = gather_list(tokens, "shard")

    lane = jnp.arange(width, dtype=jnp.int32) % HEAD_DIM
    half = HEAD_DIM // 2
    frequency = jnp.exp(-math.log(rope_base) * 2.0 * (lane % half).astype(F32) / HEAD_DIM)
    angles = jnp.arange(seq, dtype=F32)[:, None] * frequency[None, :]
    sign = jnp.where(lane < half, -1.0, 1.0)
    ids = segment_ids[0]
    tables = (
        jnp.cos(angles),
        jnp.sin(angles) * sign[None, :],
        jnp.broadcast_to(ids[:, None], (seq, LANES)),
        jnp.pad(ids, (HALF, HALF), constant_values=-1)[None],
    )

    def about(pieces):
        return [(j, h, a.shape) for j, h, a in pieces]

    queries, keys, values, attended, normed1, qkv_w = pl.pallas_call(
        functools.partial(attention_kernel, about(qkv_pieces), n, heads),
        in_specs=[SMEM_SPEC] + [VMEM_SPEC] * (4 + n) + [ANY_SPEC] * len(qkv_pieces),
        out_shape=(
            shape((seq, width), BF16),
            shape((seq + 2 * HALF, width), BF16),
            shape((seq + 2 * HALF, width), BF16),
            shape((seq, width), BF16),
            shape((seq, model), BF16),
            shape((model, 3 * width), BF16),
        ),
        scratch_shapes=[pltpu.SemaphoreType.DMA((len(qkv_pieces),))],
        compiler_params=params,
        cost_estimate=work(40 * seq * model * width),
        name="attention",
    )(place, *tables, *toks, *[a for _, _, a in qkv_pieces])

    def once_attended():
        return attended

    far_done = [toks[n // 2], qkv_pieces[1][2]]
    out_pieces = gather_weight(after(w_out, *far_done), once_attended)
    in_pieces = split_weight(after(in_to, *far_done), once_attended)
    atts = gather_list(attended[:, :head_cols], "shard")
    cots = gather_list(after(cotangent, atts[n // 2]), "shard")
    blocks = [shape((rows, model), BF16)] * n
    hidden, normed2, up, in_w = pl.pallas_call(
        functools.partial(up_kernel, about(out_pieces), about(in_pieces), n),
        in_specs=[SMEM_SPEC] + [ANY_SPEC] * (2 * n + len(out_pieces) + len(in_pieces)),
        out_specs=[ANY_SPEC] * 4,
        out_shape=[
            shape((rows, model), F32),
            shape((seq, model), BF16),
            shape((seq, 2 * padded), F32),
            shape((model, 2 * padded), BF16),
        ],
        scratch_shapes=[
            pltpu.VMEM((n, rows, model), BF16),
            pltpu.VMEM((n, seq, head_cols), BF16),
            pltpu.VMEM((model, model), BF16),
            pltpu.VMEM((model, 2 * padded), BF16),
            pltpu.VMEM((rows, model), F32),
            pltpu.VMEM((seq, model), BF16),
            pltpu.VMEM((seq, 2 * padded), F32),
            pltpu.SemaphoreType.DMA((len(out_pieces),)),
            pltpu.SemaphoreType.DMA((len(in_pieces),)),
            pltpu.SemaphoreType.DMA((n,)),
            pltpu.SemaphoreType.DMA((n,)),
            pltpu.SemaphoreType.DMA((2 * n + 2,)),
        ],
        compiler_params=params,
        cost_estimate=work(12 * seq * model * padded),
        name="up_projection",
    )(place, *toks, *atts, *[a for _, _, a in out_pieces], *[a for _, _, a in in_pieces])
    down_w = jnp.pad(w_down, ((0, -ff % 16), (0, 0)))
    act, dup, *dnormed2_blocks = pl.pallas_call(
        functools.partial(dup_kernel, n),
        in_specs=[ANY_SPEC] * (3 + n),
        out_specs=[ANY_SPEC] * (2 + n),
        out_shape=[shape((seq, padded), BF16), shape((seq, 2 * padded), BF16)] + blocks,
        scratch_shapes=[
            pltpu.VMEM((seq, 2 * padded), F32),
            pltpu.VMEM((n, rows, model), BF16),
            pltpu.VMEM((model, 2 * padded), BF16),
            pltpu.VMEM((padded, model), BF16),
            pltpu.VMEM((seq, padded), BF16),
            pltpu.VMEM((seq, 2 * padded), BF16),
            pltpu.VMEM((n, rows, model), BF16),
            pltpu.SemaphoreType.DMA,
            pltpu.SemaphoreType.DMA,
            pltpu.SemaphoreType.DMA((n,)),
            pltpu.SemaphoreType.DMA((n,)),
            pltpu.SemaphoreType.DMA((3 * n,)),
        ],
        compiler_params=params,
        cost_estimate=work(14 * seq * model * padded),
        name="dup",
    )(up, in_w, down_w, *cots)

    slots = replicas // 2
    chunk = part // replicas
    lanes = max(LANES, model // replicas)
    tiles = up_tiles(ff)
    in_counts = [tiles - tiles // 2, tiles // 2]
    orders = [near, far]
    in_shapes = [shape((slots, n * c, chunk, LANES), BF16) for c in in_counts for _ in range(2)]
    down_shape = shape((slots, ff, lanes), BF16)

    top = bits_of("shard") - 1
    sums = scatter_bits(enumerate(dnormed2_blocks), "shard", range(top - 1))
    low, high = 1 << (top - 1), 1 << top
    mine, other = pl.pallas_call(
        add_kernel,
        in_specs=[VMEM_SPEC] * 4,
        out_shape=[shape((rows, model), F32), shape((rows, model), BF16)],
        compiler_params=pltpu.CompilerParams(vmem_limit_bytes=16 << 20),
        name="near_sum",
    )(
        sums[0],
        swap(sums[low].astype(BF16), "shard", top - 1),
        sums[high],
        swap(sums[low | high].astype(BF16), "shard", top - 1),
    )
    in_flows = pl.pallas_call(
        ordered(functools.partial(in_kernel, n, ff, in_counts, orders), 3, 1),
        in_specs=[SMEM_SPEC] + [VMEM_SPEC] * 2 + [ANY_SPEC],
        out_shape=in_shapes,
        scratch_shapes=[pltpu.VMEM((part, 2 * padded + LANES), F32)],
        compiler_params=params,
        cost_estimate=work(8 * seq * model * padded),
        name="in_gradient",
    )(place, normed2, dup, other)
    dhidden, dproj = pl.pallas_call(
        ordered(norm_back_kernel, 4, 1),
        in_specs=[VMEM_SPEC] * 4 + [ANY_SPEC],
        out_shape=[shape((rows, model), F32), shape((rows, model), BF16)],
        compiler_params=pltpu.CompilerParams(vmem_limit_bytes=24 << 20),
        name="norm_back",
    )(mine, swap(other, "shard", top), hidden, cotangent, in_flows[0])
    down_keep, down_send, *mlp_blocks = pl.pallas_call(
        ordered(functools.partial(down_kernel, n, ff, near), 3 + n, 1),
        in_specs=[SMEM_SPEC] + [VMEM_SPEC] * (2 + n) + [ANY_SPEC],
        out_shape=[down_shape, down_shape] + blocks,
        scratch_shapes=[pltpu.VMEM((padded, model), F32)],
        compiler_params=params,
        cost_estimate=work(8 * seq * model * padded),
        name="down_gradient",
    )(place, act, down_w, *cots, dproj)
    dprojs = gather_list(dproj, "shard")

    out_shape = shape((slots, part, lanes), BF16)
    dqkv, out_keep, out_send = pl.pallas_call(
        ordered(functools.partial(attention_back_kernel, n, heads, near), n + 10, 1),
        in_specs=[SMEM_SPEC] + [VMEM_SPEC] * (n + 9) + [ANY_SPEC],
        out_shape=[shape((seq, 3 * width), BF16), out_shape, out_shape],
        scratch_shapes=[
            pltpu.VMEM((seq, width), BF16),
            pltpu.VMEM((seq + 2 * HALF, width), F32),
            pltpu.VMEM((seq + 2 * HALF, width), F32),
            pltpu.VMEM((part, model), F32),
        ],
        compiler_params=params,
        cost_estimate=work(40 * seq * model * width),
        name="attention_back",
    )(place, *dprojs, w_out, attended, queries, keys, values, *tables, down_keep)

    mlp_blocks = [after(b, dprojs[n // 2]) for b in mlp_blocks]
    mlp = scatter_sum_list(mlp_blocks, "shard")
    output = (hidden + mlp).astype(BF16)

    qkv_tiles = 3 * width // LANES
    qkv_shape = shape((slots, n * qkv_tiles, chunk, LANES), BF16)
    qkv_keep, qkv_send = pl.pallas_call(
        functools.partial(qkv_kernel, n, near),
        in_specs=[SMEM_SPEC] + [VMEM_SPEC] * 2,
        out_shape=[qkv_shape, qkv_shape],
        scratch_shapes=[pltpu.VMEM((part, 3 * width), F32)],
        compiler_params=params,
        cost_estimate=work(12 * seq * model * width),
        name="qkv_gradient",
    )(place, normed1, dqkv)
    dnormed1_blocks = pl.pallas_call(
        ordered(functools.partial(project_back_kernel, n), 3, 1),
        in_specs=[SMEM_SPEC] + [VMEM_SPEC] * 2 + [ANY_SPEC],
        out_shape=blocks,
        compiler_params=params,
        cost_estimate=work(6 * seq * model * width),
        name="project_back",
    )(place, dqkv, qkv_w, qkv_keep)
    dnormed1 = scatter_sum_list(dnormed1_blocks, "shard")
    hat1, scale1 = normalise(tokens.astype(F32))
    input_grad = dhidden + norm_backward(dnormed1, hat1, scale1)

    def turned(share, tiles):
        return turn(share.reshape(n, tiles, chunk, LANES), n).reshape(n * tiles, chunk, LANES)

    gates = [dqkv, qkv_keep, dnormed1_blocks[0]]
    in_pairs = []
    for f, (count, order) in enumerate(zip(in_counts, orders)):
        share = replica_reduce(in_flows[2 * f], in_flows[2 * f + 1], order, gates)
        in_pairs.append(replica_spread(turned(share, count), order))
    down_pair = replica_spread(replica_reduce(down_keep, down_send, near, gates), near)
    out_pair = replica_spread(replica_reduce(out_keep, out_send, near), near)
    qkv_share = turned(replica_reduce(qkv_keep, qkv_send, near), qkv_tiles)
    qkv_pair = replica_spread(qkv_share, near)

    in_total, ln2_total = columns_out(
        place, in_pairs, in_counts, orders, w_in, gain2, n, ff=ff
    )
    down_total = rows_out(place, down_pair, model, near)
    out_total = rows_out(place, out_pair, model, near)
    qkv_total, ln1_total = columns_out(
        place,
        [qkv_pair],
        [qkv_tiles],
        [near],
        w_qkv,
        gain1,
        n,
        head_cols=head_cols,
        width=width,
    )
    return (
        output,
        input_grad,
        ln1_total,
        qkv_total,
        out_total,
        ln2_total,
        in_total,
        down_total,
    )


def solution(mesh):
    return jax.shard_map(
        shards,
        mesh=mesh,
        in_specs=(
            P(("rep", "shard"), None),
            P("rep", None),
            P("shard"),
            P("shard", None),
            P("shard", None),
            P("shard"),
            P("shard", None),
            P("shard", None),
            P(("rep", "shard"), None),
        ),
        out_specs=(
            P(("rep", "shard"), None),
            P(("rep", "shard"), None),
            P("shard"),
            P("shard", None),
            P("shard", None),
            P("shard"),
            P("shard", None),
            P("shard", None),
        ),
        check_vma=False,
    )
```

```python
import functools
import math

import jax
import jax.numpy as jnp
from jax import lax
from jax.experimental import pallas as pl
from jax.experimental.pallas import tpu as pltpu
from jax.sharding import PartitionSpec as P

HEADS = 16
HEAD_DIM = 64
HALF = 64
QB = 128
LANES = 128

norm_epsilon = 1e-05
rope_base = 10000.0
masked_score = -1e30

F32 = jnp.float32
BF16 = jnp.bfloat16
VMEM_LIMIT = 52 << 20


def bits_of(axis):
    return lax.axis_size(axis).bit_length() - 1


def bit_of(axis, bit):
    return (lax.axis_index(axis) >> bit) & 1


def swap(x, axis, bit):
    size = lax.axis_size(axis)
    return lax.ppermute(x, axis, [(i, i ^ (1 << bit)) for i in range(size)])


def gather_list(x, axis):
    blocks = {0: x}
    for bit in reversed(range(bits_of(axis))):
        for j in list(blocks):
            blocks[j | 1 << bit] = swap(blocks[j], axis, bit)
    return [blocks[j] for j in range(len(blocks))]


def scatter_bits(blocks, axis, bits):
    blocks = dict(blocks)
    for bit in bits:
        for j in [j for j in blocks if j >> bit & 1]:
            got = swap(blocks.pop(j).astype(BF16), axis, bit)
            k = j ^ (1 << bit)
            blocks[k] = blocks[k].astype(F32) + got.astype(F32)
    return blocks


def scatter_sum_list(blocks, axis):
    return scatter_bits(enumerate(blocks), axis, range(bits_of(axis)))[0]


def parity():
    return bit_of("rep", 0) ^ bit_of("rep", 1)


def half_by_replica(x, dim):
    shape = x.shape
    x = x.reshape(shape[:dim] + (2, shape[dim] // 2) + shape[dim + 1 :])
    return lax.dynamic_index_in_dim(x, parity(), dim, keepdims=False)


def fetch_far(send, dim, top, gate):
    got = swap(half_by_replica(send, dim), "shard", top)
    kept = got if gate is None else after(got, gate())
    first, second = jnp.split(kept, 2, axis=dim)
    return [
        (1 << top, 0, got),
        (1 << top, 1, swap(first, "rep", 0)),
        (1 << top, 2, swap(second, "rep", 1)),
    ]


def gather_weight(x, gate=None):
    top = bits_of("shard") - 1
    pieces = [(0, None, x)] + fetch_far(x, 0, top, gate)
    for bit in reversed(range(top)):
        pieces += [(j | 1 << bit, h, swap(a, "shard", bit)) for j, h, a in pieces]
    return pieces


def split_weight(x, gate=None):
    me = lax.axis_index("shard")
    top = bits_of("shard") - 1

    def part_for(a, bit):
        start = ((me & (a.shape[0] - 1)) >> bit ^ 1) << bit
        return lax.dynamic_slice_in_dim(a, start, 1 << bit)

    pieces = [(0, None, x)] + fetch_far(part_for(x, top), 1, top, gate)
    for bit in reversed(range(top)):
        pieces += [(j | 1 << bit, h, swap(part_for(a, bit), "shard", bit)) for j, h, a in pieces]
    return pieces


def add_halves(keep, got):
    def total(a, b):
        return (keep[a:b].astype(F32) + got[a:b].astype(F32)).astype(BF16)

    size = keep.shape[0]
    if size == 1:
        return total(0, 1), None
    return total(0, size // 2), total(size // 2, size)


def gated(value, gates, step):
    return after(value, *gates[step]) if step < len(gates) else value


def replica_reduce(keep, send, order, gates=()):
    for step, bit in enumerate(order):
        keep, send = add_halves(keep, gated(swap(send, "rep", bit), gates, step))
    return keep[0]


class PairReduce:
    def __init__(self, p, q, orders):
        self.p, self.q, self.orders = p, q, orders

    def step(self, i, gates=()):
        p, q = self.p, self.q
        got_p = swap(p[1], "rep", self.orders[0][i])
        got_q = swap(q[1], "rep", self.orders[1][i])
        if gates:
            got_p, got_q = after(got_p, *gates), after(got_q, *gates)
        self.p, self.q = add_halves(p[0], got_p), add_halves(q[0], got_q)

    def finish(self, gates=()):
        rows = self.p[0].shape[1]
        keep, send = (jnp.concatenate(x, axis=1) for x in zip(self.p, self.q))
        share = replica_reduce(keep, send, self.orders[0][2:], gates)
        return share[:rows], share[rows:]


def pair_gather(p, q, orders):
    rows = p.shape[0]
    now = jnp.concatenate([p, q])[None]
    for bit in reversed(orders[0][2:]):
        now = jnp.concatenate([now, swap(now, "rep", bit)])
    pairs = []
    for x, order in zip((now[:, :rows], now[:, rows:]), orders):
        x = jnp.concatenate([x, swap(x, "rep", order[1])])
        pairs.append((x, swap(x, "rep", order[0])))
    return pairs


def turn(x, n):
    pieces = {0: x}
    for bit in reversed(range(n.bit_length() - 1)):
        for j in list(pieces):
            half = pieces[j].shape[0] // 2
            pieces[j | 1 << bit] = swap(pieces[j][half:], "shard", bit)
            pieces[j] = pieces[j][:half]
    return jnp.concatenate([pieces[j] for j in range(n)])


def slot_mask(slot, order):
    count = len(order)
    return sum(((slot >> (count - 1 - i)) & 1) << bit for i, bit in enumerate(order))


def slot_of(mask, order):
    count = len(order)
    return sum(((mask >> bit) & 1) << (count - 1 - i) for i, bit in enumerate(order))


def dot(a, b, dims):
    return lax.dot_general(a, b, (dims, ((), ())), preferred_element_type=F32)


def normalise(values):
    centred = values - jnp.mean(values, axis=-1, keepdims=True)
    scale = lax.rsqrt(jnp.mean(centred * centred, axis=-1, keepdims=True) + norm_epsilon)
    return centred * scale, scale


def weight_copies(pieces, refs, target, me, sems, rep, by_owner, rows):
    copies = []
    for i, ((j, half, shape), ref) in enumerate(zip(pieces, refs)):
        start = (me ^ j if by_owner else j) * rows
        count = rows
        if half is not None:
            own = (rep ^ (rep >> 1)) & 1
            count = rows // 2 if half == 0 else rows // 4
            start = start + (own if half == 0 else 1 - own) * (rows // 2)
            start = start + (rows // 4 if half == 2 else 0)
        source = ref.at[me & (shape[0] - 1)] if len(shape) == 3 else ref
        place = target.at[pl.ds(pl.multiple_of(start, count), count), :]
        copies.append(pltpu.make_async_copy(source, place, sems.at[i]))
    return copies


def partner(x):
    width = x.shape[-1]
    lane = lax.broadcasted_iota(jnp.int32, x.shape, 1)
    front = (lane % HEAD_DIM) < HEAD_DIM // 2
    return jnp.where(
        front,
        pltpu.roll(x, width - HEAD_DIM // 2, 1),
        pltpu.roll(x, HEAD_DIM // 2, 1),
    )


def head_masks(heads, width):
    lane = lax.broadcasted_iota(jnp.int32, (QB, width), 1) // HEAD_DIM
    return [lane == h for h in range(heads)]


def stack_heads(x, masks):
    x = x.astype(F32)
    return jnp.concatenate([jnp.where(m, x, 0.0) for m in masks], axis=0).astype(BF16)


def merge_heads(x, masks):
    total = None
    for h, m in enumerate(masks):
        part = jnp.where(m, x[h * QB : (h + 1) * QB], 0.0)
        total = part if total is None else total + part
    return total


def window_bias(ids_q, ids_k):
    row = lax.broadcasted_iota(jnp.int32, (QB, QB + 2 * HALF), 0)
    col = lax.broadcasted_iota(jnp.int32, (QB, QB + 2 * HALF), 1)
    ids_q = jnp.concatenate([ids_q] * ((QB + 2 * HALF) // LANES), axis=1)
    allowed = (col >= row) & (col <= row + 2 * HALF) & (ids_q == ids_k)
    return jnp.where(allowed, 0.0, masked_score)


def block_probs(stacked_q, keys, bias, heads):
    scores = dot(stacked_q, keys, ((1,), (1,)))
    rows, cols = scores.shape
    scores = (scores.reshape(heads, QB, cols) + bias[None]).reshape(rows, cols)
    weights = jnp.exp(scores - jnp.max(scores, axis=-1, keepdims=True))
    return weights * (1.0 / jnp.sum(weights, axis=-1, keepdims=True))


def column_chunk(ref, chunk, cols):
    if cols >= LANES:
        return ref[:, pl.ds(pl.multiple_of(chunk * cols, cols), cols)]
    per = LANES // cols
    tile = ref[:, pl.ds(pl.multiple_of(chunk // per * LANES, LANES), LANES)]
    result = tile
    for k in range(1, per):
        result = jnp.where(chunk % per == k, pltpu.roll(tile, LANES - k * cols, 1), result)
    return result


def row_chunk(ref, chunk, rows, start):
    if rows % 8 == 0:
        return ref[pl.ds(pl.multiple_of(chunk * rows, rows), rows), start : start + LANES]
    per = 8 // rows
    tile = ref[pl.ds(pl.multiple_of(chunk // per * 8, 8), 8), start : start + LANES]
    result = tile[:rows]
    for k in range(1, per):
        result = jnp.where(chunk % per == k, tile[k * rows : (k + 1) * rows], result)
    return result


def take_columns(ref, offset, valid, size):
    begin = offset // LANES * LANES
    end = -(-(offset + valid) // LANES) * LANES
    x = ref[:, begin:end].astype(F32)
    if offset != begin:
        x = pltpu.roll(x, end - offset, 1)
    x = x[:, :size]
    if valid != size:
        lane = lax.broadcasted_iota(jnp.int32, x.shape, 1)
        x = jnp.where(lane < valid, x, 0.0)
    return x


def split_kernel(n, blocks, valid, size, gain_ref, w_ref, out_ref):
    gain = gain_ref[...]
    for owner in range(n):
        for b in range(blocks):
            x = take_columns(w_ref, (b * n + owner) * valid, valid, size)
            out_ref[owner, :, b * size : (b + 1) * size] = (x * gain).astype(BF16)


def split_columns(w, gain, n, blocks, valid, size):
    rows, cols = w.shape
    step = min(rows, 64)
    return pl.pallas_call(
        functools.partial(split_kernel, n, blocks, valid, size),
        grid=(rows // step,),
        in_specs=[
            pl.BlockSpec((step, 1), lambda i: (i, 0)),
            pl.BlockSpec((step, cols), lambda i: (i, 0)),
        ],
        out_specs=pl.BlockSpec((n, step, blocks * size), lambda i: (0, i, 0)),
        out_shape=jax.ShapeDtypeStruct((n, rows, blocks * size), BF16),
        compiler_params=pltpu.CompilerParams(vmem_limit_bytes=24 << 20),
        name="split_columns",
    )(gain, w)


def attention_kernel(
    pieces, n, heads, place_ref, cos_ref, sin_ref, idq_ref, idk_ref, *refs
):
    tok_refs, refs = refs[:n], refs[n:]
    piece_refs, refs = refs[: len(pieces)], refs[len(pieces) :]
    q_ref, k_ref, v_ref, out_ref, normed_ref, w_ref, sems = refs
    seq, width = q_ref.shape
    rows = seq // n
    me, rep = place_ref[0], place_ref[1]
    copies = weight_copies(
        pieces, piece_refs, w_ref, me, sems, rep, True, w_ref.shape[0] // n
    )
    for c in copies:
        c.start()
    edge = jnp.zeros((HALF, width), BF16)
    for ref in (k_ref, v_ref):
        ref[0:HALF, :] = edge
        ref[seq + HALF : seq + 2 * HALF, :] = edge
    for c in copies:
        c.wait()
    for j in range(n):
        start = (me ^ j) * rows
        at = pl.ds(pl.multiple_of(start, rows), rows)
        shifted = pl.ds(pl.multiple_of(start + HALF, HALF), rows)
        hat, _ = normalise(tok_refs[j][...].astype(F32))
        normed = hat.astype(BF16)
        normed_ref[at, :] = normed
        qkv = jnp.dot(normed, w_ref[...], preferred_element_type=F32)
        cos, sin = cos_ref[at, :], sin_ref[at, :]
        q, k = qkv[:, 0:width], qkv[:, width : 2 * width]
        rotated = (q * cos + partner(q) * sin).astype(BF16)
        q_ref[at, :] = (rotated.astype(F32) * (1.0 / math.sqrt(HEAD_DIM))).astype(BF16)
        k_ref[shifted, :] = (k * cos + partner(k) * sin).astype(BF16)
        v_ref[shifted, :] = qkv[:, 2 * width : 3 * width].astype(BF16)
    masks = head_masks(heads, width)

    def attend(i, carry):
        at = pl.ds(pl.multiple_of(i * QB, QB), QB)
        window = pl.ds(pl.multiple_of(i * QB, QB), QB + 2 * HALF)
        bias = window_bias(idq_ref[at, :], idk_ref[0:1, window])
        probs = block_probs(stack_heads(q_ref[at, :], masks), k_ref[window, :], bias, heads)
        mixed = jnp.dot(probs.astype(BF16), v_ref[window, :], preferred_element_type=F32)
        out_ref[at, :] = merge_heads(mixed, masks).astype(BF16)
        return carry

    lax.fori_loop(0, seq // QB, attend, 0, unroll=2)


def up_kernel(out_pieces, in_pieces, n, place_ref, *refs):
    tok_refs, refs = refs[:n], refs[n:]
    att_refs, refs = refs[:n], refs[n:]
    out_refs, refs = refs[: len(out_pieces)], refs[len(out_pieces) :]
    in_refs, refs = refs[: len(in_pieces)], refs[len(in_pieces) :]
    hidden_out, normed_out, up_out, in_out, *refs = refs
    tok, att, w_out, w_in, hidden_own, normed, up, *refs = refs
    out_sems, in_sems, att_sems, tok_sems, sems = refs
    me, rep = place_ref[0], place_ref[1]
    rows, model = tok_refs[0].shape
    copy = pltpu.make_async_copy
    att_copies = [copy(att_refs[j], att.at[j], att_sems.at[j]) for j in range(n)]
    tok_copies = [copy(tok_refs[j], tok.at[j], tok_sems.at[j]) for j in range(n)]
    part = model // n
    out_copies = weight_copies(out_pieces, out_refs, w_out, me, out_sems, rep, False, part)
    in_copies = weight_copies(in_pieces, in_refs, w_in, me, in_sems, rep, True, part)
    for c in att_copies + tok_copies[:1] + out_copies + in_copies + tok_copies[1:]:
        c.start()
    for c in att_copies + out_copies:
        c.wait()
    sent = []
    for j in range(n):
        at = pl.ds(pl.multiple_of((me ^ j) * rows, rows), rows)
        here = slice(j * rows, (j + 1) * rows)
        tok_copies[j].wait()
        hidden = tok[j].astype(F32)
        for i in range(n):
            hidden = hidden + jnp.dot(
                att[i, at, :], w_out[i * part : (i + 1) * part, :], preferred_element_type=F32
            )
        if j == 0:
            hidden_own[...] = hidden
            sent.append(copy(hidden_own, hidden_out, sems.at[2 * n]))
            sent[-1].start()
        hat, _ = normalise(hidden)
        low = hat.astype(BF16)
        normed[here, :] = low
        if j == 0:
            for c in in_copies:
                c.wait()
            sent.append(copy(w_in, in_out, sems.at[2 * n + 1]))
            sent[-1].start()
        up[here, :] = jnp.dot(low, w_in[...], preferred_element_type=F32)
        sent += [
            copy(normed.at[here, :], normed_out.at[here, :], sems.at[2 * j]),
            copy(up.at[here, :], up_out.at[here, :], sems.at[2 * j + 1]),
        ]
        for c in sent[-2:]:
            c.start()
    for c in sent:
        c.wait()


def dup_kernel(n, up_ref, w_in_ref, down_ref, *refs):
    cot_refs, refs = refs[:n], refs[n:]
    act_out, dup_out, *refs = refs
    dnormed_outs, refs = refs[:n], refs[n:]
    up, cot, w_in, w_down, act, dup, dnormed, in_sem, down_sem, up_sems, cot_sems, sems = refs
    rows, model = cot_refs[0].shape
    padded = w_down.shape[0]
    given = down_ref.shape[0]
    if given != padded:
        w_down[given:padded, :] = jnp.zeros((padded - given, model), BF16)
    copy = pltpu.make_async_copy
    down_copy = copy(down_ref, w_down.at[0:given, :], down_sem)
    in_copy = copy(w_in_ref, w_in, in_sem)
    cot_copies = [copy(cot_refs[j], cot.at[j], cot_sems.at[j]) for j in range(n)]
    up_copies = []
    for j in range(n):
        here = slice(j * rows, (j + 1) * rows)
        up_copies.append(copy(up_ref.at[here, :], up.at[here, :], up_sems.at[j]))
    for c in [up_copies[0], cot_copies[0], down_copy, in_copy]:
        c.start()
    for c in up_copies[1:] + cot_copies[1:]:
        c.start()
    sent = []
    for j in range(n):
        here = slice(j * rows, (j + 1) * rows)
        up_copies[j].wait()
        gate, lin = up[here, :padded], up[here, padded:]
        phi = 0.5 + 0.5 * lax.erf(gate * (1.0 / math.sqrt(2.0)))
        gelu = gate * phi
        slope = phi + gate * jnp.exp(gate * gate * -0.5) * (1.0 / math.sqrt(2.0 * math.pi))
        act[here, :] = (gelu * lin).astype(BF16)
        cot_copies[j].wait()
        if j == 0:
            down_copy.wait()
        dact = dot(cot[j], w_down[...], ((1,), (1,)))
        dup[here, :padded] = (dact * lin * slope).astype(BF16)
        dup[here, padded:] = (dact * gelu).astype(BF16)
        if j == 0:
            in_copy.wait()
        dnormed[j] = dot(dup[here, :], w_in[...], ((1,), (1,))).astype(BF16)
        sent += [
            copy(dnormed.at[j], dnormed_outs[j], sems.at[3 * j]),
            copy(act.at[here, :], act_out.at[here, :], sems.at[3 * j + 1]),
            copy(dup.at[here, :], dup_out.at[here, :], sems.at[3 * j + 2]),
        ]
        for c in sent[-3:]:
            c.start()
    for c in sent:
        c.wait()


def store_slots(keep_ref, send_ref, rep, order, write):
    half = keep_ref.shape[0]
    for slot in range(2 * half):
        target = keep_ref if slot < half else send_ref
        write(target, slot % half, rep ^ slot_mask(slot, order))


def up_tiles(ff):
    return 2 * (ff // LANES) + 1


def down_kernel(n, ff, far, place_ref, act, w_down, *refs):
    cot_refs, refs = refs[:n], refs[n:]
    keep, send, *refs = refs
    mlp_refs, refs = refs[:n], refs[n:]
    (down_sum,) = refs
    rows, model = cot_refs[0].shape
    cols = model // (2 * keep.shape[0])
    total = None
    for j in range(n):
        term = dot(act[j * rows : (j + 1) * rows, :], cot_refs[j][...], ((0,), (0,)))
        total = term if total is None else total + term
    down_sum[...] = total

    def write(target, slot, c):
        target[slot] = column_chunk(down_sum, c, cols)[:ff].astype(BF16)

    store_slots(keep, send, place_ref[1], far, write)
    given = w_down.shape[0]
    for j in range(n):
        low = act[j * rows : (j + 1) * rows, 0:given]
        mlp_refs[j][...] = jnp.dot(low, w_down[...], preferred_element_type=F32).astype(BF16)


def write_flows(total, starts, counts, orders, flows, index, rep):
    begin = 0
    for f, (count, order) in enumerate(zip(counts, orders)):
        keep, send = flows[2 * f], flows[2 * f + 1]
        chunk = keep.shape[2]

        def write(target, slot, c):
            for t in range(count):
                value = row_chunk(total, c, chunk, starts[begin + t])
                target[slot, index * count + t] = value.astype(BF16)

        store_slots(keep, send, rep, order, write)
        begin += count


def in_kernel(n, ff, counts, orders, place_ref, normed, dup, *refs):
    flows, in_sum = refs[:-1], refs[-1]
    me, rep = place_ref[0], place_ref[1]
    part = normed.shape[1] // n
    padded = dup.shape[1] // 2
    whole, rest = ff // LANES, ff % LANES
    starts = [t * LANES for t in range(whole)] + [padded + t * LANES for t in range(whole)]
    starts.append(2 * padded)
    for owner in range(n):
        block = dot(normed[:, owner * part : (owner + 1) * part], dup[...], ((0,), (0,)))
        in_sum[:, : 2 * padded] = block
        first = block[:, whole * LANES : (whole + 1) * LANES]
        second = block[:, padded + whole * LANES : padded + (whole + 1) * LANES]
        lane = lax.broadcasted_iota(jnp.int32, first.shape, 1)
        in_sum[:, 2 * padded :] = jnp.where(lane < rest, first, pltpu.roll(second, rest, 1))
        write_flows(in_sum, starts, counts, orders, flows, me ^ owner, rep)


def add_kernel(a_ref, b_ref, c_ref, d_ref, mine_ref, other_ref):
    mine_ref[...] = a_ref[...].astype(F32) + b_ref[...].astype(F32)
    other_ref[...] = (c_ref[...].astype(F32) + d_ref[...].astype(F32)).astype(BF16)


def norm_back_kernel(mine, got, hidden, cotangent, dhidden, dproj):
    hat, scale = normalise(hidden[...])
    e = mine[...] + got[...].astype(F32)
    value = cotangent[...].astype(F32) + norm_backward(e, hat, scale)
    dhidden[...] = value
    dproj[...] = value.astype(BF16)


def attention_back_kernel(n, heads, far, place_ref, *refs):
    dproj_refs, refs = refs[:n], refs[n:]
    w_out, att, q_ref, k_ref, v_ref, cos_ref, sin_ref, idq_ref, idk_ref, *refs = refs
    dqkv, out_keep, out_send, da, dk, dv, out_sum = refs
    me, rep = place_ref[0], place_ref[1]
    seq, width = q_ref.shape
    rows, model = dproj_refs[0].shape
    part = model // n
    dk[...] = jnp.zeros_like(dk)
    dv[...] = jnp.zeros_like(dv)
    head_cols = heads * HEAD_DIM
    total = None
    for j in range(n):
        at = pl.ds(pl.multiple_of((me ^ j) * rows, rows), rows)
        dproj = dproj_refs[j][...]
        da[at, 0:head_cols] = dot(dproj, w_out[...], ((1,), (1,))).astype(BF16)
        term = dot(att[at, :], dproj, ((0,), (0,)))
        total = term if total is None else total + term
    if head_cols != width:
        da[:, head_cols:] = jnp.zeros((seq, width - head_cols), BF16)
    out_sum[...] = total[0:part]
    cols = model // (2 * out_keep.shape[0])

    def write_out(target, slot, c):
        target[slot] = column_chunk(out_sum, c, cols).astype(BF16)

    store_slots(out_keep, out_send, rep, far, write_out)
    masks = head_masks(heads, width)

    def back(i, carry):
        at = pl.ds(pl.multiple_of(i * QB, QB), QB)
        window = pl.ds(pl.multiple_of(i * QB, QB), QB + 2 * HALF)
        bias = window_bias(idq_ref[at, :], idk_ref[0:1, window])
        queries = stack_heads(q_ref[at, :], masks)
        keys = k_ref[window, :]
        probs = block_probs(queries, keys, bias, heads)
        grads = stack_heads(da[at, :], masks)
        dprobs = dot(grads, v_ref[window, :], ((1,), (1,)))
        delta = jnp.sum(probs * dprobs, axis=-1, keepdims=True)
        dscores = (probs * (dprobs - delta)).astype(BF16)
        dq = merge_heads(jnp.dot(dscores, keys, preferred_element_type=F32), masks)
        dq = dq * (1.0 / math.sqrt(HEAD_DIM))
        cos, sin = cos_ref[at, :], sin_ref[at, :]
        dqkv[at, 0:width] = (dq * cos - partner(dq) * sin).astype(BF16)
        dk[window, :] += dot(dscores, queries, ((0,), (0,)))
        dv[window, :] += dot(probs.astype(BF16), grads, ((0,), (0,)))
        return carry

    lax.fori_loop(0, seq // QB, back, 0, unroll=2)

    def finish(i, carry):
        at = pl.ds(pl.multiple_of(i * QB, QB), QB)
        shifted = pl.ds(pl.multiple_of(i * QB + HALF, HALF), QB)
        cos, sin = cos_ref[at, :], sin_ref[at, :]
        g = dk[shifted, :]
        dqkv[at, width : 2 * width] = (g * cos - partner(g) * sin).astype(BF16)
        dqkv[at, 2 * width : 3 * width] = dv[shifted, :].astype(BF16)
        return carry

    lax.fori_loop(0, seq // QB, finish, 0)


def qkv_kernel(n, counts, orders, place_ref, normed, dqkv, *refs):
    flows, qkv_sum = refs[:-1], refs[-1]
    me, rep = place_ref[0], place_ref[1]
    part = normed.shape[1] // n
    starts = [t * LANES for t in range(sum(counts))]
    for owner in range(n):
        qkv_sum[...] = dot(normed[:, owner * part : (owner + 1) * part], dqkv[...], ((0,), (0,)))
        write_flows(qkv_sum, starts, counts, orders, flows, me ^ owner, rep)


def project_back_kernel(n, place_ref, dqkv, w_qkv, *out_refs):
    rows = out_refs[0].shape[0]
    for j in range(n):
        at = pl.ds(pl.multiple_of((place_ref[0] ^ j) * rows, rows), rows)
        out_refs[j][...] = dot(dqkv[at, :], w_qkv[...], ((1,), (1,))).astype(BF16)


def place_piece(canvas, piece, offset, valid):
    shift = offset % LANES
    height, size = piece.shape
    count = -(-(shift + valid) // LANES)
    if count * LANES > size:
        piece = jnp.concatenate([piece, jnp.zeros((height, count * LANES - size), F32)], axis=1)
    if shift:
        piece = pltpu.roll(piece, shift, 1)
    lane = lax.broadcasted_iota(jnp.int32, (height, LANES), 1)
    for t in range(count):
        tile = piece[:, t * LANES : (t + 1) * LANES]
        low, high = shift - t * LANES, shift + valid - t * LANES
        if low > 0 or high < LANES:
            tile = jnp.where((lane >= low) & (lane < high), tile, 0.0)
        index = offset // LANES + t
        canvas[index] = tile if index not in canvas else canvas[index] + tile


def columns_out_kernel(n, ff, head_cols, width, counts, orders, place_ref, gain_ref, w_ref, *refs):
    me, rep = place_ref[0], place_ref[1]
    *parts, out_ref, ln_ref = refs
    half = parts[0].shape[0]
    slots = [slot_of(rep ^ pl.program_id(0), order) for order in orders]

    def read(owner, t):
        f = 0
        while t >= counts[f]:
            t -= counts[f]
            f += 1
        slot, index = slots[f], (me ^ owner) * counts[f] + t
        at = slot & (half - 1)
        now, got = parts[2 * f][at, index], parts[2 * f + 1][at, index]
        return jnp.where(slot < half, now, got).astype(F32)

    canvas = {}
    for owner in range(n):
        tile = functools.partial(read, owner)

        if ff:
            whole, rest = ff // LANES, ff % LANES
            last = tile(2 * whole)
            gate = jnp.concatenate([tile(t) for t in range(whole)] + [last], axis=1)
            last = pltpu.roll(last, LANES - rest, 1)
            lin = jnp.concatenate([tile(whole + t) for t in range(whole)] + [last], axis=1)
            place_piece(canvas, gate, owner * ff, ff)
            place_piece(canvas, lin, (n + owner) * ff, ff)
        else:
            per = width // LANES
            for b in range(3):
                piece = jnp.concatenate([tile(b * per + t) for t in range(per)], axis=1)
                place_piece(canvas, piece, (b * n + owner) * head_cols, head_cols)
    gain = gain_ref[...]
    total = None
    for index, value in canvas.items():
        at = slice(index * LANES, (index + 1) * LANES)
        term = value * w_ref[:, at].astype(F32)
        total = term if total is None else total + term
        out_ref[:, at] = value * gain
    ln_ref[...] = jnp.sum(total, axis=1, keepdims=True)


def columns_out(place, pairs, counts, orders, weight, gain, n, ff=0, head_cols=0, width=0):
    parts = [a for pair in pairs for a in pair]
    chunk = parts[0].shape[2]
    part, cols = weight.shape
    count = part // chunk
    part_specs = [pl.BlockSpec(a.shape, lambda i: (0, 0, 0, 0)) for a in parts]
    total, ln = pl.pallas_call(
        functools.partial(columns_out_kernel, n, ff, head_cols, width, counts, orders),
        grid=(count,),
        in_specs=[
            pl.BlockSpec(memory_space=pltpu.SMEM),
            pl.BlockSpec((None, chunk, 1), lambda i: (i, 0, 0)),
            pl.BlockSpec((None, chunk, cols), lambda i: (i, 0, 0)),
            *part_specs,
        ],
        out_specs=[
            pl.BlockSpec((None, chunk, cols), lambda i: (i, 0, 0)),
            pl.BlockSpec((None, chunk, 1), lambda i: (i, 0, 0)),
        ],
        out_shape=[
            jax.ShapeDtypeStruct((count, chunk, cols), F32),
            jax.ShapeDtypeStruct((count, chunk, 1), F32),
        ],
        compiler_params=pltpu.CompilerParams(vmem_limit_bytes=32 << 20),
        name="columns_out",
    )(place, gain.reshape(count, chunk, 1), weight.reshape(count, chunk, cols), *parts)
    return total.reshape(part, cols), ln.reshape(part)


def rows_out_kernel(order, cols, skip, place_ref, *refs):
    *parts, out_ref = refs
    rep = place_ref[1]

    def chunk(c):
        half = parts[0].shape[0]
        slot = slot_of(rep ^ c, order)
        at = slot & (half - 1)
        rows = slice(skip, skip + out_ref.shape[0])
        return jnp.where(slot < half, parts[0][at, rows], parts[1][at, rows]).astype(F32)

    count = out_ref.shape[1] // cols
    if cols >= LANES:
        for c in range(count):
            out_ref[:, c * cols : (c + 1) * cols] = chunk(c)
    else:
        per = LANES // cols
        lane = lax.broadcasted_iota(jnp.int32, out_ref.shape[:1] + (LANES,), 1) // cols
        for t in range(count // per):
            value = chunk(per * t)
            for k in range(1, per):
                value = jnp.where(lane == k, pltpu.roll(chunk(per * t + k), k * cols, 1), value)
            out_ref[:, t * LANES : (t + 1) * LANES] = value


def rows_out(place, pair, skip, rows, model, order):
    return pl.pallas_call(
        functools.partial(rows_out_kernel, order, model // (2 * pair[0].shape[0]), skip),
        in_specs=[pl.BlockSpec(memory_space=pltpu.SMEM)]
        + [pl.BlockSpec(memory_space=pltpu.VMEM)] * 2,
        out_shape=jax.ShapeDtypeStruct((rows, model), F32),
        compiler_params=pltpu.CompilerParams(vmem_limit_bytes=32 << 20),
        name="rows_out",
    )(place, *pair)


def ordered(kernel, first, count):
    def body(*refs):
        kernel(*refs[:first], *refs[first + count :])

    return body


def work(flops):
    return pl.CostEstimate(flops=int(flops), bytes_accessed=1 << 22, transcendentals=0)


SMEM_SPEC = pl.BlockSpec(memory_space=pltpu.SMEM)
VMEM_SPEC = pl.BlockSpec(memory_space=pltpu.VMEM)
ANY_SPEC = pl.BlockSpec(memory_space=pl.ANY)


def norm_backward(grad_hat, normed, scale):
    return (
        grad_hat
        - jnp.mean(grad_hat, axis=-1, keepdims=True)
        - normed * jnp.mean(grad_hat * normed, axis=-1, keepdims=True)
    ) * scale


def after(value, *earlier):
    return lax.optimization_barrier((value,) + earlier)[0]


def shards(tokens, segment_ids, ln1_gain, w_qkv, w_out, ln2_gain, w_in, w_down, cotangent):
    n = lax.axis_size("shard")
    replicas = lax.axis_size("rep")
    me = lax.axis_index("shard")
    place = jnp.stack([me, lax.axis_index("rep")]).astype(jnp.int32)
    rows, model = tokens.shape
    seq = rows * n
    part = model // n
    ff = w_down.shape[0]
    heads = HEADS // n
    head_cols = heads * HEAD_DIM
    width = max(LANES, head_cols)
    padded = -(-ff // LANES) * LANES
    near = list(range(bits_of("rep")))
    far = near[1:2] + near[:1] + near[2:]
    shape = jax.ShapeDtypeStruct
    params = pltpu.CompilerParams(vmem_limit_bytes=VMEM_LIMIT)

    gain1 = ln1_gain.astype(F32)[:, None]
    gain2 = ln2_gain.astype(F32)[:, None]
    qkv_to = split_columns(w_qkv, gain1, n, 3, head_cols, width)
    in_to = split_columns(w_in, gain2, n, 2, ff, padded)
    qkv_pieces = split_weight(qkv_to)

    toks = gather_list(tokens, "shard")

    lane = jnp.arange(width, dtype=jnp.int32) % HEAD_DIM
    half = HEAD_DIM // 2
    frequency = jnp.exp(-math.log(rope_base) * 2.0 * (lane % half).astype(F32) / HEAD_DIM)
    angles = jnp.arange(seq, dtype=F32)[:, None] * frequency[None, :]
    sign = jnp.where(lane < half, -1.0, 1.0)
    ids = segment_ids[0]
    tables = (
        jnp.cos(angles),
        jnp.sin(angles) * sign[None, :],
        jnp.broadcast_to(ids[:, None], (seq, LANES)),
        jnp.pad(ids, (HALF, HALF), constant_values=-1)[None],
    )

    def about(pieces):
        return [(j, h, a.shape) for j, h, a in pieces]

    queries, keys, values, attended, normed1, qkv_w = pl.pallas_call(
        functools.partial(attention_kernel, about(qkv_pieces), n, heads),
        in_specs=[SMEM_SPEC] + [VMEM_SPEC] * (4 + n) + [ANY_SPEC] * len(qkv_pieces),
        out_shape=(
            shape((seq, width), BF16),
            shape((seq + 2 * HALF, width), BF16),
            shape((seq + 2 * HALF, width), BF16),
            shape((seq, width), BF16),
            shape((seq, model), BF16),
            shape((model, 3 * width), BF16),
        ),
        scratch_shapes=[pltpu.SemaphoreType.DMA((len(qkv_pieces),))],
        compiler_params=params,
        cost_estimate=work(40 * seq * model * width),
        name="attention",
    )(place, *tables, *toks, *[a for _, _, a in qkv_pieces])

    atts = gather_list(attended[:, :head_cols], "shard")

    def once_attended():
        return atts[1]

    far_done = [toks[n // 2], qkv_pieces[1][2]]
    out_pieces = gather_weight(after(w_out, *far_done), once_attended)
    in_pieces = split_weight(after(in_to, *far_done), once_attended)
    cots = gather_list(after(cotangent, atts[n // 2]), "shard")
    blocks = [shape((rows, model), BF16)] * n
    hidden, normed2, up, in_w = pl.pallas_call(
        functools.partial(up_kernel, about(out_pieces), about(in_pieces), n),
        in_specs=[SMEM_SPEC] + [ANY_SPEC] * (2 * n + len(out_pieces) + len(in_pieces)),
        out_specs=[ANY_SPEC] * 4,
        out_shape=[
            shape((rows, model), F32),
            shape((seq, model), BF16),
            shape((seq, 2 * padded), F32),
            shape((model, 2 * padded), BF16),
        ],
        scratch_shapes=[
            pltpu.VMEM((n, rows, model), BF16),
            pltpu.VMEM((n, seq, head_cols), BF16),
            pltpu.VMEM((model, model), BF16),
            pltpu.VMEM((model, 2 * padded), BF16),
            pltpu.VMEM((rows, model), F32),
            pltpu.VMEM((seq, model), BF16),
            pltpu.VMEM((seq, 2 * padded), F32),
            pltpu.SemaphoreType.DMA((len(out_pieces),)),
            pltpu.SemaphoreType.DMA((len(in_pieces),)),
            pltpu.SemaphoreType.DMA((n,)),
            pltpu.SemaphoreType.DMA((n,)),
            pltpu.SemaphoreType.DMA((2 * n + 2,)),
        ],
        compiler_params=params,
        cost_estimate=work(12 * seq * model * padded),
        name="up_projection",
    )(place, *toks, *atts, *[a for _, _, a in out_pieces], *[a for _, _, a in in_pieces])
    down_w = jnp.pad(w_down, ((0, -ff % 16), (0, 0)))
    act, dup, *dnormed2_blocks = pl.pallas_call(
        functools.partial(dup_kernel, n),
        in_specs=[ANY_SPEC] * (3 + n),
        out_specs=[ANY_SPEC] * (2 + n),
        out_shape=[shape((seq, padded), BF16), shape((seq, 2 * padded), BF16)] + blocks,
        scratch_shapes=[
            pltpu.VMEM((seq, 2 * padded), F32),
            pltpu.VMEM((n, rows, model), BF16),
            pltpu.VMEM((model, 2 * padded), BF16),
            pltpu.VMEM((padded, model), BF16),
            pltpu.VMEM((seq, padded), BF16),
            pltpu.VMEM((seq, 2 * padded), BF16),
            pltpu.VMEM((n, rows, model), BF16),
            pltpu.SemaphoreType.DMA,
            pltpu.SemaphoreType.DMA,
            pltpu.SemaphoreType.DMA((n,)),
            pltpu.SemaphoreType.DMA((n,)),
            pltpu.SemaphoreType.DMA((3 * n,)),
        ],
        compiler_params=params,
        cost_estimate=work(14 * seq * model * padded),
        name="dup",
    )(up, in_w, down_w, *cots)

    slots = replicas // 2
    chunk = part // replicas
    lanes = max(LANES, model // replicas)
    tiles = up_tiles(ff)
    second = max(1, tiles * 3 // 11)
    in_counts = [tiles - second, second]
    orders = [near, far]
    in_shapes = [shape((slots, n * c, chunk, LANES), BF16) for c in in_counts for _ in range(2)]
    down_shape = shape((slots, ff, lanes), BF16)

    top = bits_of("shard") - 1
    sums = scatter_bits(enumerate(dnormed2_blocks), "shard", range(top - 1))
    low, high = 1 << (top - 1), 1 << top
    mine, other = pl.pallas_call(
        add_kernel,
        in_specs=[VMEM_SPEC] * 4,
        out_shape=[shape((rows, model), F32), shape((rows, model), BF16)],
        compiler_params=pltpu.CompilerParams(vmem_limit_bytes=16 << 20),
        name="near_sum",
    )(
        sums[0],
        swap(sums[low].astype(BF16), "shard", top - 1),
        sums[high],
        swap(sums[low | high].astype(BF16), "shard", top - 1),
    )
    in_flows = pl.pallas_call(
        ordered(functools.partial(in_kernel, n, ff, in_counts, orders), 3, 1),
        in_specs=[SMEM_SPEC] + [VMEM_SPEC] * 2 + [ANY_SPEC],
        out_shape=in_shapes,
        scratch_shapes=[pltpu.VMEM((part, 2 * padded + LANES), F32)],
        compiler_params=params,
        cost_estimate=work(8 * seq * model * padded),
        name="in_gradient",
    )(place, normed2, dup, other)
    def flow_rows(a):
        return a.reshape(a.shape[0], -1, LANES)

    in_flows = [flow_rows(a) for a in in_flows]
    in_reduce = PairReduce(in_flows[:2], in_flows[2:], orders)
    dhidden, dproj = pl.pallas_call(
        ordered(norm_back_kernel, 4, 1),
        in_specs=[VMEM_SPEC] * 4 + [ANY_SPEC],
        out_shape=[shape((rows, model), F32), shape((rows, model), BF16)],
        compiler_params=pltpu.CompilerParams(vmem_limit_bytes=24 << 20),
        name="norm_back",
    )(mine, swap(other, "shard", top), hidden, cotangent, in_flows[0])
    down_keep, down_send, *mlp_blocks = pl.pallas_call(
        ordered(functools.partial(down_kernel, n, ff, far), 3 + n, 1),
        in_specs=[SMEM_SPEC] + [VMEM_SPEC] * (2 + n) + [ANY_SPEC],
        out_shape=[down_shape, down_shape] + blocks,
        scratch_shapes=[pltpu.VMEM((padded, model), F32)],
        compiler_params=params,
        cost_estimate=work(8 * seq * model * padded),
        name="down_gradient",
    )(place, act, down_w, *cots, dproj)
    dprojs = gather_list(dproj, "shard")
    in_reduce.step(0, [dprojs[n // 2]])

    out_shape = shape((slots, part, lanes), BF16)
    dqkv, out_keep, out_send = pl.pallas_call(
        ordered(functools.partial(attention_back_kernel, n, heads, far), n + 10, 3),
        in_specs=[SMEM_SPEC] + [VMEM_SPEC] * (n + 9) + [ANY_SPEC] * 3,
        out_shape=[shape((seq, 3 * width), BF16), out_shape, out_shape],
        scratch_shapes=[
            pltpu.VMEM((seq, width), BF16),
            pltpu.VMEM((seq + 2 * HALF, width), F32),
            pltpu.VMEM((seq + 2 * HALF, width), F32),
            pltpu.VMEM((part, model), F32),
        ],
        compiler_params=params,
        cost_estimate=work(40 * seq * model * width),
        name="attention_back",
    )(place, *dprojs, w_out, attended, queries, keys, values, *tables, down_keep, in_reduce.p[1], in_reduce.q[1])

    mlp_blocks = [after(b, dprojs[n // 2]) for b in mlp_blocks]
    mlp = scatter_sum_list(mlp_blocks, "shard")
    output = (hidden + mlp).astype(BF16)

    qkv_tiles = 3 * width // LANES
    qkv_counts = [qkv_tiles - qkv_tiles // 3, qkv_tiles // 3]
    in_reduce.step(1, [dqkv])
    qkv_flows = pl.pallas_call(
        ordered(functools.partial(qkv_kernel, n, qkv_counts, orders), 3, 2),
        in_specs=[SMEM_SPEC] + [VMEM_SPEC] * 2 + [ANY_SPEC] * 2,
        out_shape=[shape((slots, n * c, chunk, LANES), BF16) for c in qkv_counts for _ in range(2)],
        scratch_shapes=[pltpu.VMEM((part, 3 * width), F32)],
        compiler_params=params,
        cost_estimate=work(12 * seq * model * width),
        name="qkv_gradient",
    )(place, normed1, dqkv, in_reduce.p[1], in_reduce.q[1])
    qkv_flows = [flow_rows(a) for a in qkv_flows]
    dnormed1_blocks = pl.pallas_call(
        ordered(functools.partial(project_back_kernel, n), 3, 1),
        in_specs=[SMEM_SPEC] + [VMEM_SPEC] * 2 + [ANY_SPEC],
        out_shape=blocks,
        compiler_params=params,
        cost_estimate=work(6 * seq * model * width),
        name="project_back",
    )(place, dqkv, qkv_w, qkv_flows[0])
    dnormed1 = scatter_sum_list(dnormed1_blocks, "shard")
    hat1, scale1 = normalise(tokens.astype(F32))
    input_grad = dhidden + norm_backward(dnormed1, hat1, scale1)

    def turned(p, q, counts):
        sizes = [c * chunk for c in counts]
        whole = jnp.concatenate([p.reshape(n, sizes[0], LANES), q.reshape(n, sizes[1], LANES)], 1)
        whole = turn(whole, n)
        return whole[:, : sizes[0]].reshape(-1, LANES), whole[:, sizes[0] :].reshape(-1, LANES)

    def tiles_of(pair, count):
        rows = n * count * chunk
        return [a[:, :rows].reshape(a.shape[0], n * count, chunk, LANES) for a in pair]

    attention_done = [qkv_flows[0], dnormed1_blocks[0]]
    down_share = replica_reduce(down_keep, down_send, far, [[dqkv], attention_done])
    in_p, in_q = turned(*in_reduce.finish([attention_done]), in_counts)
    in_p, in_q = pair_gather(jnp.concatenate([in_p, down_share]), in_q, orders)

    split = qkv_flows[2].shape[1]
    qkv_q = [jnp.concatenate(x, axis=1) for x in zip(qkv_flows[2:], (out_keep, out_send))]
    qkv_reduce = PairReduce(qkv_flows[:2], qkv_q, orders)
    qkv_reduce.step(0)
    qkv_reduce.step(1)
    qkv_p, qkv_q = qkv_reduce.finish()
    out_share = qkv_q[split:]
    qkv_p, qkv_q = turned(qkv_p, qkv_q[:split], qkv_counts)
    qkv_p, qkv_q = pair_gather(qkv_p, jnp.concatenate([qkv_q, out_share]), orders)

    in_total, ln2_total = columns_out(
        place,
        [tiles_of(in_p, in_counts[0]), tiles_of(in_q, in_counts[1])],
        in_counts,
        orders,
        w_in,
        gain2,
        n,
        ff=ff,
    )
    down_total = rows_out(place, in_p, n * in_counts[0] * chunk, ff, model, near)
    out_total = rows_out(place, qkv_q, split, part, model, far)
    qkv_total, ln1_total = columns_out(
        place,
        [tiles_of(qkv_p, qkv_counts[0]), tiles_of(qkv_q, qkv_counts[1])],
        qkv_counts,
        orders,
        w_qkv,
        gain1,
        n,
        head_cols=head_cols,
        width=width,
    )
    return (
        output,
        input_grad,
        ln1_total,
        qkv_total,
        out_total,
        ln2_total,
        in_total,
        down_total,
    )


def solution(mesh):
    return jax.shard_map(
        shards,
        mesh=mesh,
        in_specs=(
            P(("rep", "shard"), None),
            P("rep", None),
            P("shard"),
            P("shard", None),
            P("shard", None),
            P("shard"),
            P("shard", None),
            P("shard", None),
            P(("rep", "shard"), None),
        ),
        out_specs=(
            P(("rep", "shard"), None),
            P(("rep", "shard"), None),
            P("shard"),
            P("shard", None),
            P("shard", None),
            P("shard"),
            P("shard", None),
            P("shard", None),
        ),
        check_vma=False,
    )
```

```python
import functools
import math

import jax
import jax.numpy as jnp
from jax import lax
from jax.experimental import pallas as pl
from jax.experimental.pallas import tpu as pltpu
from jax.sharding import PartitionSpec as P

HEADS = 16
HEAD_DIM = 64
HALF = 64
QB = 128
LANES = 128

norm_epsilon = 1e-05
rope_base = 10000.0
masked_score = -1e30

F32 = jnp.float32
BF16 = jnp.bfloat16
VMEM_LIMIT = 52 << 20


def bits_of(axis):
    return lax.axis_size(axis).bit_length() - 1


def bit_of(axis, bit):
    return (lax.axis_index(axis) >> bit) & 1


def swap(x, axis, bit):
    size = lax.axis_size(axis)
    return lax.ppermute(x, axis, [(i, i ^ (1 << bit)) for i in range(size)])


def add_halves(keep, got):
    def total(a, b):
        return (keep[a:b].astype(F32) + got[a:b].astype(F32)).astype(BF16)

    size = keep.shape[0]
    if size == 1:
        return total(0, 1), None
    return total(0, size // 2), total(size // 2, size)


def block_order(n):
    bits = n.bit_length() - 1
    return [sum(((k >> b) & 1) << (bits - 1 - b) for b in range(bits)) for k in range(n)]


class Group:
    def __init__(self, array, held):
        self.array, self.held = array, held


def join(groups, bit, arrays, axis):
    held, start = [], 0
    for group in groups:
        held += [(j | 1 << bit, code, start + first, rows) for j, code, first, rows in group.held]
        start += group.array.shape[axis]
    array = arrays[0] if len(arrays) == 1 else jnp.concatenate(arrays, axis=axis)
    return Group(swap(array, "shard", bit), held)


def gather_rows(x, gate=None):
    rows = x.shape[0]
    groups = [Group(x, [(0, None, 0, rows)])]
    for bit in reversed(range(bits_of("shard"))):
        arrays = [g.array for g in groups]
        if gate is not None and len(arrays) > 1:
            arrays[-1] = after(arrays[-1], *gate())
        groups = groups + [join(groups, bit, arrays, 0)]
    return groups


def parity():
    return bit_of("rep", 0) ^ bit_of("rep", 1)


def half_by_replica(x, dim):
    shape = x.shape
    x = x.reshape(shape[:dim] + (2, shape[dim] // 2) + shape[dim + 1 :])
    return lax.dynamic_index_in_dim(x, parity(), dim, keepdims=False)


def fetch_far(send, dim, top, gate):
    got = swap(half_by_replica(send, dim), "shard", top)
    kept = got if gate is None else after(got, gate)
    first, second = jnp.split(kept, 2, axis=dim)
    size = got.shape[dim]
    return [
        Group(got, [(1 << top, 0, 0, size)]),
        Group(swap(first, "rep", 0), [(1 << top, 1, 0, size // 2)]),
        Group(swap(second, "rep", 1), [(1 << top, 2, 0, size // 2)]),
    ]


def gather_weight(x, gate=None):
    top = bits_of("shard") - 1
    groups = [Group(x, [(0, None, 0, x.shape[0])])] + fetch_far(x, 0, top, gate)
    for bit in reversed(range(top)):
        groups = groups + [join(groups, bit, [g.array for g in groups], 0)]
    return groups


def split_weight(x, gate=None):
    me = lax.axis_index("shard")
    top = bits_of("shard") - 1

    def part_for(a, bit):
        start = ((me & (a.shape[0] - 1)) >> bit ^ 1) << bit
        return lax.dynamic_slice_in_dim(a, start, 1 << bit)

    groups = [Group(x, [(0, None, 0, x.shape[1])])] + fetch_far(part_for(x, top), 1, top, gate)
    for bit in reversed(range(top)):
        groups = groups + [join(groups, bit, [part_for(g.array, bit) for g in groups], 1)]
    return groups


def gated(value, gates, step):
    return after(value, *gates[step]) if step < len(gates) else value


def replica_reduce(keep, send, order, gates=()):
    for step, bit in enumerate(order):
        keep, send = add_halves(keep, gated(swap(send, "rep", bit), gates, step))
    return keep[0]


def replica_spread(x, order):
    now = x[None]
    for bit in reversed(order[1:]):
        now = jnp.concatenate([now, swap(now, "rep", bit)])
    return now, swap(now, "rep", order[0])


class PairReduce:
    def __init__(self, p, q, orders):
        self.p, self.q, self.orders = p, q, orders

    def step(self, i, gates=()):
        p, q = self.p, self.q
        got_p = swap(p[1], "rep", self.orders[0][i])
        got_q = swap(q[1], "rep", self.orders[1][i])
        if gates:
            got_p, got_q = after(got_p, *gates), after(got_q, *gates)
        self.p, self.q = add_halves(p[0], got_p), add_halves(q[0], got_q)

    def finish(self, gates=()):
        rows = self.p[0].shape[1]
        keep, send = (jnp.concatenate(x, axis=1) for x in zip(self.p, self.q))
        share = replica_reduce(keep, send, self.orders[0][2:], gates)
        return share[:rows], share[rows:]


def pair_gather(p, q, orders):
    rows = p.shape[0]
    now = jnp.concatenate([p, q])[None]
    for bit in reversed(orders[0][2:]):
        now = jnp.concatenate([now, swap(now, "rep", bit)])
    pairs = []
    for x, order in zip((now[:, :rows], now[:, rows:]), orders):
        x = jnp.concatenate([x, swap(x, "rep", order[1])])
        pairs.append((x, swap(x, "rep", order[0])))
    return pairs


def turn(x, n):
    x = x[:, None]
    for bit in reversed(range(n.bit_length() - 1)):
        half = x.shape[0] // 2
        x = jnp.concatenate([x[:half], swap(x[half:], "shard", bit)], axis=1)
    return x[0]


def from_place(j, n):
    bits = n.bit_length() - 1
    return sum(((j >> b) & 1) << (bits - 1 - b) for b in range(bits))


def slot_mask(slot, order):
    count = len(order)
    return sum(((slot >> (count - 1 - i)) & 1) << bit for i, bit in enumerate(order))


def slot_of(mask, order):
    count = len(order)
    return sum(((mask >> bit) & 1) << (count - 1 - i) for i, bit in enumerate(order))


def dot(a, b, dims):
    return lax.dot_general(a, b, (dims, ((), ())), preferred_element_type=F32)


def normalise(values):
    centred = values - jnp.mean(values, axis=-1, keepdims=True)
    scale = lax.rsqrt(jnp.mean(centred * centred, axis=-1, keepdims=True) + norm_epsilon)
    return centred * scale, scale


def held_of(groups):
    return [(g.held, g.array.shape) for g in groups]


def arrays_of(groups):
    return [g.array for g in groups]


def pieces_of(held):
    return sum(len(h) for h, _ in held)


def blocks_of(held, refs):
    found = {}
    for (pieces, _), ref in zip(held, refs):
        for j, _, first, rows in pieces:
            found[j] = ref.at[first : first + rows, :]
    return [found[j] for j in range(len(found))]


def weight_copies(held, refs, target, me, sems, rep, by_owner, rows):
    copies = []
    own = (rep ^ (rep >> 1)) & 1
    for (pieces, shape), ref in zip(held, refs):
        source = ref.at[me & (shape[0] - 1)] if len(shape) == 3 else ref
        for j, code, first, count in pieces:
            start = (me ^ j if by_owner else j) * rows
            if code is not None:
                start = start + (own if code == 0 else 1 - own) * (rows // 2)
                start = start + (rows // 4 if code == 2 else 0)
            place = target.at[pl.ds(pl.multiple_of(start, count), count), :]
            sem = sems.at[len(copies)]
            copies.append(pltpu.make_async_copy(source.at[first : first + count, :], place, sem))
    return copies


def partner(x):
    width = x.shape[-1]
    lane = lax.broadcasted_iota(jnp.int32, x.shape, 1)
    front = (lane % HEAD_DIM) < HEAD_DIM // 2
    return jnp.where(
        front,
        pltpu.roll(x, width - HEAD_DIM // 2, 1),
        pltpu.roll(x, HEAD_DIM // 2, 1),
    )


def head_masks(heads, width):
    lane = lax.broadcasted_iota(jnp.int32, (QB, width), 1) // HEAD_DIM
    return [lane == h for h in range(heads)]


def stack_heads(x, masks):
    x = x.astype(F32)
    return jnp.concatenate([jnp.where(m, x, 0.0) for m in masks], axis=0).astype(BF16)


def merge_heads(x, masks):
    total = None
    for h, m in enumerate(masks):
        part = jnp.where(m, x[h * QB : (h + 1) * QB], 0.0)
        total = part if total is None else total + part
    return total


def window_bias(ids_q, ids_k):
    row = lax.broadcasted_iota(jnp.int32, (QB, QB + 2 * HALF), 0)
    col = lax.broadcasted_iota(jnp.int32, (QB, QB + 2 * HALF), 1)
    ids_q = jnp.concatenate([ids_q] * ((QB + 2 * HALF) // LANES), axis=1)
    allowed = (col >= row) & (col <= row + 2 * HALF) & (ids_q == ids_k)
    return jnp.where(allowed, 0.0, masked_score)


def block_probs(stacked_q, keys, bias, heads):
    scores = dot(stacked_q, keys, ((1,), (1,)))
    rows, cols = scores.shape
    scores = (scores.reshape(heads, QB, cols) + bias[None]).reshape(rows, cols)
    weights = jnp.exp(scores - jnp.max(scores, axis=-1, keepdims=True))
    return weights * (1.0 / jnp.sum(weights, axis=-1, keepdims=True))


def column_chunk(ref, chunk, cols):
    if cols >= LANES:
        return ref[:, pl.ds(pl.multiple_of(chunk * cols, cols), cols)]
    per = LANES // cols
    tile = ref[:, pl.ds(pl.multiple_of(chunk // per * LANES, LANES), LANES)]
    result = tile
    for k in range(1, per):
        result = jnp.where(chunk % per == k, pltpu.roll(tile, LANES - k * cols, 1), result)
    return result


def row_chunk(ref, chunk, rows, start):
    if rows % 8 == 0:
        return ref[pl.ds(pl.multiple_of(chunk * rows, rows), rows), start : start + LANES]
    per = 8 // rows
    tile = ref[pl.ds(pl.multiple_of(chunk // per * 8, 8), 8), start : start + LANES]
    result = tile[:rows]
    for k in range(1, per):
        result = jnp.where(chunk % per == k, tile[k * rows : (k + 1) * rows], result)
    return result


def take_columns(ref, offset, valid, size):
    begin = offset // LANES * LANES
    end = -(-(offset + valid) // LANES) * LANES
    x = ref[:, begin:end].astype(F32)
    if offset != begin:
        x = pltpu.roll(x, end - offset, 1)
    x = x[:, :size]
    if valid != size:
        lane = lax.broadcasted_iota(jnp.int32, x.shape, 1)
        x = jnp.where(lane < valid, x, 0.0)
    return x


def split_kernel(n, blocks, valid, size, gain_ref, w_ref, out_ref):
    gain = gain_ref[...]
    for owner in range(n):
        for b in range(blocks):
            x = take_columns(w_ref, (b * n + owner) * valid, valid, size)
            out_ref[owner, :, b * size : (b + 1) * size] = (x * gain).astype(BF16)


def split_columns(w, gain, n, blocks, valid, size):
    rows, cols = w.shape
    step = min(rows, 64)
    return pl.pallas_call(
        functools.partial(split_kernel, n, blocks, valid, size),
        grid=(rows // step,),
        in_specs=[
            pl.BlockSpec((step, 1), lambda i: (i, 0)),
            pl.BlockSpec((step, cols), lambda i: (i, 0)),
        ],
        out_specs=pl.BlockSpec((n, step, blocks * size), lambda i: (0, i, 0)),
        out_shape=jax.ShapeDtypeStruct((n, rows, blocks * size), BF16),
        compiler_params=pltpu.CompilerParams(vmem_limit_bytes=24 << 20),
        name="split_columns",
    )(gain, w)


def attention_kernel(
    tok_held, held, n, heads, place_ref, cos_ref, sin_ref, idq_ref, idk_ref, *refs
):
    tok_refs, refs = blocks_of(tok_held, refs), refs[len(tok_held) :]
    piece_refs, refs = refs[: len(held)], refs[len(held) :]
    q_ref, k_ref, v_ref, out_ref, normed_ref, w_ref, sems = refs
    seq, width = q_ref.shape
    rows = seq // n
    me, rep = place_ref[0], place_ref[1]
    copies = weight_copies(
        held, piece_refs, w_ref, me, sems, rep, True, w_ref.shape[0] // n
    )
    for c in copies:
        c.start()
    edge = jnp.zeros((HALF, width), BF16)
    for ref in (k_ref, v_ref):
        ref[0:HALF, :] = edge
        ref[seq + HALF : seq + 2 * HALF, :] = edge
    for c in copies:
        c.wait()
    for j in range(n):
        start = (me ^ j) * rows
        at = pl.ds(pl.multiple_of(start, rows), rows)
        shifted = pl.ds(pl.multiple_of(start + HALF, HALF), rows)
        hat, _ = normalise(tok_refs[j][...].astype(F32))
        normed = hat.astype(BF16)
        normed_ref[at, :] = normed
        qkv = jnp.dot(normed, w_ref[...], preferred_element_type=F32)
        cos, sin = cos_ref[at, :], sin_ref[at, :]
        q, k = qkv[:, 0:width], qkv[:, width : 2 * width]
        rotated = (q * cos + partner(q) * sin).astype(BF16)
        q_ref[at, :] = (rotated.astype(F32) * (1.0 / math.sqrt(HEAD_DIM))).astype(BF16)
        k_ref[shifted, :] = (k * cos + partner(k) * sin).astype(BF16)
        v_ref[shifted, :] = qkv[:, 2 * width : 3 * width].astype(BF16)
    masks = head_masks(heads, width)

    def attend(i, carry):
        at = pl.ds(pl.multiple_of(i * QB, QB), QB)
        window = pl.ds(pl.multiple_of(i * QB, QB), QB + 2 * HALF)
        bias = window_bias(idq_ref[at, :], idk_ref[0:1, window])
        probs = block_probs(stack_heads(q_ref[at, :], masks), k_ref[window, :], bias, heads)
        mixed = jnp.dot(probs.astype(BF16), v_ref[window, :], preferred_element_type=F32)
        out_ref[at, :] = merge_heads(mixed, masks).astype(BF16)
        return carry

    lax.fori_loop(0, seq // QB, attend, 0, unroll=2)


def up_kernel(tok_held, att_held, out_held, in_held, n, place_ref, *refs):
    tok_refs, refs = blocks_of(tok_held, refs), refs[len(tok_held) :]
    att_refs, refs = blocks_of(att_held, refs), refs[len(att_held) :]
    out_refs, refs = refs[: len(out_held)], refs[len(out_held) :]
    in_refs, refs = refs[: len(in_held)], refs[len(in_held) :]
    hidden_out, normed_out, up_out, in_out, *refs = refs
    tok, att, w_out, w_in, hidden_own, normed, up, *refs = refs
    out_sems, in_sems, att_sems, tok_sems, sems = refs
    me, rep = place_ref[0], place_ref[1]
    rows, model = tok_refs[0].shape
    copy = pltpu.make_async_copy
    att_copies = [copy(att_refs[j], att.at[j], att_sems.at[j]) for j in range(n)]
    tok_copies = [copy(tok_refs[j], tok.at[j], tok_sems.at[j]) for j in range(n)]
    part = model // n
    out_copies = weight_copies(out_held, out_refs, w_out, me, out_sems, rep, False, part)
    in_copies = weight_copies(in_held, in_refs, w_in, me, in_sems, rep, True, part)
    for c in att_copies + tok_copies[:1] + out_copies + in_copies + tok_copies[1:]:
        c.start()
    for c in att_copies + out_copies:
        c.wait()
    sent = []
    for j in range(n):
        at = pl.ds(pl.multiple_of((me ^ j) * rows, rows), rows)
        here = slice(j * rows, (j + 1) * rows)
        tok_copies[j].wait()
        hidden = tok[j].astype(F32)
        for i in range(n):
            hidden = hidden + jnp.dot(
                att[i, at, :], w_out[i * part : (i + 1) * part, :], preferred_element_type=F32
            )
        if j == 0:
            hidden_own[...] = hidden
            sent.append(copy(hidden_own, hidden_out, sems.at[2 * n]))
            sent[-1].start()
        hat, _ = normalise(hidden)
        low = hat.astype(BF16)
        normed[here, :] = low
        if j == 0:
            for c in in_copies:
                c.wait()
            sent.append(copy(w_in, in_out, sems.at[2 * n + 1]))
            sent[-1].start()
        up[here, :] = jnp.dot(low, w_in[...], preferred_element_type=F32)
        sent += [
            copy(normed.at[here, :], normed_out.at[here, :], sems.at[2 * j]),
            copy(up.at[here, :], up_out.at[here, :], sems.at[2 * j + 1]),
        ]
        for c in sent[-2:]:
            c.start()
    for c in sent:
        c.wait()


def dup_kernel(cot_held, n, up_ref, w_in_ref, down_ref, *refs):
    cot_refs, refs = blocks_of(cot_held, refs), refs[len(cot_held) :]
    act_out, dup_out, keep_out, send_out, *refs = refs
    up, cot, w_in, w_down, act, dup, dnormed, in_sem, down_sem, up_sems, cot_sems, sems = refs
    rows, model = cot_refs[0].shape
    padded = w_down.shape[0]
    given = down_ref.shape[0]
    if given != padded:
        w_down[given:padded, :] = jnp.zeros((padded - given, model), BF16)
    copy = pltpu.make_async_copy
    down_copy = copy(down_ref, w_down.at[0:given, :], down_sem)
    in_copy = copy(w_in_ref, w_in, in_sem)
    cot_copies = [copy(cot_refs[j], cot.at[j], cot_sems.at[j]) for j in range(n)]
    up_copies = []
    for j in range(n):
        here = slice(j * rows, (j + 1) * rows)
        up_copies.append(copy(up_ref.at[here, :], up.at[here, :], up_sems.at[j]))
    for c in [up_copies[0], cot_copies[0], down_copy, in_copy]:
        c.start()
    for c in up_copies[1:] + cot_copies[1:]:
        c.start()
    sent = []
    order = block_order(n)
    for j in range(n):
        here = slice(j * rows, (j + 1) * rows)
        place = order.index(j)
        target = (keep_out if place < n // 2 else send_out).at[place % (n // 2)]
        up_copies[j].wait()
        gate, lin = up[here, :padded], up[here, padded:]
        phi = 0.5 + 0.5 * lax.erf(gate * (1.0 / math.sqrt(2.0)))
        gelu = gate * phi
        slope = phi + gate * jnp.exp(gate * gate * -0.5) * (1.0 / math.sqrt(2.0 * math.pi))
        act[here, :] = (gelu * lin).astype(BF16)
        cot_copies[j].wait()
        if j == 0:
            down_copy.wait()
        dact = dot(cot[j], w_down[...], ((1,), (1,)))
        dup[here, :padded] = (dact * lin * slope).astype(BF16)
        dup[here, padded:] = (dact * gelu).astype(BF16)
        if j == 0:
            in_copy.wait()
        dnormed[j] = dot(dup[here, :], w_in[...], ((1,), (1,))).astype(BF16)
        sent += [
            copy(dnormed.at[j], target, sems.at[3 * j]),
            copy(act.at[here, :], act_out.at[here, :], sems.at[3 * j + 1]),
            copy(dup.at[here, :], dup_out.at[here, :], sems.at[3 * j + 2]),
        ]
        for c in sent[-3:]:
            c.start()
    for c in sent:
        c.wait()


def store_slots(keep_ref, send_ref, rep, order, write):
    half = keep_ref.shape[0]
    for slot in range(2 * half):
        target = keep_ref if slot < half else send_ref
        write(target, slot % half, rep ^ slot_mask(slot, order))


def up_tiles(ff):
    return 2 * (ff // LANES) + 1


def put_block(keep, send, j, value):
    half = keep.shape[0]
    place = block_order(2 * half).index(j)
    target = keep if place < half else send
    target[place % half] = value.astype(BF16)


def down_kernel(cot_held, n, ff, order, place_ref, act, w_down, *refs):
    cot_refs, refs = blocks_of(cot_held, refs), refs[len(cot_held) :]
    keep, send, mlp_keep, mlp_send, down_sum = refs
    rows, model = cot_refs[0].shape
    cols = model // (2 * keep.shape[0])
    total = None
    for j in range(n):
        term = dot(act[j * rows : (j + 1) * rows, :], cot_refs[j][...], ((0,), (0,)))
        total = term if total is None else total + term
    down_sum[...] = total

    def write(target, slot, c):
        target[slot] = column_chunk(down_sum, c, cols)[:ff].astype(BF16)

    store_slots(keep, send, place_ref[1], order, write)
    given = w_down.shape[0]
    for j in range(n):
        low = act[j * rows : (j + 1) * rows, 0:given]
        put_block(mlp_keep, mlp_send, j, jnp.dot(low, w_down[...], preferred_element_type=F32))


def write_flows(total, starts, counts, orders, flows, index, rep):
    begin = 0
    for f, (count, order) in enumerate(zip(counts, orders)):
        keep, send = flows[2 * f], flows[2 * f + 1]
        chunk = keep.shape[2]

        def write(target, slot, c):
            for t in range(count):
                value = row_chunk(total, c, chunk, starts[begin + t])
                target[slot, index * count + t] = value.astype(BF16)

        store_slots(keep, send, rep, order, write)
        begin += count


def in_kernel(n, ff, counts, orders, place_ref, normed, dup, *refs):
    flows, in_sum = refs[:-1], refs[-1]
    me, rep = place_ref[0], place_ref[1]
    part = normed.shape[1] // n
    padded = dup.shape[1] // 2
    whole, rest = ff // LANES, ff % LANES
    starts = [t * LANES for t in range(whole)] + [padded + t * LANES for t in range(whole)]
    starts.append(2 * padded)
    for owner in range(n):
        block = dot(normed[:, owner * part : (owner + 1) * part], dup[...], ((0,), (0,)))
        in_sum[:, : 2 * padded] = block
        first = block[:, whole * LANES : (whole + 1) * LANES]
        second = block[:, padded + whole * LANES : padded + (whole + 1) * LANES]
        lane = lax.broadcasted_iota(jnp.int32, first.shape, 1)
        in_sum[:, 2 * padded :] = jnp.where(lane < rest, first, pltpu.roll(second, rest, 1))
        write_flows(in_sum, starts, counts, orders, flows, me ^ owner, rep)


def add_kernel(keep_ref, got_ref, mine_ref, other_ref):
    mine_ref[...] = keep_ref[0].astype(F32) + got_ref[0].astype(F32)
    other_ref[...] = (keep_ref[1].astype(F32) + got_ref[1].astype(F32)).astype(BF16)


def near_sums(keep, send, name):
    bits = bits_of("shard")
    for bit in range(bits - 2):
        keep, send = add_halves(keep, swap(send, "shard", bit))
    _, rows, model = keep.shape
    return pl.pallas_call(
        add_kernel,
        out_shape=[
            jax.ShapeDtypeStruct((rows, model), F32),
            jax.ShapeDtypeStruct((rows, model), BF16),
        ],
        compiler_params=pltpu.CompilerParams(vmem_limit_bytes=16 << 20),
        name=name,
    )(keep, swap(send, "shard", bits - 2))


def output_kernel(mine, got, hidden, out_ref):
    out_ref[...] = (hidden[...] + mine[...] + got[...].astype(F32)).astype(BF16)


def input_kernel(mine, got, tokens, dhidden, out_ref):
    hat, scale = normalise(tokens[...].astype(F32))
    e = mine[...] + got[...].astype(F32)
    out_ref[...] = dhidden[...] + norm_backward(e, hat, scale)


def norm_back_kernel(mine, got, hidden, cotangent, dhidden, dproj):
    hat, scale = normalise(hidden[...])
    e = mine[...] + got[...].astype(F32)
    value = cotangent[...].astype(F32) + norm_backward(e, hat, scale)
    dhidden[...] = value
    dproj[...] = value.astype(BF16)


def attention_back_kernel(held, n, heads, order, place_ref, *refs):
    dproj_refs, refs = blocks_of(held, refs), refs[len(held) :]
    w_out, att, q_ref, k_ref, v_ref, cos_ref, sin_ref, idq_ref, idk_ref, *refs = refs
    dqkv, out_keep, out_send, da, dk, dv, out_sum = refs
    me, rep = place_ref[0], place_ref[1]
    seq, width = q_ref.shape
    rows, model = dproj_refs[0].shape
    part = model // n
    dk[...] = jnp.zeros_like(dk)
    dv[...] = jnp.zeros_like(dv)
    head_cols = heads * HEAD_DIM
    total = None
    for j in range(n):
        at = pl.ds(pl.multiple_of((me ^ j) * rows, rows), rows)
        dproj = dproj_refs[j][...]
        da[at, 0:head_cols] = dot(dproj, w_out[...], ((1,), (1,))).astype(BF16)
        term = dot(att[at, :], dproj, ((0,), (0,)))
        total = term if total is None else total + term
    if head_cols != width:
        da[:, head_cols:] = jnp.zeros((seq, width - head_cols), BF16)
    out_sum[...] = total[0:part]
    cols = model // (2 * out_keep.shape[0])

    def write_out(target, slot, c):
        target[slot] = column_chunk(out_sum, c, cols).astype(BF16)

    store_slots(out_keep, out_send, rep, order, write_out)
    masks = head_masks(heads, width)

    def back(i, carry):
        at = pl.ds(pl.multiple_of(i * QB, QB), QB)
        window = pl.ds(pl.multiple_of(i * QB, QB), QB + 2 * HALF)
        bias = window_bias(idq_ref[at, :], idk_ref[0:1, window])
        queries = stack_heads(q_ref[at, :], masks)
        keys = k_ref[window, :]
        probs = block_probs(queries, keys, bias, heads)
        grads = stack_heads(da[at, :], masks)
        dprobs = dot(grads, v_ref[window, :], ((1,), (1,)))
        delta = jnp.sum(probs * dprobs, axis=-1, keepdims=True)
        dscores = (probs * (dprobs - delta)).astype(BF16)
        dq = merge_heads(jnp.dot(dscores, keys, preferred_element_type=F32), masks)
        dq = dq * (1.0 / math.sqrt(HEAD_DIM))
        cos, sin = cos_ref[at, :], sin_ref[at, :]
        dqkv[at, 0:width] = (dq * cos - partner(dq) * sin).astype(BF16)
        dk[window, :] += dot(dscores, queries, ((0,), (0,)))
        dv[window, :] += dot(probs.astype(BF16), grads, ((0,), (0,)))
        return carry

    lax.fori_loop(0, seq // QB, back, 0, unroll=2)

    def finish(i, carry):
        at = pl.ds(pl.multiple_of(i * QB, QB), QB)
        shifted = pl.ds(pl.multiple_of(i * QB + HALF, HALF), QB)
        cos, sin = cos_ref[at, :], sin_ref[at, :]
        g = dk[shifted, :]
        dqkv[at, width : 2 * width] = (g * cos - partner(g) * sin).astype(BF16)
        dqkv[at, 2 * width : 3 * width] = dv[shifted, :].astype(BF16)
        return carry

    lax.fori_loop(0, seq // QB, finish, 0)


def qkv_kernel(n, counts, orders, place_ref, normed, dqkv, *refs):
    flows, qkv_sum = refs[:-1], refs[-1]
    me, rep = place_ref[0], place_ref[1]
    part = normed.shape[1] // n
    starts = [t * LANES for t in range(sum(counts))]
    for owner in range(n):
        qkv_sum[...] = dot(normed[:, owner * part : (owner + 1) * part], dqkv[...], ((0,), (0,)))
        write_flows(qkv_sum, starts, counts, orders, flows, me ^ owner, rep)


def project_back_kernel(n, place_ref, dqkv, w_qkv, keep, send):
    rows = keep.shape[1]
    for j in range(n):
        at = pl.ds(pl.multiple_of((place_ref[0] ^ j) * rows, rows), rows)
        put_block(keep, send, j, dot(dqkv[at, :], w_qkv[...], ((1,), (1,))))


def place_piece(canvas, piece, offset, valid):
    shift = offset % LANES
    height, size = piece.shape
    count = -(-(shift + valid) // LANES)
    if count * LANES > size:
        piece = jnp.concatenate([piece, jnp.zeros((height, count * LANES - size), F32)], axis=1)
    if shift:
        piece = pltpu.roll(piece, shift, 1)
    lane = lax.broadcasted_iota(jnp.int32, (height, LANES), 1)
    for t in range(count):
        tile = piece[:, t * LANES : (t + 1) * LANES]
        low, high = shift - t * LANES, shift + valid - t * LANES
        if low > 0 or high < LANES:
            tile = jnp.where((lane >= low) & (lane < high), tile, 0.0)
        index = offset // LANES + t
        canvas[index] = tile if index not in canvas else canvas[index] + tile


def columns_out_kernel(n, ff, head_cols, width, counts, orders, place_ref, gain_ref, w_ref, *refs):
    me, rep = place_ref[0], place_ref[1]
    *parts, out_ref, ln_ref = refs
    half = parts[0].shape[0]
    slots = [slot_of(rep ^ pl.program_id(0), order) for order in orders]

    def read(owner, t):
        f = 0
        while t >= counts[f]:
            t -= counts[f]
            f += 1
        slot, index = slots[f], from_place(me ^ owner, n) * counts[f] + t
        at = slot & (half - 1)
        now, got = parts[2 * f][at, index], parts[2 * f + 1][at, index]
        return jnp.where(slot < half, now, got).astype(F32)

    canvas = {}
    for owner in range(n):
        tile = functools.partial(read, owner)

        if ff:
            whole, rest = ff // LANES, ff % LANES
            last = tile(2 * whole)
            gate = jnp.concatenate([tile(t) for t in range(whole)] + [last], axis=1)
            last = pltpu.roll(last, LANES - rest, 1)
            lin = jnp.concatenate([tile(whole + t) for t in range(whole)] + [last], axis=1)
            place_piece(canvas, gate, owner * ff, ff)
            place_piece(canvas, lin, (n + owner) * ff, ff)
        else:
            per = width // LANES
            for b in range(3):
                piece = jnp.concatenate([tile(b * per + t) for t in range(per)], axis=1)
                place_piece(canvas, piece, (b * n + owner) * head_cols, head_cols)
    gain = gain_ref[...]
    total = None
    for index, value in canvas.items():
        at = slice(index * LANES, (index + 1) * LANES)
        term = value * w_ref[:, at].astype(F32)
        total = term if total is None else total + term
        out_ref[:, at] = value * gain
    ln_ref[...] = jnp.sum(total, axis=1, keepdims=True)


def columns_out(place, pairs, counts, orders, weight, gain, n, ff=0, head_cols=0, width=0):
    parts = [a for pair in pairs for a in pair]
    chunk = parts[0].shape[2]
    part, cols = weight.shape
    count = part // chunk
    part_specs = [pl.BlockSpec(a.shape, lambda i: (0, 0, 0, 0)) for a in parts]
    total, ln = pl.pallas_call(
        functools.partial(columns_out_kernel, n, ff, head_cols, width, counts, orders),
        grid=(count,),
        in_specs=[
            pl.BlockSpec(memory_space=pltpu.SMEM),
            pl.BlockSpec((None, chunk, 1), lambda i: (i, 0, 0)),
            pl.BlockSpec((None, chunk, cols), lambda i: (i, 0, 0)),
            *part_specs,
        ],
        out_specs=[
            pl.BlockSpec((None, chunk, cols), lambda i: (i, 0, 0)),
            pl.BlockSpec((None, chunk, 1), lambda i: (i, 0, 0)),
        ],
        out_shape=[
            jax.ShapeDtypeStruct((count, chunk, cols), F32),
            jax.ShapeDtypeStruct((count, chunk, 1), F32),
        ],
        compiler_params=pltpu.CompilerParams(vmem_limit_bytes=32 << 20),
        name="columns_out",
    )(place, gain.reshape(count, chunk, 1), weight.reshape(count, chunk, cols), *parts)
    return total.reshape(part, cols), ln.reshape(part)


def rows_out_kernel(order, cols, skip, place_ref, *refs):
    *parts, out_ref = refs
    rep = place_ref[1]

    def chunk(c):
        half = parts[0].shape[0]
        slot = slot_of(rep ^ c, order)
        at = slot & (half - 1)
        rows = slice(skip, skip + out_ref.shape[0])
        return jnp.where(slot < half, parts[0][at, rows], parts[1][at, rows]).astype(F32)

    count = out_ref.shape[1] // cols
    if cols >= LANES:
        for c in range(count):
            out_ref[:, c * cols : (c + 1) * cols] = chunk(c)
    else:
        per = LANES // cols
        lane = lax.broadcasted_iota(jnp.int32, out_ref.shape[:1] + (LANES,), 1) // cols
        for t in range(count // per):
            value = chunk(per * t)
            for k in range(1, per):
                value = jnp.where(lane == k, pltpu.roll(chunk(per * t + k), k * cols, 1), value)
            out_ref[:, t * LANES : (t + 1) * LANES] = value


def rows_out(place, pair, skip, rows, model, order):
    return pl.pallas_call(
        functools.partial(rows_out_kernel, order, model // (2 * pair[0].shape[0]), skip),
        in_specs=[pl.BlockSpec(memory_space=pltpu.SMEM)]
        + [pl.BlockSpec(memory_space=pltpu.VMEM)] * 2,
        out_shape=jax.ShapeDtypeStruct((rows, model), F32),
        compiler_params=pltpu.CompilerParams(vmem_limit_bytes=32 << 20),
        name="rows_out",
    )(place, *pair)


def ordered(kernel, first, count):
    def body(*refs):
        kernel(*refs[:first], *refs[first + count :])

    return body


def work(flops):
    return pl.CostEstimate(flops=int(flops), bytes_accessed=1 << 22, transcendentals=0)


SMEM_SPEC = pl.BlockSpec(memory_space=pltpu.SMEM)
VMEM_SPEC = pl.BlockSpec(memory_space=pltpu.VMEM)
ANY_SPEC = pl.BlockSpec(memory_space=pl.ANY)


def norm_backward(grad_hat, normed, scale):
    return (
        grad_hat
        - jnp.mean(grad_hat, axis=-1, keepdims=True)
        - normed * jnp.mean(grad_hat * normed, axis=-1, keepdims=True)
    ) * scale


def after(value, *earlier):
    return lax.optimization_barrier((value,) + earlier)[0]


def shards(tokens, segment_ids, ln1_gain, w_qkv, w_out, ln2_gain, w_in, w_down, cotangent):
    n = lax.axis_size("shard")
    replicas = lax.axis_size("rep")
    me = lax.axis_index("shard")
    place = jnp.stack([me, lax.axis_index("rep")]).astype(jnp.int32)
    rows, model = tokens.shape
    seq = rows * n
    part = model // n
    ff = w_down.shape[0]
    heads = HEADS // n
    head_cols = heads * HEAD_DIM
    width = max(LANES, head_cols)
    padded = -(-ff // LANES) * LANES
    near = list(range(bits_of("rep")))
    far = near[1:2] + near[:1] + near[2:]
    shape = jax.ShapeDtypeStruct
    params = pltpu.CompilerParams(vmem_limit_bytes=VMEM_LIMIT)

    gain1 = ln1_gain.astype(F32)[:, None]
    gain2 = ln2_gain.astype(F32)[:, None]
    qkv_to = split_columns(w_qkv, gain1, n, 3, head_cols, width)
    in_to = split_columns(w_in, gain2, n, 2, ff, padded)
    toks = gather_rows(tokens)
    qkv_groups = split_weight(qkv_to)
    out_groups = gather_weight(w_out)

    lane = jnp.arange(width, dtype=jnp.int32) % HEAD_DIM
    half = HEAD_DIM // 2
    frequency = jnp.exp(-math.log(rope_base) * 2.0 * (lane % half).astype(F32) / HEAD_DIM)
    angles = jnp.arange(seq, dtype=F32)[:, None] * frequency[None, :]
    sign = jnp.where(lane < half, -1.0, 1.0)
    ids = segment_ids[0]
    tables = (
        jnp.cos(angles),
        jnp.sin(angles) * sign[None, :],
        jnp.broadcast_to(ids[:, None], (seq, LANES)),
        jnp.pad(ids, (HALF, HALF), constant_values=-1)[None],
    )

    queries, keys, values, attended, normed1, qkv_w = pl.pallas_call(
        ordered(
            functools.partial(attention_kernel, held_of(toks), held_of(qkv_groups), n, heads),
            5 + len(toks) + len(qkv_groups),
            2,
        ),
        in_specs=[SMEM_SPEC]
        + [VMEM_SPEC] * (4 + len(toks))
        + [ANY_SPEC] * (len(qkv_groups) + 2),
        out_shape=(
            shape((seq, width), BF16),
            shape((seq + 2 * HALF, width), BF16),
            shape((seq + 2 * HALF, width), BF16),
            shape((seq, width), BF16),
            shape((seq, model), BF16),
            shape((model, 3 * width), BF16),
        ),
        scratch_shapes=[pltpu.SemaphoreType.DMA((pieces_of(held_of(qkv_groups)),))],
        compiler_params=params,
        cost_estimate=work(40 * seq * model * width),
        name="attention",
    )(place, *tables, *arrays_of(toks + qkv_groups + out_groups[2:4]))

    far_done = [toks[1].array, qkv_groups[1].array, out_groups[1].array]
    in_groups = split_weight(after(in_to, *far_done), attended)
    atts = gather_rows(attended[:, :head_cols])
    block_shape = shape((n // 2, rows, model), BF16)
    hidden, normed2, up, in_w = pl.pallas_call(
        functools.partial(
            up_kernel, held_of(toks), held_of(atts), held_of(out_groups), held_of(in_groups), n
        ),
        in_specs=[SMEM_SPEC] + [ANY_SPEC] * len(toks + atts + out_groups + in_groups),
        out_specs=[ANY_SPEC] * 4,
        out_shape=[
            shape((rows, model), F32),
            shape((seq, model), BF16),
            shape((seq, 2 * padded), F32),
            shape((model, 2 * padded), BF16),
        ],
        scratch_shapes=[
            pltpu.VMEM((n, rows, model), BF16),
            pltpu.VMEM((n, seq, head_cols), BF16),
            pltpu.VMEM((model, model), BF16),
            pltpu.VMEM((model, 2 * padded), BF16),
            pltpu.VMEM((rows, model), F32),
            pltpu.VMEM((seq, model), BF16),
            pltpu.VMEM((seq, 2 * padded), F32),
            pltpu.SemaphoreType.DMA((pieces_of(held_of(out_groups)),)),
            pltpu.SemaphoreType.DMA((pieces_of(held_of(in_groups)),)),
            pltpu.SemaphoreType.DMA((n,)),
            pltpu.SemaphoreType.DMA((n,)),
            pltpu.SemaphoreType.DMA((2 * n + 2,)),
        ],
        compiler_params=params,
        cost_estimate=work(12 * seq * model * padded),
        name="up_projection",
    )(place, *arrays_of(toks + atts + out_groups + in_groups))
    cots = gather_rows(after(cotangent, atts[1].array), lambda: (up,))
    down_w = jnp.pad(w_down, ((0, -ff % 16), (0, 0)))
    act, dup, dnormed2_keep, dnormed2_send = pl.pallas_call(
        functools.partial(dup_kernel, held_of(cots), n),
        in_specs=[ANY_SPEC] * (3 + len(cots)),
        out_specs=[ANY_SPEC] * 4,
        out_shape=[shape((seq, padded), BF16), shape((seq, 2 * padded), BF16)] + [block_shape] * 2,
        scratch_shapes=[
            pltpu.VMEM((seq, 2 * padded), F32),
            pltpu.VMEM((n, rows, model), BF16),
            pltpu.VMEM((model, 2 * padded), BF16),
            pltpu.VMEM((padded, model), BF16),
            pltpu.VMEM((seq, padded), BF16),
            pltpu.VMEM((seq, 2 * padded), BF16),
            pltpu.VMEM((n, rows, model), BF16),
            pltpu.SemaphoreType.DMA,
            pltpu.SemaphoreType.DMA,
            pltpu.SemaphoreType.DMA((n,)),
            pltpu.SemaphoreType.DMA((n,)),
            pltpu.SemaphoreType.DMA((3 * n,)),
        ],
        compiler_params=params,
        cost_estimate=work(14 * seq * model * padded),
        name="dup",
    )(up, in_w, down_w, *arrays_of(cots))

    slots = replicas // 2
    chunk = part // replicas
    lanes = max(LANES, model // replicas)
    tiles = up_tiles(ff)
    orders = [near, far]
    in_counts = [tiles - tiles // 2, tiles // 2]
    in_shapes = [shape((slots, n * c, chunk, LANES), BF16) for c in in_counts for _ in range(2)]
    down_shape = shape((slots, ff, lanes), BF16)
    top = bits_of("shard") - 1

    def flow_rows(a):
        return a.reshape(a.shape[0], -1, LANES)

    mine, other = near_sums(dnormed2_keep, dnormed2_send, "near_sum_2")
    in_flows = pl.pallas_call(
        ordered(functools.partial(in_kernel, n, ff, in_counts, orders), 3, 1),
        in_specs=[SMEM_SPEC] + [VMEM_SPEC] * 2 + [ANY_SPEC],
        out_shape=in_shapes,
        scratch_shapes=[pltpu.VMEM((part, 2 * padded + LANES), F32)],
        compiler_params=params,
        cost_estimate=work(8 * seq * model * padded),
        name="in_gradient",
    )(place, normed2, dup, other)
    in_flows = [flow_rows(a) for a in in_flows]
    in_reduce = PairReduce(in_flows[:2], in_flows[2:], orders)
    dhidden, dproj = pl.pallas_call(
        ordered(norm_back_kernel, 4, 1),
        in_specs=[VMEM_SPEC] * 4 + [ANY_SPEC],
        out_shape=[shape((rows, model), F32), shape((rows, model), BF16)],
        compiler_params=pltpu.CompilerParams(vmem_limit_bytes=24 << 20),
        name="norm_back",
    )(mine, swap(other, "shard", top), hidden, cotangent, in_flows[0])
    down_keep, down_send, mlp_keep, mlp_send = pl.pallas_call(
        ordered(functools.partial(down_kernel, held_of(cots), n, ff, far), 3 + len(cots), 1),
        in_specs=[SMEM_SPEC] + [VMEM_SPEC] * (2 + len(cots)) + [ANY_SPEC],
        out_shape=[down_shape] * 2 + [block_shape] * 2,
        scratch_shapes=[pltpu.VMEM((padded, model), F32)],
        compiler_params=params,
        cost_estimate=work(8 * seq * model * padded),
        name="down_gradient",
    )(place, act, down_w, *arrays_of(cots), dproj)
    dprojs = gather_rows(dproj)
    mlp_mine, mlp_other = near_sums(mlp_keep, mlp_send, "near_sum_mlp")
    in_reduce.step(0, [dprojs[1].array])

    out_shape = shape((slots, part, lanes), BF16)
    dqkv, out_keep, out_send = pl.pallas_call(
        ordered(
            functools.partial(attention_back_kernel, held_of(dprojs), n, heads, far),
            len(dprojs) + 10,
            3,
        ),
        in_specs=[SMEM_SPEC] + [VMEM_SPEC] * (len(dprojs) + 9) + [ANY_SPEC] * 3,
        out_shape=[shape((seq, 3 * width), BF16), out_shape, out_shape],
        scratch_shapes=[
            pltpu.VMEM((seq, width), BF16),
            pltpu.VMEM((seq + 2 * HALF, width), F32),
            pltpu.VMEM((seq + 2 * HALF, width), F32),
            pltpu.VMEM((part, model), F32),
        ],
        compiler_params=params,
        cost_estimate=work(40 * seq * model * width),
        name="attention_back",
    )(
        place,
        *arrays_of(dprojs),
        w_out,
        attended,
        queries,
        keys,
        values,
        *tables,
        mlp_other,
        in_reduce.p[1],
        in_reduce.q[1],
    )

    qkv_tiles = 3 * width // LANES
    qkv_counts = [qkv_tiles - qkv_tiles // 3, qkv_tiles // 3]
    in_reduce.step(1, [dqkv])
    down_reduce = add_halves(down_keep, after(swap(down_send, "rep", far[0]), dqkv))
    qkv_flows = pl.pallas_call(
        ordered(functools.partial(qkv_kernel, n, qkv_counts, orders), 3, 3),
        in_specs=[SMEM_SPEC] + [VMEM_SPEC] * 2 + [ANY_SPEC] * 3,
        out_shape=[shape((slots, n * c, chunk, LANES), BF16) for c in qkv_counts for _ in range(2)],
        scratch_shapes=[pltpu.VMEM((part, 3 * width), F32)],
        compiler_params=params,
        cost_estimate=work(12 * seq * model * width),
        name="qkv_gradient",
    )(place, normed1, dqkv, in_reduce.p[1], in_reduce.q[1], down_reduce[1])
    qkv_flows = [flow_rows(a) for a in qkv_flows]
    output = pl.pallas_call(
        ordered(output_kernel, 3, 1),
        in_specs=[VMEM_SPEC] * 3 + [ANY_SPEC],
        out_shape=shape((rows, model), BF16),
        compiler_params=pltpu.CompilerParams(vmem_limit_bytes=16 << 20),
        name="output",
    )(mlp_mine, swap(mlp_other, "shard", top), hidden, qkv_flows[0])
    dnormed1_keep, dnormed1_send = pl.pallas_call(
        ordered(functools.partial(project_back_kernel, n), 3, 1),
        in_specs=[SMEM_SPEC] + [VMEM_SPEC] * 2 + [ANY_SPEC],
        out_shape=[block_shape] * 2,
        compiler_params=params,
        cost_estimate=work(6 * seq * model * width),
        name="project_back",
    )(place, dqkv, qkv_w, output)
    mine, other = near_sums(dnormed1_keep, dnormed1_send, "near_sum_1")
    input_grad = pl.pallas_call(
        input_kernel,
        out_shape=shape((rows, model), F32),
        compiler_params=pltpu.CompilerParams(vmem_limit_bytes=24 << 20),
        name="input_grad",
    )(mine, swap(other, "shard", top), tokens, dhidden)

    def turned(p, q, counts):
        sizes = [c * chunk for c in counts]
        whole = jnp.concatenate([p.reshape(n, sizes[0], LANES), q.reshape(n, sizes[1], LANES)], 1)
        whole = turn(whole, n)
        return whole[:, : sizes[0]].reshape(-1, LANES), whole[:, sizes[0] :].reshape(-1, LANES)

    def tiles_of(pair, count):
        size = n * count * chunk
        return [a[:, :size].reshape(a.shape[0], n * count, chunk, LANES) for a in pair]

    in_p, in_q = turned(*in_reduce.finish([[other]]), in_counts)
    in_p, in_q = pair_gather(in_p, in_q, orders)
    down_share = replica_reduce(*down_reduce, far[1:], [[other]])
    down_pair = replica_spread(down_share, far)

    split = qkv_flows[2].shape[1]
    qkv_q = [jnp.concatenate(x, axis=1) for x in zip(qkv_flows[2:], (out_keep, out_send))]
    att_reduce = PairReduce(qkv_flows[:2], qkv_q, orders)
    att_reduce.step(0, [other])
    att_reduce.step(1, [input_grad])
    att_p, att_q = att_reduce.finish()
    qkv_p, qkv_q = turned(att_p, att_q[:split], qkv_counts)
    att_p, att_q = pair_gather(qkv_p, jnp.concatenate([qkv_q, att_q[split:]]), orders)

    in_total, ln2_total = columns_out(
        place,
        [tiles_of(in_p, in_counts[0]), tiles_of(in_q, in_counts[1])],
        in_counts,
        orders,
        w_in,
        gain2,
        n,
        ff=ff,
    )
    down_total = rows_out(place, down_pair, 0, ff, model, far)
    out_total = rows_out(place, att_q, split, part, model, far)
    qkv_total, ln1_total = columns_out(
        place,
        [tiles_of(att_p, qkv_counts[0]), tiles_of(att_q, qkv_counts[1])],
        qkv_counts,
        orders,
        w_qkv,
        gain1,
        n,
        head_cols=head_cols,
        width=width,
    )
    return (
        output,
        input_grad,
        ln1_total,
        qkv_total,
        out_total,
        ln2_total,
        in_total,
        down_total,
    )


def solution(mesh):
    return jax.shard_map(
        shards,
        mesh=mesh,
        in_specs=(
            P(("rep", "shard"), None),
            P("rep", None),
            P("shard"),
            P("shard", None),
            P("shard", None),
            P("shard"),
            P("shard", None),
            P("shard", None),
            P(("rep", "shard"), None),
        ),
        out_specs=(
            P(("rep", "shard"), None),
            P(("rep", "shard"), None),
            P("shard"),
            P("shard", None),
            P("shard", None),
            P("shard"),
            P("shard", None),
            P("shard", None),
        ),
        check_vma=False,
    )
```

```python
import functools
import math

import jax
import jax.numpy as jnp
from jax import lax
from jax.experimental import pallas as pl
from jax.experimental.pallas import tpu as pltpu
from jax.sharding import PartitionSpec as P

HEADS = 16
HEAD_DIM = 64
HALF = 64
QB = 128
LANES = 128

norm_epsilon = 1e-05
rope_base = 10000.0
masked_score = -1e30

F32 = jnp.float32
BF16 = jnp.bfloat16
VMEM_LIMIT = 52 << 20


def bits_of(axis):
    return lax.axis_size(axis).bit_length() - 1


def bit_of(axis, bit):
    return (lax.axis_index(axis) >> bit) & 1


def swap(x, axis, bit):
    size = lax.axis_size(axis)
    return lax.ppermute(x, axis, [(i, i ^ (1 << bit)) for i in range(size)])


def add_halves(keep, got):
    def total(a, b):
        return (keep[a:b].astype(F32) + got[a:b].astype(F32)).astype(BF16)

    size = keep.shape[0]
    if size == 1:
        return total(0, 1), None
    return total(0, size // 2), total(size // 2, size)


def block_order(n):
    bits = n.bit_length() - 1
    return [sum(((k >> b) & 1) << (bits - 1 - b) for b in range(bits)) for k in range(n)]


class Group:
    def __init__(self, array, held):
        self.array, self.held = array, held


def join(groups, bit, arrays, axis):
    held, start = [], 0
    for group in groups:
        held += [(j | 1 << bit, code, start + first, rows) for j, code, first, rows in group.held]
        start += group.array.shape[axis]
    array = arrays[0] if len(arrays) == 1 else jnp.concatenate(arrays, axis=axis)
    return Group(swap(array, "shard", bit), held)


def gather_rows(x, gate=None, apart=False):
    rows = x.shape[0]
    groups = [Group(x, [(0, None, 0, rows)])]
    for bit in reversed(range(bits_of("shard"))):
        arrays = [g.array for g in groups]
        if gate is not None and len(arrays) > 1:
            arrays[-1] = after(arrays[-1], *gate())
        if apart:
            groups = groups + [join([g], bit, [a], 0) for g, a in zip(groups, arrays)]
        else:
            groups = groups + [join(groups, bit, arrays, 0)]
    return groups


def parity():
    return bit_of("rep", 0) ^ bit_of("rep", 1)


def half_by_replica(x, dim):
    shape = x.shape
    x = x.reshape(shape[:dim] + (2, shape[dim] // 2) + shape[dim + 1 :])
    return lax.dynamic_index_in_dim(x, parity(), dim, keepdims=False)


def fetch_far(send, dim, top, gate):
    got = swap(half_by_replica(send, dim), "shard", top)
    kept = got if gate is None else after(got, gate)
    first, second = jnp.split(kept, 2, axis=dim)
    size = got.shape[dim]
    return [
        Group(got, [(1 << top, 0, 0, size)]),
        Group(swap(first, "rep", 0), [(1 << top, 1, 0, size // 2)]),
        Group(swap(second, "rep", 1), [(1 << top, 2, 0, size // 2)]),
    ]


def gather_weight(x, gate=None):
    top = bits_of("shard") - 1
    groups = [Group(x, [(0, None, 0, x.shape[0])])] + fetch_far(x, 0, top, gate)
    for bit in reversed(range(top)):
        groups = groups + [join(groups, bit, [g.array for g in groups], 0)]
    return groups


def split_weight(x, gate=None):
    me = lax.axis_index("shard")
    top = bits_of("shard") - 1

    def part_for(a, bit):
        start = ((me & (a.shape[0] - 1)) >> bit ^ 1) << bit
        return lax.dynamic_slice_in_dim(a, start, 1 << bit)

    groups = [Group(x, [(0, None, 0, x.shape[1])])] + fetch_far(part_for(x, top), 1, top, gate)
    for bit in reversed(range(top)):
        groups = groups + [join(groups, bit, [part_for(g.array, bit) for g in groups], 1)]
    return groups


def gated(value, gates, step):
    return after(value, *gates[step]) if step < len(gates) else value


def replica_reduce(keep, send, order, gates=()):
    for step, bit in enumerate(order):
        keep, send = add_halves(keep, gated(swap(send, "rep", bit), gates, step))
    return keep[0]


def replica_spread(x, order):
    now = x[None]
    for bit in reversed(order[1:]):
        now = jnp.concatenate([now, swap(now, "rep", bit)])
    return now, swap(now, "rep", order[0])


class PairReduce:
    def __init__(self, p, q, orders):
        self.p, self.q, self.orders = p, q, orders

    def step(self, i, gates=()):
        p, q = self.p, self.q
        got_p = swap(p[1], "rep", self.orders[0][i])
        got_q = swap(q[1], "rep", self.orders[1][i])
        if gates:
            got_p, got_q = after(got_p, *gates), after(got_q, *gates)
        self.p, self.q = add_halves(p[0], got_p), add_halves(q[0], got_q)

    def finish(self, gates=()):
        rows = self.p[0].shape[1]
        keep, send = (jnp.concatenate(x, axis=1) for x in zip(self.p, self.q))
        share = replica_reduce(keep, send, self.orders[0][2:], gates)
        return share[:rows], share[rows:]


def pair_gather(p, q, orders):
    rows = p.shape[0]
    now = jnp.concatenate([p, q])[None]
    for bit in reversed(orders[0][2:]):
        now = jnp.concatenate([now, swap(now, "rep", bit)])
    pairs = []
    for x, order in zip((now[:, :rows], now[:, rows:]), orders):
        x = jnp.concatenate([x, swap(x, "rep", order[1])])
        pairs.append((x, swap(x, "rep", order[0])))
    return pairs


def turn(x, n):
    x = x[:, None]
    for bit in reversed(range(n.bit_length() - 1)):
        half = x.shape[0] // 2
        x = jnp.concatenate([x[:half], swap(x[half:], "shard", bit)], axis=1)
    return x[0]


def from_place(j, n):
    bits = n.bit_length() - 1
    return sum(((j >> b) & 1) << (bits - 1 - b) for b in range(bits))


def slot_mask(slot, order):
    count = len(order)
    return sum(((slot >> (count - 1 - i)) & 1) << bit for i, bit in enumerate(order))


def slot_of(mask, order):
    count = len(order)
    return sum(((mask >> bit) & 1) << (count - 1 - i) for i, bit in enumerate(order))


def dot(a, b, dims):
    return lax.dot_general(a, b, (dims, ((), ())), preferred_element_type=F32)


def normalise(values):
    centred = values - jnp.mean(values, axis=-1, keepdims=True)
    scale = lax.rsqrt(jnp.mean(centred * centred, axis=-1, keepdims=True) + norm_epsilon)
    return centred * scale, scale


def held_of(groups):
    return [(g.held, g.array.shape) for g in groups]


def arrays_of(groups):
    return [g.array for g in groups]


def pieces_of(held):
    return sum(len(h) for h, _ in held)


def blocks_of(held, refs):
    found = {}
    for (pieces, _), ref in zip(held, refs):
        for j, _, first, rows in pieces:
            found[j] = ref.at[first : first + rows, :]
    return [found[j] for j in range(len(found))]


def weight_copies(held, refs, target, me, sems, rep, by_owner, rows):
    copies = []
    own = (rep ^ (rep >> 1)) & 1
    for (pieces, shape), ref in zip(held, refs):
        source = ref.at[me & (shape[0] - 1)] if len(shape) == 3 else ref
        for j, code, first, count in pieces:
            start = (me ^ j if by_owner else j) * rows
            if code is not None:
                start = start + (own if code == 0 else 1 - own) * (rows // 2)
                start = start + (rows // 4 if code == 2 else 0)
            place = target.at[pl.ds(pl.multiple_of(start, count), count), :]
            sem = sems.at[len(copies)]
            copies.append(pltpu.make_async_copy(source.at[first : first + count, :], place, sem))
    return copies


def partner(x):
    width = x.shape[-1]
    lane = lax.broadcasted_iota(jnp.int32, x.shape, 1)
    front = (lane % HEAD_DIM) < HEAD_DIM // 2
    return jnp.where(
        front,
        pltpu.roll(x, width - HEAD_DIM // 2, 1),
        pltpu.roll(x, HEAD_DIM // 2, 1),
    )


def head_masks(heads, width):
    lane = lax.broadcasted_iota(jnp.int32, (QB, width), 1) // HEAD_DIM
    return [lane == h for h in range(heads)]


def stack_heads(x, masks):
    x = x.astype(F32)
    return jnp.concatenate([jnp.where(m, x, 0.0) for m in masks], axis=0).astype(BF16)


def merge_heads(x, masks):
    total = None
    for h, m in enumerate(masks):
        part = jnp.where(m, x[h * QB : (h + 1) * QB], 0.0)
        total = part if total is None else total + part
    return total


def window_bias(ids_q, ids_k):
    row = lax.broadcasted_iota(jnp.int32, (QB, QB + 2 * HALF), 0)
    col = lax.broadcasted_iota(jnp.int32, (QB, QB + 2 * HALF), 1)
    ids_q = jnp.concatenate([ids_q] * ((QB + 2 * HALF) // LANES), axis=1)
    allowed = (col >= row) & (col <= row + 2 * HALF) & (ids_q == ids_k)
    return jnp.where(allowed, 0.0, masked_score)


def block_probs(stacked_q, keys, bias, heads):
    scores = dot(stacked_q, keys, ((1,), (1,)))
    rows, cols = scores.shape
    scores = (scores.reshape(heads, QB, cols) + bias[None]).reshape(rows, cols)
    weights = jnp.exp(scores - jnp.max(scores, axis=-1, keepdims=True))
    return weights * (1.0 / jnp.sum(weights, axis=-1, keepdims=True))


def column_chunk(ref, chunk, cols):
    if cols >= LANES:
        return ref[:, pl.ds(pl.multiple_of(chunk * cols, cols), cols)]
    per = LANES // cols
    tile = ref[:, pl.ds(pl.multiple_of(chunk // per * LANES, LANES), LANES)]
    result = tile
    for k in range(1, per):
        result = jnp.where(chunk % per == k, pltpu.roll(tile, LANES - k * cols, 1), result)
    return result


def row_chunk(ref, chunk, rows, start):
    if rows % 8 == 0:
        return ref[pl.ds(pl.multiple_of(chunk * rows, rows), rows), start : start + LANES]
    per = 8 // rows
    tile = ref[pl.ds(pl.multiple_of(chunk // per * 8, 8), 8), start : start + LANES]
    result = tile[:rows]
    for k in range(1, per):
        result = jnp.where(chunk % per == k, tile[k * rows : (k + 1) * rows], result)
    return result


def take_columns(ref, offset, valid, size):
    begin = offset // LANES * LANES
    end = -(-(offset + valid) // LANES) * LANES
    x = ref[:, begin:end].astype(F32)
    if offset != begin:
        x = pltpu.roll(x, end - offset, 1)
    x = x[:, :size]
    if valid != size:
        lane = lax.broadcasted_iota(jnp.int32, x.shape, 1)
        x = jnp.where(lane < valid, x, 0.0)
    return x


def split_kernel(n, blocks, valid, size, gain_ref, w_ref, out_ref):
    gain = gain_ref[...]
    for owner in range(n):
        for b in range(blocks):
            x = take_columns(w_ref, (b * n + owner) * valid, valid, size)
            out_ref[owner, :, b * size : (b + 1) * size] = (x * gain).astype(BF16)


def split_columns(w, gain, n, blocks, valid, size):
    rows, cols = w.shape
    step = min(rows, 64)
    return pl.pallas_call(
        functools.partial(split_kernel, n, blocks, valid, size),
        grid=(rows // step,),
        in_specs=[
            pl.BlockSpec((step, 1), lambda i: (i, 0)),
            pl.BlockSpec((step, cols), lambda i: (i, 0)),
        ],
        out_specs=pl.BlockSpec((n, step, blocks * size), lambda i: (0, i, 0)),
        out_shape=jax.ShapeDtypeStruct((n, rows, blocks * size), BF16),
        compiler_params=pltpu.CompilerParams(vmem_limit_bytes=24 << 20),
        name="split_columns",
    )(gain, w)


def attention_kernel(
    tok_held, held, n, heads, place_ref, cos_ref, sin_ref, idq_ref, idk_ref, *refs
):
    tok_refs, refs = blocks_of(tok_held, refs), refs[len(tok_held) :]
    piece_refs, refs = refs[: len(held)], refs[len(held) :]
    q_ref, k_ref, v_ref, out_ref, normed_ref, w_ref, sems = refs
    seq, width = q_ref.shape
    rows = seq // n
    me, rep = place_ref[0], place_ref[1]
    copies = weight_copies(
        held, piece_refs, w_ref, me, sems, rep, True, w_ref.shape[0] // n
    )
    for c in copies:
        c.start()
    edge = jnp.zeros((HALF, width), BF16)
    for ref in (k_ref, v_ref):
        ref[0:HALF, :] = edge
        ref[seq + HALF : seq + 2 * HALF, :] = edge
    for c in copies:
        c.wait()
    for j in range(n):
        start = (me ^ j) * rows
        at = pl.ds(pl.multiple_of(start, rows), rows)
        shifted = pl.ds(pl.multiple_of(start + HALF, HALF), rows)
        hat, _ = normalise(tok_refs[j][...].astype(F32))
        normed = hat.astype(BF16)
        normed_ref[at, :] = normed
        qkv = jnp.dot(normed, w_ref[...], preferred_element_type=F32)
        cos, sin = cos_ref[at, :], sin_ref[at, :]
        q, k = qkv[:, 0:width], qkv[:, width : 2 * width]
        rotated = (q * cos + partner(q) * sin).astype(BF16)
        q_ref[at, :] = (rotated.astype(F32) * (1.0 / math.sqrt(HEAD_DIM))).astype(BF16)
        k_ref[shifted, :] = (k * cos + partner(k) * sin).astype(BF16)
        v_ref[shifted, :] = qkv[:, 2 * width : 3 * width].astype(BF16)
    masks = head_masks(heads, width)

    def attend(i, carry):
        at = pl.ds(pl.multiple_of(i * QB, QB), QB)
        window = pl.ds(pl.multiple_of(i * QB, QB), QB + 2 * HALF)
        bias = window_bias(idq_ref[at, :], idk_ref[0:1, window])
        probs = block_probs(stack_heads(q_ref[at, :], masks), k_ref[window, :], bias, heads)
        mixed = jnp.dot(probs.astype(BF16), v_ref[window, :], preferred_element_type=F32)
        out_ref[at, :] = merge_heads(mixed, masks).astype(BF16)
        return carry

    lax.fori_loop(0, seq // QB, attend, 0, unroll=2)


def up_kernel(tok_held, att_held, out_held, in_held, n, place_ref, *refs):
    tok_refs, refs = blocks_of(tok_held, refs), refs[len(tok_held) :]
    att_refs, refs = blocks_of(att_held, refs), refs[len(att_held) :]
    out_refs, refs = refs[: len(out_held)], refs[len(out_held) :]
    in_refs, refs = refs[: len(in_held)], refs[len(in_held) :]
    hidden_out, normed_out, up_out, in_out, *refs = refs
    tok, att, w_out, w_in, hidden_own, normed, up, *refs = refs
    out_sems, in_sems, att_sems, tok_sems, sems = refs
    me, rep = place_ref[0], place_ref[1]
    rows, model = tok_refs[0].shape
    copy = pltpu.make_async_copy
    att_copies = [copy(att_refs[j], att.at[j], att_sems.at[j]) for j in range(n)]
    tok_copies = [copy(tok_refs[j], tok.at[j], tok_sems.at[j]) for j in range(n)]
    part = model // n
    out_copies = weight_copies(out_held, out_refs, w_out, me, out_sems, rep, False, part)
    in_copies = weight_copies(in_held, in_refs, w_in, me, in_sems, rep, True, part)
    for c in att_copies + tok_copies[:1] + out_copies + in_copies + tok_copies[1:]:
        c.start()
    for c in att_copies + out_copies:
        c.wait()
    sent = []
    for j in range(n):
        at = pl.ds(pl.multiple_of((me ^ j) * rows, rows), rows)
        here = slice(j * rows, (j + 1) * rows)
        tok_copies[j].wait()
        hidden = tok[j].astype(F32)
        for i in range(n):
            hidden = hidden + jnp.dot(
                att[i, at, :], w_out[i * part : (i + 1) * part, :], preferred_element_type=F32
            )
        if j == 0:
            hidden_own[...] = hidden
            sent.append(copy(hidden_own, hidden_out, sems.at[2 * n]))
            sent[-1].start()
        hat, _ = normalise(hidden)
        low = hat.astype(BF16)
        normed[here, :] = low
        if j == 0:
            for c in in_copies:
                c.wait()
            sent.append(copy(w_in, in_out, sems.at[2 * n + 1]))
            sent[-1].start()
        up[here, :] = jnp.dot(low, w_in[...], preferred_element_type=F32)
        sent += [
            copy(normed.at[here, :], normed_out.at[here, :], sems.at[2 * j]),
            copy(up.at[here, :], up_out.at[here, :], sems.at[2 * j + 1]),
        ]
        for c in sent[-2:]:
            c.start()
    for c in sent:
        c.wait()


def dup_kernel(cot_held, n, up_ref, w_in_ref, down_ref, *refs):
    cot_refs, refs = blocks_of(cot_held, refs), refs[len(cot_held) :]
    act_out, dup_out, keep_out, send_out, *refs = refs
    up, cot, w_in, w_down, act, dup, dnormed, in_sem, down_sem, up_sems, cot_sems, sems = refs
    rows, model = cot_refs[0].shape
    padded = w_down.shape[0]
    given = down_ref.shape[0]
    if given != padded:
        w_down[given:padded, :] = jnp.zeros((padded - given, model), BF16)
    copy = pltpu.make_async_copy
    down_copy = copy(down_ref, w_down.at[0:given, :], down_sem)
    in_copy = copy(w_in_ref, w_in, in_sem)
    cot_copies = [copy(cot_refs[j], cot.at[j], cot_sems.at[j]) for j in range(n)]
    up_copies = []
    for j in range(n):
        here = slice(j * rows, (j + 1) * rows)
        up_copies.append(copy(up_ref.at[here, :], up.at[here, :], up_sems.at[j]))
    for c in [up_copies[0], cot_copies[0], down_copy, in_copy]:
        c.start()
    for c in up_copies[1:] + cot_copies[1:]:
        c.start()
    sent = []
    order = block_order(n)
    for j in range(n):
        here = slice(j * rows, (j + 1) * rows)
        place = order.index(j)
        target = (keep_out if place < n // 2 else send_out).at[place % (n // 2)]
        up_copies[j].wait()
        gate, lin = up[here, :padded], up[here, padded:]
        phi = 0.5 + 0.5 * lax.erf(gate * (1.0 / math.sqrt(2.0)))
        gelu = gate * phi
        slope = phi + gate * jnp.exp(gate * gate * -0.5) * (1.0 / math.sqrt(2.0 * math.pi))
        act[here, :] = (gelu * lin).astype(BF16)
        cot_copies[j].wait()
        if j == 0:
            down_copy.wait()
        dact = dot(cot[j], w_down[...], ((1,), (1,)))
        dup[here, :padded] = (dact * lin * slope).astype(BF16)
        dup[here, padded:] = (dact * gelu).astype(BF16)
        if j == 0:
            in_copy.wait()
        dnormed[j] = dot(dup[here, :], w_in[...], ((1,), (1,))).astype(BF16)
        sent += [
            copy(dnormed.at[j], target, sems.at[3 * j]),
            copy(act.at[here, :], act_out.at[here, :], sems.at[3 * j + 1]),
            copy(dup.at[here, :], dup_out.at[here, :], sems.at[3 * j + 2]),
        ]
        for c in sent[-3:]:
            c.start()
    for c in sent:
        c.wait()


def store_slots(keep_ref, send_ref, rep, order, write):
    half = keep_ref.shape[0]
    for slot in range(2 * half):
        target = keep_ref if slot < half else send_ref
        write(target, slot % half, rep ^ slot_mask(slot, order))


def up_tiles(ff):
    return 2 * (ff // LANES) + 1


def put_block(keep, send, j, value):
    half = keep.shape[0]
    place = block_order(2 * half).index(j)
    target = keep if place < half else send
    target[place % half] = value.astype(BF16)


def down_kernel(cot_held, n, ff, order, place_ref, act, w_down, *refs):
    cot_refs, refs = blocks_of(cot_held, refs), refs[len(cot_held) :]
    keep, send, mlp_keep, mlp_send, down_sum = refs
    rows, model = cot_refs[0].shape
    cols = model // (2 * keep.shape[0])
    total = None
    for j in range(n):
        term = dot(act[j * rows : (j + 1) * rows, :], cot_refs[j][...], ((0,), (0,)))
        total = term if total is None else total + term
    down_sum[...] = total

    def write(target, slot, c):
        target[slot] = column_chunk(down_sum, c, cols)[:ff].astype(BF16)

    store_slots(keep, send, place_ref[1], order, write)
    given = w_down.shape[0]
    for j in range(n):
        low = act[j * rows : (j + 1) * rows, 0:given]
        put_block(mlp_keep, mlp_send, j, jnp.dot(low, w_down[...], preferred_element_type=F32))


def write_flows(total, starts, counts, orders, flows, index, rep):
    begin = 0
    for f, (count, order) in enumerate(zip(counts, orders)):
        keep, send = flows[2 * f], flows[2 * f + 1]
        chunk = keep.shape[2]

        def write(target, slot, c):
            for t in range(count):
                value = row_chunk(total, c, chunk, starts[begin + t])
                target[slot, index * count + t] = value.astype(BF16)

        store_slots(keep, send, rep, order, write)
        begin += count


def in_kernel(n, ff, counts, orders, place_ref, normed, dup, *refs):
    flows, in_sum = refs[:-1], refs[-1]
    me, rep = place_ref[0], place_ref[1]
    part = normed.shape[1] // n
    padded = dup.shape[1] // 2
    whole, rest = ff // LANES, ff % LANES
    starts = [t * LANES for t in range(whole)] + [padded + t * LANES for t in range(whole)]
    starts.append(2 * padded)
    for owner in range(n):
        block = dot(normed[:, owner * part : (owner + 1) * part], dup[...], ((0,), (0,)))
        in_sum[:, : 2 * padded] = block
        first = block[:, whole * LANES : (whole + 1) * LANES]
        second = block[:, padded + whole * LANES : padded + (whole + 1) * LANES]
        lane = lax.broadcasted_iota(jnp.int32, first.shape, 1)
        in_sum[:, 2 * padded :] = jnp.where(lane < rest, first, pltpu.roll(second, rest, 1))
        write_flows(in_sum, starts, counts, orders, flows, me ^ owner, rep)


def add_kernel(keep_ref, got_ref, mine_ref, other_ref):
    mine_ref[...] = keep_ref[0].astype(F32) + got_ref[0].astype(F32)
    other_ref[...] = (keep_ref[1].astype(F32) + got_ref[1].astype(F32)).astype(BF16)


def near_sums(keep, send, name):
    bits = bits_of("shard")
    for bit in range(bits - 2):
        keep, send = add_halves(keep, swap(send, "shard", bit))
    _, rows, model = keep.shape
    return pl.pallas_call(
        add_kernel,
        out_shape=[
            jax.ShapeDtypeStruct((rows, model), F32),
            jax.ShapeDtypeStruct((rows, model), BF16),
        ],
        compiler_params=pltpu.CompilerParams(vmem_limit_bytes=16 << 20),
        name=name,
    )(keep, swap(send, "shard", bits - 2))


def output_kernel(mine, got, hidden, out_ref):
    out_ref[...] = (hidden[...] + mine[...] + got[...].astype(F32)).astype(BF16)


def input_kernel(mine, got, tokens, dhidden, out_ref):
    hat, scale = normalise(tokens[...].astype(F32))
    e = mine[...] + got[...].astype(F32)
    out_ref[...] = dhidden[...] + norm_backward(e, hat, scale)


def norm_back_kernel(mine, got, hidden, cotangent, dhidden, dproj):
    hat, scale = normalise(hidden[...])
    e = mine[...] + got[...].astype(F32)
    value = cotangent[...].astype(F32) + norm_backward(e, hat, scale)
    dhidden[...] = value
    dproj[...] = value.astype(BF16)


def attention_back_kernel(held, n, heads, order, place_ref, *refs):
    dproj_refs, refs = blocks_of(held, refs), refs[len(held) :]
    w_out, att, q_ref, k_ref, v_ref, cos_ref, sin_ref, idq_ref, idk_ref, *refs = refs
    dqkv, out_keep, out_send, da, dk, dv, out_sum = refs
    me, rep = place_ref[0], place_ref[1]
    seq, width = q_ref.shape
    rows, model = dproj_refs[0].shape
    part = model // n
    dk[...] = jnp.zeros_like(dk)
    dv[...] = jnp.zeros_like(dv)
    head_cols = heads * HEAD_DIM
    total = None
    for j in range(n):
        at = pl.ds(pl.multiple_of((me ^ j) * rows, rows), rows)
        dproj = dproj_refs[j][...]
        da[at, 0:head_cols] = dot(dproj, w_out[...], ((1,), (1,))).astype(BF16)
        term = dot(att[at, :], dproj, ((0,), (0,)))
        total = term if total is None else total + term
    if head_cols != width:
        da[:, head_cols:] = jnp.zeros((seq, width - head_cols), BF16)
    out_sum[...] = total[0:part]
    cols = model // (2 * out_keep.shape[0])

    def write_out(target, slot, c):
        target[slot] = column_chunk(out_sum, c, cols).astype(BF16)

    store_slots(out_keep, out_send, rep, order, write_out)
    masks = head_masks(heads, width)

    def back(i, carry):
        at = pl.ds(pl.multiple_of(i * QB, QB), QB)
        window = pl.ds(pl.multiple_of(i * QB, QB), QB + 2 * HALF)
        bias = window_bias(idq_ref[at, :], idk_ref[0:1, window])
        queries = stack_heads(q_ref[at, :], masks)
        keys = k_ref[window, :]
        probs = block_probs(queries, keys, bias, heads)
        grads = stack_heads(da[at, :], masks)
        dprobs = dot(grads, v_ref[window, :], ((1,), (1,)))
        delta = jnp.sum(probs * dprobs, axis=-1, keepdims=True)
        dscores = (probs * (dprobs - delta)).astype(BF16)
        dq = merge_heads(jnp.dot(dscores, keys, preferred_element_type=F32), masks)
        dq = dq * (1.0 / math.sqrt(HEAD_DIM))
        cos, sin = cos_ref[at, :], sin_ref[at, :]
        dqkv[at, 0:width] = (dq * cos - partner(dq) * sin).astype(BF16)
        dk[window, :] += dot(dscores, queries, ((0,), (0,)))
        dv[window, :] += dot(probs.astype(BF16), grads, ((0,), (0,)))
        return carry

    lax.fori_loop(0, seq // QB, back, 0, unroll=2)

    def finish(i, carry):
        at = pl.ds(pl.multiple_of(i * QB, QB), QB)
        shifted = pl.ds(pl.multiple_of(i * QB + HALF, HALF), QB)
        cos, sin = cos_ref[at, :], sin_ref[at, :]
        g = dk[shifted, :]
        dqkv[at, width : 2 * width] = (g * cos - partner(g) * sin).astype(BF16)
        dqkv[at, 2 * width : 3 * width] = dv[shifted, :].astype(BF16)
        return carry

    lax.fori_loop(0, seq // QB, finish, 0)


def qkv_kernel(n, counts, orders, place_ref, normed, dqkv, *refs):
    flows, qkv_sum = refs[:-1], refs[-1]
    me, rep = place_ref[0], place_ref[1]
    part = normed.shape[1] // n
    starts = [t * LANES for t in range(sum(counts))]
    for owner in range(n):
        qkv_sum[...] = dot(normed[:, owner * part : (owner + 1) * part], dqkv[...], ((0,), (0,)))
        write_flows(qkv_sum, starts, counts, orders, flows, me ^ owner, rep)


def project_back_kernel(n, place_ref, dqkv, w_qkv, keep, send):
    rows = keep.shape[1]
    for j in range(n):
        at = pl.ds(pl.multiple_of((place_ref[0] ^ j) * rows, rows), rows)
        put_block(keep, send, j, dot(dqkv[at, :], w_qkv[...], ((1,), (1,))))


def place_piece(canvas, piece, offset, valid):
    shift = offset % LANES
    height, size = piece.shape
    count = -(-(shift + valid) // LANES)
    if count * LANES > size:
        piece = jnp.concatenate([piece, jnp.zeros((height, count * LANES - size), F32)], axis=1)
    if shift:
        piece = pltpu.roll(piece, shift, 1)
    lane = lax.broadcasted_iota(jnp.int32, (height, LANES), 1)
    for t in range(count):
        tile = piece[:, t * LANES : (t + 1) * LANES]
        low, high = shift - t * LANES, shift + valid - t * LANES
        if low > 0 or high < LANES:
            tile = jnp.where((lane >= low) & (lane < high), tile, 0.0)
        index = offset // LANES + t
        canvas[index] = tile if index not in canvas else canvas[index] + tile


def columns_out_kernel(n, ff, head_cols, width, counts, orders, place_ref, gain_ref, w_ref, *refs):
    me, rep = place_ref[0], place_ref[1]
    *parts, out_ref, ln_ref = refs
    half = parts[0].shape[0]
    slots = [slot_of(rep ^ pl.program_id(0), order) for order in orders]

    def read(owner, t):
        f = 0
        while t >= counts[f]:
            t -= counts[f]
            f += 1
        slot, index = slots[f], from_place(me ^ owner, n) * counts[f] + t
        at = slot & (half - 1)
        now, got = parts[2 * f][at, index], parts[2 * f + 1][at, index]
        return jnp.where(slot < half, now, got).astype(F32)

    canvas = {}
    for owner in range(n):
        tile = functools.partial(read, owner)

        if ff:
            whole, rest = ff // LANES, ff % LANES
            last = tile(2 * whole)
            gate = jnp.concatenate([tile(t) for t in range(whole)] + [last], axis=1)
            last = pltpu.roll(last, LANES - rest, 1)
            lin = jnp.concatenate([tile(whole + t) for t in range(whole)] + [last], axis=1)
            place_piece(canvas, gate, owner * ff, ff)
            place_piece(canvas, lin, (n + owner) * ff, ff)
        else:
            per = width // LANES
            for b in range(3):
                piece = jnp.concatenate([tile(b * per + t) for t in range(per)], axis=1)
                place_piece(canvas, piece, (b * n + owner) * head_cols, head_cols)
    gain = gain_ref[...]
    total = None
    for index, value in canvas.items():
        at = slice(index * LANES, (index + 1) * LANES)
        term = value * w_ref[:, at].astype(F32)
        total = term if total is None else total + term
        out_ref[:, at] = value * gain
    ln_ref[...] = jnp.sum(total, axis=1, keepdims=True)


def columns_out(place, pairs, counts, orders, weight, gain, n, ff=0, head_cols=0, width=0):
    parts = [a for pair in pairs for a in pair]
    chunk = parts[0].shape[2]
    part, cols = weight.shape
    count = part // chunk
    part_specs = [pl.BlockSpec(a.shape, lambda i: (0, 0, 0, 0)) for a in parts]
    total, ln = pl.pallas_call(
        functools.partial(columns_out_kernel, n, ff, head_cols, width, counts, orders),
        grid=(count,),
        in_specs=[
            pl.BlockSpec(memory_space=pltpu.SMEM),
            pl.BlockSpec((None, chunk, 1), lambda i: (i, 0, 0)),
            pl.BlockSpec((None, chunk, cols), lambda i: (i, 0, 0)),
            *part_specs,
        ],
        out_specs=[
            pl.BlockSpec((None, chunk, cols), lambda i: (i, 0, 0)),
            pl.BlockSpec((None, chunk, 1), lambda i: (i, 0, 0)),
        ],
        out_shape=[
            jax.ShapeDtypeStruct((count, chunk, cols), F32),
            jax.ShapeDtypeStruct((count, chunk, 1), F32),
        ],
        compiler_params=pltpu.CompilerParams(vmem_limit_bytes=32 << 20),
        name="columns_out",
    )(place, gain.reshape(count, chunk, 1), weight.reshape(count, chunk, cols), *parts)
    return total.reshape(part, cols), ln.reshape(part)


def rows_out_kernel(order, cols, skip, place_ref, *refs):
    *parts, out_ref = refs
    rep = place_ref[1]

    def chunk(c):
        half = parts[0].shape[0]
        slot = slot_of(rep ^ c, order)
        at = slot & (half - 1)
        rows = slice(skip, skip + out_ref.shape[0])
        return jnp.where(slot < half, parts[0][at, rows], parts[1][at, rows]).astype(F32)

    count = out_ref.shape[1] // cols
    if cols >= LANES:
        for c in range(count):
            out_ref[:, c * cols : (c + 1) * cols] = chunk(c)
    else:
        per = LANES // cols
        lane = lax.broadcasted_iota(jnp.int32, out_ref.shape[:1] + (LANES,), 1) // cols
        for t in range(count // per):
            value = chunk(per * t)
            for k in range(1, per):
                value = jnp.where(lane == k, pltpu.roll(chunk(per * t + k), k * cols, 1), value)
            out_ref[:, t * LANES : (t + 1) * LANES] = value


def rows_out(place, pair, skip, rows, model, order):
    return pl.pallas_call(
        functools.partial(rows_out_kernel, order, model // (2 * pair[0].shape[0]), skip),
        in_specs=[pl.BlockSpec(memory_space=pltpu.SMEM)]
        + [pl.BlockSpec(memory_space=pltpu.VMEM)] * 2,
        out_shape=jax.ShapeDtypeStruct((rows, model), F32),
        compiler_params=pltpu.CompilerParams(vmem_limit_bytes=32 << 20),
        name="rows_out",
    )(place, *pair)


def ordered(kernel, first, count):
    def body(*refs):
        kernel(*refs[:first], *refs[first + count :])

    return body


def work(flops):
    return pl.CostEstimate(flops=int(flops), bytes_accessed=1 << 22, transcendentals=0)


SMEM_SPEC = pl.BlockSpec(memory_space=pltpu.SMEM)
VMEM_SPEC = pl.BlockSpec(memory_space=pltpu.VMEM)
ANY_SPEC = pl.BlockSpec(memory_space=pl.ANY)


def norm_backward(grad_hat, normed, scale):
    return (
        grad_hat
        - jnp.mean(grad_hat, axis=-1, keepdims=True)
        - normed * jnp.mean(grad_hat * normed, axis=-1, keepdims=True)
    ) * scale


def after(value, *earlier):
    return lax.optimization_barrier((value,) + earlier)[0]


def shards(tokens, segment_ids, ln1_gain, w_qkv, w_out, ln2_gain, w_in, w_down, cotangent):
    n = lax.axis_size("shard")
    replicas = lax.axis_size("rep")
    me = lax.axis_index("shard")
    place = jnp.stack([me, lax.axis_index("rep")]).astype(jnp.int32)
    rows, model = tokens.shape
    seq = rows * n
    part = model // n
    ff = w_down.shape[0]
    heads = HEADS // n
    head_cols = heads * HEAD_DIM
    width = max(LANES, head_cols)
    padded = -(-ff // LANES) * LANES
    near = list(range(bits_of("rep")))
    far = near[1:2] + near[:1] + near[2:]
    shape = jax.ShapeDtypeStruct
    params = pltpu.CompilerParams(vmem_limit_bytes=VMEM_LIMIT)

    gain1 = ln1_gain.astype(F32)[:, None]
    gain2 = ln2_gain.astype(F32)[:, None]
    qkv_to = split_columns(w_qkv, gain1, n, 3, head_cols, width)
    in_to = split_columns(w_in, gain2, n, 2, ff, padded)
    qkv_groups = split_weight(qkv_to)
    out_groups = gather_weight(w_out)
    toks = gather_rows(tokens, lambda: (out_groups[1].array,), apart=True)

    lane = jnp.arange(width, dtype=jnp.int32) % HEAD_DIM
    half = HEAD_DIM // 2
    frequency = jnp.exp(-math.log(rope_base) * 2.0 * (lane % half).astype(F32) / HEAD_DIM)
    angles = jnp.arange(seq, dtype=F32)[:, None] * frequency[None, :]
    sign = jnp.where(lane < half, -1.0, 1.0)
    ids = segment_ids[0]
    tables = (
        jnp.cos(angles),
        jnp.sin(angles) * sign[None, :],
        jnp.broadcast_to(ids[:, None], (seq, LANES)),
        jnp.pad(ids, (HALF, HALF), constant_values=-1)[None],
    )

    queries, keys, values, attended, normed1, qkv_w = pl.pallas_call(
        ordered(
            functools.partial(attention_kernel, held_of(toks), held_of(qkv_groups), n, heads),
            5 + len(toks) + len(qkv_groups),
            2,
        ),
        in_specs=[SMEM_SPEC]
        + [VMEM_SPEC] * (4 + len(toks))
        + [ANY_SPEC] * (len(qkv_groups) + 2),
        out_shape=(
            shape((seq, width), BF16),
            shape((seq + 2 * HALF, width), BF16),
            shape((seq + 2 * HALF, width), BF16),
            shape((seq, width), BF16),
            shape((seq, model), BF16),
            shape((model, 3 * width), BF16),
        ),
        scratch_shapes=[pltpu.SemaphoreType.DMA((pieces_of(held_of(qkv_groups)),))],
        compiler_params=params,
        cost_estimate=work(40 * seq * model * width),
        name="attention",
    )(place, *tables, *arrays_of(toks + qkv_groups + out_groups[2:4]))

    far_done = [toks[1].array, qkv_groups[1].array]
    in_groups = split_weight(after(in_to, *far_done), attended)
    atts = gather_rows(attended[:, :head_cols])
    block_shape = shape((n // 2, rows, model), BF16)
    hidden, normed2, up, in_w = pl.pallas_call(
        functools.partial(
            up_kernel, held_of(toks), held_of(atts), held_of(out_groups), held_of(in_groups), n
        ),
        in_specs=[SMEM_SPEC] + [ANY_SPEC] * len(toks + atts + out_groups + in_groups),
        out_specs=[ANY_SPEC] * 4,
        out_shape=[
            shape((rows, model), F32),
            shape((seq, model), BF16),
            shape((seq, 2 * padded), F32),
            shape((model, 2 * padded), BF16),
        ],
        scratch_shapes=[
            pltpu.VMEM((n, rows, model), BF16),
            pltpu.VMEM((n, seq, head_cols), BF16),
            pltpu.VMEM((model, model), BF16),
            pltpu.VMEM((model, 2 * padded), BF16),
            pltpu.VMEM((rows, model), F32),
            pltpu.VMEM((seq, model), BF16),
            pltpu.VMEM((seq, 2 * padded), F32),
            pltpu.SemaphoreType.DMA((pieces_of(held_of(out_groups)),)),
            pltpu.SemaphoreType.DMA((pieces_of(held_of(in_groups)),)),
            pltpu.SemaphoreType.DMA((n,)),
            pltpu.SemaphoreType.DMA((n,)),
            pltpu.SemaphoreType.DMA((2 * n + 2,)),
        ],
        compiler_params=params,
        cost_estimate=work(12 * seq * model * padded),
        name="up_projection",
    )(place, *arrays_of(toks + atts + out_groups + in_groups))
    cots = gather_rows(after(cotangent, atts[1].array), lambda: (up,))
    down_w = jnp.pad(w_down, ((0, -ff % 16), (0, 0)))
    act, dup, dnormed2_keep, dnormed2_send = pl.pallas_call(
        functools.partial(dup_kernel, held_of(cots), n),
        in_specs=[ANY_SPEC] * (3 + len(cots)),
        out_specs=[ANY_SPEC] * 4,
        out_shape=[shape((seq, padded), BF16), shape((seq, 2 * padded), BF16)] + [block_shape] * 2,
        scratch_shapes=[
            pltpu.VMEM((seq, 2 * padded), F32),
            pltpu.VMEM((n, rows, model), BF16),
            pltpu.VMEM((model, 2 * padded), BF16),
            pltpu.VMEM((padded, model), BF16),
            pltpu.VMEM((seq, padded), BF16),
            pltpu.VMEM((seq, 2 * padded), BF16),
            pltpu.VMEM((n, rows, model), BF16),
            pltpu.SemaphoreType.DMA,
            pltpu.SemaphoreType.DMA,
            pltpu.SemaphoreType.DMA((n,)),
            pltpu.SemaphoreType.DMA((n,)),
            pltpu.SemaphoreType.DMA((3 * n,)),
        ],
        compiler_params=params,
        cost_estimate=work(14 * seq * model * padded),
        name="dup",
    )(up, in_w, down_w, *arrays_of(cots))

    slots = replicas // 2
    chunk = part // replicas
    lanes = max(LANES, model // replicas)
    tiles = up_tiles(ff)
    orders = [near, far]
    in_counts = [tiles - tiles // 2, tiles // 2]
    in_shapes = [shape((slots, n * c, chunk, LANES), BF16) for c in in_counts for _ in range(2)]
    down_shape = shape((slots, ff, lanes), BF16)
    top = bits_of("shard") - 1

    def flow_rows(a):
        return a.reshape(a.shape[0], -1, LANES)

    mine, other = near_sums(dnormed2_keep, dnormed2_send, "near_sum_2")
    in_flows = pl.pallas_call(
        ordered(functools.partial(in_kernel, n, ff, in_counts, orders), 3, 1),
        in_specs=[SMEM_SPEC] + [VMEM_SPEC] * 2 + [ANY_SPEC],
        out_shape=in_shapes,
        scratch_shapes=[pltpu.VMEM((part, 2 * padded + LANES), F32)],
        compiler_params=params,
        cost_estimate=work(8 * seq * model * padded),
        name="in_gradient",
    )(place, normed2, dup, other)
    in_flows = [flow_rows(a) for a in in_flows]
    in_reduce = PairReduce(in_flows[:2], in_flows[2:], orders)
    dhidden, dproj = pl.pallas_call(
        ordered(norm_back_kernel, 4, 1),
        in_specs=[VMEM_SPEC] * 4 + [ANY_SPEC],
        out_shape=[shape((rows, model), F32), shape((rows, model), BF16)],
        compiler_params=pltpu.CompilerParams(vmem_limit_bytes=24 << 20),
        name="norm_back",
    )(mine, swap(other, "shard", top), hidden, cotangent, in_flows[0])
    down_keep, down_send, mlp_keep, mlp_send = pl.pallas_call(
        ordered(functools.partial(down_kernel, held_of(cots), n, ff, far), 3 + len(cots), 1),
        in_specs=[SMEM_SPEC] + [VMEM_SPEC] * (2 + len(cots)) + [ANY_SPEC],
        out_shape=[down_shape] * 2 + [block_shape] * 2,
        scratch_shapes=[pltpu.VMEM((padded, model), F32)],
        compiler_params=params,
        cost_estimate=work(8 * seq * model * padded),
        name="down_gradient",
    )(place, act, down_w, *arrays_of(cots), dproj)
    dprojs = gather_rows(dproj)
    mlp_mine, mlp_other = near_sums(mlp_keep, mlp_send, "near_sum_mlp")
    in_reduce.step(0, [dprojs[1].array])

    out_shape = shape((slots, part, lanes), BF16)
    dqkv, out_keep, out_send = pl.pallas_call(
        ordered(
            functools.partial(attention_back_kernel, held_of(dprojs), n, heads, far),
            len(dprojs) + 10,
            3,
        ),
        in_specs=[SMEM_SPEC] + [VMEM_SPEC] * (len(dprojs) + 9) + [ANY_SPEC] * 3,
        out_shape=[shape((seq, 3 * width), BF16), out_shape, out_shape],
        scratch_shapes=[
            pltpu.VMEM((seq, width), BF16),
            pltpu.VMEM((seq + 2 * HALF, width), F32),
            pltpu.VMEM((seq + 2 * HALF, width), F32),
            pltpu.VMEM((part, model), F32),
        ],
        compiler_params=params,
        cost_estimate=work(40 * seq * model * width),
        name="attention_back",
    )(
        place,
        *arrays_of(dprojs),
        w_out,
        attended,
        queries,
        keys,
        values,
        *tables,
        mlp_other,
        in_reduce.p[1],
        in_reduce.q[1],
    )

    qkv_tiles = 3 * width // LANES
    qkv_counts = [qkv_tiles - qkv_tiles // 3, qkv_tiles // 3]
    in_reduce.step(1, [dqkv])
    down_reduce = add_halves(down_keep, after(swap(down_send, "rep", far[0]), dqkv))
    qkv_flows = pl.pallas_call(
        ordered(functools.partial(qkv_kernel, n, qkv_counts, orders), 3, 3),
        in_specs=[SMEM_SPEC] + [VMEM_SPEC] * 2 + [ANY_SPEC] * 3,
        out_shape=[shape((slots, n * c, chunk, LANES), BF16) for c in qkv_counts for _ in range(2)],
        scratch_shapes=[pltpu.VMEM((part, 3 * width), F32)],
        compiler_params=params,
        cost_estimate=work(12 * seq * model * width),
        name="qkv_gradient",
    )(place, normed1, dqkv, in_reduce.p[1], in_reduce.q[1], down_reduce[1])
    qkv_flows = [flow_rows(a) for a in qkv_flows]
    split = qkv_flows[2].shape[1]
    qkv_q = [jnp.concatenate(x, axis=1) for x in zip(qkv_flows[2:], (out_keep, out_send))]
    att_reduce = PairReduce(qkv_flows[:2], qkv_q, orders)
    att_reduce.step(0)
    att_first = att_reduce.p[1]
    output = pl.pallas_call(
        ordered(output_kernel, 3, 1),
        in_specs=[VMEM_SPEC] * 3 + [ANY_SPEC],
        out_shape=shape((rows, model), BF16),
        compiler_params=pltpu.CompilerParams(vmem_limit_bytes=16 << 20),
        name="output",
    )(mlp_mine, swap(mlp_other, "shard", top), hidden, qkv_flows[0])
    dnormed1_keep, dnormed1_send = pl.pallas_call(
        ordered(functools.partial(project_back_kernel, n), 3, 3),
        in_specs=[SMEM_SPEC] + [VMEM_SPEC] * 2 + [ANY_SPEC] * 3,
        out_shape=[block_shape] * 2,
        compiler_params=params,
        cost_estimate=work(6 * seq * model * width),
        name="project_back",
    )(place, dqkv, qkv_w, output, att_first, att_reduce.q[1])
    mine, other = near_sums(dnormed1_keep, dnormed1_send, "near_sum_1")
    input_grad = pl.pallas_call(
        input_kernel,
        out_shape=shape((rows, model), F32),
        compiler_params=pltpu.CompilerParams(vmem_limit_bytes=24 << 20),
        name="input_grad",
    )(mine, swap(other, "shard", top), tokens, dhidden)

    def turned(p, q, counts):
        sizes = [c * chunk for c in counts]
        whole = jnp.concatenate([p.reshape(n, sizes[0], LANES), q.reshape(n, sizes[1], LANES)], 1)
        whole = turn(whole, n)
        return whole[:, : sizes[0]].reshape(-1, LANES), whole[:, sizes[0] :].reshape(-1, LANES)

    def tiles_of(pair, count):
        size = n * count * chunk
        return [a[:, :size].reshape(a.shape[0], n * count, chunk, LANES) for a in pair]

    in_p, in_q = turned(*in_reduce.finish([[qkv_flows[0]]]), in_counts)
    in_p, in_q = pair_gather(in_p, in_q, orders)
    down_share = replica_reduce(*down_reduce, far[1:], [[att_first]])

    att_reduce.step(1, [dnormed1_keep])
    att_p, att_q = att_reduce.finish([[other]])
    down_pair = replica_spread(after(down_share, att_p), far)
    qkv_p, qkv_q = turned(att_p, att_q[:split], qkv_counts)
    att_p, att_q = pair_gather(qkv_p, jnp.concatenate([qkv_q, att_q[split:]]), orders)

    in_total, ln2_total = columns_out(
        place,
        [tiles_of(in_p, in_counts[0]), tiles_of(in_q, in_counts[1])],
        in_counts,
        orders,
        w_in,
        gain2,
        n,
        ff=ff,
    )
    down_total = rows_out(place, down_pair, 0, ff, model, far)
    out_total = rows_out(place, att_q, split, part, model, far)
    qkv_total, ln1_total = columns_out(
        place,
        [tiles_of(att_p, qkv_counts[0]), tiles_of(att_q, qkv_counts[1])],
        qkv_counts,
        orders,
        w_qkv,
        gain1,
        n,
        head_cols=head_cols,
        width=width,
    )
    return (
        output,
        input_grad,
        ln1_total,
        qkv_total,
        out_total,
        ln2_total,
        in_total,
        down_total,
    )


def solution(mesh):
    return jax.shard_map(
        shards,
        mesh=mesh,
        in_specs=(
            P(("rep", "shard"), None),
            P("rep", None),
            P("shard"),
            P("shard", None),
            P("shard", None),
            P("shard"),
            P("shard", None),
            P("shard", None),
            P(("rep", "shard"), None),
        ),
        out_specs=(
            P(("rep", "shard"), None),
            P(("rep", "shard"), None),
            P("shard"),
            P("shard", None),
            P("shard", None),
            P("shard"),
            P("shard", None),
            P("shard", None),
        ),
        check_vma=False,
    )
```

```python
import functools
import math

import jax
import jax.numpy as jnp
from jax import lax
from jax.experimental import pallas as pl
from jax.experimental.pallas import tpu as pltpu
from jax.sharding import PartitionSpec as P

HEADS = 16
HEAD_DIM = 64
HALF = 64
QB = 128
LANES = 128

norm_epsilon = 1e-05
rope_base = 10000.0
masked_score = -1e30

F32 = jnp.float32
BF16 = jnp.bfloat16
VMEM_LIMIT = 52 << 20


def bits_of(axis):
    return lax.axis_size(axis).bit_length() - 1


def bit_of(axis, bit):
    return (lax.axis_index(axis) >> bit) & 1


def swap(x, axis, bit):
    size = lax.axis_size(axis)
    return lax.ppermute(x, axis, [(i, i ^ (1 << bit)) for i in range(size)])


def add_halves(keep, got):
    def total(a, b):
        return (keep[a:b].astype(F32) + got[a:b].astype(F32)).astype(BF16)

    size = keep.shape[0]
    if size == 1:
        return total(0, 1), None
    return total(0, size // 2), total(size // 2, size)


def block_order(n):
    bits = n.bit_length() - 1
    return [sum(((k >> b) & 1) << (bits - 1 - b) for b in range(bits)) for k in range(n)]


class Group:
    def __init__(self, array, held):
        self.array, self.held = array, held


def join(groups, bit, arrays, axis):
    held, start = [], 0
    for group in groups:
        held += [(j | 1 << bit, code, start + first, rows) for j, code, first, rows in group.held]
        start += group.array.shape[axis]
    array = arrays[0] if len(arrays) == 1 else jnp.concatenate(arrays, axis=axis)
    return Group(swap(array, "shard", bit), held)


def gather_rows(x, gate=None, apart=False):
    rows = x.shape[0]
    groups = [Group(x, [(0, None, 0, rows)])]
    for bit in reversed(range(bits_of("shard"))):
        arrays = [g.array for g in groups]
        if gate is not None and len(arrays) > 1:
            arrays[-1] = after(arrays[-1], *gate())
        if apart:
            groups = groups + [join([g], bit, [a], 0) for g, a in zip(groups, arrays)]
        else:
            groups = groups + [join(groups, bit, arrays, 0)]
    return groups


def parity(bits):
    return functools.reduce(lambda a, b: a ^ b, [bit_of("rep", bit) for bit in bits])


def half_by_replica(x, dim, bits):
    shape = x.shape
    x = x.reshape(shape[:dim] + (2, shape[dim] // 2) + shape[dim + 1 :])
    return lax.dynamic_index_in_dim(x, parity(bits), dim, keepdims=False)


def fetch_far(send, dim, top, gate, bits):
    got = swap(half_by_replica(send, dim, bits), "shard", top)
    kept = got if gate is None else after(got, gate)
    size = got.shape[dim]
    count = len(bits)
    parts = jnp.split(kept, count, axis=dim)
    return [Group(got, [(1 << top, (0, bits), 0, size)])] + [
        Group(swap(part, "rep", bit), [(1 << top, (1 + k, bits), 0, size // count)])
        for k, (part, bit) in enumerate(zip(parts, bits))
    ]


def gather_weight(x, gate, bits):
    top = bits_of("shard") - 1
    groups = [Group(x, [(0, None, 0, x.shape[0])])] + fetch_far(x, 0, top, gate, bits)
    for bit in reversed(range(top)):
        groups = groups + [join(groups, bit, [g.array for g in groups], 0)]
    return groups


def split_weight(x, gate, bits):
    me = lax.axis_index("shard")
    top = bits_of("shard") - 1

    def part_for(a, bit):
        start = ((me & (a.shape[0] - 1)) >> bit ^ 1) << bit
        return lax.dynamic_slice_in_dim(a, start, 1 << bit)

    groups = [Group(x, [(0, None, 0, x.shape[1])])]
    groups += fetch_far(part_for(x, top), 1, top, gate, bits)
    for bit in reversed(range(top)):
        groups = groups + [join(groups, bit, [part_for(g.array, bit) for g in groups], 1)]
    return groups


def gated(value, gates, step):
    return after(value, *gates[step]) if step < len(gates) else value


def replica_reduce(keep, send, order, gates=()):
    for step, bit in enumerate(order):
        keep, send = add_halves(keep, gated(swap(send, "rep", bit), gates, step))
    return keep[0]


def replica_spread(x, order):
    now = x[None]
    for bit in reversed(order[1:]):
        now = jnp.concatenate([now, swap(now, "rep", bit)])
    return now, swap(now, "rep", order[0])


class PairReduce:
    def __init__(self, p, q, orders):
        self.p, self.q, self.orders = p, q, orders

    def step(self, i, gates=()):
        p, q = self.p, self.q
        got_p = swap(p[1], "rep", self.orders[0][i])
        got_q = swap(q[1], "rep", self.orders[1][i])
        if gates:
            got_p, got_q = after(got_p, *gates), after(got_q, *gates)
        self.p, self.q = add_halves(p[0], got_p), add_halves(q[0], got_q)

    def finish(self, gates=()):
        rows = self.p[0].shape[1]
        keep, send = (jnp.concatenate(x, axis=1) for x in zip(self.p, self.q))
        share = replica_reduce(keep, send, self.orders[0][2:], gates)
        return share[:rows], share[rows:]


def pair_gather(p, q, orders):
    rows = p.shape[0]
    now = jnp.concatenate([p, q])[None]
    for bit in reversed(orders[0][2:]):
        now = jnp.concatenate([now, swap(now, "rep", bit)])
    pairs = []
    for x, order in zip((now[:, :rows], now[:, rows:]), orders):
        x = jnp.concatenate([x, swap(x, "rep", order[1])])
        pairs.append((x, swap(x, "rep", order[0])))
    return pairs


def turn(x, n):
    x = x[:, None]
    for bit in reversed(range(n.bit_length() - 1)):
        half = x.shape[0] // 2
        x = jnp.concatenate([x[:half], swap(x[half:], "shard", bit)], axis=1)
    return x[0]


def from_place(j, n):
    bits = n.bit_length() - 1
    return sum(((j >> b) & 1) << (bits - 1 - b) for b in range(bits))


def slot_mask(slot, order):
    count = len(order)
    return sum(((slot >> (count - 1 - i)) & 1) << bit for i, bit in enumerate(order))


def slot_of(mask, order):
    count = len(order)
    return sum(((mask >> bit) & 1) << (count - 1 - i) for i, bit in enumerate(order))


def dot(a, b, dims):
    return lax.dot_general(a, b, (dims, ((), ())), preferred_element_type=F32)


def normalise(values):
    centred = values - jnp.mean(values, axis=-1, keepdims=True)
    scale = lax.rsqrt(jnp.mean(centred * centred, axis=-1, keepdims=True) + norm_epsilon)
    return centred * scale, scale


def held_of(groups):
    return [(g.held, g.array.shape) for g in groups]


def arrays_of(groups):
    return [g.array for g in groups]


def pieces_of(held):
    return sum(len(h) for h, _ in held)


def blocks_of(held, refs):
    found = {}
    for (pieces, _), ref in zip(held, refs):
        for j, _, first, rows in pieces:
            found[j] = ref.at[first : first + rows, :]
    return [found[j] for j in range(len(found))]


def weight_copies(held, refs, target, me, sems, rep, by_owner, rows):
    copies = []
    for (pieces, shape), ref in zip(held, refs):
        source = ref.at[me & (shape[0] - 1)] if len(shape) == 3 else ref
        for j, code, first, count in pieces:
            start = (me ^ j if by_owner else j) * rows
            if code is not None:
                place, bits = code
                own = functools.reduce(lambda a, b: a ^ b, [(rep >> bit) & 1 for bit in bits])
                start = start + (own if place == 0 else 1 - own) * (rows // 2)
                start = start + max(place - 1, 0) * (rows // 2 // len(bits))
            place = target.at[pl.ds(pl.multiple_of(start, count), count), :]
            sem = sems.at[len(copies)]
            copies.append(pltpu.make_async_copy(source.at[first : first + count, :], place, sem))
    return copies


def partner(x):
    width = x.shape[-1]
    lane = lax.broadcasted_iota(jnp.int32, x.shape, 1)
    front = (lane % HEAD_DIM) < HEAD_DIM // 2
    return jnp.where(
        front,
        pltpu.roll(x, width - HEAD_DIM // 2, 1),
        pltpu.roll(x, HEAD_DIM // 2, 1),
    )


def head_masks(heads, width):
    lane = lax.broadcasted_iota(jnp.int32, (QB, width), 1) // HEAD_DIM
    return [lane == h for h in range(heads)]


def stack_heads(x, masks):
    x = x.astype(F32)
    return jnp.concatenate([jnp.where(m, x, 0.0) for m in masks], axis=0).astype(BF16)


def merge_heads(x, masks):
    total = None
    for h, m in enumerate(masks):
        part = jnp.where(m, x[h * QB : (h + 1) * QB], 0.0)
        total = part if total is None else total + part
    return total


def window_bias(ids_q, ids_k):
    row = lax.broadcasted_iota(jnp.int32, (QB, QB + 2 * HALF), 0)
    col = lax.broadcasted_iota(jnp.int32, (QB, QB + 2 * HALF), 1)
    ids_q = jnp.concatenate([ids_q] * ((QB + 2 * HALF) // LANES), axis=1)
    allowed = (col >= row) & (col <= row + 2 * HALF) & (ids_q == ids_k)
    return jnp.where(allowed, 0.0, masked_score)


def block_probs(stacked_q, keys, bias, heads):
    scores = dot(stacked_q, keys, ((1,), (1,)))
    rows, cols = scores.shape
    scores = (scores.reshape(heads, QB, cols) + bias[None]).reshape(rows, cols)
    weights = jnp.exp(scores - jnp.max(scores, axis=-1, keepdims=True))
    return weights * (1.0 / jnp.sum(weights, axis=-1, keepdims=True))


def column_chunk(ref, chunk, cols):
    if cols >= LANES:
        return ref[:, pl.ds(pl.multiple_of(chunk * cols, cols), cols)]
    per = LANES // cols
    tile = ref[:, pl.ds(pl.multiple_of(chunk // per * LANES, LANES), LANES)]
    result = tile
    for k in range(1, per):
        result = jnp.where(chunk % per == k, pltpu.roll(tile, LANES - k * cols, 1), result)
    return result


def row_chunk(ref, chunk, rows, start):
    if rows % 8 == 0:
        return ref[pl.ds(pl.multiple_of(chunk * rows, rows), rows), start : start + LANES]
    per = 8 // rows
    tile = ref[pl.ds(pl.multiple_of(chunk // per * 8, 8), 8), start : start + LANES]
    result = tile[:rows]
    for k in range(1, per):
        result = jnp.where(chunk % per == k, tile[k * rows : (k + 1) * rows], result)
    return result


def take_columns(ref, offset, valid, size):
    begin = offset // LANES * LANES
    end = -(-(offset + valid) // LANES) * LANES
    x = ref[:, begin:end].astype(F32)
    if offset != begin:
        x = pltpu.roll(x, end - offset, 1)
    x = x[:, :size]
    if valid != size:
        lane = lax.broadcasted_iota(jnp.int32, x.shape, 1)
        x = jnp.where(lane < valid, x, 0.0)
    return x


def split_kernel(n, blocks, valid, size, gain_ref, w_ref, out_ref):
    gain = gain_ref[...]
    for owner in range(n):
        for b in range(blocks):
            x = take_columns(w_ref, (b * n + owner) * valid, valid, size)
            out_ref[owner, :, b * size : (b + 1) * size] = (x * gain).astype(BF16)


def split_columns(w, gain, n, blocks, valid, size):
    rows, cols = w.shape
    step = min(rows, 64)
    return pl.pallas_call(
        functools.partial(split_kernel, n, blocks, valid, size),
        grid=(rows // step,),
        in_specs=[
            pl.BlockSpec((step, 1), lambda i: (i, 0)),
            pl.BlockSpec((step, cols), lambda i: (i, 0)),
        ],
        out_specs=pl.BlockSpec((n, step, blocks * size), lambda i: (0, i, 0)),
        out_shape=jax.ShapeDtypeStruct((n, rows, blocks * size), BF16),
        compiler_params=pltpu.CompilerParams(vmem_limit_bytes=24 << 20),
        name="split_columns",
    )(gain, w)


def attention_kernel(
    tok_held, held, n, heads, place_ref, cos_ref, sin_ref, idq_ref, idk_ref, *refs
):
    tok_refs, refs = blocks_of(tok_held, refs), refs[len(tok_held) :]
    piece_refs, refs = refs[: len(held)], refs[len(held) :]
    q_ref, k_ref, v_ref, out_ref, normed_ref, w_ref, sems = refs
    seq, width = q_ref.shape
    rows = seq // n
    me, rep = place_ref[0], place_ref[1]
    copies = weight_copies(
        held, piece_refs, w_ref, me, sems, rep, True, w_ref.shape[0] // n
    )
    for c in copies:
        c.start()
    edge = jnp.zeros((HALF, width), BF16)
    for ref in (k_ref, v_ref):
        ref[0:HALF, :] = edge
        ref[seq + HALF : seq + 2 * HALF, :] = edge
    for c in copies:
        c.wait()
    for j in range(n):
        start = (me ^ j) * rows
        at = pl.ds(pl.multiple_of(start, rows), rows)
        shifted = pl.ds(pl.multiple_of(start + HALF, HALF), rows)
        hat, _ = normalise(tok_refs[j][...].astype(F32))
        normed = hat.astype(BF16)
        normed_ref[at, :] = normed
        qkv = jnp.dot(normed, w_ref[...], preferred_element_type=F32)
        cos, sin = cos_ref[at, :], sin_ref[at, :]
        q, k = qkv[:, 0:width], qkv[:, width : 2 * width]
        rotated = (q * cos + partner(q) * sin).astype(BF16)
        q_ref[at, :] = (rotated.astype(F32) * (1.0 / math.sqrt(HEAD_DIM))).astype(BF16)
        k_ref[shifted, :] = (k * cos + partner(k) * sin).astype(BF16)
        v_ref[shifted, :] = qkv[:, 2 * width : 3 * width].astype(BF16)
    masks = head_masks(heads, width)

    def attend(i, carry):
        at = pl.ds(pl.multiple_of(i * QB, QB), QB)
        window = pl.ds(pl.multiple_of(i * QB, QB), QB + 2 * HALF)
        bias = window_bias(idq_ref[at, :], idk_ref[0:1, window])
        probs = block_probs(stack_heads(q_ref[at, :], masks), k_ref[window, :], bias, heads)
        mixed = jnp.dot(probs.astype(BF16), v_ref[window, :], preferred_element_type=F32)
        out_ref[at, :] = merge_heads(mixed, masks).astype(BF16)
        return carry

    lax.fori_loop(0, seq // QB, attend, 0, unroll=2)


def up_kernel(tok_held, att_held, out_held, in_held, n, place_ref, *refs):
    tok_refs, refs = blocks_of(tok_held, refs), refs[len(tok_held) :]
    att_refs, refs = blocks_of(att_held, refs), refs[len(att_held) :]
    out_refs, refs = refs[: len(out_held)], refs[len(out_held) :]
    in_refs, refs = refs[: len(in_held)], refs[len(in_held) :]
    hidden_out, normed_out, up_out, in_out, *refs = refs
    tok, att, w_out, w_in, hidden_own, normed, up, *refs = refs
    out_sems, in_sems, att_sems, tok_sems, sems = refs
    me, rep = place_ref[0], place_ref[1]
    rows, model = tok_refs[0].shape
    copy = pltpu.make_async_copy
    att_copies = [copy(att_refs[j], att.at[j], att_sems.at[j]) for j in range(n)]
    tok_copies = [copy(tok_refs[j], tok.at[j], tok_sems.at[j]) for j in range(n)]
    part = model // n
    out_copies = weight_copies(out_held, out_refs, w_out, me, out_sems, rep, False, part)
    in_copies = weight_copies(in_held, in_refs, w_in, me, in_sems, rep, True, part)
    for c in att_copies + tok_copies[:1] + out_copies + in_copies + tok_copies[1:]:
        c.start()
    for c in att_copies + out_copies:
        c.wait()
    sent = []
    for j in range(n):
        at = pl.ds(pl.multiple_of((me ^ j) * rows, rows), rows)
        here = slice(j * rows, (j + 1) * rows)
        tok_copies[j].wait()
        hidden = tok[j].astype(F32)
        for i in range(n):
            hidden = hidden + jnp.dot(
                att[i, at, :], w_out[i * part : (i + 1) * part, :], preferred_element_type=F32
            )
        if j == 0:
            hidden_own[...] = hidden
            sent.append(copy(hidden_own, hidden_out, sems.at[2 * n]))
            sent[-1].start()
        hat, _ = normalise(hidden)
        low = hat.astype(BF16)
        normed[here, :] = low
        if j == 0:
            for c in in_copies:
                c.wait()
            sent.append(copy(w_in, in_out, sems.at[2 * n + 1]))
            sent[-1].start()
        up[here, :] = jnp.dot(low, w_in[...], preferred_element_type=F32)
        sent += [
            copy(normed.at[here, :], normed_out.at[here, :], sems.at[2 * j]),
            copy(up.at[here, :], up_out.at[here, :], sems.at[2 * j + 1]),
        ]
        for c in sent[-2:]:
            c.start()
    for c in sent:
        c.wait()


def dup_kernel(cot_held, n, up_ref, w_in_ref, down_ref, *refs):
    cot_refs, refs = blocks_of(cot_held, refs), refs[len(cot_held) :]
    act_out, dup_out, keep_out, send_out, *refs = refs
    up, cot, w_in, w_down, act, dup, dnormed, in_sem, down_sem, up_sems, cot_sems, sems = refs
    rows, model = cot_refs[0].shape
    padded = w_down.shape[0]
    given = down_ref.shape[0]
    if given != padded:
        w_down[given:padded, :] = jnp.zeros((padded - given, model), BF16)
    copy = pltpu.make_async_copy
    down_copy = copy(down_ref, w_down.at[0:given, :], down_sem)
    in_copy = copy(w_in_ref, w_in, in_sem)
    cot_copies = [copy(cot_refs[j], cot.at[j], cot_sems.at[j]) for j in range(n)]
    up_copies = []
    for j in range(n):
        here = slice(j * rows, (j + 1) * rows)
        up_copies.append(copy(up_ref.at[here, :], up.at[here, :], up_sems.at[j]))
    for c in [up_copies[0], cot_copies[0], down_copy, in_copy]:
        c.start()
    for c in up_copies[1:] + cot_copies[1:]:
        c.start()
    sent = []
    order = block_order(n)
    for j in range(n):
        here = slice(j * rows, (j + 1) * rows)
        place = order.index(j)
        target = (keep_out if place < n // 2 else send_out).at[place % (n // 2)]
        up_copies[j].wait()
        gate, lin = up[here, :padded], up[here, padded:]
        phi = 0.5 + 0.5 * lax.erf(gate * (1.0 / math.sqrt(2.0)))
        gelu = gate * phi
        slope = phi + gate * jnp.exp(gate * gate * -0.5) * (1.0 / math.sqrt(2.0 * math.pi))
        act[here, :] = (gelu * lin).astype(BF16)
        cot_copies[j].wait()
        if j == 0:
            down_copy.wait()
        dact = dot(cot[j], w_down[...], ((1,), (1,)))
        dup[here, :padded] = (dact * lin * slope).astype(BF16)
        dup[here, padded:] = (dact * gelu).astype(BF16)
        if j == 0:
            in_copy.wait()
        dnormed[j] = dot(dup[here, :], w_in[...], ((1,), (1,))).astype(BF16)
        sent += [
            copy(dnormed.at[j], target, sems.at[3 * j]),
            copy(act.at[here, :], act_out.at[here, :], sems.at[3 * j + 1]),
            copy(dup.at[here, :], dup_out.at[here, :], sems.at[3 * j + 2]),
        ]
        for c in sent[-3:]:
            c.start()
    for c in sent:
        c.wait()


def store_slots(keep_ref, send_ref, rep, order, write):
    half = keep_ref.shape[0]
    for slot in range(2 * half):
        target = keep_ref if slot < half else send_ref
        write(target, slot % half, rep ^ slot_mask(slot, order))


def up_tiles(ff):
    return 2 * (ff // LANES) + 1


def put_block(keep, send, j, value):
    half = keep.shape[0]
    place = block_order(2 * half).index(j)
    target = keep if place < half else send
    target[place % half] = value.astype(BF16)


def down_kernel(cot_held, n, ff, order, place_ref, act, w_down, *refs):
    cot_refs, refs = blocks_of(cot_held, refs), refs[len(cot_held) :]
    keep, send, mlp_keep, mlp_send, down_sum = refs
    rows, model = cot_refs[0].shape
    cols = model // (2 * keep.shape[0])
    total = None
    for j in range(n):
        term = dot(act[j * rows : (j + 1) * rows, :], cot_refs[j][...], ((0,), (0,)))
        total = term if total is None else total + term
    down_sum[...] = total

    def write(target, slot, c):
        target[slot] = column_chunk(down_sum, c, cols)[:ff].astype(BF16)

    store_slots(keep, send, place_ref[1], order, write)
    given = w_down.shape[0]
    for j in range(n):
        low = act[j * rows : (j + 1) * rows, 0:given]
        put_block(mlp_keep, mlp_send, j, jnp.dot(low, w_down[...], preferred_element_type=F32))


def write_flows(total, starts, counts, orders, flows, index, rep):
    begin = 0
    for f, (count, order) in enumerate(zip(counts, orders)):
        keep, send = flows[2 * f], flows[2 * f + 1]
        chunk = keep.shape[2]

        def write(target, slot, c):
            for t in range(count):
                value = row_chunk(total, c, chunk, starts[begin + t])
                target[slot, index * count + t] = value.astype(BF16)

        store_slots(keep, send, rep, order, write)
        begin += count


def in_kernel(n, ff, counts, orders, place_ref, normed, dup, *refs):
    flows, in_sum = refs[:-1], refs[-1]
    me, rep = place_ref[0], place_ref[1]
    part = normed.shape[1] // n
    padded = dup.shape[1] // 2
    whole, rest = ff // LANES, ff % LANES
    starts = [t * LANES for t in range(whole)] + [padded + t * LANES for t in range(whole)]
    starts.append(2 * padded)
    for owner in range(n):
        block = dot(normed[:, owner * part : (owner + 1) * part], dup[...], ((0,), (0,)))
        in_sum[:, : 2 * padded] = block
        first = block[:, whole * LANES : (whole + 1) * LANES]
        second = block[:, padded + whole * LANES : padded + (whole + 1) * LANES]
        lane = lax.broadcasted_iota(jnp.int32, first.shape, 1)
        in_sum[:, 2 * padded :] = jnp.where(lane < rest, first, pltpu.roll(second, rest, 1))
        write_flows(in_sum, starts, counts, orders, flows, me ^ owner, rep)


def add_kernel(keep_ref, got_ref, mine_ref, other_ref):
    mine_ref[...] = keep_ref[0].astype(F32) + got_ref[0].astype(F32)
    other_ref[...] = (keep_ref[1].astype(F32) + got_ref[1].astype(F32)).astype(BF16)


def near_sums(keep, send, name, gate=None):
    bits = bits_of("shard")
    for bit in range(bits - 2):
        keep, send = add_halves(keep, swap(send, "shard", bit))
    _, rows, model = keep.shape
    got = swap(send, "shard", bits - 2)
    if gate is not None:
        got = after(got, gate)
    return pl.pallas_call(
        add_kernel,
        out_shape=[
            jax.ShapeDtypeStruct((rows, model), F32),
            jax.ShapeDtypeStruct((rows, model), BF16),
        ],
        compiler_params=pltpu.CompilerParams(vmem_limit_bytes=16 << 20),
        name=name,
    )(keep, got)


def output_kernel(mine, got, hidden, out_ref):
    out_ref[...] = (hidden[...] + mine[...] + got[...].astype(F32)).astype(BF16)


def input_kernel(mine, got, tokens, dhidden, out_ref):
    hat, scale = normalise(tokens[...].astype(F32))
    e = mine[...] + got[...].astype(F32)
    out_ref[...] = dhidden[...] + norm_backward(e, hat, scale)


def norm_back_kernel(mine, got, hidden, cotangent, dhidden, dproj):
    hat, scale = normalise(hidden[...])
    e = mine[...] + got[...].astype(F32)
    value = cotangent[...].astype(F32) + norm_backward(e, hat, scale)
    dhidden[...] = value
    dproj[...] = value.astype(BF16)


def attention_back_kernel(held, n, heads, order, place_ref, *refs):
    dproj_refs, refs = blocks_of(held, refs), refs[len(held) :]
    w_out, att, q_ref, k_ref, v_ref, cos_ref, sin_ref, idq_ref, idk_ref, *refs = refs
    dqkv, out_keep, out_send, da, dk, dv, out_sum = refs
    me, rep = place_ref[0], place_ref[1]
    seq, width = q_ref.shape
    rows, model = dproj_refs[0].shape
    part = model // n
    dk[...] = jnp.zeros_like(dk)
    dv[...] = jnp.zeros_like(dv)
    head_cols = heads * HEAD_DIM
    total = None
    for j in range(n):
        at = pl.ds(pl.multiple_of((me ^ j) * rows, rows), rows)
        dproj = dproj_refs[j][...]
        da[at, 0:head_cols] = dot(dproj, w_out[...], ((1,), (1,))).astype(BF16)
        term = dot(att[at, :], dproj, ((0,), (0,)))
        total = term if total is None else total + term
    if head_cols != width:
        da[:, head_cols:] = jnp.zeros((seq, width - head_cols), BF16)
    out_sum[...] = total[0:part]
    cols = model // (2 * out_keep.shape[0])

    def write_out(target, slot, c):
        target[slot] = column_chunk(out_sum, c, cols).astype(BF16)

    store_slots(out_keep, out_send, rep, order, write_out)
    masks = head_masks(heads, width)

    def back(i, carry):
        at = pl.ds(pl.multiple_of(i * QB, QB), QB)
        window = pl.ds(pl.multiple_of(i * QB, QB), QB + 2 * HALF)
        bias = window_bias(idq_ref[at, :], idk_ref[0:1, window])
        queries = stack_heads(q_ref[at, :], masks)
        keys = k_ref[window, :]
        probs = block_probs(queries, keys, bias, heads)
        grads = stack_heads(da[at, :], masks)
        dprobs = dot(grads, v_ref[window, :], ((1,), (1,)))
        delta = jnp.sum(probs * dprobs, axis=-1, keepdims=True)
        dscores = (probs * (dprobs - delta)).astype(BF16)
        dq = merge_heads(jnp.dot(dscores, keys, preferred_element_type=F32), masks)
        dq = dq * (1.0 / math.sqrt(HEAD_DIM))
        cos, sin = cos_ref[at, :], sin_ref[at, :]
        dqkv[at, 0:width] = (dq * cos - partner(dq) * sin).astype(BF16)
        dk[window, :] += dot(dscores, queries, ((0,), (0,)))
        dv[window, :] += dot(probs.astype(BF16), grads, ((0,), (0,)))
        return carry

    lax.fori_loop(0, seq // QB, back, 0, unroll=2)

    def finish(i, carry):
        at = pl.ds(pl.multiple_of(i * QB, QB), QB)
        shifted = pl.ds(pl.multiple_of(i * QB + HALF, HALF), QB)
        cos, sin = cos_ref[at, :], sin_ref[at, :]
        g = dk[shifted, :]
        dqkv[at, width : 2 * width] = (g * cos - partner(g) * sin).astype(BF16)
        dqkv[at, 2 * width : 3 * width] = dv[shifted, :].astype(BF16)
        return carry

    lax.fori_loop(0, seq // QB, finish, 0)


def qkv_kernel(n, counts, orders, place_ref, normed, dqkv, *refs):
    flows, qkv_sum = refs[:-1], refs[-1]
    me, rep = place_ref[0], place_ref[1]
    part = normed.shape[1] // n
    starts = [t * LANES for t in range(sum(counts))]
    for owner in range(n):
        qkv_sum[...] = dot(normed[:, owner * part : (owner + 1) * part], dqkv[...], ((0,), (0,)))
        write_flows(qkv_sum, starts, counts, orders, flows, me ^ owner, rep)


def project_back_kernel(n, place_ref, dqkv, w_qkv, keep, send):
    rows = keep.shape[1]
    for j in range(n):
        at = pl.ds(pl.multiple_of((place_ref[0] ^ j) * rows, rows), rows)
        put_block(keep, send, j, dot(dqkv[at, :], w_qkv[...], ((1,), (1,))))


def place_piece(canvas, piece, offset, valid):
    shift = offset % LANES
    height, size = piece.shape
    count = -(-(shift + valid) // LANES)
    if count * LANES > size:
        piece = jnp.concatenate([piece, jnp.zeros((height, count * LANES - size), F32)], axis=1)
    if shift:
        piece = pltpu.roll(piece, shift, 1)
    lane = lax.broadcasted_iota(jnp.int32, (height, LANES), 1)
    for t in range(count):
        tile = piece[:, t * LANES : (t + 1) * LANES]
        low, high = shift - t * LANES, shift + valid - t * LANES
        if low > 0 or high < LANES:
            tile = jnp.where((lane >= low) & (lane < high), tile, 0.0)
        index = offset // LANES + t
        canvas[index] = tile if index not in canvas else canvas[index] + tile


def columns_out_kernel(n, ff, head_cols, width, counts, orders, place_ref, gain_ref, w_ref, *refs):
    me, rep = place_ref[0], place_ref[1]
    *parts, out_ref, ln_ref = refs
    half = parts[0].shape[0]
    slots = [slot_of(rep ^ pl.program_id(0), order) for order in orders]

    def read(owner, t):
        f = 0
        while t >= counts[f]:
            t -= counts[f]
            f += 1
        slot, index = slots[f], from_place(me ^ owner, n) * counts[f] + t
        at = slot & (half - 1)
        now, got = parts[2 * f][at, index], parts[2 * f + 1][at, index]
        return jnp.where(slot < half, now, got).astype(F32)

    canvas = {}
    for owner in range(n):
        tile = functools.partial(read, owner)

        if ff:
            whole, rest = ff // LANES, ff % LANES
            last = tile(2 * whole)
            gate = jnp.concatenate([tile(t) for t in range(whole)] + [last], axis=1)
            last = pltpu.roll(last, LANES - rest, 1)
            lin = jnp.concatenate([tile(whole + t) for t in range(whole)] + [last], axis=1)
            place_piece(canvas, gate, owner * ff, ff)
            place_piece(canvas, lin, (n + owner) * ff, ff)
        else:
            per = width // LANES
            for b in range(3):
                piece = jnp.concatenate([tile(b * per + t) for t in range(per)], axis=1)
                place_piece(canvas, piece, (b * n + owner) * head_cols, head_cols)
    gain = gain_ref[...]
    total = None
    for index, value in canvas.items():
        at = slice(index * LANES, (index + 1) * LANES)
        term = value * w_ref[:, at].astype(F32)
        total = term if total is None else total + term
        out_ref[:, at] = value * gain
    ln_ref[...] = jnp.sum(total, axis=1, keepdims=True)


def columns_out(place, pairs, counts, orders, weight, gain, n, ff=0, head_cols=0, width=0):
    parts = [a for pair in pairs for a in pair]
    chunk = parts[0].shape[2]
    part, cols = weight.shape
    count = part // chunk
    part_specs = [pl.BlockSpec(a.shape, lambda i: (0, 0, 0, 0)) for a in parts]
    total, ln = pl.pallas_call(
        functools.partial(columns_out_kernel, n, ff, head_cols, width, counts, orders),
        grid=(count,),
        in_specs=[
            pl.BlockSpec(memory_space=pltpu.SMEM),
            pl.BlockSpec((None, chunk, 1), lambda i: (i, 0, 0)),
            pl.BlockSpec((None, chunk, cols), lambda i: (i, 0, 0)),
            *part_specs,
        ],
        out_specs=[
            pl.BlockSpec((None, chunk, cols), lambda i: (i, 0, 0)),
            pl.BlockSpec((None, chunk, 1), lambda i: (i, 0, 0)),
        ],
        out_shape=[
            jax.ShapeDtypeStruct((count, chunk, cols), F32),
            jax.ShapeDtypeStruct((count, chunk, 1), F32),
        ],
        compiler_params=pltpu.CompilerParams(vmem_limit_bytes=32 << 20),
        name="columns_out",
    )(place, gain.reshape(count, chunk, 1), weight.reshape(count, chunk, cols), *parts)
    return total.reshape(part, cols), ln.reshape(part)


def rows_out_kernel(order, cols, skip, place_ref, *refs):
    *parts, out_ref = refs
    rep = place_ref[1]

    def chunk(c):
        half = parts[0].shape[0]
        slot = slot_of(rep ^ c, order)
        at = slot & (half - 1)
        rows = slice(skip, skip + out_ref.shape[0])
        return jnp.where(slot < half, parts[0][at, rows], parts[1][at, rows]).astype(F32)

    count = out_ref.shape[1] // cols
    if cols >= LANES:
        for c in range(count):
            out_ref[:, c * cols : (c + 1) * cols] = chunk(c)
    else:
        per = LANES // cols
        lane = lax.broadcasted_iota(jnp.int32, out_ref.shape[:1] + (LANES,), 1) // cols
        for t in range(count // per):
            value = chunk(per * t)
            for k in range(1, per):
                value = jnp.where(lane == k, pltpu.roll(chunk(per * t + k), k * cols, 1), value)
            out_ref[:, t * LANES : (t + 1) * LANES] = value


def rows_out(place, pair, skip, rows, model, order):
    return pl.pallas_call(
        functools.partial(rows_out_kernel, order, model // (2 * pair[0].shape[0]), skip),
        in_specs=[pl.BlockSpec(memory_space=pltpu.SMEM)]
        + [pl.BlockSpec(memory_space=pltpu.VMEM)] * 2,
        out_shape=jax.ShapeDtypeStruct((rows, model), F32),
        compiler_params=pltpu.CompilerParams(vmem_limit_bytes=32 << 20),
        name="rows_out",
    )(place, *pair)


def ordered(kernel, first, count):
    def body(*refs):
        kernel(*refs[:first], *refs[first + count :])

    return body


def work(flops):
    return pl.CostEstimate(flops=int(flops), bytes_accessed=1 << 22, transcendentals=0)


SMEM_SPEC = pl.BlockSpec(memory_space=pltpu.SMEM)
VMEM_SPEC = pl.BlockSpec(memory_space=pltpu.VMEM)
ANY_SPEC = pl.BlockSpec(memory_space=pl.ANY)


def norm_backward(grad_hat, normed, scale):
    return (
        grad_hat
        - jnp.mean(grad_hat, axis=-1, keepdims=True)
        - normed * jnp.mean(grad_hat * normed, axis=-1, keepdims=True)
    ) * scale


def after(value, *earlier):
    return lax.optimization_barrier((value,) + earlier)[0]


def shards(tokens, segment_ids, ln1_gain, w_qkv, w_out, ln2_gain, w_in, w_down, cotangent):
    n = lax.axis_size("shard")
    replicas = lax.axis_size("rep")
    me = lax.axis_index("shard")
    place = jnp.stack([me, lax.axis_index("rep")]).astype(jnp.int32)
    rows, model = tokens.shape
    seq = rows * n
    part = model // n
    ff = w_down.shape[0]
    heads = HEADS // n
    head_cols = heads * HEAD_DIM
    width = max(LANES, head_cols)
    padded = -(-ff // LANES) * LANES
    near = list(range(bits_of("rep")))
    far = near[1:2] + near[:1] + near[2:]
    shape = jax.ShapeDtypeStruct
    params = pltpu.CompilerParams(vmem_limit_bytes=VMEM_LIMIT)

    gain1 = ln1_gain.astype(F32)[:, None]
    gain2 = ln2_gain.astype(F32)[:, None]
    qkv_to = split_columns(w_qkv, gain1, n, 3, head_cols, width)
    in_to = split_columns(w_in, gain2, n, 2, ff, padded)
    qkv_groups = split_weight(qkv_to, None, (0, 1))
    toks = gather_rows(tokens, apart=True)

    lane = jnp.arange(width, dtype=jnp.int32) % HEAD_DIM
    half = HEAD_DIM // 2
    frequency = jnp.exp(-math.log(rope_base) * 2.0 * (lane % half).astype(F32) / HEAD_DIM)
    angles = jnp.arange(seq, dtype=F32)[:, None] * frequency[None, :]
    sign = jnp.where(lane < half, -1.0, 1.0)
    ids = segment_ids[0]
    tables = (
        jnp.cos(angles),
        jnp.sin(angles) * sign[None, :],
        jnp.broadcast_to(ids[:, None], (seq, LANES)),
        jnp.pad(ids, (HALF, HALF), constant_values=-1)[None],
    )

    queries, keys, values, attended, normed1, qkv_w = pl.pallas_call(
        ordered(
            functools.partial(attention_kernel, held_of(toks), held_of(qkv_groups), n, heads),
            5 + len(toks) + len(qkv_groups),
            0,
        ),
        in_specs=[SMEM_SPEC]
        + [VMEM_SPEC] * (4 + len(toks))
        + [ANY_SPEC] * len(qkv_groups),
        out_shape=(
            shape((seq, width), BF16),
            shape((seq + 2 * HALF, width), BF16),
            shape((seq + 2 * HALF, width), BF16),
            shape((seq, width), BF16),
            shape((seq, model), BF16),
            shape((model, 3 * width), BF16),
        ),
        scratch_shapes=[pltpu.SemaphoreType.DMA((pieces_of(held_of(qkv_groups)),))],
        compiler_params=params,
        cost_estimate=work(40 * seq * model * width),
        name="attention",
    )(place, *tables, *arrays_of(toks + qkv_groups))

    far_done = [toks[1].array, qkv_groups[1].array]
    out_groups = gather_weight(after(w_out, *far_done), attended, (2,))
    in_groups = split_weight(after(in_to, *far_done), attended, (0, 1))
    atts = gather_rows(attended[:, :head_cols])
    block_shape = shape((n // 2, rows, model), BF16)
    hidden, normed2, up, in_w = pl.pallas_call(
        functools.partial(
            up_kernel, held_of(toks), held_of(atts), held_of(out_groups), held_of(in_groups), n
        ),
        in_specs=[SMEM_SPEC] + [ANY_SPEC] * len(toks + atts + out_groups + in_groups),
        out_specs=[ANY_SPEC] * 4,
        out_shape=[
            shape((rows, model), F32),
            shape((seq, model), BF16),
            shape((seq, 2 * padded), F32),
            shape((model, 2 * padded), BF16),
        ],
        scratch_shapes=[
            pltpu.VMEM((n, rows, model), BF16),
            pltpu.VMEM((n, seq, head_cols), BF16),
            pltpu.VMEM((model, model), BF16),
            pltpu.VMEM((model, 2 * padded), BF16),
            pltpu.VMEM((rows, model), F32),
            pltpu.VMEM((seq, model), BF16),
            pltpu.VMEM((seq, 2 * padded), F32),
            pltpu.SemaphoreType.DMA((pieces_of(held_of(out_groups)),)),
            pltpu.SemaphoreType.DMA((pieces_of(held_of(in_groups)),)),
            pltpu.SemaphoreType.DMA((n,)),
            pltpu.SemaphoreType.DMA((n,)),
            pltpu.SemaphoreType.DMA((2 * n + 2,)),
        ],
        compiler_params=params,
        cost_estimate=work(12 * seq * model * padded),
        name="up_projection",
    )(place, *arrays_of(toks + atts + out_groups + in_groups))
    cots = gather_rows(after(cotangent, atts[1].array), lambda: (up,))
    down_w = jnp.pad(w_down, ((0, -ff % 16), (0, 0)))
    act, dup, dnormed2_keep, dnormed2_send = pl.pallas_call(
        functools.partial(dup_kernel, held_of(cots), n),
        in_specs=[ANY_SPEC] * (3 + len(cots)),
        out_specs=[ANY_SPEC] * 4,
        out_shape=[shape((seq, padded), BF16), shape((seq, 2 * padded), BF16)] + [block_shape] * 2,
        scratch_shapes=[
            pltpu.VMEM((seq, 2 * padded), F32),
            pltpu.VMEM((n, rows, model), BF16),
            pltpu.VMEM((model, 2 * padded), BF16),
            pltpu.VMEM((padded, model), BF16),
            pltpu.VMEM((seq, padded), BF16),
            pltpu.VMEM((seq, 2 * padded), BF16),
            pltpu.VMEM((n, rows, model), BF16),
            pltpu.SemaphoreType.DMA,
            pltpu.SemaphoreType.DMA,
            pltpu.SemaphoreType.DMA((n,)),
            pltpu.SemaphoreType.DMA((n,)),
            pltpu.SemaphoreType.DMA((3 * n,)),
        ],
        compiler_params=params,
        cost_estimate=work(14 * seq * model * padded),
        name="dup",
    )(up, in_w, down_w, *arrays_of(cots))

    slots = replicas // 2
    chunk = part // replicas
    lanes = max(LANES, model // replicas)
    tiles = up_tiles(ff)
    orders = [near, far]
    in_counts = [tiles - tiles // 2, tiles // 2]
    in_shapes = [shape((slots, n * c, chunk, LANES), BF16) for c in in_counts for _ in range(2)]
    down_shape = shape((slots, ff, lanes), BF16)
    top = bits_of("shard") - 1

    def flow_rows(a):
        return a.reshape(a.shape[0], -1, LANES)

    mine, other = near_sums(dnormed2_keep, dnormed2_send, "near_sum_2")
    in_flows = pl.pallas_call(
        ordered(functools.partial(in_kernel, n, ff, in_counts, orders), 3, 1),
        in_specs=[SMEM_SPEC] + [VMEM_SPEC] * 2 + [ANY_SPEC],
        out_shape=in_shapes,
        scratch_shapes=[pltpu.VMEM((part, 2 * padded + LANES), F32)],
        compiler_params=params,
        cost_estimate=work(8 * seq * model * padded),
        name="in_gradient",
    )(place, normed2, dup, other)
    in_flows = [flow_rows(a) for a in in_flows]
    in_reduce = PairReduce(in_flows[:2], in_flows[2:], orders)
    dhidden, dproj = pl.pallas_call(
        ordered(norm_back_kernel, 4, 1),
        in_specs=[VMEM_SPEC] * 4 + [ANY_SPEC],
        out_shape=[shape((rows, model), F32), shape((rows, model), BF16)],
        compiler_params=pltpu.CompilerParams(vmem_limit_bytes=24 << 20),
        name="norm_back",
    )(mine, swap(other, "shard", top), hidden, cotangent, in_flows[0])
    down_keep, down_send, mlp_keep, mlp_send = pl.pallas_call(
        ordered(functools.partial(down_kernel, held_of(cots), n, ff, far), 3 + len(cots), 1),
        in_specs=[SMEM_SPEC] + [VMEM_SPEC] * (2 + len(cots)) + [ANY_SPEC],
        out_shape=[down_shape] * 2 + [block_shape] * 2,
        scratch_shapes=[pltpu.VMEM((padded, model), F32)],
        compiler_params=params,
        cost_estimate=work(8 * seq * model * padded),
        name="down_gradient",
    )(place, act, down_w, *arrays_of(cots), dproj)
    dprojs = gather_rows(dproj, lambda: (down_keep,))
    in_reduce.step(0, [dprojs[1].array])

    out_shape = shape((slots, part, lanes), BF16)
    dqkv, out_keep, out_send = pl.pallas_call(
        ordered(
            functools.partial(attention_back_kernel, held_of(dprojs), n, heads, far),
            len(dprojs) + 10,
            2,
        ),
        in_specs=[SMEM_SPEC] + [VMEM_SPEC] * (len(dprojs) + 9) + [ANY_SPEC] * 2,
        out_shape=[shape((seq, 3 * width), BF16), out_shape, out_shape],
        scratch_shapes=[
            pltpu.VMEM((seq, width), BF16),
            pltpu.VMEM((seq + 2 * HALF, width), F32),
            pltpu.VMEM((seq + 2 * HALF, width), F32),
            pltpu.VMEM((part, model), F32),
        ],
        compiler_params=params,
        cost_estimate=work(40 * seq * model * width),
        name="attention_back",
    )(
        place,
        *arrays_of(dprojs),
        w_out,
        attended,
        queries,
        keys,
        values,
        *tables,
        in_reduce.p[1],
        in_reduce.q[1],
    )

    mlp_mine, mlp_other = near_sums(mlp_keep, mlp_send, "near_sum_mlp", dqkv)
    qkv_tiles = 3 * width // LANES
    qkv_counts = [qkv_tiles - qkv_tiles // 3, qkv_tiles // 3]
    in_reduce.step(1, [dqkv])
    down_reduce = add_halves(down_keep, after(swap(down_send, "rep", far[0]), dqkv))
    qkv_flows = pl.pallas_call(
        ordered(functools.partial(qkv_kernel, n, qkv_counts, orders), 3, 4),
        in_specs=[SMEM_SPEC] + [VMEM_SPEC] * 2 + [ANY_SPEC] * 4,
        out_shape=[shape((slots, n * c, chunk, LANES), BF16) for c in qkv_counts for _ in range(2)],
        scratch_shapes=[pltpu.VMEM((part, 3 * width), F32)],
        compiler_params=params,
        cost_estimate=work(12 * seq * model * width),
        name="qkv_gradient",
    )(place, normed1, dqkv, in_reduce.p[1], in_reduce.q[1], down_reduce[1], mlp_other)
    qkv_flows = [flow_rows(a) for a in qkv_flows]
    split = qkv_flows[2].shape[1]
    qkv_q = [jnp.concatenate(x, axis=1) for x in zip(qkv_flows[2:], (out_keep, out_send))]
    att_reduce = PairReduce(qkv_flows[:2], qkv_q, orders)
    att_reduce.step(0)
    att_first = att_reduce.p[1]
    output = pl.pallas_call(
        ordered(output_kernel, 3, 1),
        in_specs=[VMEM_SPEC] * 3 + [ANY_SPEC],
        out_shape=shape((rows, model), BF16),
        compiler_params=pltpu.CompilerParams(vmem_limit_bytes=16 << 20),
        name="output",
    )(mlp_mine, swap(mlp_other, "shard", top), hidden, qkv_flows[0])
    dnormed1_keep, dnormed1_send = pl.pallas_call(
        ordered(functools.partial(project_back_kernel, n), 3, 3),
        in_specs=[SMEM_SPEC] + [VMEM_SPEC] * 2 + [ANY_SPEC] * 3,
        out_shape=[block_shape] * 2,
        compiler_params=params,
        cost_estimate=work(6 * seq * model * width),
        name="project_back",
    )(place, dqkv, qkv_w, output, att_first, att_reduce.q[1])
    mine, other = near_sums(dnormed1_keep, dnormed1_send, "near_sum_1")
    input_grad = pl.pallas_call(
        input_kernel,
        out_shape=shape((rows, model), F32),
        compiler_params=pltpu.CompilerParams(vmem_limit_bytes=24 << 20),
        name="input_grad",
    )(mine, swap(other, "shard", top), tokens, dhidden)

    def turned(p, q, counts):
        sizes = [c * chunk for c in counts]
        whole = jnp.concatenate([p.reshape(n, sizes[0], LANES), q.reshape(n, sizes[1], LANES)], 1)
        whole = turn(whole, n)
        return whole[:, : sizes[0]].reshape(-1, LANES), whole[:, sizes[0] :].reshape(-1, LANES)

    def tiles_of(pair, count):
        size = n * count * chunk
        return [a[:, :size].reshape(a.shape[0], n * count, chunk, LANES) for a in pair]

    in_p, in_q = turned(*in_reduce.finish([[qkv_flows[0]]]), in_counts)
    down_share = replica_reduce(*down_reduce, far[1:], [[att_first]])

    att_reduce.step(1, [dnormed1_keep])
    att_p, att_q = att_reduce.finish([[other]])
    att_done = att_p[:16]
    in_p, in_q = pair_gather(after(in_p, att_done), after(in_q, att_done), orders)
    down_pair = replica_spread(after(down_share, att_done), far)
    qkv_p, qkv_q = turned(att_p, att_q[:split], qkv_counts)
    att_p, att_q = pair_gather(qkv_p, jnp.concatenate([qkv_q, att_q[split:]]), orders)

    in_total, ln2_total = columns_out(
        place,
        [tiles_of(in_p, in_counts[0]), tiles_of(in_q, in_counts[1])],
        in_counts,
        orders,
        w_in,
        gain2,
        n,
        ff=ff,
    )
    down_total = rows_out(place, down_pair, 0, ff, model, far)
    out_total = rows_out(place, att_q, split, part, model, far)
    qkv_total, ln1_total = columns_out(
        place,
        [tiles_of(att_p, qkv_counts[0]), tiles_of(att_q, qkv_counts[1])],
        qkv_counts,
        orders,
        w_qkv,
        gain1,
        n,
        head_cols=head_cols,
        width=width,
    )
    return (
        output,
        input_grad,
        ln1_total,
        qkv_total,
        out_total,
        ln2_total,
        in_total,
        down_total,
    )


def solution(mesh):
    return jax.shard_map(
        shards,
        mesh=mesh,
        in_specs=(
            P(("rep", "shard"), None),
            P("rep", None),
            P("shard"),
            P("shard", None),
            P("shard", None),
            P("shard"),
            P("shard", None),
            P("shard", None),
            P(("rep", "shard"), None),
        ),
        out_specs=(
            P(("rep", "shard"), None),
            P(("rep", "shard"), None),
            P("shard"),
            P("shard", None),
            P("shard", None),
            P("shard"),
            P("shard", None),
            P("shard", None),
        ),
        check_vma=False,
    )
```

```python
import functools
import math

import jax
import jax.numpy as jnp
from jax import lax
from jax.experimental import pallas as pl
from jax.experimental.pallas import tpu as pltpu
from jax.sharding import PartitionSpec as P

HEADS = 16
HEAD_DIM = 64
HALF = 64
QB = 128
LANES = 128

norm_epsilon = 1e-05
rope_base = 10000.0
masked_score = -1e30

F32 = jnp.float32
BF16 = jnp.bfloat16
VMEM_LIMIT = 52 << 20


def bits_of(axis):
    return lax.axis_size(axis).bit_length() - 1


def bit_of(axis, bit):
    return (lax.axis_index(axis) >> bit) & 1


def swap(x, axis, bit):
    size = lax.axis_size(axis)
    return lax.ppermute(x, axis, [(i, i ^ (1 << bit)) for i in range(size)])


def add_halves(keep, got):
    def total(a, b):
        return (keep[a:b].astype(F32) + got[a:b].astype(F32)).astype(BF16)

    size = keep.shape[0]
    if size == 1:
        return total(0, 1), None
    return total(0, size // 2), total(size // 2, size)


def block_order(n):
    bits = n.bit_length() - 1
    return [sum(((k >> b) & 1) << (bits - 1 - b) for b in range(bits)) for k in range(n)]


class Group:
    def __init__(self, array, held):
        self.array, self.held = array, held


def join(groups, bit, arrays, axis):
    held, start = [], 0
    for group in groups:
        held += [(j | 1 << bit, code, start + first, rows) for j, code, first, rows in group.held]
        start += group.array.shape[axis]
    array = arrays[0] if len(arrays) == 1 else jnp.concatenate(arrays, axis=axis)
    return Group(swap(array, "shard", bit), held)


def gather_rows(x, gate=None, apart=False):
    rows = x.shape[0]
    groups = [Group(x, [(0, None, 0, rows)])]
    for bit in reversed(range(bits_of("shard"))):
        arrays = [g.array for g in groups]
        if gate is not None and len(arrays) > 1:
            arrays[-1] = after(arrays[-1], *gate())
        if apart:
            groups = groups + [join([g], bit, [a], 0) for g, a in zip(groups, arrays)]
        else:
            groups = groups + [join(groups, bit, arrays, 0)]
    return groups


def parity(bits):
    return functools.reduce(lambda a, b: a ^ b, [bit_of("rep", bit) for bit in bits])


def half_by_replica(x, dim, bits):
    shape = x.shape
    x = x.reshape(shape[:dim] + (2, shape[dim] // 2) + shape[dim + 1 :])
    return lax.dynamic_index_in_dim(x, parity(bits), dim, keepdims=False)


def fetch_far(send, dim, top, gate, bits):
    got = swap(half_by_replica(send, dim, bits), "shard", top)
    kept = after(got, *gate) if gate else got
    size = got.shape[dim]
    count = len(bits)
    parts = jnp.split(kept, count, axis=dim)
    return [Group(got, [(1 << top, (0, bits), 0, size)])] + [
        Group(swap(part, "rep", bit), [(1 << top, (1 + k, bits), 0, size // count)])
        for k, (part, bit) in enumerate(zip(parts, bits))
    ]


def gather_weight(x, gate, bits):
    top = bits_of("shard") - 1
    groups = [Group(x, [(0, None, 0, x.shape[0])])] + fetch_far(x, 0, top, gate, bits)
    for bit in reversed(range(top)):
        groups = groups + [join(groups, bit, [g.array for g in groups], 0)]
    return groups


def split_weight(x, gate, bits):
    me = lax.axis_index("shard")
    top = bits_of("shard") - 1

    def part_for(a, bit):
        start = ((me & (a.shape[0] - 1)) >> bit ^ 1) << bit
        return lax.dynamic_slice_in_dim(a, start, 1 << bit)

    groups = [Group(x, [(0, None, 0, x.shape[1])])]
    groups += fetch_far(part_for(x, top), 1, top, gate, bits)
    for bit in reversed(range(top)):
        groups = groups + [join(groups, bit, [part_for(g.array, bit) for g in groups], 1)]
    return groups


def gated(value, gates, step):
    return after(value, *gates[step]) if step < len(gates) else value


def replica_reduce(keep, send, order, gates=()):
    for step, bit in enumerate(order):
        keep, send = add_halves(keep, gated(swap(send, "rep", bit), gates, step))
    return keep[0]


def replica_spread(x, order):
    now = x[None]
    for bit in reversed(order[1:]):
        now = jnp.concatenate([now, swap(now, "rep", bit)])
    return now, swap(now, "rep", order[0])


class PairReduce:
    def __init__(self, p, q, orders):
        self.p, self.q, self.orders = p, q, orders

    def step(self, i, gates=()):
        p, q = self.p, self.q
        got_p = swap(p[1], "rep", self.orders[0][i])
        got_q = swap(q[1], "rep", self.orders[1][i])
        if gates:
            got_p, got_q = after(got_p, *gates), after(got_q, *gates)
        self.p, self.q = add_halves(p[0], got_p), add_halves(q[0], got_q)

    def finish(self, gates=()):
        rows = self.p[0].shape[1]
        keep, send = (jnp.concatenate(x, axis=1) for x in zip(self.p, self.q))
        share = replica_reduce(keep, send, self.orders[0][2:], gates)
        return share[:rows], share[rows:]


def pair_gather(p, q, orders):
    rows = p.shape[0]
    now = jnp.concatenate([p, q])[None]
    for bit in reversed(orders[0][2:]):
        now = jnp.concatenate([now, swap(now, "rep", bit)])
    pairs = []
    for x, order in zip((now[:, :rows], now[:, rows:]), orders):
        x = jnp.concatenate([x, swap(x, "rep", order[1])])
        pairs.append((x, swap(x, "rep", order[0])))
    return pairs


def turn(x, n):
    x = x[:, None]
    for bit in reversed(range(n.bit_length() - 1)):
        half = x.shape[0] // 2
        x = jnp.concatenate([x[:half], swap(x[half:], "shard", bit)], axis=1)
    return x[0]


def from_place(j, n):
    bits = n.bit_length() - 1
    return sum(((j >> b) & 1) << (bits - 1 - b) for b in range(bits))


def slot_mask(slot, order):
    count = len(order)
    return sum(((slot >> (count - 1 - i)) & 1) << bit for i, bit in enumerate(order))


def slot_of(mask, order):
    count = len(order)
    return sum(((mask >> bit) & 1) << (count - 1 - i) for i, bit in enumerate(order))


def dot(a, b, dims):
    return lax.dot_general(a, b, (dims, ((), ())), preferred_element_type=F32)


def normalise(values):
    centred = values - jnp.mean(values, axis=-1, keepdims=True)
    scale = lax.rsqrt(jnp.mean(centred * centred, axis=-1, keepdims=True) + norm_epsilon)
    return centred * scale, scale


def held_of(groups):
    return [(g.held, g.array.shape) for g in groups]


def arrays_of(groups):
    return [g.array for g in groups]


def pieces_of(held):
    return sum(len(h) for h, _ in held)


def blocks_of(held, refs):
    found = {}
    for (pieces, _), ref in zip(held, refs):
        for j, _, first, rows in pieces:
            found[j] = ref.at[first : first + rows, :]
    return [found[j] for j in range(len(found))]


def weight_copies(held, refs, target, me, sems, rep, by_owner, rows):
    copies = []
    for (pieces, shape), ref in zip(held, refs):
        source = ref.at[me & (shape[0] - 1)] if len(shape) == 3 else ref
        for j, code, first, count in pieces:
            start = (me ^ j if by_owner else j) * rows
            if code is not None:
                place, bits = code
                own = functools.reduce(lambda a, b: a ^ b, [(rep >> bit) & 1 for bit in bits])
                start = start + (own if place == 0 else 1 - own) * (rows // 2)
                start = start + max(place - 1, 0) * (rows // 2 // len(bits))
            place = target.at[pl.ds(pl.multiple_of(start, count), count), :]
            sem = sems.at[len(copies)]
            copies.append(pltpu.make_async_copy(source.at[first : first + count, :], place, sem))
    return copies


def partner(x):
    width = x.shape[-1]
    lane = lax.broadcasted_iota(jnp.int32, x.shape, 1)
    front = (lane % HEAD_DIM) < HEAD_DIM // 2
    return jnp.where(
        front,
        pltpu.roll(x, width - HEAD_DIM // 2, 1),
        pltpu.roll(x, HEAD_DIM // 2, 1),
    )


def head_masks(heads, width):
    lane = lax.broadcasted_iota(jnp.int32, (QB, width), 1) // HEAD_DIM
    return [lane == h for h in range(heads)]


def stack_heads(x, masks):
    x = x.astype(F32)
    return jnp.concatenate([jnp.where(m, x, 0.0) for m in masks], axis=0).astype(BF16)


def merge_heads(x, masks):
    total = None
    for h, m in enumerate(masks):
        part = jnp.where(m, x[h * QB : (h + 1) * QB], 0.0)
        total = part if total is None else total + part
    return total


def window_bias(ids_q, ids_k):
    row = lax.broadcasted_iota(jnp.int32, (QB, QB + 2 * HALF), 0)
    col = lax.broadcasted_iota(jnp.int32, (QB, QB + 2 * HALF), 1)
    ids_q = jnp.concatenate([ids_q] * ((QB + 2 * HALF) // LANES), axis=1)
    allowed = (col >= row) & (col <= row + 2 * HALF) & (ids_q == ids_k)
    return jnp.where(allowed, 0.0, masked_score)


def block_probs(stacked_q, keys, bias, heads):
    scores = dot(stacked_q, keys, ((1,), (1,)))
    rows, cols = scores.shape
    scores = (scores.reshape(heads, QB, cols) + bias[None]).reshape(rows, cols)
    weights = jnp.exp(scores - jnp.max(scores, axis=-1, keepdims=True))
    return weights * (1.0 / jnp.sum(weights, axis=-1, keepdims=True))


def column_chunk(ref, chunk, cols):
    if cols >= LANES:
        return ref[:, pl.ds(pl.multiple_of(chunk * cols, cols), cols)]
    per = LANES // cols
    tile = ref[:, pl.ds(pl.multiple_of(chunk // per * LANES, LANES), LANES)]
    result = tile
    for k in range(1, per):
        result = jnp.where(chunk % per == k, pltpu.roll(tile, LANES - k * cols, 1), result)
    return result


def row_chunk(ref, chunk, rows, start):
    if rows % 8 == 0:
        return ref[pl.ds(pl.multiple_of(chunk * rows, rows), rows), start : start + LANES]
    per = 8 // rows
    tile = ref[pl.ds(pl.multiple_of(chunk // per * 8, 8), 8), start : start + LANES]
    result = tile[:rows]
    for k in range(1, per):
        result = jnp.where(chunk % per == k, tile[k * rows : (k + 1) * rows], result)
    return result


def take_columns(ref, offset, valid, size):
    begin = offset // LANES * LANES
    end = -(-(offset + valid) // LANES) * LANES
    x = ref[:, begin:end].astype(F32)
    if offset != begin:
        x = pltpu.roll(x, end - offset, 1)
    x = x[:, :size]
    if valid != size:
        lane = lax.broadcasted_iota(jnp.int32, x.shape, 1)
        x = jnp.where(lane < valid, x, 0.0)
    return x


def split_kernel(n, blocks, valid, size, gain_ref, w_ref, out_ref):
    gain = gain_ref[...]
    for owner in range(n):
        for b in range(blocks):
            x = take_columns(w_ref, (b * n + owner) * valid, valid, size)
            out_ref[owner, :, b * size : (b + 1) * size] = (x * gain).astype(BF16)


def split_columns(w, gain, n, blocks, valid, size):
    rows, cols = w.shape
    step = min(rows, 64)
    return pl.pallas_call(
        functools.partial(split_kernel, n, blocks, valid, size),
        grid=(rows // step,),
        in_specs=[
            pl.BlockSpec((step, 1), lambda i: (i, 0)),
            pl.BlockSpec((step, cols), lambda i: (i, 0)),
        ],
        out_specs=pl.BlockSpec((n, step, blocks * size), lambda i: (0, i, 0)),
        out_shape=jax.ShapeDtypeStruct((n, rows, blocks * size), BF16),
        compiler_params=pltpu.CompilerParams(vmem_limit_bytes=24 << 20),
        name="split_columns",
    )(gain, w)


def attention_kernel(
    tok_held, held, n, heads, place_ref, cos_ref, sin_ref, idq_ref, idk_ref, *refs
):
    tok_refs, refs = blocks_of(tok_held, refs), refs[len(tok_held) :]
    piece_refs, refs = refs[: len(held)], refs[len(held) :]
    q_ref, k_ref, v_ref, out_ref, normed_ref, w_ref, sems = refs
    seq, width = q_ref.shape
    rows = seq // n
    me, rep = place_ref[0], place_ref[1]
    copies = weight_copies(
        held, piece_refs, w_ref, me, sems, rep, True, w_ref.shape[0] // n
    )
    for c in copies:
        c.start()
    edge = jnp.zeros((HALF, width), BF16)
    for ref in (k_ref, v_ref):
        ref[0:HALF, :] = edge
        ref[seq + HALF : seq + 2 * HALF, :] = edge
    for c in copies:
        c.wait()
    for j in range(n):
        start = (me ^ j) * rows
        at = pl.ds(pl.multiple_of(start, rows), rows)
        shifted = pl.ds(pl.multiple_of(start + HALF, HALF), rows)
        hat, _ = normalise(tok_refs[j][...].astype(F32))
        normed = hat.astype(BF16)
        normed_ref[at, :] = normed
        qkv = jnp.dot(normed, w_ref[...], preferred_element_type=F32)
        cos, sin = cos_ref[at, :], sin_ref[at, :]
        q, k = qkv[:, 0:width], qkv[:, width : 2 * width]
        rotated = (q * cos + partner(q) * sin).astype(BF16)
        q_ref[at, :] = (rotated.astype(F32) * (1.0 / math.sqrt(HEAD_DIM))).astype(BF16)
        k_ref[shifted, :] = (k * cos + partner(k) * sin).astype(BF16)
        v_ref[shifted, :] = qkv[:, 2 * width : 3 * width].astype(BF16)
    masks = head_masks(heads, width)

    def attend(i, carry):
        at = pl.ds(pl.multiple_of(i * QB, QB), QB)
        window = pl.ds(pl.multiple_of(i * QB, QB), QB + 2 * HALF)
        bias = window_bias(idq_ref[at, :], idk_ref[0:1, window])
        probs = block_probs(stack_heads(q_ref[at, :], masks), k_ref[window, :], bias, heads)
        mixed = jnp.dot(probs.astype(BF16), v_ref[window, :], preferred_element_type=F32)
        out_ref[at, :] = merge_heads(mixed, masks).astype(BF16)
        return carry

    lax.fori_loop(0, seq // QB, attend, 0, unroll=2)


def up_kernel(tok_held, att_held, out_held, in_held, n, place_ref, *refs):
    tok_refs, refs = blocks_of(tok_held, refs), refs[len(tok_held) :]
    att_refs, refs = blocks_of(att_held, refs), refs[len(att_held) :]
    out_refs, refs = refs[: len(out_held)], refs[len(out_held) :]
    in_refs, refs = refs[: len(in_held)], refs[len(in_held) :]
    hidden_out, normed_out, up_out, in_out, *refs = refs
    tok, att, w_out, w_in, hidden_own, normed, up, *refs = refs
    out_sems, in_sems, att_sems, tok_sems, sems = refs
    me, rep = place_ref[0], place_ref[1]
    rows, model = tok_refs[0].shape
    copy = pltpu.make_async_copy
    att_copies = [copy(att_refs[j], att.at[j], att_sems.at[j]) for j in range(n)]
    tok_copies = [copy(tok_refs[j], tok.at[j], tok_sems.at[j]) for j in range(n)]
    part = model // n
    out_copies = weight_copies(out_held, out_refs, w_out, me, out_sems, rep, False, part)
    in_copies = weight_copies(in_held, in_refs, w_in, me, in_sems, rep, True, part)
    for c in att_copies + tok_copies[:1] + out_copies + in_copies + tok_copies[1:]:
        c.start()
    for c in att_copies + out_copies:
        c.wait()
    sent = []
    for j in range(n):
        at = pl.ds(pl.multiple_of((me ^ j) * rows, rows), rows)
        here = slice(j * rows, (j + 1) * rows)
        tok_copies[j].wait()
        hidden = tok[j].astype(F32)
        for i in range(n):
            hidden = hidden + jnp.dot(
                att[i, at, :], w_out[i * part : (i + 1) * part, :], preferred_element_type=F32
            )
        if j == 0:
            hidden_own[...] = hidden
            sent.append(copy(hidden_own, hidden_out, sems.at[2 * n]))
            sent[-1].start()
        hat, _ = normalise(hidden)
        low = hat.astype(BF16)
        normed[here, :] = low
        if j == 0:
            for c in in_copies:
                c.wait()
            sent.append(copy(w_in, in_out, sems.at[2 * n + 1]))
            sent[-1].start()
        up[here, :] = jnp.dot(low, w_in[...], preferred_element_type=F32)
        sent += [
            copy(normed.at[here, :], normed_out.at[here, :], sems.at[2 * j]),
            copy(up.at[here, :], up_out.at[here, :], sems.at[2 * j + 1]),
        ]
        for c in sent[-2:]:
            c.start()
    for c in sent:
        c.wait()


def dup_kernel(cot_held, n, up_ref, w_in_ref, down_ref, *refs):
    cot_refs, refs = blocks_of(cot_held, refs), refs[len(cot_held) :]
    act_out, dup_out, keep_out, send_out, *refs = refs
    up, cot, w_in, w_down, act, dup, dnormed, in_sem, down_sem, up_sems, cot_sems, sems = refs
    rows, model = cot_refs[0].shape
    padded = w_down.shape[0]
    given = down_ref.shape[0]
    if given != padded:
        w_down[given:padded, :] = jnp.zeros((padded - given, model), BF16)
    copy = pltpu.make_async_copy
    down_copy = copy(down_ref, w_down.at[0:given, :], down_sem)
    in_copy = copy(w_in_ref, w_in, in_sem)
    cot_copies = [copy(cot_refs[j], cot.at[j], cot_sems.at[j]) for j in range(n)]
    up_copies = []
    for j in range(n):
        here = slice(j * rows, (j + 1) * rows)
        up_copies.append(copy(up_ref.at[here, :], up.at[here, :], up_sems.at[j]))
    for c in [up_copies[0], cot_copies[0], down_copy, in_copy]:
        c.start()
    for c in up_copies[1:] + cot_copies[1:]:
        c.start()
    sent = []
    order = block_order(n)
    for j in range(n):
        here = slice(j * rows, (j + 1) * rows)
        place = order.index(j)
        target = (keep_out if place < n // 2 else send_out).at[place % (n // 2)]
        up_copies[j].wait()
        gate, lin = up[here, :padded], up[here, padded:]
        phi = 0.5 + 0.5 * lax.erf(gate * (1.0 / math.sqrt(2.0)))
        gelu = gate * phi
        slope = phi + gate * jnp.exp(gate * gate * -0.5) * (1.0 / math.sqrt(2.0 * math.pi))
        act[here, :] = (gelu * lin).astype(BF16)
        cot_copies[j].wait()
        if j == 0:
            down_copy.wait()
        dact = dot(cot[j], w_down[...], ((1,), (1,)))
        dup[here, :padded] = (dact * lin * slope).astype(BF16)
        dup[here, padded:] = (dact * gelu).astype(BF16)
        if j == 0:
            in_copy.wait()
        dnormed[j] = dot(dup[here, :], w_in[...], ((1,), (1,))).astype(BF16)
        sent += [
            copy(dnormed.at[j], target, sems.at[3 * j]),
            copy(act.at[here, :], act_out.at[here, :], sems.at[3 * j + 1]),
            copy(dup.at[here, :], dup_out.at[here, :], sems.at[3 * j + 2]),
        ]
        for c in sent[-3:]:
            c.start()
    for c in sent:
        c.wait()


def store_slots(keep_ref, send_ref, rep, order, write):
    half = keep_ref.shape[0]
    for slot in range(2 * half):
        target = keep_ref if slot < half else send_ref
        write(target, slot % half, rep ^ slot_mask(slot, order))


def up_tiles(ff):
    return 2 * (ff // LANES) + 1


def put_block(keep, send, j, value):
    half = keep.shape[0]
    place = block_order(2 * half).index(j)
    target = keep if place < half else send
    target[place % half] = value.astype(BF16)


def down_kernel(cot_held, n, ff, order, place_ref, act, w_down, *refs):
    cot_refs, refs = blocks_of(cot_held, refs), refs[len(cot_held) :]
    keep, send, mlp_keep, mlp_send, down_sum = refs
    rows, model = cot_refs[0].shape
    cols = model // (2 * keep.shape[0])
    total = None
    for j in range(n):
        term = dot(act[j * rows : (j + 1) * rows, :], cot_refs[j][...], ((0,), (0,)))
        total = term if total is None else total + term
    down_sum[...] = total

    def write(target, slot, c):
        target[slot] = column_chunk(down_sum, c, cols)[:ff].astype(BF16)

    store_slots(keep, send, place_ref[1], order, write)
    given = w_down.shape[0]
    for j in range(n):
        low = act[j * rows : (j + 1) * rows, 0:given]
        put_block(mlp_keep, mlp_send, j, jnp.dot(low, w_down[...], preferred_element_type=F32))


def write_flows(total, starts, counts, orders, flows, index, rep):
    begin = 0
    for f, (count, order) in enumerate(zip(counts, orders)):
        keep, send = flows[2 * f], flows[2 * f + 1]
        chunk = keep.shape[2]

        def write(target, slot, c):
            for t in range(count):
                value = row_chunk(total, c, chunk, starts[begin + t])
                target[slot, index * count + t] = value.astype(BF16)

        store_slots(keep, send, rep, order, write)
        begin += count


def in_kernel(n, ff, counts, orders, place_ref, normed, dup, *refs):
    flows, in_sum = refs[:-1], refs[-1]
    me, rep = place_ref[0], place_ref[1]
    part = normed.shape[1] // n
    padded = dup.shape[1] // 2
    whole, rest = ff // LANES, ff % LANES
    starts = [t * LANES for t in range(whole)] + [padded + t * LANES for t in range(whole)]
    starts.append(2 * padded)
    for owner in range(n):
        block = dot(normed[:, owner * part : (owner + 1) * part], dup[...], ((0,), (0,)))
        in_sum[:, : 2 * padded] = block
        first = block[:, whole * LANES : (whole + 1) * LANES]
        second = block[:, padded + whole * LANES : padded + (whole + 1) * LANES]
        lane = lax.broadcasted_iota(jnp.int32, first.shape, 1)
        in_sum[:, 2 * padded :] = jnp.where(lane < rest, first, pltpu.roll(second, rest, 1))
        write_flows(in_sum, starts, counts, orders, flows, me ^ owner, rep)


def add_kernel(keep_ref, got_ref, mine_ref, other_ref):
    mine_ref[...] = keep_ref[0].astype(F32) + got_ref[0].astype(F32)
    other_ref[...] = (keep_ref[1].astype(F32) + got_ref[1].astype(F32)).astype(BF16)


def near_sums(keep, send, name, gate=None):
    bits = bits_of("shard")
    for bit in range(bits - 2):
        keep, send = add_halves(keep, swap(send, "shard", bit))
    _, rows, model = keep.shape
    got = swap(send, "shard", bits - 2)
    if gate is not None:
        got = after(got, gate)
    return pl.pallas_call(
        add_kernel,
        out_shape=[
            jax.ShapeDtypeStruct((rows, model), F32),
            jax.ShapeDtypeStruct((rows, model), BF16),
        ],
        compiler_params=pltpu.CompilerParams(vmem_limit_bytes=16 << 20),
        name=name,
    )(keep, got)


def output_kernel(mine, got, hidden, out_ref):
    out_ref[...] = (hidden[...] + mine[...] + got[...].astype(F32)).astype(BF16)


def input_kernel(mine, got, tokens, dhidden, out_ref):
    hat, scale = normalise(tokens[...].astype(F32))
    e = mine[...] + got[...].astype(F32)
    out_ref[...] = dhidden[...] + norm_backward(e, hat, scale)


def norm_back_kernel(mine, got, hidden, cotangent, dhidden, dproj):
    hat, scale = normalise(hidden[...])
    e = mine[...] + got[...].astype(F32)
    value = cotangent[...].astype(F32) + norm_backward(e, hat, scale)
    dhidden[...] = value
    dproj[...] = value.astype(BF16)


def attention_back_kernel(held, n, heads, order, place_ref, *refs):
    dproj_refs, refs = blocks_of(held, refs), refs[len(held) :]
    w_out, att, q_ref, k_ref, v_ref, cos_ref, sin_ref, idq_ref, idk_ref, *refs = refs
    dqkv, out_keep, out_send, da, dk, dv, out_sum = refs
    me, rep = place_ref[0], place_ref[1]
    seq, width = q_ref.shape
    rows, model = dproj_refs[0].shape
    part = model // n
    dk[...] = jnp.zeros_like(dk)
    dv[...] = jnp.zeros_like(dv)
    head_cols = heads * HEAD_DIM
    total = None
    for j in range(n):
        at = pl.ds(pl.multiple_of((me ^ j) * rows, rows), rows)
        dproj = dproj_refs[j][...]
        da[at, 0:head_cols] = dot(dproj, w_out[...], ((1,), (1,))).astype(BF16)
        term = dot(att[at, :], dproj, ((0,), (0,)))
        total = term if total is None else total + term
    if head_cols != width:
        da[:, head_cols:] = jnp.zeros((seq, width - head_cols), BF16)
    out_sum[...] = total[0:part]
    cols = model // (2 * out_keep.shape[0])

    def write_out(target, slot, c):
        target[slot] = column_chunk(out_sum, c, cols).astype(BF16)

    store_slots(out_keep, out_send, rep, order, write_out)
    masks = head_masks(heads, width)

    def back(i, carry):
        at = pl.ds(pl.multiple_of(i * QB, QB), QB)
        window = pl.ds(pl.multiple_of(i * QB, QB), QB + 2 * HALF)
        bias = window_bias(idq_ref[at, :], idk_ref[0:1, window])
        queries = stack_heads(q_ref[at, :], masks)
        keys = k_ref[window, :]
        probs = block_probs(queries, keys, bias, heads)
        grads = stack_heads(da[at, :], masks)
        dprobs = dot(grads, v_ref[window, :], ((1,), (1,)))
        delta = jnp.sum(probs * dprobs, axis=-1, keepdims=True)
        dscores = (probs * (dprobs - delta)).astype(BF16)
        dq = merge_heads(jnp.dot(dscores, keys, preferred_element_type=F32), masks)
        dq = dq * (1.0 / math.sqrt(HEAD_DIM))
        cos, sin = cos_ref[at, :], sin_ref[at, :]
        dqkv[at, 0:width] = (dq * cos - partner(dq) * sin).astype(BF16)
        dk[window, :] += dot(dscores, queries, ((0,), (0,)))
        dv[window, :] += dot(probs.astype(BF16), grads, ((0,), (0,)))
        return carry

    lax.fori_loop(0, seq // QB, back, 0, unroll=2)

    def finish(i, carry):
        at = pl.ds(pl.multiple_of(i * QB, QB), QB)
        shifted = pl.ds(pl.multiple_of(i * QB + HALF, HALF), QB)
        cos, sin = cos_ref[at, :], sin_ref[at, :]
        g = dk[shifted, :]
        dqkv[at, width : 2 * width] = (g * cos - partner(g) * sin).astype(BF16)
        dqkv[at, 2 * width : 3 * width] = dv[shifted, :].astype(BF16)
        return carry

    lax.fori_loop(0, seq // QB, finish, 0)


def qkv_kernel(n, counts, orders, place_ref, normed, dqkv, *refs):
    flows, qkv_sum = refs[:-1], refs[-1]
    me, rep = place_ref[0], place_ref[1]
    part = normed.shape[1] // n
    starts = [t * LANES for t in range(sum(counts))]
    for owner in range(n):
        qkv_sum[...] = dot(normed[:, owner * part : (owner + 1) * part], dqkv[...], ((0,), (0,)))
        write_flows(qkv_sum, starts, counts, orders, flows, me ^ owner, rep)


def project_back_kernel(n, place_ref, dqkv, w_qkv, keep, send):
    rows = keep.shape[1]
    for j in range(n):
        at = pl.ds(pl.multiple_of((place_ref[0] ^ j) * rows, rows), rows)
        put_block(keep, send, j, dot(dqkv[at, :], w_qkv[...], ((1,), (1,))))


def place_piece(canvas, piece, offset, valid):
    shift = offset % LANES
    height, size = piece.shape
    count = -(-(shift + valid) // LANES)
    if count * LANES > size:
        piece = jnp.concatenate([piece, jnp.zeros((height, count * LANES - size), F32)], axis=1)
    if shift:
        piece = pltpu.roll(piece, shift, 1)
    lane = lax.broadcasted_iota(jnp.int32, (height, LANES), 1)
    for t in range(count):
        tile = piece[:, t * LANES : (t + 1) * LANES]
        low, high = shift - t * LANES, shift + valid - t * LANES
        if low > 0 or high < LANES:
            tile = jnp.where((lane >= low) & (lane < high), tile, 0.0)
        index = offset // LANES + t
        canvas[index] = tile if index not in canvas else canvas[index] + tile


def columns_out_kernel(n, ff, head_cols, width, counts, orders, place_ref, gain_ref, w_ref, *refs):
    me, rep = place_ref[0], place_ref[1]
    *parts, out_ref, ln_ref = refs
    half = parts[0].shape[0]
    slots = [slot_of(rep ^ pl.program_id(0), order) for order in orders]

    def read(owner, t):
        f = 0
        while t >= counts[f]:
            t -= counts[f]
            f += 1
        slot, index = slots[f], from_place(me ^ owner, n) * counts[f] + t
        at = slot & (half - 1)
        now, got = parts[2 * f][at, index], parts[2 * f + 1][at, index]
        return jnp.where(slot < half, now, got).astype(F32)

    canvas = {}
    for owner in range(n):
        tile = functools.partial(read, owner)

        if ff:
            whole, rest = ff // LANES, ff % LANES
            last = tile(2 * whole)
            gate = jnp.concatenate([tile(t) for t in range(whole)] + [last], axis=1)
            last = pltpu.roll(last, LANES - rest, 1)
            lin = jnp.concatenate([tile(whole + t) for t in range(whole)] + [last], axis=1)
            place_piece(canvas, gate, owner * ff, ff)
            place_piece(canvas, lin, (n + owner) * ff, ff)
        else:
            per = width // LANES
            for b in range(3):
                piece = jnp.concatenate([tile(b * per + t) for t in range(per)], axis=1)
                place_piece(canvas, piece, (b * n + owner) * head_cols, head_cols)
    gain = gain_ref[...]
    total = None
    for index, value in canvas.items():
        at = slice(index * LANES, (index + 1) * LANES)
        term = value * w_ref[:, at].astype(F32)
        total = term if total is None else total + term
        out_ref[:, at] = value * gain
    ln_ref[...] = jnp.sum(total, axis=1, keepdims=True)


def columns_out(place, pairs, counts, orders, weight, gain, n, ff=0, head_cols=0, width=0):
    parts = [a for pair in pairs for a in pair]
    chunk = parts[0].shape[2]
    part, cols = weight.shape
    count = part // chunk
    part_specs = [pl.BlockSpec(a.shape, lambda i: (0, 0, 0, 0)) for a in parts]
    total, ln = pl.pallas_call(
        functools.partial(columns_out_kernel, n, ff, head_cols, width, counts, orders),
        grid=(count,),
        in_specs=[
            pl.BlockSpec(memory_space=pltpu.SMEM),
            pl.BlockSpec((None, chunk, 1), lambda i: (i, 0, 0)),
            pl.BlockSpec((None, chunk, cols), lambda i: (i, 0, 0)),
            *part_specs,
        ],
        out_specs=[
            pl.BlockSpec((None, chunk, cols), lambda i: (i, 0, 0)),
            pl.BlockSpec((None, chunk, 1), lambda i: (i, 0, 0)),
        ],
        out_shape=[
            jax.ShapeDtypeStruct((count, chunk, cols), F32),
            jax.ShapeDtypeStruct((count, chunk, 1), F32),
        ],
        compiler_params=pltpu.CompilerParams(vmem_limit_bytes=32 << 20),
        name="columns_out",
    )(place, gain.reshape(count, chunk, 1), weight.reshape(count, chunk, cols), *parts)
    return total.reshape(part, cols), ln.reshape(part)


def rows_out_kernel(order, cols, skip, place_ref, *refs):
    *parts, out_ref = refs
    rep = place_ref[1]

    def chunk(c):
        half = parts[0].shape[0]
        slot = slot_of(rep ^ c, order)
        at = slot & (half - 1)
        rows = slice(skip, skip + out_ref.shape[0])
        return jnp.where(slot < half, parts[0][at, rows], parts[1][at, rows]).astype(F32)

    count = out_ref.shape[1] // cols
    if cols >= LANES:
        for c in range(count):
            out_ref[:, c * cols : (c + 1) * cols] = chunk(c)
    else:
        per = LANES // cols
        lane = lax.broadcasted_iota(jnp.int32, out_ref.shape[:1] + (LANES,), 1) // cols
        for t in range(count // per):
            value = chunk(per * t)
            for k in range(1, per):
                value = jnp.where(lane == k, pltpu.roll(chunk(per * t + k), k * cols, 1), value)
            out_ref[:, t * LANES : (t + 1) * LANES] = value


def rows_out(place, pair, skip, rows, model, order):
    return pl.pallas_call(
        functools.partial(rows_out_kernel, order, model // (2 * pair[0].shape[0]), skip),
        in_specs=[pl.BlockSpec(memory_space=pltpu.SMEM)]
        + [pl.BlockSpec(memory_space=pltpu.VMEM)] * 2,
        out_shape=jax.ShapeDtypeStruct((rows, model), F32),
        compiler_params=pltpu.CompilerParams(vmem_limit_bytes=32 << 20),
        name="rows_out",
    )(place, *pair)


def ordered(kernel, first, count):
    def body(*refs):
        kernel(*refs[:first], *refs[first + count :])

    return body


def work(flops):
    return pl.CostEstimate(flops=int(flops), bytes_accessed=1 << 22, transcendentals=0)


SMEM_SPEC = pl.BlockSpec(memory_space=pltpu.SMEM)
VMEM_SPEC = pl.BlockSpec(memory_space=pltpu.VMEM)
ANY_SPEC = pl.BlockSpec(memory_space=pl.ANY)


def norm_backward(grad_hat, normed, scale):
    return (
        grad_hat
        - jnp.mean(grad_hat, axis=-1, keepdims=True)
        - normed * jnp.mean(grad_hat * normed, axis=-1, keepdims=True)
    ) * scale


def after(value, *earlier):
    return lax.optimization_barrier((value,) + earlier)[0]


def shards(tokens, segment_ids, ln1_gain, w_qkv, w_out, ln2_gain, w_in, w_down, cotangent):
    n = lax.axis_size("shard")
    replicas = lax.axis_size("rep")
    me = lax.axis_index("shard")
    place = jnp.stack([me, lax.axis_index("rep")]).astype(jnp.int32)
    rows, model = tokens.shape
    seq = rows * n
    part = model // n
    ff = w_down.shape[0]
    heads = HEADS // n
    head_cols = heads * HEAD_DIM
    width = max(LANES, head_cols)
    padded = -(-ff // LANES) * LANES
    near = list(range(bits_of("rep")))
    far = near[1:2] + near[:1] + near[2:]
    shape = jax.ShapeDtypeStruct
    params = pltpu.CompilerParams(vmem_limit_bytes=VMEM_LIMIT)

    gain1 = ln1_gain.astype(F32)[:, None]
    gain2 = ln2_gain.astype(F32)[:, None]
    qkv_to = split_columns(w_qkv, gain1, n, 3, head_cols, width)
    in_to = split_columns(w_in, gain2, n, 2, ff, padded)
    lane = jnp.arange(width, dtype=jnp.int32) % HEAD_DIM
    half = HEAD_DIM // 2
    frequency = jnp.exp(-math.log(rope_base) * 2.0 * (lane % half).astype(F32) / HEAD_DIM)
    angles = jnp.arange(seq, dtype=F32)[:, None] * frequency[None, :]
    sign = jnp.where(lane < half, -1.0, 1.0)
    ids = segment_ids[0]
    tables = (
        jnp.cos(angles),
        jnp.sin(angles) * sign[None, :],
        jnp.broadcast_to(ids[:, None], (seq, LANES)),
        jnp.pad(ids, (HALF, HALF), constant_values=-1)[None],
    )

    qkv_groups = split_weight(qkv_to, (tables[0], tables[1], in_to), (0, 1))
    toks = gather_rows(tokens, apart=True)

    queries, keys, values, attended, normed1, qkv_w = pl.pallas_call(
        ordered(
            functools.partial(attention_kernel, held_of(toks), held_of(qkv_groups), n, heads),
            5 + len(toks) + len(qkv_groups),
            0,
        ),
        in_specs=[SMEM_SPEC]
        + [VMEM_SPEC] * (4 + len(toks))
        + [ANY_SPEC] * len(qkv_groups),
        out_shape=(
            shape((seq, width), BF16),
            shape((seq + 2 * HALF, width), BF16),
            shape((seq + 2 * HALF, width), BF16),
            shape((seq, width), BF16),
            shape((seq, model), BF16),
            shape((model, 3 * width), BF16),
        ),
        scratch_shapes=[pltpu.SemaphoreType.DMA((pieces_of(held_of(qkv_groups)),))],
        compiler_params=params,
        cost_estimate=work(40 * seq * model * width),
        name="attention",
    )(place, *tables, *arrays_of(toks + qkv_groups))

    out_groups = gather_weight(after(w_out, toks[1].array), (attended,), (2,))
    in_groups = split_weight(after(in_to, qkv_groups[1].array), (attended,), (0, 1))
    atts = gather_rows(attended[:, :head_cols])
    block_shape = shape((n // 2, rows, model), BF16)
    hidden, normed2, up, in_w = pl.pallas_call(
        functools.partial(
            up_kernel, held_of(toks), held_of(atts), held_of(out_groups), held_of(in_groups), n
        ),
        in_specs=[SMEM_SPEC] + [ANY_SPEC] * len(toks + atts + out_groups + in_groups),
        out_specs=[ANY_SPEC] * 4,
        out_shape=[
            shape((rows, model), F32),
            shape((seq, model), BF16),
            shape((seq, 2 * padded), F32),
            shape((model, 2 * padded), BF16),
        ],
        scratch_shapes=[
            pltpu.VMEM((n, rows, model), BF16),
            pltpu.VMEM((n, seq, head_cols), BF16),
            pltpu.VMEM((model, model), BF16),
            pltpu.VMEM((model, 2 * padded), BF16),
            pltpu.VMEM((rows, model), F32),
            pltpu.VMEM((seq, model), BF16),
            pltpu.VMEM((seq, 2 * padded), F32),
            pltpu.SemaphoreType.DMA((pieces_of(held_of(out_groups)),)),
            pltpu.SemaphoreType.DMA((pieces_of(held_of(in_groups)),)),
            pltpu.SemaphoreType.DMA((n,)),
            pltpu.SemaphoreType.DMA((n,)),
            pltpu.SemaphoreType.DMA((2 * n + 2,)),
        ],
        compiler_params=params,
        cost_estimate=work(12 * seq * model * padded),
        name="up_projection",
    )(place, *arrays_of(toks + atts + out_groups + in_groups))
    cots = gather_rows(after(cotangent, atts[1].array), lambda: (up,))
    down_w = jnp.pad(w_down, ((0, -ff % 16), (0, 0)))
    act, dup, dnormed2_keep, dnormed2_send = pl.pallas_call(
        functools.partial(dup_kernel, held_of(cots), n),
        in_specs=[ANY_SPEC] * (3 + len(cots)),
        out_specs=[ANY_SPEC] * 4,
        out_shape=[shape((seq, padded), BF16), shape((seq, 2 * padded), BF16)] + [block_shape] * 2,
        scratch_shapes=[
            pltpu.VMEM((seq, 2 * padded), F32),
            pltpu.VMEM((n, rows, model), BF16),
            pltpu.VMEM((model, 2 * padded), BF16),
            pltpu.VMEM((padded, model), BF16),
            pltpu.VMEM((seq, padded), BF16),
            pltpu.VMEM((seq, 2 * padded), BF16),
            pltpu.VMEM((n, rows, model), BF16),
            pltpu.SemaphoreType.DMA,
            pltpu.SemaphoreType.DMA,
            pltpu.SemaphoreType.DMA((n,)),
            pltpu.SemaphoreType.DMA((n,)),
            pltpu.SemaphoreType.DMA((3 * n,)),
        ],
        compiler_params=params,
        cost_estimate=work(14 * seq * model * padded),
        name="dup",
    )(up, in_w, down_w, *arrays_of(cots))

    slots = replicas // 2
    chunk = part // replicas
    lanes = max(LANES, model // replicas)
    tiles = up_tiles(ff)
    orders = [near, far]
    in_counts = [tiles - tiles // 2, tiles // 2]
    in_shapes = [shape((slots, n * c, chunk, LANES), BF16) for c in in_counts for _ in range(2)]
    down_shape = shape((slots, ff, lanes), BF16)
    top = bits_of("shard") - 1

    def flow_rows(a):
        return a.reshape(a.shape[0], -1, LANES)

    mine, other = near_sums(dnormed2_keep, dnormed2_send, "near_sum_2")
    in_flows = pl.pallas_call(
        ordered(functools.partial(in_kernel, n, ff, in_counts, orders), 3, 1),
        in_specs=[SMEM_SPEC] + [VMEM_SPEC] * 2 + [ANY_SPEC],
        out_shape=in_shapes,
        scratch_shapes=[pltpu.VMEM((part, 2 * padded + LANES), F32)],
        compiler_params=params,
        cost_estimate=work(8 * seq * model * padded),
        name="in_gradient",
    )(place, normed2, dup, other)
    in_flows = [flow_rows(a) for a in in_flows]
    in_reduce = PairReduce(in_flows[:2], in_flows[2:], orders)
    dhidden, dproj = pl.pallas_call(
        ordered(norm_back_kernel, 4, 1),
        in_specs=[VMEM_SPEC] * 4 + [ANY_SPEC],
        out_shape=[shape((rows, model), F32), shape((rows, model), BF16)],
        compiler_params=pltpu.CompilerParams(vmem_limit_bytes=24 << 20),
        name="norm_back",
    )(mine, swap(other, "shard", top), hidden, cotangent, in_flows[0])
    down_keep, down_send, mlp_keep, mlp_send = pl.pallas_call(
        ordered(functools.partial(down_kernel, held_of(cots), n, ff, far), 3 + len(cots), 1),
        in_specs=[SMEM_SPEC] + [VMEM_SPEC] * (2 + len(cots)) + [ANY_SPEC],
        out_shape=[down_shape] * 2 + [block_shape] * 2,
        scratch_shapes=[pltpu.VMEM((padded, model), F32)],
        compiler_params=params,
        cost_estimate=work(8 * seq * model * padded),
        name="down_gradient",
    )(place, act, down_w, *arrays_of(cots), dproj)
    dprojs = gather_rows(dproj, lambda: (down_keep,))
    in_reduce.step(0, [dprojs[1].array])

    out_shape = shape((slots, part, lanes), BF16)
    dqkv, out_keep, out_send = pl.pallas_call(
        ordered(
            functools.partial(attention_back_kernel, held_of(dprojs), n, heads, far),
            len(dprojs) + 10,
            2,
        ),
        in_specs=[SMEM_SPEC] + [VMEM_SPEC] * (len(dprojs) + 9) + [ANY_SPEC] * 2,
        out_shape=[shape((seq, 3 * width), BF16), out_shape, out_shape],
        scratch_shapes=[
            pltpu.VMEM((seq, width), BF16),
            pltpu.VMEM((seq + 2 * HALF, width), F32),
            pltpu.VMEM((seq + 2 * HALF, width), F32),
            pltpu.VMEM((part, model), F32),
        ],
        compiler_params=params,
        cost_estimate=work(40 * seq * model * width),
        name="attention_back",
    )(
        place,
        *arrays_of(dprojs),
        w_out,
        attended,
        queries,
        keys,
        values,
        *tables,
        in_reduce.p[1],
        in_reduce.q[1],
    )

    mlp_mine, mlp_other = near_sums(mlp_keep, mlp_send, "near_sum_mlp", dqkv)
    qkv_tiles = 3 * width // LANES
    qkv_counts = [qkv_tiles - qkv_tiles // 3, qkv_tiles // 3]
    in_reduce.step(1, [dqkv])
    down_reduce = add_halves(down_keep, after(swap(down_send, "rep", far[0]), dqkv))
    qkv_flows = pl.pallas_call(
        ordered(functools.partial(qkv_kernel, n, qkv_counts, orders), 3, 4),
        in_specs=[SMEM_SPEC] + [VMEM_SPEC] * 2 + [ANY_SPEC] * 4,
        out_shape=[shape((slots, n * c, chunk, LANES), BF16) for c in qkv_counts for _ in range(2)],
        scratch_shapes=[pltpu.VMEM((part, 3 * width), F32)],
        compiler_params=params,
        cost_estimate=work(12 * seq * model * width),
        name="qkv_gradient",
    )(place, normed1, dqkv, in_reduce.p[1], in_reduce.q[1], down_reduce[1], mlp_other)
    qkv_flows = [flow_rows(a) for a in qkv_flows]
    split = qkv_flows[2].shape[1]
    qkv_q = [jnp.concatenate(x, axis=1) for x in zip(qkv_flows[2:], (out_keep, out_send))]
    att_reduce = PairReduce(qkv_flows[:2], qkv_q, orders)
    att_reduce.step(0)
    att_first = att_reduce.p[1]
    output = pl.pallas_call(
        ordered(output_kernel, 3, 1),
        in_specs=[VMEM_SPEC] * 3 + [ANY_SPEC],
        out_shape=shape((rows, model), BF16),
        compiler_params=pltpu.CompilerParams(vmem_limit_bytes=16 << 20),
        name="output",
    )(mlp_mine, swap(mlp_other, "shard", top), hidden, qkv_flows[0])
    dnormed1_keep, dnormed1_send = pl.pallas_call(
        ordered(functools.partial(project_back_kernel, n), 3, 3),
        in_specs=[SMEM_SPEC] + [VMEM_SPEC] * 2 + [ANY_SPEC] * 3,
        out_shape=[block_shape] * 2,
        compiler_params=params,
        cost_estimate=work(6 * seq * model * width),
        name="project_back",
    )(place, dqkv, qkv_w, output, att_first, att_reduce.q[1])
    mine, other = near_sums(dnormed1_keep, dnormed1_send, "near_sum_1")
    input_grad = pl.pallas_call(
        input_kernel,
        out_shape=shape((rows, model), F32),
        compiler_params=pltpu.CompilerParams(vmem_limit_bytes=24 << 20),
        name="input_grad",
    )(mine, swap(other, "shard", top), tokens, dhidden)

    def turned(p, q, counts):
        sizes = [c * chunk for c in counts]
        whole = jnp.concatenate([p.reshape(n, sizes[0], LANES), q.reshape(n, sizes[1], LANES)], 1)
        whole = turn(whole, n)
        return whole[:, : sizes[0]].reshape(-1, LANES), whole[:, sizes[0] :].reshape(-1, LANES)

    def tiles_of(pair, count):
        size = n * count * chunk
        return [a[:, :size].reshape(a.shape[0], n * count, chunk, LANES) for a in pair]

    in_p, in_q = turned(*in_reduce.finish([[qkv_flows[0]]]), in_counts)
    down_share = replica_reduce(*down_reduce, far[1:], [[att_first]])

    att_reduce.step(1, [dnormed1_keep])
    att_p, att_q = att_reduce.finish([[other]])
    att_done = att_p[:16]
    in_p, in_q = pair_gather(in_p, in_q, orders)
    down_pair = replica_spread(after(down_share, att_done), far)
    qkv_p, qkv_q = turned(att_p, att_q[:split], qkv_counts)
    att_p, att_q = pair_gather(qkv_p, jnp.concatenate([qkv_q, att_q[split:]]), orders)

    in_total, ln2_total = columns_out(
        place,
        [tiles_of(in_p, in_counts[0]), tiles_of(in_q, in_counts[1])],
        in_counts,
        orders,
        w_in,
        gain2,
        n,
        ff=ff,
    )
    down_total = rows_out(place, down_pair, 0, ff, model, far)
    out_total = rows_out(place, att_q, split, part, model, far)
    qkv_total, ln1_total = columns_out(
        place,
        [tiles_of(att_p, qkv_counts[0]), tiles_of(att_q, qkv_counts[1])],
        qkv_counts,
        orders,
        w_qkv,
        gain1,
        n,
        head_cols=head_cols,
        width=width,
    )
    return (
        output,
        input_grad,
        ln1_total,
        qkv_total,
        out_total,
        ln2_total,
        in_total,
        down_total,
    )


def solution(mesh):
    return jax.shard_map(
        shards,
        mesh=mesh,
        in_specs=(
            P(("rep", "shard"), None),
            P("rep", None),
            P("shard"),
            P("shard", None),
            P("shard", None),
            P("shard"),
            P("shard", None),
            P("shard", None),
            P(("rep", "shard"), None),
        ),
        out_specs=(
            P(("rep", "shard"), None),
            P(("rep", "shard"), None),
            P("shard"),
            P("shard", None),
            P("shard", None),
            P("shard"),
            P("shard", None),
            P("shard", None),
        ),
        check_vma=False,
    )
```

```python
import functools
import math

import jax
import jax.numpy as jnp
from jax import lax
from jax.experimental import pallas as pl
from jax.experimental.pallas import tpu as pltpu
from jax.sharding import PartitionSpec as P

HEADS = 16
HEAD_DIM = 64
HALF = 64
QB = 128
LANES = 128

norm_epsilon = 1e-05
rope_base = 10000.0
masked_score = -1e30

F32 = jnp.float32
BF16 = jnp.bfloat16
VMEM_LIMIT = 52 << 20


def bits_of(axis):
    return lax.axis_size(axis).bit_length() - 1


def bit_of(axis, bit):
    return (lax.axis_index(axis) >> bit) & 1


def swap(x, axis, bit):
    size = lax.axis_size(axis)
    return lax.ppermute(x, axis, [(i, i ^ (1 << bit)) for i in range(size)])


def add_halves(keep, got):
    def total(a, b):
        return (keep[a:b].astype(F32) + got[a:b].astype(F32)).astype(BF16)

    size = keep.shape[0]
    if size == 1:
        return total(0, 1), None
    return total(0, size // 2), total(size // 2, size)


def block_order(n):
    bits = n.bit_length() - 1
    return [sum(((k >> b) & 1) << (bits - 1 - b) for b in range(bits)) for k in range(n)]


class Group:
    def __init__(self, array, held):
        self.array, self.held = array, held


def join(groups, bit, arrays, axis):
    held, start = [], 0
    for group in groups:
        held += [(j | 1 << bit, code, start + first, rows) for j, code, first, rows in group.held]
        start += group.array.shape[axis]
    array = arrays[0] if len(arrays) == 1 else jnp.concatenate(arrays, axis=axis)
    return Group(swap(array, "shard", bit), held)


def gather_rows(x, gate=None, apart=False):
    rows = x.shape[0]
    groups = [Group(x, [(0, None, 0, rows)])]
    for bit in reversed(range(bits_of("shard"))):
        arrays = [g.array for g in groups]
        if gate is not None and len(arrays) > 1:
            arrays[-1] = after(arrays[-1], *gate())
        if apart:
            groups = groups + [join([g], bit, [a], 0) for g, a in zip(groups, arrays)]
        else:
            groups = groups + [join(groups, bit, arrays, 0)]
    return groups


def parity(bits):
    return functools.reduce(lambda a, b: a ^ b, [bit_of("rep", bit) for bit in bits])


def half_by_replica(x, dim, bits):
    shape = x.shape
    x = x.reshape(shape[:dim] + (2, shape[dim] // 2) + shape[dim + 1 :])
    return lax.dynamic_index_in_dim(x, parity(bits), dim, keepdims=False)


def fetch_far(send, dim, top, gate, bits):
    got = swap(half_by_replica(send, dim, bits), "shard", top)
    kept = after(got, *gate) if gate else got
    size = got.shape[dim]
    count = len(bits)
    parts = jnp.split(kept, count, axis=dim)
    return [Group(got, [(1 << top, (0, bits), 0, size)])] + [
        Group(swap(part, "rep", bit), [(1 << top, (1 + k, bits), 0, size // count)])
        for k, (part, bit) in enumerate(zip(parts, bits))
    ]


def gather_weight(x, gate, bits):
    top = bits_of("shard") - 1
    groups = [Group(x, [(0, None, 0, x.shape[0])])] + fetch_far(x, 0, top, gate, bits)
    for bit in reversed(range(top)):
        groups = groups + [join(groups, bit, [g.array for g in groups], 0)]
    return groups


def split_weight(x, gate, bits):
    me = lax.axis_index("shard")
    top = bits_of("shard") - 1

    def part_for(a, bit):
        start = ((me & (a.shape[0] - 1)) >> bit ^ 1) << bit
        return lax.dynamic_slice_in_dim(a, start, 1 << bit)

    groups = [Group(x, [(0, None, 0, x.shape[1])])]
    groups += fetch_far(part_for(x, top), 1, top, gate, bits)
    for bit in reversed(range(top)):
        groups = groups + [join(groups, bit, [part_for(g.array, bit) for g in groups], 1)]
    return groups


def gated(value, gates, step):
    return after(value, *gates[step]) if step < len(gates) else value


def replica_reduce(keep, send, order, gates=()):
    for step, bit in enumerate(order):
        keep, send = add_halves(keep, gated(swap(send, "rep", bit), gates, step))
    return keep[0]


def replica_spread(x, order):
    now = x[None]
    for bit in reversed(order[1:]):
        now = jnp.concatenate([now, swap(now, "rep", bit)])
    return now, swap(now, "rep", order[0])


class PairReduce:
    def __init__(self, p, q, orders):
        self.p, self.q, self.orders = p, q, orders

    def step(self, i, gates=()):
        p, q = self.p, self.q
        got_p = swap(p[1], "rep", self.orders[0][i])
        got_q = swap(q[1], "rep", self.orders[1][i])
        if gates:
            got_p, got_q = after(got_p, *gates), after(got_q, *gates)
        self.p, self.q = add_halves(p[0], got_p), add_halves(q[0], got_q)

    def finish(self, gates=()):
        rows = self.p[0].shape[1]
        keep, send = (jnp.concatenate(x, axis=1) for x in zip(self.p, self.q))
        share = replica_reduce(keep, send, self.orders[0][2:], gates)
        return share[:rows], share[rows:]


def pair_gather(p, q, orders):
    rows = p.shape[0]
    now = jnp.concatenate([p, q])[None]
    for bit in reversed(orders[0][2:]):
        now = jnp.concatenate([now, swap(now, "rep", bit)])
    pairs = []
    for x, order in zip((now[:, :rows], now[:, rows:]), orders):
        x = jnp.concatenate([x, swap(x, "rep", order[1])])
        pairs.append((x, swap(x, "rep", order[0])))
    return pairs


def turn(x, n):
    x = x[:, None]
    for bit in reversed(range(n.bit_length() - 1)):
        half = x.shape[0] // 2
        x = jnp.concatenate([x[:half], swap(x[half:], "shard", bit)], axis=1)
    return x[0]


def from_place(j, n):
    bits = n.bit_length() - 1
    return sum(((j >> b) & 1) << (bits - 1 - b) for b in range(bits))


def slot_mask(slot, order):
    count = len(order)
    return sum(((slot >> (count - 1 - i)) & 1) << bit for i, bit in enumerate(order))


def slot_of(mask, order):
    count = len(order)
    return sum(((mask >> bit) & 1) << (count - 1 - i) for i, bit in enumerate(order))


def dot(a, b, dims):
    return lax.dot_general(a, b, (dims, ((), ())), preferred_element_type=F32)


def normalise(values):
    centred = values - jnp.mean(values, axis=-1, keepdims=True)
    scale = lax.rsqrt(jnp.mean(centred * centred, axis=-1, keepdims=True) + norm_epsilon)
    return centred * scale, scale


def held_of(groups):
    return [(g.held, g.array.shape) for g in groups]


def arrays_of(groups):
    return [g.array for g in groups]


def pieces_of(held):
    return sum(len(h) for h, _ in held)


def blocks_of(held, refs):
    found = {}
    for (pieces, _), ref in zip(held, refs):
        for j, _, first, rows in pieces:
            found[j] = ref.at[first : first + rows, :]
    return [found[j] for j in range(len(found))]


def weight_copies(held, refs, target, me, sems, rep, by_owner, rows):
    copies = []
    for (pieces, shape), ref in zip(held, refs):
        source = ref.at[me & (shape[0] - 1)] if len(shape) == 3 else ref
        for j, code, first, count in pieces:
            start = (me ^ j if by_owner else j) * rows
            if code is not None:
                place, bits = code
                own = functools.reduce(lambda a, b: a ^ b, [(rep >> bit) & 1 for bit in bits])
                start = start + (own if place == 0 else 1 - own) * (rows // 2)
                start = start + max(place - 1, 0) * (rows // 2 // len(bits))
            place = target.at[pl.ds(pl.multiple_of(start, count), count), :]
            sem = sems.at[len(copies)]
            copies.append(pltpu.make_async_copy(source.at[first : first + count, :], place, sem))
    return copies


def partner(x):
    width = x.shape[-1]
    lane = lax.broadcasted_iota(jnp.int32, x.shape, 1)
    front = (lane % HEAD_DIM) < HEAD_DIM // 2
    return jnp.where(
        front,
        pltpu.roll(x, width - HEAD_DIM // 2, 1),
        pltpu.roll(x, HEAD_DIM // 2, 1),
    )


def head_masks(heads, width):
    lane = lax.broadcasted_iota(jnp.int32, (QB, width), 1) // HEAD_DIM
    return [lane == h for h in range(heads)]


def stack_heads(x, masks):
    x = x.astype(F32)
    return jnp.concatenate([jnp.where(m, x, 0.0) for m in masks], axis=0).astype(BF16)


def merge_heads(x, masks):
    total = None
    for h, m in enumerate(masks):
        part = jnp.where(m, x[h * QB : (h + 1) * QB], 0.0)
        total = part if total is None else total + part
    return total


def window_bias(ids_q, ids_k):
    row = lax.broadcasted_iota(jnp.int32, (QB, QB + 2 * HALF), 0)
    col = lax.broadcasted_iota(jnp.int32, (QB, QB + 2 * HALF), 1)
    ids_q = jnp.concatenate([ids_q] * ((QB + 2 * HALF) // LANES), axis=1)
    allowed = (col >= row) & (col <= row + 2 * HALF) & (ids_q == ids_k)
    return jnp.where(allowed, 0.0, masked_score)


def block_probs(stacked_q, keys, bias, heads):
    scores = dot(stacked_q, keys, ((1,), (1,)))
    rows, cols = scores.shape
    scores = (scores.reshape(heads, QB, cols) + bias[None]).reshape(rows, cols)
    weights = jnp.exp(scores - jnp.max(scores, axis=-1, keepdims=True))
    return weights * (1.0 / jnp.sum(weights, axis=-1, keepdims=True))


def column_chunk(ref, chunk, cols):
    if cols >= LANES:
        return ref[:, pl.ds(pl.multiple_of(chunk * cols, cols), cols)]
    per = LANES // cols
    tile = ref[:, pl.ds(pl.multiple_of(chunk // per * LANES, LANES), LANES)]
    result = tile
    for k in range(1, per):
        result = jnp.where(chunk % per == k, pltpu.roll(tile, LANES - k * cols, 1), result)
    return result


def row_chunk(ref, chunk, rows, start):
    if rows % 8 == 0:
        return ref[pl.ds(pl.multiple_of(chunk * rows, rows), rows), start : start + LANES]
    per = 8 // rows
    tile = ref[pl.ds(pl.multiple_of(chunk // per * 8, 8), 8), start : start + LANES]
    result = tile[:rows]
    for k in range(1, per):
        result = jnp.where(chunk % per == k, tile[k * rows : (k + 1) * rows], result)
    return result


def take_columns(ref, offset, valid, size):
    begin = offset // LANES * LANES
    end = -(-(offset + valid) // LANES) * LANES
    x = ref[:, begin:end].astype(F32)
    if offset != begin:
        x = pltpu.roll(x, end - offset, 1)
    x = x[:, :size]
    if valid != size:
        lane = lax.broadcasted_iota(jnp.int32, x.shape, 1)
        x = jnp.where(lane < valid, x, 0.0)
    return x


def split_kernel(n, blocks, valid, size, gain_ref, w_ref, out_ref):
    gain = gain_ref[...]
    for owner in range(n):
        for b in range(blocks):
            x = take_columns(w_ref, (b * n + owner) * valid, valid, size)
            out_ref[owner, :, b * size : (b + 1) * size] = (x * gain).astype(BF16)


def split_columns(w, gain, n, blocks, valid, size):
    rows, cols = w.shape
    step = min(rows, 64)
    return pl.pallas_call(
        functools.partial(split_kernel, n, blocks, valid, size),
        grid=(rows // step,),
        in_specs=[
            pl.BlockSpec((step, 1), lambda i: (i, 0)),
            pl.BlockSpec((step, cols), lambda i: (i, 0)),
        ],
        out_specs=pl.BlockSpec((n, step, blocks * size), lambda i: (0, i, 0)),
        out_shape=jax.ShapeDtypeStruct((n, rows, blocks * size), BF16),
        compiler_params=pltpu.CompilerParams(vmem_limit_bytes=24 << 20),
        name="split_columns",
    )(gain, w)


def attention_kernel(
    tok_held, held, n, heads, place_ref, cos_ref, sin_ref, idq_ref, idk_ref, *refs
):
    tok_refs, refs = blocks_of(tok_held, refs), refs[len(tok_held) :]
    piece_refs, refs = refs[: len(held)], refs[len(held) :]
    q_ref, k_ref, v_ref, out_ref, normed_ref, w_ref, sems = refs
    seq, width = q_ref.shape
    rows = seq // n
    me, rep = place_ref[0], place_ref[1]
    copies = weight_copies(
        held, piece_refs, w_ref, me, sems, rep, True, w_ref.shape[0] // n
    )
    for c in copies:
        c.start()
    edge = jnp.zeros((HALF, width), BF16)
    for ref in (k_ref, v_ref):
        ref[0:HALF, :] = edge
        ref[seq + HALF : seq + 2 * HALF, :] = edge
    for c in copies:
        c.wait()
    for j in range(n):
        start = (me ^ j) * rows
        at = pl.ds(pl.multiple_of(start, rows), rows)
        shifted = pl.ds(pl.multiple_of(start + HALF, HALF), rows)
        hat, _ = normalise(tok_refs[j][...].astype(F32))
        normed = hat.astype(BF16)
        normed_ref[at, :] = normed
        qkv = jnp.dot(normed, w_ref[...], preferred_element_type=F32)
        cos, sin = cos_ref[at, :], sin_ref[at, :]
        q, k = qkv[:, 0:width], qkv[:, width : 2 * width]
        rotated = (q * cos + partner(q) * sin).astype(BF16)
        q_ref[at, :] = (rotated.astype(F32) * (1.0 / math.sqrt(HEAD_DIM))).astype(BF16)
        k_ref[shifted, :] = (k * cos + partner(k) * sin).astype(BF16)
        v_ref[shifted, :] = qkv[:, 2 * width : 3 * width].astype(BF16)
    masks = head_masks(heads, width)

    def attend(i, carry):
        at = pl.ds(pl.multiple_of(i * QB, QB), QB)
        window = pl.ds(pl.multiple_of(i * QB, QB), QB + 2 * HALF)
        bias = window_bias(idq_ref[at, :], idk_ref[0:1, window])
        probs = block_probs(stack_heads(q_ref[at, :], masks), k_ref[window, :], bias, heads)
        mixed = jnp.dot(probs.astype(BF16), v_ref[window, :], preferred_element_type=F32)
        out_ref[at, :] = merge_heads(mixed, masks).astype(BF16)
        return carry

    lax.fori_loop(0, seq // QB, attend, 0, unroll=2)


def up_kernel(tok_held, att_held, out_held, in_held, n, place_ref, *refs):
    tok_refs, refs = blocks_of(tok_held, refs), refs[len(tok_held) :]
    att_refs, refs = blocks_of(att_held, refs), refs[len(att_held) :]
    out_refs, refs = refs[: len(out_held)], refs[len(out_held) :]
    in_refs, refs = refs[: len(in_held)], refs[len(in_held) :]
    hidden_out, normed_out, up_out, in_out, *refs = refs
    tok, att, w_out, w_in, hidden_own, normed, up, *refs = refs
    out_sems, in_sems, att_sems, tok_sems, sems = refs
    me, rep = place_ref[0], place_ref[1]
    rows, model = tok_refs[0].shape
    copy = pltpu.make_async_copy
    att_copies = [copy(att_refs[j], att.at[j], att_sems.at[j]) for j in range(n)]
    tok_copies = [copy(tok_refs[j], tok.at[j], tok_sems.at[j]) for j in range(n)]
    part = model // n
    out_copies = weight_copies(out_held, out_refs, w_out, me, out_sems, rep, False, part)
    in_copies = weight_copies(in_held, in_refs, w_in, me, in_sems, rep, True, part)
    for c in att_copies + tok_copies[:1] + out_copies + in_copies + tok_copies[1:]:
        c.start()
    for c in att_copies + out_copies:
        c.wait()
    sent = []
    for j in range(n):
        at = pl.ds(pl.multiple_of((me ^ j) * rows, rows), rows)
        here = slice(j * rows, (j + 1) * rows)
        tok_copies[j].wait()
        hidden = tok[j].astype(F32)
        for i in range(n):
            hidden = hidden + jnp.dot(
                att[i, at, :], w_out[i * part : (i + 1) * part, :], preferred_element_type=F32
            )
        if j == 0:
            hidden_own[...] = hidden
            sent.append(copy(hidden_own, hidden_out, sems.at[2 * n]))
            sent[-1].start()
        hat, _ = normalise(hidden)
        low = hat.astype(BF16)
        normed[here, :] = low
        if j == 0:
            for c in in_copies:
                c.wait()
            sent.append(copy(w_in, in_out, sems.at[2 * n + 1]))
            sent[-1].start()
        up[here, :] = jnp.dot(low, w_in[...], preferred_element_type=F32)
        sent += [
            copy(normed.at[here, :], normed_out.at[here, :], sems.at[2 * j]),
            copy(up.at[here, :], up_out.at[here, :], sems.at[2 * j + 1]),
        ]
        for c in sent[-2:]:
            c.start()
    for c in sent:
        c.wait()


def dup_kernel(cot_held, n, up_ref, w_in_ref, down_ref, *refs):
    cot_refs, refs = blocks_of(cot_held, refs), refs[len(cot_held) :]
    act_out, dup_out, keep_out, send_out, *refs = refs
    up, cot, w_in, w_down, act, dup, dnormed, in_sem, down_sem, up_sems, cot_sems, sems = refs
    rows, model = cot_refs[0].shape
    padded = w_down.shape[0]
    given = down_ref.shape[0]
    if given != padded:
        w_down[given:padded, :] = jnp.zeros((padded - given, model), BF16)
    copy = pltpu.make_async_copy
    down_copy = copy(down_ref, w_down.at[0:given, :], down_sem)
    in_copy = copy(w_in_ref, w_in, in_sem)
    cot_copies = [copy(cot_refs[j], cot.at[j], cot_sems.at[j]) for j in range(n)]
    up_copies = []
    for j in range(n):
        here = slice(j * rows, (j + 1) * rows)
        up_copies.append(copy(up_ref.at[here, :], up.at[here, :], up_sems.at[j]))
    for c in [up_copies[0], cot_copies[0], down_copy, in_copy]:
        c.start()
    for c in up_copies[1:] + cot_copies[1:]:
        c.start()
    sent = []
    order = block_order(n)
    for j in range(n):
        here = slice(j * rows, (j + 1) * rows)
        place = order.index(j)
        target = (keep_out if place < n // 2 else send_out).at[place % (n // 2)]
        up_copies[j].wait()
        gate, lin = up[here, :padded], up[here, padded:]
        phi = 0.5 + 0.5 * lax.erf(gate * (1.0 / math.sqrt(2.0)))
        gelu = gate * phi
        slope = phi + gate * jnp.exp(gate * gate * -0.5) * (1.0 / math.sqrt(2.0 * math.pi))
        act[here, :] = (gelu * lin).astype(BF16)
        cot_copies[j].wait()
        if j == 0:
            down_copy.wait()
        dact = dot(cot[j], w_down[...], ((1,), (1,)))
        dup[here, :padded] = (dact * lin * slope).astype(BF16)
        dup[here, padded:] = (dact * gelu).astype(BF16)
        if j == 0:
            in_copy.wait()
        dnormed[j] = dot(dup[here, :], w_in[...], ((1,), (1,))).astype(BF16)
        sent += [
            copy(dnormed.at[j], target, sems.at[3 * j]),
            copy(act.at[here, :], act_out.at[here, :], sems.at[3 * j + 1]),
            copy(dup.at[here, :], dup_out.at[here, :], sems.at[3 * j + 2]),
        ]
        for c in sent[-3:]:
            c.start()
    for c in sent:
        c.wait()


def store_slots(keep_ref, send_ref, rep, order, write):
    half = keep_ref.shape[0]
    for slot in range(2 * half):
        target = keep_ref if slot < half else send_ref
        write(target, slot % half, rep ^ slot_mask(slot, order))


def up_tiles(ff):
    return 2 * (ff // LANES) + 1


def put_block(keep, send, j, value):
    half = keep.shape[0]
    place = block_order(2 * half).index(j)
    target = keep if place < half else send
    target[place % half] = value.astype(BF16)


def down_kernel(cot_held, n, ff, order, place_ref, act, w_down, *refs):
    cot_refs, refs = blocks_of(cot_held, refs), refs[len(cot_held) :]
    keep, send, mlp_keep, mlp_send, down_sum = refs
    rows, model = cot_refs[0].shape
    cols = model // (2 * keep.shape[0])
    total = None
    for j in range(n):
        term = dot(act[j * rows : (j + 1) * rows, :], cot_refs[j][...], ((0,), (0,)))
        total = term if total is None else total + term
    down_sum[...] = total

    def write(target, slot, c):
        target[slot] = column_chunk(down_sum, c, cols)[:ff].astype(BF16)

    store_slots(keep, send, place_ref[1], order, write)
    given = w_down.shape[0]
    for j in range(n):
        low = act[j * rows : (j + 1) * rows, 0:given]
        put_block(mlp_keep, mlp_send, j, jnp.dot(low, w_down[...], preferred_element_type=F32))


def write_flows(total, starts, counts, orders, flows, index, rep):
    begin = 0
    for f, (count, order) in enumerate(zip(counts, orders)):
        keep, send = flows[2 * f], flows[2 * f + 1]
        chunk = keep.shape[2]

        def write(target, slot, c):
            for t in range(count):
                value = row_chunk(total, c, chunk, starts[begin + t])
                target[slot, index * count + t] = value.astype(BF16)

        store_slots(keep, send, rep, order, write)
        begin += count


def in_kernel(n, ff, counts, orders, place_ref, normed, dup, *refs):
    flows, in_sum = refs[:-1], refs[-1]
    me, rep = place_ref[0], place_ref[1]
    part = normed.shape[1] // n
    padded = dup.shape[1] // 2
    whole, rest = ff // LANES, ff % LANES
    starts = [t * LANES for t in range(whole)] + [padded + t * LANES for t in range(whole)]
    starts.append(2 * padded)
    for owner in range(n):
        block = dot(normed[:, owner * part : (owner + 1) * part], dup[...], ((0,), (0,)))
        in_sum[:, : 2 * padded] = block
        first = block[:, whole * LANES : (whole + 1) * LANES]
        second = block[:, padded + whole * LANES : padded + (whole + 1) * LANES]
        lane = lax.broadcasted_iota(jnp.int32, first.shape, 1)
        in_sum[:, 2 * padded :] = jnp.where(lane < rest, first, pltpu.roll(second, rest, 1))
        write_flows(in_sum, starts, counts, orders, flows, me ^ owner, rep)


def add_kernel(keep_ref, got_ref, mine_ref, other_ref):
    mine_ref[...] = keep_ref[0].astype(F32) + got_ref[0].astype(F32)
    other_ref[...] = (keep_ref[1].astype(F32) + got_ref[1].astype(F32)).astype(BF16)


def near_sums(keep, send, name, gate=None):
    bits = bits_of("shard")
    for bit in range(bits - 2):
        keep, send = add_halves(keep, swap(send, "shard", bit))
    _, rows, model = keep.shape
    got = swap(send, "shard", bits - 2)
    if gate is not None:
        got = after(got, gate)
    return pl.pallas_call(
        add_kernel,
        out_shape=[
            jax.ShapeDtypeStruct((rows, model), F32),
            jax.ShapeDtypeStruct((rows, model), BF16),
        ],
        compiler_params=pltpu.CompilerParams(vmem_limit_bytes=16 << 20),
        name=name,
    )(keep, got)


def output_kernel(mine, got, hidden, out_ref):
    out_ref[...] = (hidden[...] + mine[...] + got[...].astype(F32)).astype(BF16)


def input_kernel(mine, got, tokens, dhidden, out_ref):
    hat, scale = normalise(tokens[...].astype(F32))
    e = mine[...] + got[...].astype(F32)
    out_ref[...] = dhidden[...] + norm_backward(e, hat, scale)


def norm_back_kernel(mine, got, hidden, cotangent, dhidden, dproj):
    hat, scale = normalise(hidden[...])
    e = mine[...] + got[...].astype(F32)
    value = cotangent[...].astype(F32) + norm_backward(e, hat, scale)
    dhidden[...] = value
    dproj[...] = value.astype(BF16)


def attention_back_kernel(held, n, heads, order, place_ref, *refs):
    dproj_refs, refs = blocks_of(held, refs), refs[len(held) :]
    w_out, att, q_ref, k_ref, v_ref, cos_ref, sin_ref, idq_ref, idk_ref, *refs = refs
    dqkv, out_keep, out_send, da, dk, dv, out_sum = refs
    me, rep = place_ref[0], place_ref[1]
    seq, width = q_ref.shape
    rows, model = dproj_refs[0].shape
    part = model // n
    dk[...] = jnp.zeros_like(dk)
    dv[...] = jnp.zeros_like(dv)
    head_cols = heads * HEAD_DIM
    total = None
    for j in range(n):
        at = pl.ds(pl.multiple_of((me ^ j) * rows, rows), rows)
        dproj = dproj_refs[j][...]
        da[at, 0:head_cols] = dot(dproj, w_out[...], ((1,), (1,))).astype(BF16)
        term = dot(att[at, :], dproj, ((0,), (0,)))
        total = term if total is None else total + term
    if head_cols != width:
        da[:, head_cols:] = jnp.zeros((seq, width - head_cols), BF16)
    out_sum[...] = total[0:part]
    cols = model // (2 * out_keep.shape[0])

    def write_out(target, slot, c):
        target[slot] = column_chunk(out_sum, c, cols).astype(BF16)

    store_slots(out_keep, out_send, rep, order, write_out)
    masks = head_masks(heads, width)

    def back(i, carry):
        at = pl.ds(pl.multiple_of(i * QB, QB), QB)
        window = pl.ds(pl.multiple_of(i * QB, QB), QB + 2 * HALF)
        bias = window_bias(idq_ref[at, :], idk_ref[0:1, window])
        queries = stack_heads(q_ref[at, :], masks)
        keys = k_ref[window, :]
        probs = block_probs(queries, keys, bias, heads)
        grads = stack_heads(da[at, :], masks)
        dprobs = dot(grads, v_ref[window, :], ((1,), (1,)))
        delta = jnp.sum(probs * dprobs, axis=-1, keepdims=True)
        dscores = (probs * (dprobs - delta)).astype(BF16)
        dq = merge_heads(jnp.dot(dscores, keys, preferred_element_type=F32), masks)
        dq = dq * (1.0 / math.sqrt(HEAD_DIM))
        cos, sin = cos_ref[at, :], sin_ref[at, :]
        dqkv[at, 0:width] = (dq * cos - partner(dq) * sin).astype(BF16)
        dk[window, :] += dot(dscores, queries, ((0,), (0,)))
        dv[window, :] += dot(probs.astype(BF16), grads, ((0,), (0,)))
        return carry

    lax.fori_loop(0, seq // QB, back, 0, unroll=2)

    def finish(i, carry):
        at = pl.ds(pl.multiple_of(i * QB, QB), QB)
        shifted = pl.ds(pl.multiple_of(i * QB + HALF, HALF), QB)
        cos, sin = cos_ref[at, :], sin_ref[at, :]
        g = dk[shifted, :]
        dqkv[at, width : 2 * width] = (g * cos - partner(g) * sin).astype(BF16)
        dqkv[at, 2 * width : 3 * width] = dv[shifted, :].astype(BF16)
        return carry

    lax.fori_loop(0, seq // QB, finish, 0)


def qkv_kernel(n, counts, orders, place_ref, normed, dqkv, *refs):
    flows, qkv_sum = refs[:-1], refs[-1]
    me, rep = place_ref[0], place_ref[1]
    part = normed.shape[1] // n
    starts = [t * LANES for t in range(sum(counts))]
    for owner in range(n):
        qkv_sum[...] = dot(normed[:, owner * part : (owner + 1) * part], dqkv[...], ((0,), (0,)))
        write_flows(qkv_sum, starts, counts, orders, flows, me ^ owner, rep)


def project_back_kernel(n, place_ref, dqkv, w_qkv, keep, send):
    rows = keep.shape[1]
    for j in range(n):
        at = pl.ds(pl.multiple_of((place_ref[0] ^ j) * rows, rows), rows)
        put_block(keep, send, j, dot(dqkv[at, :], w_qkv[...], ((1,), (1,))))


def place_piece(canvas, piece, offset, valid):
    shift = offset % LANES
    height, size = piece.shape
    count = -(-(shift + valid) // LANES)
    if count * LANES > size:
        piece = jnp.concatenate([piece, jnp.zeros((height, count * LANES - size), F32)], axis=1)
    if shift:
        piece = pltpu.roll(piece, shift, 1)
    lane = lax.broadcasted_iota(jnp.int32, (height, LANES), 1)
    for t in range(count):
        tile = piece[:, t * LANES : (t + 1) * LANES]
        low, high = shift - t * LANES, shift + valid - t * LANES
        if low > 0 or high < LANES:
            tile = jnp.where((lane >= low) & (lane < high), tile, 0.0)
        index = offset // LANES + t
        canvas[index] = tile if index not in canvas else canvas[index] + tile


def columns_out_kernel(n, ff, head_cols, width, counts, orders, place_ref, gain_ref, w_ref, *refs):
    me, rep = place_ref[0], place_ref[1]
    *parts, out_ref, ln_ref = refs
    half = parts[0].shape[0]
    slots = [slot_of(rep ^ pl.program_id(0), order) for order in orders]

    def read(owner, t):
        f = 0
        while t >= counts[f]:
            t -= counts[f]
            f += 1
        slot, index = slots[f], from_place(me ^ owner, n) * counts[f] + t
        at = slot & (half - 1)
        now, got = parts[2 * f][at, index], parts[2 * f + 1][at, index]
        return jnp.where(slot < half, now, got).astype(F32)

    canvas = {}
    for owner in range(n):
        tile = functools.partial(read, owner)

        if ff:
            whole, rest = ff // LANES, ff % LANES
            last = tile(2 * whole)
            gate = jnp.concatenate([tile(t) for t in range(whole)] + [last], axis=1)
            last = pltpu.roll(last, LANES - rest, 1)
            lin = jnp.concatenate([tile(whole + t) for t in range(whole)] + [last], axis=1)
            place_piece(canvas, gate, owner * ff, ff)
            place_piece(canvas, lin, (n + owner) * ff, ff)
        else:
            per = width // LANES
            for b in range(3):
                piece = jnp.concatenate([tile(b * per + t) for t in range(per)], axis=1)
                place_piece(canvas, piece, (b * n + owner) * head_cols, head_cols)
    gain = gain_ref[...]
    total = None
    for index, value in canvas.items():
        at = slice(index * LANES, (index + 1) * LANES)
        term = value * w_ref[:, at].astype(F32)
        total = term if total is None else total + term
        out_ref[:, at] = value * gain
    ln_ref[...] = jnp.sum(total, axis=1, keepdims=True)


def columns_out(place, pairs, counts, orders, weight, gain, n, ff=0, head_cols=0, width=0):
    parts = [a for pair in pairs for a in pair]
    chunk = parts[0].shape[2]
    part, cols = weight.shape
    count = part // chunk
    part_specs = [pl.BlockSpec(a.shape, lambda i: (0, 0, 0, 0)) for a in parts]
    total, ln = pl.pallas_call(
        functools.partial(columns_out_kernel, n, ff, head_cols, width, counts, orders),
        grid=(count,),
        in_specs=[
            pl.BlockSpec(memory_space=pltpu.SMEM),
            pl.BlockSpec((None, chunk, 1), lambda i: (i, 0, 0)),
            pl.BlockSpec((None, chunk, cols), lambda i: (i, 0, 0)),
            *part_specs,
        ],
        out_specs=[
            pl.BlockSpec((None, chunk, cols), lambda i: (i, 0, 0)),
            pl.BlockSpec((None, chunk, 1), lambda i: (i, 0, 0)),
        ],
        out_shape=[
            jax.ShapeDtypeStruct((count, chunk, cols), F32),
            jax.ShapeDtypeStruct((count, chunk, 1), F32),
        ],
        compiler_params=pltpu.CompilerParams(vmem_limit_bytes=32 << 20),
        name="columns_out",
    )(place, gain.reshape(count, chunk, 1), weight.reshape(count, chunk, cols), *parts)
    return total.reshape(part, cols), ln.reshape(part)


def rows_out_kernel(order, cols, skip, place_ref, *refs):
    *parts, out_ref = refs
    rep = place_ref[1]

    def chunk(c):
        half = parts[0].shape[0]
        slot = slot_of(rep ^ c, order)
        at = slot & (half - 1)
        rows = slice(skip, skip + out_ref.shape[0])
        return jnp.where(slot < half, parts[0][at, rows], parts[1][at, rows]).astype(F32)

    count = out_ref.shape[1] // cols
    if cols >= LANES:
        for c in range(count):
            out_ref[:, c * cols : (c + 1) * cols] = chunk(c)
    else:
        per = LANES // cols
        lane = lax.broadcasted_iota(jnp.int32, out_ref.shape[:1] + (LANES,), 1) // cols
        for t in range(count // per):
            value = chunk(per * t)
            for k in range(1, per):
                value = jnp.where(lane == k, pltpu.roll(chunk(per * t + k), k * cols, 1), value)
            out_ref[:, t * LANES : (t + 1) * LANES] = value


def rows_out(place, pair, skip, rows, model, order):
    return pl.pallas_call(
        functools.partial(rows_out_kernel, order, model // (2 * pair[0].shape[0]), skip),
        in_specs=[pl.BlockSpec(memory_space=pltpu.SMEM)]
        + [pl.BlockSpec(memory_space=pltpu.VMEM)] * 2,
        out_shape=jax.ShapeDtypeStruct((rows, model), F32),
        compiler_params=pltpu.CompilerParams(vmem_limit_bytes=32 << 20),
        name="rows_out",
    )(place, *pair)


def ordered(kernel, first, count):
    def body(*refs):
        kernel(*refs[:first], *refs[first + count :])

    return body


def work(flops):
    return pl.CostEstimate(flops=int(flops), bytes_accessed=1 << 22, transcendentals=0)


SMEM_SPEC = pl.BlockSpec(memory_space=pltpu.SMEM)
VMEM_SPEC = pl.BlockSpec(memory_space=pltpu.VMEM)
ANY_SPEC = pl.BlockSpec(memory_space=pl.ANY)


def norm_backward(grad_hat, normed, scale):
    return (
        grad_hat
        - jnp.mean(grad_hat, axis=-1, keepdims=True)
        - normed * jnp.mean(grad_hat * normed, axis=-1, keepdims=True)
    ) * scale


def after(value, *earlier):
    return lax.optimization_barrier((value,) + earlier)[0]


def shards(tokens, segment_ids, ln1_gain, w_qkv, w_out, ln2_gain, w_in, w_down, cotangent):
    n = lax.axis_size("shard")
    replicas = lax.axis_size("rep")
    me = lax.axis_index("shard")
    place = jnp.stack([me, lax.axis_index("rep")]).astype(jnp.int32)
    rows, model = tokens.shape
    seq = rows * n
    part = model // n
    ff = w_down.shape[0]
    heads = HEADS // n
    head_cols = heads * HEAD_DIM
    width = max(LANES, head_cols)
    padded = -(-ff // LANES) * LANES
    near = list(range(bits_of("rep")))
    far = near[1:2] + near[:1] + near[2:]
    shape = jax.ShapeDtypeStruct
    params = pltpu.CompilerParams(vmem_limit_bytes=VMEM_LIMIT)

    gain1 = ln1_gain.astype(F32)[:, None]
    gain2 = ln2_gain.astype(F32)[:, None]
    qkv_to = split_columns(w_qkv, gain1, n, 3, head_cols, width)
    in_to = split_columns(w_in, gain2, n, 2, ff, padded)
    lane = jnp.arange(width, dtype=jnp.int32) % HEAD_DIM
    half = HEAD_DIM // 2
    frequency = jnp.exp(-math.log(rope_base) * 2.0 * (lane % half).astype(F32) / HEAD_DIM)
    angles = jnp.arange(seq, dtype=F32)[:, None] * frequency[None, :]
    sign = jnp.where(lane < half, -1.0, 1.0)
    ids = segment_ids[0]
    tables = (
        jnp.cos(angles),
        jnp.sin(angles) * sign[None, :],
        jnp.broadcast_to(ids[:, None], (seq, LANES)),
        jnp.pad(ids, (HALF, HALF), constant_values=-1)[None],
    )

    qkv_groups = split_weight(qkv_to, (tables[0], tables[1], in_to), (0, 1))
    toks = gather_rows(tokens, apart=True)

    queries, keys, values, attended, normed1, qkv_w = pl.pallas_call(
        ordered(
            functools.partial(attention_kernel, held_of(toks), held_of(qkv_groups), n, heads),
            5 + len(toks) + len(qkv_groups),
            0,
        ),
        in_specs=[SMEM_SPEC]
        + [VMEM_SPEC] * (4 + len(toks))
        + [ANY_SPEC] * len(qkv_groups),
        out_shape=(
            shape((seq, width), BF16),
            shape((seq + 2 * HALF, width), BF16),
            shape((seq + 2 * HALF, width), BF16),
            shape((seq, width), BF16),
            shape((seq, model), BF16),
            shape((model, 3 * width), BF16),
        ),
        scratch_shapes=[pltpu.SemaphoreType.DMA((pieces_of(held_of(qkv_groups)),))],
        compiler_params=params,
        cost_estimate=work(40 * seq * model * width),
        name="attention",
    )(place, *tables, *arrays_of(toks + qkv_groups))

    out_groups = gather_weight(after(w_out, toks[1].array), (attended,), (2,))
    in_groups = split_weight(after(in_to, qkv_groups[1].array), (attended,), (0, 1))
    atts = gather_rows(attended[:, :head_cols])
    block_shape = shape((n // 2, rows, model), BF16)
    hidden, normed2, up, in_w = pl.pallas_call(
        functools.partial(
            up_kernel, held_of(toks), held_of(atts), held_of(out_groups), held_of(in_groups), n
        ),
        in_specs=[SMEM_SPEC] + [ANY_SPEC] * len(toks + atts + out_groups + in_groups),
        out_specs=[ANY_SPEC] * 4,
        out_shape=[
            shape((rows, model), F32),
            shape((seq, model), BF16),
            shape((seq, 2 * padded), F32),
            shape((model, 2 * padded), BF16),
        ],
        scratch_shapes=[
            pltpu.VMEM((n, rows, model), BF16),
            pltpu.VMEM((n, seq, head_cols), BF16),
            pltpu.VMEM((model, model), BF16),
            pltpu.VMEM((model, 2 * padded), BF16),
            pltpu.VMEM((rows, model), F32),
            pltpu.VMEM((seq, model), BF16),
            pltpu.VMEM((seq, 2 * padded), F32),
            pltpu.SemaphoreType.DMA((pieces_of(held_of(out_groups)),)),
            pltpu.SemaphoreType.DMA((pieces_of(held_of(in_groups)),)),
            pltpu.SemaphoreType.DMA((n,)),
            pltpu.SemaphoreType.DMA((n,)),
            pltpu.SemaphoreType.DMA((2 * n + 2,)),
        ],
        compiler_params=params,
        cost_estimate=work(12 * seq * model * padded),
        name="up_projection",
    )(place, *arrays_of(toks + atts + out_groups + in_groups))
    cots = gather_rows(after(cotangent, atts[1].array), lambda: (up,))
    down_w = jnp.pad(w_down, ((0, -ff % 16), (0, 0)))
    act, dup, dnormed2_keep, dnormed2_send = pl.pallas_call(
        functools.partial(dup_kernel, held_of(cots), n),
        in_specs=[ANY_SPEC] * (3 + len(cots)),
        out_specs=[ANY_SPEC] * 4,
        out_shape=[shape((seq, padded), BF16), shape((seq, 2 * padded), BF16)] + [block_shape] * 2,
        scratch_shapes=[
            pltpu.VMEM((seq, 2 * padded), F32),
            pltpu.VMEM((n, rows, model), BF16),
            pltpu.VMEM((model, 2 * padded), BF16),
            pltpu.VMEM((padded, model), BF16),
            pltpu.VMEM((seq, padded), BF16),
            pltpu.VMEM((seq, 2 * padded), BF16),
            pltpu.VMEM((n, rows, model), BF16),
            pltpu.SemaphoreType.DMA,
            pltpu.SemaphoreType.DMA,
            pltpu.SemaphoreType.DMA((n,)),
            pltpu.SemaphoreType.DMA((n,)),
            pltpu.SemaphoreType.DMA((3 * n,)),
        ],
        compiler_params=params,
        cost_estimate=work(14 * seq * model * padded),
        name="dup",
    )(up, in_w, down_w, *arrays_of(cots))

    slots = replicas // 2
    chunk = part // replicas
    lanes = max(LANES, model // replicas)
    tiles = up_tiles(ff)
    orders = [near, far]
    in_counts = [tiles - tiles // 2, tiles // 2]
    in_shapes = [shape((slots, n * c, chunk, LANES), BF16) for c in in_counts for _ in range(2)]
    down_shape = shape((slots, ff, lanes), BF16)
    top = bits_of("shard") - 1

    def flow_rows(a):
        return a.reshape(a.shape[0], -1, LANES)

    mine, other = near_sums(dnormed2_keep, dnormed2_send, "near_sum_2")
    in_flows = pl.pallas_call(
        ordered(functools.partial(in_kernel, n, ff, in_counts, orders), 3, 1),
        in_specs=[SMEM_SPEC] + [VMEM_SPEC] * 2 + [ANY_SPEC],
        out_shape=in_shapes,
        scratch_shapes=[pltpu.VMEM((part, 2 * padded + LANES), F32)],
        compiler_params=params,
        cost_estimate=work(8 * seq * model * padded),
        name="in_gradient",
    )(place, normed2, dup, other)
    in_flows = [flow_rows(a) for a in in_flows]
    in_reduce = PairReduce(in_flows[:2], in_flows[2:], orders)
    dhidden, dproj = pl.pallas_call(
        ordered(norm_back_kernel, 4, 1),
        in_specs=[VMEM_SPEC] * 4 + [ANY_SPEC],
        out_shape=[shape((rows, model), F32), shape((rows, model), BF16)],
        compiler_params=pltpu.CompilerParams(vmem_limit_bytes=24 << 20),
        name="norm_back",
    )(mine, swap(other, "shard", top), hidden, cotangent, in_flows[0])
    down_keep, down_send, mlp_keep, mlp_send = pl.pallas_call(
        ordered(functools.partial(down_kernel, held_of(cots), n, ff, far), 3 + len(cots), 1),
        in_specs=[SMEM_SPEC] + [VMEM_SPEC] * (2 + len(cots)) + [ANY_SPEC],
        out_shape=[down_shape] * 2 + [block_shape] * 2,
        scratch_shapes=[pltpu.VMEM((padded, model), F32)],
        compiler_params=params,
        cost_estimate=work(8 * seq * model * padded),
        name="down_gradient",
    )(place, act, down_w, *arrays_of(cots), dproj)
    dprojs = gather_rows(dproj, lambda: (down_keep,))
    in_reduce.step(0, [dprojs[1].array])

    out_shape = shape((slots, part, lanes), BF16)
    dqkv, out_keep, out_send = pl.pallas_call(
        ordered(
            functools.partial(attention_back_kernel, held_of(dprojs), n, heads, far),
            len(dprojs) + 10,
            2,
        ),
        in_specs=[SMEM_SPEC] + [VMEM_SPEC] * (len(dprojs) + 9) + [ANY_SPEC] * 2,
        out_shape=[shape((seq, 3 * width), BF16), out_shape, out_shape],
        scratch_shapes=[
            pltpu.VMEM((seq, width), BF16),
            pltpu.VMEM((seq + 2 * HALF, width), F32),
            pltpu.VMEM((seq + 2 * HALF, width), F32),
            pltpu.VMEM((part, model), F32),
        ],
        compiler_params=params,
        cost_estimate=work(40 * seq * model * width),
        name="attention_back",
    )(
        place,
        *arrays_of(dprojs),
        w_out,
        attended,
        queries,
        keys,
        values,
        *tables,
        in_reduce.p[1],
        in_reduce.q[1],
    )

    mlp_mine, mlp_other = near_sums(mlp_keep, mlp_send, "near_sum_mlp", dqkv)
    qkv_tiles = 3 * width // LANES
    qkv_counts = [qkv_tiles - qkv_tiles // 3, qkv_tiles // 3]
    in_reduce.step(1, [dqkv])
    qkv_flows = pl.pallas_call(
        ordered(functools.partial(qkv_kernel, n, qkv_counts, orders), 3, 3),
        in_specs=[SMEM_SPEC] + [VMEM_SPEC] * 2 + [ANY_SPEC] * 3,
        out_shape=[shape((slots, n * c, chunk, LANES), BF16) for c in qkv_counts for _ in range(2)],
        scratch_shapes=[pltpu.VMEM((part, 3 * width), F32)],
        compiler_params=params,
        cost_estimate=work(12 * seq * model * width),
        name="qkv_gradient",
    )(place, normed1, dqkv, in_reduce.p[1], in_reduce.q[1], mlp_other)
    qkv_flows = [flow_rows(a) for a in qkv_flows]
    split = qkv_flows[2].shape[1]
    qkv_q = [jnp.concatenate(x, axis=1) for x in zip(qkv_flows[2:], (out_keep, out_send))]
    att_reduce = PairReduce(qkv_flows[:2], qkv_q, orders)
    att_reduce.step(0)
    att_first = att_reduce.p[1]
    att_reduce.step(1)
    output = pl.pallas_call(
        ordered(output_kernel, 3, 1),
        in_specs=[VMEM_SPEC] * 3 + [ANY_SPEC],
        out_shape=shape((rows, model), BF16),
        compiler_params=pltpu.CompilerParams(vmem_limit_bytes=16 << 20),
        name="output",
    )(mlp_mine, swap(mlp_other, "shard", top), hidden, qkv_flows[0])
    dnormed1_keep, dnormed1_send = pl.pallas_call(
        ordered(functools.partial(project_back_kernel, n), 3, 1),
        in_specs=[SMEM_SPEC] + [VMEM_SPEC] * 2 + [ANY_SPEC],
        out_shape=[block_shape] * 2,
        compiler_params=params,
        cost_estimate=work(6 * seq * model * width),
        name="project_back",
    )(place, dqkv, qkv_w, att_first)
    mine, other = near_sums(dnormed1_keep, dnormed1_send, "near_sum_1")
    input_grad = pl.pallas_call(
        input_kernel,
        out_shape=shape((rows, model), F32),
        compiler_params=pltpu.CompilerParams(vmem_limit_bytes=24 << 20),
        name="input_grad",
    )(mine, swap(other, "shard", top), tokens, dhidden)

    def turned(p, q, counts):
        sizes = [c * chunk for c in counts]
        whole = jnp.concatenate([p.reshape(n, sizes[0], LANES), q.reshape(n, sizes[1], LANES)], 1)
        whole = turn(whole, n)
        return whole[:, : sizes[0]].reshape(-1, LANES), whole[:, sizes[0] :].reshape(-1, LANES)

    def tiles_of(pair, count):
        size = n * count * chunk
        return [a[:, :size].reshape(a.shape[0], n * count, chunk, LANES) for a in pair]

    in_p, in_q = turned(*in_reduce.finish([[qkv_flows[0]]]), in_counts)
    down_send = after(down_send, dqkv)
    down_share = replica_reduce(down_keep, down_send, far, [[qkv_flows[0]], [att_first]])

    att_p, att_q = att_reduce.finish()
    att_done = att_p[:16]
    in_p, in_q = pair_gather(in_p, in_q, orders)
    down_pair = replica_spread(after(down_share, att_done), far)
    qkv_p, qkv_q = turned(att_p, att_q[:split], qkv_counts)
    att_p, att_q = pair_gather(qkv_p, jnp.concatenate([qkv_q, att_q[split:]]), orders)

    in_total, ln2_total = columns_out(
        place,
        [tiles_of(in_p, in_counts[0]), tiles_of(in_q, in_counts[1])],
        in_counts,
        orders,
        w_in,
        gain2,
        n,
        ff=ff,
    )
    down_total = rows_out(place, down_pair, 0, ff, model, far)
    out_total = rows_out(place, att_q, split, part, model, far)
    qkv_total, ln1_total = columns_out(
        place,
        [tiles_of(att_p, qkv_counts[0]), tiles_of(att_q, qkv_counts[1])],
        qkv_counts,
        orders,
        w_qkv,
        gain1,
        n,
        head_cols=head_cols,
        width=width,
    )
    return (
        output,
        input_grad,
        ln1_total,
        qkv_total,
        out_total,
        ln2_total,
        in_total,
        down_total,
    )


def solution(mesh):
    return jax.shard_map(
        shards,
        mesh=mesh,
        in_specs=(
            P(("rep", "shard"), None),
            P("rep", None),
            P("shard"),
            P("shard", None),
            P("shard", None),
            P("shard"),
            P("shard", None),
            P("shard", None),
            P(("rep", "shard"), None),
        ),
        out_specs=(
            P(("rep", "shard"), None),
            P(("rep", "shard"), None),
            P("shard"),
            P("shard", None),
            P("shard", None),
            P("shard"),
            P("shard", None),
            P("shard", None),
        ),
        check_vma=False,
    )
```

```python
import functools
import math

import jax
import jax.numpy as jnp
from jax import lax
from jax.experimental import pallas as pl
from jax.experimental.pallas import tpu as pltpu
from jax.sharding import PartitionSpec as P

HEADS = 16
HEAD_DIM = 64
HALF = 64
QB = 128
LANES = 128

norm_epsilon = 1e-05
rope_base = 10000.0
masked_score = -1e30

F32 = jnp.float32
BF16 = jnp.bfloat16
VMEM_LIMIT = 52 << 20


def bits_of(axis):
    return lax.axis_size(axis).bit_length() - 1


def bit_of(axis, bit):
    return (lax.axis_index(axis) >> bit) & 1


def swap(x, axis, bit):
    size = lax.axis_size(axis)
    return lax.ppermute(x, axis, [(i, i ^ (1 << bit)) for i in range(size)])


def add_halves(keep, got):
    def total(a, b):
        return (keep[a:b].astype(F32) + got[a:b].astype(F32)).astype(BF16)

    size = keep.shape[0]
    if size == 1:
        return total(0, 1), None
    return total(0, size // 2), total(size // 2, size)


def block_order(n):
    bits = n.bit_length() - 1
    return [sum(((k >> b) & 1) << (bits - 1 - b) for b in range(bits)) for k in range(n)]


class Group:
    def __init__(self, array, held):
        self.array, self.held = array, held


def join(groups, bit, arrays, axis):
    held, start = [], 0
    for group in groups:
        held += [(j | 1 << bit, code, start + first, rows) for j, code, first, rows in group.held]
        start += group.array.shape[axis]
    array = arrays[0] if len(arrays) == 1 else jnp.concatenate(arrays, axis=axis)
    return Group(swap(array, "shard", bit), held)


def gather_rows(x, gate=None, apart=False):
    rows = x.shape[0]
    groups = [Group(x, [(0, None, 0, rows)])]
    for bit in reversed(range(bits_of("shard"))):
        arrays = [g.array for g in groups]
        if gate is not None and len(arrays) > 1:
            arrays[-1] = after(arrays[-1], *gate())
        if apart:
            groups = groups + [join([g], bit, [a], 0) for g, a in zip(groups, arrays)]
        else:
            groups = groups + [join(groups, bit, arrays, 0)]
    return groups


def parity(bits):
    return functools.reduce(lambda a, b: a ^ b, [bit_of("rep", bit) for bit in bits])


def half_by_replica(x, dim, bits):
    shape = x.shape
    x = x.reshape(shape[:dim] + (2, shape[dim] // 2) + shape[dim + 1 :])
    return lax.dynamic_index_in_dim(x, parity(bits), dim, keepdims=False)


def fetch_far(send, dim, top, gate, bits):
    got = swap(half_by_replica(send, dim, bits), "shard", top)
    kept = after(got, *gate) if gate else got
    size = got.shape[dim]
    count = len(bits)
    parts = jnp.split(kept, count, axis=dim)
    return [Group(got, [(1 << top, (0, bits), 0, size)])] + [
        Group(swap(part, "rep", bit), [(1 << top, (1 + k, bits), 0, size // count)])
        for k, (part, bit) in enumerate(zip(parts, bits))
    ]


def gather_weight(x, gate, bits):
    top = bits_of("shard") - 1
    groups = [Group(x, [(0, None, 0, x.shape[0])])] + fetch_far(x, 0, top, gate, bits)
    for bit in reversed(range(top)):
        groups = groups + [join(groups, bit, [g.array for g in groups], 0)]
    return groups


def split_weight(x, gate, bits):
    me = lax.axis_index("shard")
    top = bits_of("shard") - 1

    def part_for(a, bit):
        start = ((me & (a.shape[0] - 1)) >> bit ^ 1) << bit
        return lax.dynamic_slice_in_dim(a, start, 1 << bit)

    groups = [Group(x, [(0, None, 0, x.shape[1])])]
    groups += fetch_far(part_for(x, top), 1, top, gate, bits)
    for bit in reversed(range(top)):
        groups = groups + [join(groups, bit, [part_for(g.array, bit) for g in groups], 1)]
    return groups


def gated(value, gates, step):
    return after(value, *gates[step]) if step < len(gates) else value


def replica_reduce(keep, send, order, gates=()):
    for step, bit in enumerate(order):
        keep, send = add_halves(keep, gated(swap(send, "rep", bit), gates, step))
    return keep[0]


def replica_spread(x, order):
    now = x[None]
    for bit in reversed(order[1:]):
        now = jnp.concatenate([now, swap(now, "rep", bit)])
    return now, swap(now, "rep", order[0])


class PairReduce:
    def __init__(self, p, q, orders):
        self.p, self.q, self.orders = p, q, orders

    def step(self, i, gates=()):
        p, q = self.p, self.q
        got_p = swap(p[1], "rep", self.orders[0][i])
        got_q = swap(q[1], "rep", self.orders[1][i])
        if gates:
            got_p, got_q = after(got_p, *gates), after(got_q, *gates)
        self.p, self.q = add_halves(p[0], got_p), add_halves(q[0], got_q)

    def finish(self, gates=()):
        rows = self.p[0].shape[1]
        keep, send = (jnp.concatenate(x, axis=1) for x in zip(self.p, self.q))
        share = replica_reduce(keep, send, self.orders[0][2:], gates)
        return share[:rows], share[rows:]


def pair_gather(p, q, orders):
    rows = p.shape[0]
    now = jnp.concatenate([p, q])[None]
    for bit in reversed(orders[0][2:]):
        now = jnp.concatenate([now, swap(now, "rep", bit)])
    pairs = []
    for x, order in zip((now[:, :rows], now[:, rows:]), orders):
        x = jnp.concatenate([x, swap(x, "rep", order[1])])
        pairs.append((x, swap(x, "rep", order[0])))
    return pairs


def turn(x, n):
    x = x[:, None]
    for bit in reversed(range(n.bit_length() - 1)):
        half = x.shape[0] // 2
        x = jnp.concatenate([x[:half], swap(x[half:], "shard", bit)], axis=1)
    return x[0]


def from_place(j, n):
    bits = n.bit_length() - 1
    return sum(((j >> b) & 1) << (bits - 1 - b) for b in range(bits))


def slot_mask(slot, order):
    count = len(order)
    return sum(((slot >> (count - 1 - i)) & 1) << bit for i, bit in enumerate(order))


def slot_of(mask, order):
    count = len(order)
    return sum(((mask >> bit) & 1) << (count - 1 - i) for i, bit in enumerate(order))


def dot(a, b, dims):
    return lax.dot_general(a, b, (dims, ((), ())), preferred_element_type=F32)


def normalise(values):
    centred = values - jnp.mean(values, axis=-1, keepdims=True)
    scale = lax.rsqrt(jnp.mean(centred * centred, axis=-1, keepdims=True) + norm_epsilon)
    return centred * scale, scale


def held_of(groups):
    return [(g.held, g.array.shape) for g in groups]


def arrays_of(groups):
    return [g.array for g in groups]


def pieces_of(held):
    return sum(len(h) for h, _ in held)


def blocks_of(held, refs):
    found = {}
    for (pieces, _), ref in zip(held, refs):
        for j, _, first, rows in pieces:
            found[j] = ref.at[first : first + rows, :]
    return [found[j] for j in range(len(found))]


def weight_copies(held, refs, target, me, sems, rep, by_owner, rows):
    copies = []
    for (pieces, shape), ref in zip(held, refs):
        source = ref.at[me & (shape[0] - 1)] if len(shape) == 3 else ref
        for j, code, first, count in pieces:
            start = (me ^ j if by_owner else j) * rows
            if code is not None:
                place, bits = code
                own = functools.reduce(lambda a, b: a ^ b, [(rep >> bit) & 1 for bit in bits])
                start = start + (own if place == 0 else 1 - own) * (rows // 2)
                start = start + max(place - 1, 0) * (rows // 2 // len(bits))
            place = target.at[pl.ds(pl.multiple_of(start, count), count), :]
            sem = sems.at[len(copies)]
            copies.append(pltpu.make_async_copy(source.at[first : first + count, :], place, sem))
    return copies


def partner(x):
    width = x.shape[-1]
    lane = lax.broadcasted_iota(jnp.int32, x.shape, 1)
    front = (lane % HEAD_DIM) < HEAD_DIM // 2
    return jnp.where(
        front,
        pltpu.roll(x, width - HEAD_DIM // 2, 1),
        pltpu.roll(x, HEAD_DIM // 2, 1),
    )


def head_masks(heads, width):
    lane = lax.broadcasted_iota(jnp.int32, (QB, width), 1) // HEAD_DIM
    return [lane == h for h in range(heads)]


def stack_heads(x, masks):
    x = x.astype(F32)
    return jnp.concatenate([jnp.where(m, x, 0.0) for m in masks], axis=0).astype(BF16)


def merge_heads(x, masks):
    total = None
    for h, m in enumerate(masks):
        part = jnp.where(m, x[h * QB : (h + 1) * QB], 0.0)
        total = part if total is None else total + part
    return total


def window_bias(ids_q, ids_k):
    row = lax.broadcasted_iota(jnp.int32, (QB, QB + 2 * HALF), 0)
    col = lax.broadcasted_iota(jnp.int32, (QB, QB + 2 * HALF), 1)
    ids_q = jnp.concatenate([ids_q] * ((QB + 2 * HALF) // LANES), axis=1)
    allowed = (col >= row) & (col <= row + 2 * HALF) & (ids_q == ids_k)
    return jnp.where(allowed, 0.0, masked_score)


def block_probs(stacked_q, keys, bias, heads):
    scores = dot(stacked_q, keys, ((1,), (1,)))
    rows, cols = scores.shape
    scores = (scores.reshape(heads, QB, cols) + bias[None]).reshape(rows, cols)
    weights = jnp.exp(scores - jnp.max(scores, axis=-1, keepdims=True))
    return weights * (1.0 / jnp.sum(weights, axis=-1, keepdims=True))


def column_chunk(ref, chunk, cols):
    if cols >= LANES:
        return ref[:, pl.ds(pl.multiple_of(chunk * cols, cols), cols)]
    per = LANES // cols
    tile = ref[:, pl.ds(pl.multiple_of(chunk // per * LANES, LANES), LANES)]
    result = tile
    for k in range(1, per):
        result = jnp.where(chunk % per == k, pltpu.roll(tile, LANES - k * cols, 1), result)
    return result


def row_chunk(ref, chunk, rows, start):
    if rows % 8 == 0:
        return ref[pl.ds(pl.multiple_of(chunk * rows, rows), rows), start : start + LANES]
    per = 8 // rows
    tile = ref[pl.ds(pl.multiple_of(chunk // per * 8, 8), 8), start : start + LANES]
    result = tile[:rows]
    for k in range(1, per):
        result = jnp.where(chunk % per == k, tile[k * rows : (k + 1) * rows], result)
    return result


def take_columns(ref, offset, valid, size):
    begin = offset // LANES * LANES
    end = -(-(offset + valid) // LANES) * LANES
    x = ref[:, begin:end].astype(F32)
    if offset != begin:
        x = pltpu.roll(x, end - offset, 1)
    x = x[:, :size]
    if valid != size:
        lane = lax.broadcasted_iota(jnp.int32, x.shape, 1)
        x = jnp.where(lane < valid, x, 0.0)
    return x


def split_kernel(n, blocks, valid, size, gain_ref, w_ref, out_ref):
    gain = gain_ref[...]
    for owner in range(n):
        for b in range(blocks):
            x = take_columns(w_ref, (b * n + owner) * valid, valid, size)
            out_ref[owner, :, b * size : (b + 1) * size] = (x * gain).astype(BF16)


def split_columns(w, gain, n, blocks, valid, size):
    rows, cols = w.shape
    step = min(rows, 64)
    return pl.pallas_call(
        functools.partial(split_kernel, n, blocks, valid, size),
        grid=(rows // step,),
        in_specs=[
            pl.BlockSpec((step, 1), lambda i: (i, 0)),
            pl.BlockSpec((step, cols), lambda i: (i, 0)),
        ],
        out_specs=pl.BlockSpec((n, step, blocks * size), lambda i: (0, i, 0)),
        out_shape=jax.ShapeDtypeStruct((n, rows, blocks * size), BF16),
        compiler_params=pltpu.CompilerParams(vmem_limit_bytes=24 << 20),
        name="split_columns",
    )(gain, w)


def attention_kernel(
    tok_held, held, n, heads, place_ref, cos_ref, sin_ref, idq_ref, idk_ref, *refs
):
    tok_refs, refs = blocks_of(tok_held, refs), refs[len(tok_held) :]
    piece_refs, refs = refs[: len(held)], refs[len(held) :]
    q_ref, k_ref, v_ref, out_ref, normed_ref, w_ref, sems = refs
    seq, width = q_ref.shape
    rows = seq // n
    me, rep = place_ref[0], place_ref[1]
    copies = weight_copies(
        held, piece_refs, w_ref, me, sems, rep, True, w_ref.shape[0] // n
    )
    for c in copies:
        c.start()
    edge = jnp.zeros((HALF, width), BF16)
    for ref in (k_ref, v_ref):
        ref[0:HALF, :] = edge
        ref[seq + HALF : seq + 2 * HALF, :] = edge
    for c in copies:
        c.wait()
    for j in range(n):
        start = (me ^ j) * rows
        at = pl.ds(pl.multiple_of(start, rows), rows)
        shifted = pl.ds(pl.multiple_of(start + HALF, HALF), rows)
        hat, _ = normalise(tok_refs[j][...].astype(F32))
        normed = hat.astype(BF16)
        normed_ref[at, :] = normed
        qkv = jnp.dot(normed, w_ref[...], preferred_element_type=F32)
        cos, sin = cos_ref[at, :], sin_ref[at, :]
        q, k = qkv[:, 0:width], qkv[:, width : 2 * width]
        rotated = (q * cos + partner(q) * sin).astype(BF16)
        q_ref[at, :] = (rotated.astype(F32) * (1.0 / math.sqrt(HEAD_DIM))).astype(BF16)
        k_ref[shifted, :] = (k * cos + partner(k) * sin).astype(BF16)
        v_ref[shifted, :] = qkv[:, 2 * width : 3 * width].astype(BF16)
    masks = head_masks(heads, width)

    def attend(i, carry):
        at = pl.ds(pl.multiple_of(i * QB, QB), QB)
        window = pl.ds(pl.multiple_of(i * QB, QB), QB + 2 * HALF)
        bias = window_bias(idq_ref[at, :], idk_ref[0:1, window])
        probs = block_probs(stack_heads(q_ref[at, :], masks), k_ref[window, :], bias, heads)
        mixed = jnp.dot(probs.astype(BF16), v_ref[window, :], preferred_element_type=F32)
        out_ref[at, :] = merge_heads(mixed, masks).astype(BF16)
        return carry

    lax.fori_loop(0, seq // QB, attend, 0, unroll=2)


def up_kernel(tok_held, att_held, out_held, in_held, n, place_ref, *refs):
    tok_refs, refs = blocks_of(tok_held, refs), refs[len(tok_held) :]
    att_refs, refs = blocks_of(att_held, refs), refs[len(att_held) :]
    out_refs, refs = refs[: len(out_held)], refs[len(out_held) :]
    in_refs, refs = refs[: len(in_held)], refs[len(in_held) :]
    hidden_out, normed_out, up_out, in_out, *refs = refs
    tok, att, w_out, w_in, hidden_own, normed, up, *refs = refs
    out_sems, in_sems, att_sems, tok_sems, sems = refs
    me, rep = place_ref[0], place_ref[1]
    rows, model = tok_refs[0].shape
    copy = pltpu.make_async_copy
    att_copies = [copy(att_refs[j], att.at[j], att_sems.at[j]) for j in range(n)]
    tok_copies = [copy(tok_refs[j], tok.at[j], tok_sems.at[j]) for j in range(n)]
    part = model // n
    out_copies = weight_copies(out_held, out_refs, w_out, me, out_sems, rep, False, part)
    in_copies = weight_copies(in_held, in_refs, w_in, me, in_sems, rep, True, part)
    for c in att_copies + tok_copies[:1] + out_copies + in_copies + tok_copies[1:]:
        c.start()
    for c in att_copies + out_copies:
        c.wait()
    sent = []
    for j in range(n):
        at = pl.ds(pl.multiple_of((me ^ j) * rows, rows), rows)
        here = slice(j * rows, (j + 1) * rows)
        tok_copies[j].wait()
        hidden = tok[j].astype(F32)
        for i in range(n):
            hidden = hidden + jnp.dot(
                att[i, at, :], w_out[i * part : (i + 1) * part, :], preferred_element_type=F32
            )
        if j == 0:
            hidden_own[...] = hidden
            sent.append(copy(hidden_own, hidden_out, sems.at[2 * n]))
            sent[-1].start()
        hat, _ = normalise(hidden)
        low = hat.astype(BF16)
        normed[here, :] = low
        if j == 0:
            for c in in_copies:
                c.wait()
            sent.append(copy(w_in, in_out, sems.at[2 * n + 1]))
            sent[-1].start()
        up[here, :] = jnp.dot(low, w_in[...], preferred_element_type=F32)
        sent += [
            copy(normed.at[here, :], normed_out.at[here, :], sems.at[2 * j]),
            copy(up.at[here, :], up_out.at[here, :], sems.at[2 * j + 1]),
        ]
        for c in sent[-2:]:
            c.start()
    for c in sent:
        c.wait()


def dup_kernel(cot_held, n, up_ref, w_in_ref, down_ref, *refs):
    cot_refs, refs = blocks_of(cot_held, refs), refs[len(cot_held) :]
    act_out, dup_out, keep_out, send_out, *refs = refs
    up, cot, w_in, w_down, act, dup, dnormed, in_sem, down_sem, up_sems, cot_sems, sems = refs
    rows, model = cot_refs[0].shape
    padded = w_down.shape[0]
    given = down_ref.shape[0]
    if given != padded:
        w_down[given:padded, :] = jnp.zeros((padded - given, model), BF16)
    copy = pltpu.make_async_copy
    down_copy = copy(down_ref, w_down.at[0:given, :], down_sem)
    in_copy = copy(w_in_ref, w_in, in_sem)
    cot_copies = [copy(cot_refs[j], cot.at[j], cot_sems.at[j]) for j in range(n)]
    up_copies = []
    for j in range(n):
        here = slice(j * rows, (j + 1) * rows)
        up_copies.append(copy(up_ref.at[here, :], up.at[here, :], up_sems.at[j]))
    for c in [up_copies[0], cot_copies[0], down_copy, in_copy]:
        c.start()
    for c in up_copies[1:] + cot_copies[1:]:
        c.start()
    sent = []
    order = block_order(n)
    for j in range(n):
        here = slice(j * rows, (j + 1) * rows)
        place = order.index(j)
        target = (keep_out if place < n // 2 else send_out).at[place % (n // 2)]
        up_copies[j].wait()
        gate, lin = up[here, :padded], up[here, padded:]
        phi = 0.5 + 0.5 * lax.erf(gate * (1.0 / math.sqrt(2.0)))
        gelu = gate * phi
        slope = phi + gate * jnp.exp(gate * gate * -0.5) * (1.0 / math.sqrt(2.0 * math.pi))
        act[here, :] = (gelu * lin).astype(BF16)
        cot_copies[j].wait()
        if j == 0:
            down_copy.wait()
        dact = dot(cot[j], w_down[...], ((1,), (1,)))
        dup[here, :padded] = (dact * lin * slope).astype(BF16)
        dup[here, padded:] = (dact * gelu).astype(BF16)
        if j == 0:
            in_copy.wait()
        dnormed[j] = dot(dup[here, :], w_in[...], ((1,), (1,))).astype(BF16)
        sent += [
            copy(dnormed.at[j], target, sems.at[3 * j]),
            copy(act.at[here, :], act_out.at[here, :], sems.at[3 * j + 1]),
            copy(dup.at[here, :], dup_out.at[here, :], sems.at[3 * j + 2]),
        ]
        for c in sent[-3:]:
            c.start()
    for c in sent:
        c.wait()


def store_slots(keep_ref, send_ref, rep, order, write):
    half = keep_ref.shape[0]
    for slot in range(2 * half):
        target = keep_ref if slot < half else send_ref
        write(target, slot % half, rep ^ slot_mask(slot, order))


def up_tiles(ff):
    return 2 * (ff // LANES) + 1


def put_block(keep, send, j, value):
    half = keep.shape[0]
    place = block_order(2 * half).index(j)
    target = keep if place < half else send
    target[place % half] = value.astype(BF16)


def down_kernel(cot_held, n, ff, order, place_ref, act, w_down, *refs):
    cot_refs, refs = blocks_of(cot_held, refs), refs[len(cot_held) :]
    keep, send, mlp_keep, mlp_send, down_sum = refs
    rows, model = cot_refs[0].shape
    cols = model // (2 * keep.shape[0])
    total = None
    for j in range(n):
        term = dot(act[j * rows : (j + 1) * rows, :], cot_refs[j][...], ((0,), (0,)))
        total = term if total is None else total + term
    down_sum[...] = total

    def write(target, slot, c):
        target[slot] = column_chunk(down_sum, c, cols)[:ff].astype(BF16)

    store_slots(keep, send, place_ref[1], order, write)
    given = w_down.shape[0]
    for j in range(n):
        low = act[j * rows : (j + 1) * rows, 0:given]
        put_block(mlp_keep, mlp_send, j, jnp.dot(low, w_down[...], preferred_element_type=F32))


def write_flows(total, starts, counts, orders, flows, index, rep):
    begin = 0
    for f, (count, order) in enumerate(zip(counts, orders)):
        keep, send = flows[2 * f], flows[2 * f + 1]
        chunk = keep.shape[2]

        def write(target, slot, c):
            for t in range(count):
                value = row_chunk(total, c, chunk, starts[begin + t])
                target[slot, index * count + t] = value.astype(BF16)

        store_slots(keep, send, rep, order, write)
        begin += count


def in_kernel(n, ff, counts, orders, place_ref, normed, dup, *refs):
    flows, in_sum = refs[:-1], refs[-1]
    me, rep = place_ref[0], place_ref[1]
    part = normed.shape[1] // n
    padded = dup.shape[1] // 2
    whole, rest = ff // LANES, ff % LANES
    starts = [t * LANES for t in range(whole)] + [padded + t * LANES for t in range(whole)]
    starts.append(2 * padded)
    for owner in range(n):
        block = dot(normed[:, owner * part : (owner + 1) * part], dup[...], ((0,), (0,)))
        in_sum[:, : 2 * padded] = block
        first = block[:, whole * LANES : (whole + 1) * LANES]
        second = block[:, padded + whole * LANES : padded + (whole + 1) * LANES]
        lane = lax.broadcasted_iota(jnp.int32, first.shape, 1)
        in_sum[:, 2 * padded :] = jnp.where(lane < rest, first, pltpu.roll(second, rest, 1))
        write_flows(in_sum, starts, counts, orders, flows, me ^ owner, rep)


def add_kernel(keep_ref, got_ref, mine_ref, other_ref):
    mine_ref[...] = keep_ref[0].astype(F32) + got_ref[0].astype(F32)
    other_ref[...] = (keep_ref[1].astype(F32) + got_ref[1].astype(F32)).astype(BF16)


def near_sums(keep, send, name, gate=None):
    bits = bits_of("shard")
    for bit in range(bits - 2):
        keep, send = add_halves(keep, swap(send, "shard", bit))
    _, rows, model = keep.shape
    got = swap(send, "shard", bits - 2)
    if gate is not None:
        got = after(got, gate)
    return pl.pallas_call(
        add_kernel,
        out_shape=[
            jax.ShapeDtypeStruct((rows, model), F32),
            jax.ShapeDtypeStruct((rows, model), BF16),
        ],
        compiler_params=pltpu.CompilerParams(vmem_limit_bytes=16 << 20),
        name=name,
    )(keep, got)


def output_kernel(mine, got, hidden, out_ref):
    out_ref[...] = (hidden[...] + mine[...] + got[...].astype(F32)).astype(BF16)


def input_kernel(mine, got, tokens, dhidden, out_ref):
    hat, scale = normalise(tokens[...].astype(F32))
    e = mine[...] + got[...].astype(F32)
    out_ref[...] = dhidden[...] + norm_backward(e, hat, scale)


def norm_back_kernel(mine, got, hidden, cotangent, dhidden, dproj):
    hat, scale = normalise(hidden[...])
    e = mine[...] + got[...].astype(F32)
    value = cotangent[...].astype(F32) + norm_backward(e, hat, scale)
    dhidden[...] = value
    dproj[...] = value.astype(BF16)


def attention_back_kernel(held, n, heads, order, place_ref, *refs):
    dproj_refs, refs = blocks_of(held, refs), refs[len(held) :]
    w_out, att, q_ref, k_ref, v_ref, cos_ref, sin_ref, idq_ref, idk_ref, *refs = refs
    dqkv, out_keep, out_send, da, dk, dv, out_sum = refs
    me, rep = place_ref[0], place_ref[1]
    seq, width = q_ref.shape
    rows, model = dproj_refs[0].shape
    part = model // n
    dk[...] = jnp.zeros_like(dk)
    dv[...] = jnp.zeros_like(dv)
    head_cols = heads * HEAD_DIM
    total = None
    for j in range(n):
        at = pl.ds(pl.multiple_of((me ^ j) * rows, rows), rows)
        dproj = dproj_refs[j][...]
        da[at, 0:head_cols] = dot(dproj, w_out[...], ((1,), (1,))).astype(BF16)
        term = dot(att[at, :], dproj, ((0,), (0,)))
        total = term if total is None else total + term
    if head_cols != width:
        da[:, head_cols:] = jnp.zeros((seq, width - head_cols), BF16)
    out_sum[...] = total[0:part]
    cols = model // (2 * out_keep.shape[0])

    def write_out(target, slot, c):
        target[slot] = column_chunk(out_sum, c, cols).astype(BF16)

    store_slots(out_keep, out_send, rep, order, write_out)
    masks = head_masks(heads, width)

    def back(i, carry):
        at = pl.ds(pl.multiple_of(i * QB, QB), QB)
        window = pl.ds(pl.multiple_of(i * QB, QB), QB + 2 * HALF)
        bias = window_bias(idq_ref[at, :], idk_ref[0:1, window])
        queries = stack_heads(q_ref[at, :], masks)
        keys = k_ref[window, :]
        probs = block_probs(queries, keys, bias, heads)
        grads = stack_heads(da[at, :], masks)
        dprobs = dot(grads, v_ref[window, :], ((1,), (1,)))
        delta = jnp.sum(probs * dprobs, axis=-1, keepdims=True)
        dscores = (probs * (dprobs - delta)).astype(BF16)
        dq = merge_heads(jnp.dot(dscores, keys, preferred_element_type=F32), masks)
        dq = dq * (1.0 / math.sqrt(HEAD_DIM))
        cos, sin = cos_ref[at, :], sin_ref[at, :]
        dqkv[at, 0:width] = (dq * cos - partner(dq) * sin).astype(BF16)
        dk[window, :] += dot(dscores, queries, ((0,), (0,)))
        dv[window, :] += dot(probs.astype(BF16), grads, ((0,), (0,)))
        return carry

    lax.fori_loop(0, seq // QB, back, 0, unroll=2)

    def finish(i, carry):
        at = pl.ds(pl.multiple_of(i * QB, QB), QB)
        shifted = pl.ds(pl.multiple_of(i * QB + HALF, HALF), QB)
        cos, sin = cos_ref[at, :], sin_ref[at, :]
        g = dk[shifted, :]
        dqkv[at, width : 2 * width] = (g * cos - partner(g) * sin).astype(BF16)
        dqkv[at, 2 * width : 3 * width] = dv[shifted, :].astype(BF16)
        return carry

    lax.fori_loop(0, seq // QB, finish, 0)


def qkv_kernel(n, counts, orders, place_ref, normed, dqkv, *refs):
    flows, qkv_sum = refs[:-1], refs[-1]
    me, rep = place_ref[0], place_ref[1]
    part = normed.shape[1] // n
    starts = [t * LANES for t in range(sum(counts))]
    for owner in range(n):
        qkv_sum[...] = dot(normed[:, owner * part : (owner + 1) * part], dqkv[...], ((0,), (0,)))
        write_flows(qkv_sum, starts, counts, orders, flows, me ^ owner, rep)


def project_back_kernel(n, place_ref, dqkv, w_qkv, keep, send):
    rows = keep.shape[1]
    for j in range(n):
        at = pl.ds(pl.multiple_of((place_ref[0] ^ j) * rows, rows), rows)
        put_block(keep, send, j, dot(dqkv[at, :], w_qkv[...], ((1,), (1,))))


def place_piece(canvas, piece, offset, valid):
    shift = offset % LANES
    height, size = piece.shape
    count = -(-(shift + valid) // LANES)
    if count * LANES > size:
        piece = jnp.concatenate([piece, jnp.zeros((height, count * LANES - size), F32)], axis=1)
    if shift:
        piece = pltpu.roll(piece, shift, 1)
    lane = lax.broadcasted_iota(jnp.int32, (height, LANES), 1)
    for t in range(count):
        tile = piece[:, t * LANES : (t + 1) * LANES]
        low, high = shift - t * LANES, shift + valid - t * LANES
        if low > 0 or high < LANES:
            tile = jnp.where((lane >= low) & (lane < high), tile, 0.0)
        index = offset // LANES + t
        canvas[index] = tile if index not in canvas else canvas[index] + tile


def columns_out_kernel(n, ff, head_cols, width, counts, orders, place_ref, gain_ref, w_ref, *refs):
    me, rep = place_ref[0], place_ref[1]
    *parts, out_ref, ln_ref = refs
    half = parts[0].shape[0]
    slots = [slot_of(rep ^ pl.program_id(0), order) for order in orders]

    def read(owner, t):
        f = 0
        while t >= counts[f]:
            t -= counts[f]
            f += 1
        slot, index = slots[f], from_place(me ^ owner, n) * counts[f] + t
        at = slot & (half - 1)
        now, got = parts[2 * f][at, index], parts[2 * f + 1][at, index]
        return jnp.where(slot < half, now, got).astype(F32)

    canvas = {}
    for owner in range(n):
        tile = functools.partial(read, owner)

        if ff:
            whole, rest = ff // LANES, ff % LANES
            last = tile(2 * whole)
            gate = jnp.concatenate([tile(t) for t in range(whole)] + [last], axis=1)
            last = pltpu.roll(last, LANES - rest, 1)
            lin = jnp.concatenate([tile(whole + t) for t in range(whole)] + [last], axis=1)
            place_piece(canvas, gate, owner * ff, ff)
            place_piece(canvas, lin, (n + owner) * ff, ff)
        else:
            per = width // LANES
            for b in range(3):
                piece = jnp.concatenate([tile(b * per + t) for t in range(per)], axis=1)
                place_piece(canvas, piece, (b * n + owner) * head_cols, head_cols)
    gain = gain_ref[...]
    total = None
    for index, value in canvas.items():
        at = slice(index * LANES, (index + 1) * LANES)
        term = value * w_ref[:, at].astype(F32)
        total = term if total is None else total + term
        out_ref[:, at] = value * gain
    ln_ref[...] = jnp.sum(total, axis=1, keepdims=True)


def columns_out(place, pairs, counts, orders, weight, gain, n, ff=0, head_cols=0, width=0):
    parts = [a for pair in pairs for a in pair]
    chunk = parts[0].shape[2]
    part, cols = weight.shape
    count = part // chunk
    part_specs = [pl.BlockSpec(a.shape, lambda i: (0, 0, 0, 0)) for a in parts]
    total, ln = pl.pallas_call(
        functools.partial(columns_out_kernel, n, ff, head_cols, width, counts, orders),
        grid=(count,),
        in_specs=[
            pl.BlockSpec(memory_space=pltpu.SMEM),
            pl.BlockSpec((None, chunk, 1), lambda i: (i, 0, 0)),
            pl.BlockSpec((None, chunk, cols), lambda i: (i, 0, 0)),
            *part_specs,
        ],
        out_specs=[
            pl.BlockSpec((None, chunk, cols), lambda i: (i, 0, 0)),
            pl.BlockSpec((None, chunk, 1), lambda i: (i, 0, 0)),
        ],
        out_shape=[
            jax.ShapeDtypeStruct((count, chunk, cols), F32),
            jax.ShapeDtypeStruct((count, chunk, 1), F32),
        ],
        compiler_params=pltpu.CompilerParams(vmem_limit_bytes=32 << 20),
        name="columns_out",
    )(place, gain.reshape(count, chunk, 1), weight.reshape(count, chunk, cols), *parts)
    return total.reshape(part, cols), ln.reshape(part)


def rows_out_kernel(order, cols, skip, place_ref, *refs):
    *parts, out_ref = refs
    rep = place_ref[1]

    def chunk(c):
        half = parts[0].shape[0]
        slot = slot_of(rep ^ c, order)
        at = slot & (half - 1)
        rows = slice(skip, skip + out_ref.shape[0])
        return jnp.where(slot < half, parts[0][at, rows], parts[1][at, rows]).astype(F32)

    count = out_ref.shape[1] // cols
    if cols >= LANES:
        for c in range(count):
            out_ref[:, c * cols : (c + 1) * cols] = chunk(c)
    else:
        per = LANES // cols
        lane = lax.broadcasted_iota(jnp.int32, out_ref.shape[:1] + (LANES,), 1) // cols
        for t in range(count // per):
            value = chunk(per * t)
            for k in range(1, per):
                value = jnp.where(lane == k, pltpu.roll(chunk(per * t + k), k * cols, 1), value)
            out_ref[:, t * LANES : (t + 1) * LANES] = value


def rows_out(place, pair, skip, rows, model, order):
    return pl.pallas_call(
        functools.partial(rows_out_kernel, order, model // (2 * pair[0].shape[0]), skip),
        in_specs=[pl.BlockSpec(memory_space=pltpu.SMEM)]
        + [pl.BlockSpec(memory_space=pltpu.VMEM)] * 2,
        out_shape=jax.ShapeDtypeStruct((rows, model), F32),
        compiler_params=pltpu.CompilerParams(vmem_limit_bytes=32 << 20),
        name="rows_out",
    )(place, *pair)


def ordered(kernel, first, count):
    def body(*refs):
        kernel(*refs[:first], *refs[first + count :])

    return body


def work(flops):
    return pl.CostEstimate(flops=int(flops), bytes_accessed=1 << 22, transcendentals=0)


SMEM_SPEC = pl.BlockSpec(memory_space=pltpu.SMEM)
VMEM_SPEC = pl.BlockSpec(memory_space=pltpu.VMEM)
ANY_SPEC = pl.BlockSpec(memory_space=pl.ANY)


def norm_backward(grad_hat, normed, scale):
    return (
        grad_hat
        - jnp.mean(grad_hat, axis=-1, keepdims=True)
        - normed * jnp.mean(grad_hat * normed, axis=-1, keepdims=True)
    ) * scale


def after(value, *earlier):
    return lax.optimization_barrier((value,) + earlier)[0]


def shards(tokens, segment_ids, ln1_gain, w_qkv, w_out, ln2_gain, w_in, w_down, cotangent):
    n = lax.axis_size("shard")
    replicas = lax.axis_size("rep")
    me = lax.axis_index("shard")
    place = jnp.stack([me, lax.axis_index("rep")]).astype(jnp.int32)
    rows, model = tokens.shape
    seq = rows * n
    part = model // n
    ff = w_down.shape[0]
    heads = HEADS // n
    head_cols = heads * HEAD_DIM
    width = max(LANES, head_cols)
    padded = -(-ff // LANES) * LANES
    near = list(range(bits_of("rep")))
    far = near[1:2] + near[:1] + near[2:]
    shape = jax.ShapeDtypeStruct
    params = pltpu.CompilerParams(vmem_limit_bytes=VMEM_LIMIT)

    gain1 = ln1_gain.astype(F32)[:, None]
    gain2 = ln2_gain.astype(F32)[:, None]
    qkv_to = split_columns(w_qkv, gain1, n, 3, head_cols, width)
    in_to = split_columns(w_in, gain2, n, 2, ff, padded)
    lane = jnp.arange(width, dtype=jnp.int32) % HEAD_DIM
    half = HEAD_DIM // 2
    frequency = jnp.exp(-math.log(rope_base) * 2.0 * (lane % half).astype(F32) / HEAD_DIM)
    angles = jnp.arange(seq, dtype=F32)[:, None] * frequency[None, :]
    sign = jnp.where(lane < half, -1.0, 1.0)
    ids = segment_ids[0]
    tables = (
        jnp.cos(angles),
        jnp.sin(angles) * sign[None, :],
        jnp.broadcast_to(ids[:, None], (seq, LANES)),
        jnp.pad(ids, (HALF, HALF), constant_values=-1)[None],
    )

    qkv_groups = split_weight(qkv_to, (tables[0], tables[1], in_to), (0, 1))
    toks = gather_rows(tokens, apart=True)

    queries, keys, values, attended, normed1, qkv_w = pl.pallas_call(
        ordered(
            functools.partial(attention_kernel, held_of(toks), held_of(qkv_groups), n, heads),
            5 + len(toks) + len(qkv_groups),
            0,
        ),
        in_specs=[SMEM_SPEC]
        + [VMEM_SPEC] * (4 + len(toks))
        + [ANY_SPEC] * len(qkv_groups),
        out_shape=(
            shape((seq, width), BF16),
            shape((seq + 2 * HALF, width), BF16),
            shape((seq + 2 * HALF, width), BF16),
            shape((seq, width), BF16),
            shape((seq, model), BF16),
            shape((model, 3 * width), BF16),
        ),
        scratch_shapes=[pltpu.SemaphoreType.DMA((pieces_of(held_of(qkv_groups)),))],
        compiler_params=params,
        cost_estimate=work(40 * seq * model * width),
        name="attention",
    )(place, *tables, *arrays_of(toks + qkv_groups))

    out_groups = gather_weight(after(w_out, toks[1].array), (attended,), (2,))
    in_groups = split_weight(after(in_to, qkv_groups[1].array), (attended,), (0, 1))
    atts = gather_rows(attended[:, :head_cols])
    block_shape = shape((n // 2, rows, model), BF16)
    hidden, normed2, up, in_w = pl.pallas_call(
        functools.partial(
            up_kernel, held_of(toks), held_of(atts), held_of(out_groups), held_of(in_groups), n
        ),
        in_specs=[SMEM_SPEC] + [ANY_SPEC] * len(toks + atts + out_groups + in_groups),
        out_specs=[ANY_SPEC] * 4,
        out_shape=[
            shape((rows, model), F32),
            shape((seq, model), BF16),
            shape((seq, 2 * padded), F32),
            shape((model, 2 * padded), BF16),
        ],
        scratch_shapes=[
            pltpu.VMEM((n, rows, model), BF16),
            pltpu.VMEM((n, seq, head_cols), BF16),
            pltpu.VMEM((model, model), BF16),
            pltpu.VMEM((model, 2 * padded), BF16),
            pltpu.VMEM((rows, model), F32),
            pltpu.VMEM((seq, model), BF16),
            pltpu.VMEM((seq, 2 * padded), F32),
            pltpu.SemaphoreType.DMA((pieces_of(held_of(out_groups)),)),
            pltpu.SemaphoreType.DMA((pieces_of(held_of(in_groups)),)),
            pltpu.SemaphoreType.DMA((n,)),
            pltpu.SemaphoreType.DMA((n,)),
            pltpu.SemaphoreType.DMA((2 * n + 2,)),
        ],
        compiler_params=params,
        cost_estimate=work(12 * seq * model * padded),
        name="up_projection",
    )(place, *arrays_of(toks + atts + out_groups + in_groups))
    cots = gather_rows(after(cotangent, atts[1].array), lambda: (up,), apart=True)
    down_w = jnp.pad(w_down, ((0, -ff % 16), (0, 0)))
    act, dup, dnormed2_keep, dnormed2_send = pl.pallas_call(
        functools.partial(dup_kernel, held_of(cots), n),
        in_specs=[ANY_SPEC] * (3 + len(cots)),
        out_specs=[ANY_SPEC] * 4,
        out_shape=[shape((seq, padded), BF16), shape((seq, 2 * padded), BF16)] + [block_shape] * 2,
        scratch_shapes=[
            pltpu.VMEM((seq, 2 * padded), F32),
            pltpu.VMEM((n, rows, model), BF16),
            pltpu.VMEM((model, 2 * padded), BF16),
            pltpu.VMEM((padded, model), BF16),
            pltpu.VMEM((seq, padded), BF16),
            pltpu.VMEM((seq, 2 * padded), BF16),
            pltpu.VMEM((n, rows, model), BF16),
            pltpu.SemaphoreType.DMA,
            pltpu.SemaphoreType.DMA,
            pltpu.SemaphoreType.DMA((n,)),
            pltpu.SemaphoreType.DMA((n,)),
            pltpu.SemaphoreType.DMA((3 * n,)),
        ],
        compiler_params=params,
        cost_estimate=work(14 * seq * model * padded),
        name="dup",
    )(up, in_w, down_w, *arrays_of(cots))

    slots = replicas // 2
    chunk = part // replicas
    lanes = max(LANES, model // replicas)
    tiles = up_tiles(ff)
    orders = [near, far]
    in_counts = [tiles // 2, tiles - tiles // 2]
    in_shapes = [shape((slots, n * c, chunk, LANES), BF16) for c in in_counts for _ in range(2)]
    down_shape = shape((slots, ff, lanes), BF16)
    top = bits_of("shard") - 1

    def flow_rows(a):
        return a.reshape(a.shape[0], -1, LANES)

    mine, other = near_sums(dnormed2_keep, dnormed2_send, "near_sum_2")
    in_flows = pl.pallas_call(
        ordered(functools.partial(in_kernel, n, ff, in_counts, orders), 3, 1),
        in_specs=[SMEM_SPEC] + [VMEM_SPEC] * 2 + [ANY_SPEC],
        out_shape=in_shapes,
        scratch_shapes=[pltpu.VMEM((part, 2 * padded + LANES), F32)],
        compiler_params=params,
        cost_estimate=work(8 * seq * model * padded),
        name="in_gradient",
    )(place, normed2, dup, other)
    in_flows = [flow_rows(a) for a in in_flows]
    in_reduce = PairReduce(in_flows[:2], in_flows[2:], orders)
    dhidden, dproj = pl.pallas_call(
        ordered(norm_back_kernel, 4, 1),
        in_specs=[VMEM_SPEC] * 4 + [ANY_SPEC],
        out_shape=[shape((rows, model), F32), shape((rows, model), BF16)],
        compiler_params=pltpu.CompilerParams(vmem_limit_bytes=24 << 20),
        name="norm_back",
    )(mine, swap(other, "shard", top), hidden, cotangent, in_flows[0])
    down_keep, down_send, mlp_keep, mlp_send = pl.pallas_call(
        ordered(functools.partial(down_kernel, held_of(cots), n, ff, near), 3 + len(cots), 1),
        in_specs=[SMEM_SPEC] + [VMEM_SPEC] * (2 + len(cots)) + [ANY_SPEC],
        out_shape=[down_shape] * 2 + [block_shape] * 2,
        scratch_shapes=[pltpu.VMEM((padded, model), F32)],
        compiler_params=params,
        cost_estimate=work(8 * seq * model * padded),
        name="down_gradient",
    )(place, act, down_w, *arrays_of(cots), dproj)
    dprojs = gather_rows(dproj, lambda: (down_keep,))
    in_reduce.step(0, [dprojs[1].array])

    out_shape = shape((slots, part, lanes), BF16)
    dqkv, out_keep, out_send = pl.pallas_call(
        ordered(
            functools.partial(attention_back_kernel, held_of(dprojs), n, heads, far),
            len(dprojs) + 10,
            2,
        ),
        in_specs=[SMEM_SPEC] + [VMEM_SPEC] * (len(dprojs) + 9) + [ANY_SPEC] * 2,
        out_shape=[shape((seq, 3 * width), BF16), out_shape, out_shape],
        scratch_shapes=[
            pltpu.VMEM((seq, width), BF16),
            pltpu.VMEM((seq + 2 * HALF, width), F32),
            pltpu.VMEM((seq + 2 * HALF, width), F32),
            pltpu.VMEM((part, model), F32),
        ],
        compiler_params=params,
        cost_estimate=work(40 * seq * model * width),
        name="attention_back",
    )(
        place,
        *arrays_of(dprojs),
        w_out,
        attended,
        queries,
        keys,
        values,
        *tables,
        in_reduce.p[1],
        in_reduce.q[1],
    )

    mlp_mine, mlp_other = near_sums(mlp_keep, mlp_send, "near_sum_mlp", dqkv)
    qkv_tiles = 3 * width // LANES
    qkv_counts = [qkv_tiles - qkv_tiles // 3, qkv_tiles // 3]
    in_reduce.step(1, [dqkv])
    qkv_flows = pl.pallas_call(
        ordered(functools.partial(qkv_kernel, n, qkv_counts, orders), 3, 3),
        in_specs=[SMEM_SPEC] + [VMEM_SPEC] * 2 + [ANY_SPEC] * 3,
        out_shape=[shape((slots, n * c, chunk, LANES), BF16) for c in qkv_counts for _ in range(2)],
        scratch_shapes=[pltpu.VMEM((part, 3 * width), F32)],
        compiler_params=params,
        cost_estimate=work(12 * seq * model * width),
        name="qkv_gradient",
    )(place, normed1, dqkv, in_reduce.p[1], in_reduce.q[1], mlp_other)
    qkv_flows = [flow_rows(a) for a in qkv_flows]
    split = qkv_flows[2].shape[1]
    down_first = add_halves(down_keep, after(swap(down_send, "rep", near[0]), dqkv))
    qkv_q = [jnp.concatenate(x, axis=1) for x in zip(qkv_flows[2:], (out_keep, out_send))]
    qkv_q[1] = after(qkv_q[1], down_first[1])
    att_reduce = PairReduce(qkv_flows[:2], qkv_q, orders)
    att_reduce.step(0)
    att_first = att_reduce.p[1]
    att_reduce.step(1)
    output = pl.pallas_call(
        ordered(output_kernel, 3, 1),
        in_specs=[VMEM_SPEC] * 3 + [ANY_SPEC],
        out_shape=shape((rows, model), BF16),
        compiler_params=pltpu.CompilerParams(vmem_limit_bytes=16 << 20),
        name="output",
    )(mlp_mine, swap(mlp_other, "shard", top), hidden, qkv_flows[0])
    dnormed1_keep, dnormed1_send = pl.pallas_call(
        ordered(functools.partial(project_back_kernel, n), 3, 1),
        in_specs=[SMEM_SPEC] + [VMEM_SPEC] * 2 + [ANY_SPEC],
        out_shape=[block_shape] * 2,
        compiler_params=params,
        cost_estimate=work(6 * seq * model * width),
        name="project_back",
    )(place, dqkv, qkv_w, att_first)
    mine, other = near_sums(dnormed1_keep, dnormed1_send, "near_sum_1")
    input_grad = pl.pallas_call(
        input_kernel,
        out_shape=shape((rows, model), F32),
        compiler_params=pltpu.CompilerParams(vmem_limit_bytes=24 << 20),
        name="input_grad",
    )(mine, swap(other, "shard", top), tokens, dhidden)

    def turned(p, q, counts):
        sizes = [c * chunk for c in counts]
        whole = jnp.concatenate([p.reshape(n, sizes[0], LANES), q.reshape(n, sizes[1], LANES)], 1)
        whole = turn(whole, n)
        return whole[:, : sizes[0]].reshape(-1, LANES), whole[:, sizes[0] :].reshape(-1, LANES)

    def tiles_of(pair, count):
        size = n * count * chunk
        return [a[:, :size].reshape(a.shape[0], n * count, chunk, LANES) for a in pair]

    in_p, in_q = turned(*in_reduce.finish([[qkv_flows[0]]]), in_counts)
    down_share = replica_reduce(*down_first, near[1:], [[att_first]])

    att_p, att_q = att_reduce.finish()
    att_done = att_p[:16]
    in_p, in_q = pair_gather(in_p, in_q, orders)
    down_pair = replica_spread(after(down_share, att_done), near)
    qkv_p, qkv_q = turned(att_p, att_q[:split], qkv_counts)
    att_p, att_q = pair_gather(qkv_p, jnp.concatenate([qkv_q, att_q[split:]]), orders)

    in_total, ln2_total = columns_out(
        place,
        [tiles_of(in_p, in_counts[0]), tiles_of(in_q, in_counts[1])],
        in_counts,
        orders,
        w_in,
        gain2,
        n,
        ff=ff,
    )
    down_total = rows_out(place, down_pair, 0, ff, model, near)
    out_total = rows_out(place, att_q, split, part, model, far)
    qkv_total, ln1_total = columns_out(
        place,
        [tiles_of(att_p, qkv_counts[0]), tiles_of(att_q, qkv_counts[1])],
        qkv_counts,
        orders,
        w_qkv,
        gain1,
        n,
        head_cols=head_cols,
        width=width,
    )
    return (
        output,
        input_grad,
        ln1_total,
        qkv_total,
        out_total,
        ln2_total,
        in_total,
        down_total,
    )


def solution(mesh):
    return jax.shard_map(
        shards,
        mesh=mesh,
        in_specs=(
            P(("rep", "shard"), None),
            P("rep", None),
            P("shard"),
            P("shard", None),
            P("shard", None),
            P("shard"),
            P("shard", None),
            P("shard", None),
            P(("rep", "shard"), None),
        ),
        out_specs=(
            P(("rep", "shard"), None),
            P(("rep", "shard"), None),
            P("shard"),
            P("shard", None),
            P("shard", None),
            P("shard"),
            P("shard", None),
            P("shard", None),
        ),
        check_vma=False,
    )
```

```python
import functools
import math

import jax
import jax.numpy as jnp
from jax import lax
from jax.experimental import pallas as pl
from jax.experimental.pallas import tpu as pltpu
from jax.sharding import PartitionSpec as P

HEADS = 16
HEAD_DIM = 64
HALF = 64
QB = 128
LANES = 128

norm_epsilon = 1e-05
rope_base = 10000.0
masked_score = -1e30

F32 = jnp.float32
BF16 = jnp.bfloat16
VMEM_LIMIT = 52 << 20


def bits_of(axis):
    return lax.axis_size(axis).bit_length() - 1


def bit_of(axis, bit):
    return (lax.axis_index(axis) >> bit) & 1


def swap(x, axis, bit):
    size = lax.axis_size(axis)
    return lax.ppermute(x, axis, [(i, i ^ (1 << bit)) for i in range(size)])


def add_halves(keep, got):
    def total(a, b):
        return (keep[a:b].astype(F32) + got[a:b].astype(F32)).astype(BF16)

    size = keep.shape[0]
    if size == 1:
        return total(0, 1), None
    return total(0, size // 2), total(size // 2, size)


def block_order(n):
    bits = n.bit_length() - 1
    return [sum(((k >> b) & 1) << (bits - 1 - b) for b in range(bits)) for k in range(n)]


class Group:
    def __init__(self, array, held):
        self.array, self.held = array, held


def join(groups, bit, arrays, axis):
    held, start = [], 0
    for group in groups:
        held += [(j | 1 << bit, code, start + first, rows) for j, code, first, rows in group.held]
        start += group.array.shape[axis]
    array = arrays[0] if len(arrays) == 1 else jnp.concatenate(arrays, axis=axis)
    return Group(swap(array, "shard", bit), held)


def gather_rows(x, gate=None, apart=False):
    rows = x.shape[0]
    groups = [Group(x, [(0, None, 0, rows)])]
    for bit in reversed(range(bits_of("shard"))):
        arrays = [g.array for g in groups]
        if gate is not None and len(arrays) > 1:
            arrays[-1] = after(arrays[-1], *gate())
        if apart:
            groups = groups + [join([g], bit, [a], 0) for g, a in zip(groups, arrays)]
        else:
            groups = groups + [join(groups, bit, arrays, 0)]
    return groups


def parity(bits):
    return functools.reduce(lambda a, b: a ^ b, [bit_of("rep", bit) for bit in bits])


def half_by_replica(x, dim, bits):
    shape = x.shape
    x = x.reshape(shape[:dim] + (2, shape[dim] // 2) + shape[dim + 1 :])
    return lax.dynamic_index_in_dim(x, parity(bits), dim, keepdims=False)


def fetch_far(send, dim, top, gate, bits):
    got = swap(half_by_replica(send, dim, bits), "shard", top)
    kept = after(got, *gate) if gate else got
    size = got.shape[dim]
    count = len(bits)
    parts = jnp.split(kept, count, axis=dim)
    return [Group(got, [(1 << top, (0, bits), 0, size)])] + [
        Group(swap(part, "rep", bit), [(1 << top, (1 + k, bits), 0, size // count)])
        for k, (part, bit) in enumerate(zip(parts, bits))
    ]


def gather_weight(x, gate, bits):
    top = bits_of("shard") - 1
    groups = [Group(x, [(0, None, 0, x.shape[0])])] + fetch_far(x, 0, top, gate, bits)
    for bit in reversed(range(top)):
        groups = groups + [join(groups, bit, [g.array for g in groups], 0)]
    return groups


def split_weight(x, gate, bits):
    me = lax.axis_index("shard")
    top = bits_of("shard") - 1

    def part_for(a, bit):
        start = ((me & (a.shape[0] - 1)) >> bit ^ 1) << bit
        return lax.dynamic_slice_in_dim(a, start, 1 << bit)

    groups = [Group(x, [(0, None, 0, x.shape[1])])]
    groups += fetch_far(part_for(x, top), 1, top, gate, bits)
    for bit in reversed(range(top)):
        groups = groups + [join(groups, bit, [part_for(g.array, bit) for g in groups], 1)]
    return groups


def gated(value, gates, step):
    return after(value, *gates[step]) if step < len(gates) else value


def replica_reduce(keep, send, order, gates=()):
    for step, bit in enumerate(order):
        keep, send = add_halves(keep, gated(swap(send, "rep", bit), gates, step))
    return keep[0]


def replica_spread(x, order):
    now = x[None]
    for bit in reversed(order[1:]):
        now = jnp.concatenate([now, swap(now, "rep", bit)])
    return now, swap(now, "rep", order[0])


class PairReduce:
    def __init__(self, p, q, orders):
        self.p, self.q, self.orders = p, q, orders

    def step(self, i, gates=()):
        p, q = self.p, self.q
        got_p = swap(p[1], "rep", self.orders[0][i])
        got_q = swap(q[1], "rep", self.orders[1][i])
        if gates:
            got_p, got_q = after(got_p, *gates), after(got_q, *gates)
        self.p, self.q = add_halves(p[0], got_p), add_halves(q[0], got_q)

    def finish(self, gates=()):
        rows = self.p[0].shape[1]
        keep, send = (jnp.concatenate(x, axis=1) for x in zip(self.p, self.q))
        share = replica_reduce(keep, send, self.orders[0][2:], gates)
        return share[:rows], share[rows:]


def pair_gather(p, q, orders):
    rows = p.shape[0]
    now = jnp.concatenate([p, q])[None]
    for bit in reversed(orders[0][2:]):
        now = jnp.concatenate([now, swap(now, "rep", bit)])
    pairs = []
    for x, order in zip((now[:, :rows], now[:, rows:]), orders):
        x = jnp.concatenate([x, swap(x, "rep", order[1])])
        pairs.append((x, swap(x, "rep", order[0])))
    return pairs


def turn(x, n):
    x = x[:, None]
    for bit in reversed(range(n.bit_length() - 1)):
        half = x.shape[0] // 2
        x = jnp.concatenate([x[:half], swap(x[half:], "shard", bit)], axis=1)
    return x[0]


def from_place(j, n):
    bits = n.bit_length() - 1
    return sum(((j >> b) & 1) << (bits - 1 - b) for b in range(bits))


def slot_mask(slot, order):
    count = len(order)
    return sum(((slot >> (count - 1 - i)) & 1) << bit for i, bit in enumerate(order))


def slot_of(mask, order):
    count = len(order)
    return sum(((mask >> bit) & 1) << (count - 1 - i) for i, bit in enumerate(order))


def dot(a, b, dims):
    return lax.dot_general(a, b, (dims, ((), ())), preferred_element_type=F32)


def normalise(values):
    centred = values - jnp.mean(values, axis=-1, keepdims=True)
    scale = lax.rsqrt(jnp.mean(centred * centred, axis=-1, keepdims=True) + norm_epsilon)
    return centred * scale, scale


def held_of(groups):
    return [(g.held, g.array.shape) for g in groups]


def arrays_of(groups):
    return [g.array for g in groups]


def pieces_of(held):
    return sum(len(h) for h, _ in held)


def blocks_of(held, refs):
    found = {}
    for (pieces, _), ref in zip(held, refs):
        for j, _, first, rows in pieces:
            found[j] = ref.at[first : first + rows, :]
    return [found[j] for j in range(len(found))]


def weight_copies(held, refs, target, me, sems, rep, by_owner, rows):
    copies = []
    for (pieces, shape), ref in zip(held, refs):
        source = ref.at[me & (shape[0] - 1)] if len(shape) == 3 else ref
        for j, code, first, count in pieces:
            start = (me ^ j if by_owner else j) * rows
            if code is not None:
                place, bits = code
                own = functools.reduce(lambda a, b: a ^ b, [(rep >> bit) & 1 for bit in bits])
                start = start + (own if place == 0 else 1 - own) * (rows // 2)
                start = start + max(place - 1, 0) * (rows // 2 // len(bits))
            place = target.at[pl.ds(pl.multiple_of(start, count), count), :]
            sem = sems.at[len(copies)]
            copies.append(pltpu.make_async_copy(source.at[first : first + count, :], place, sem))
    return copies


def partner(x):
    width = x.shape[-1]
    lane = lax.broadcasted_iota(jnp.int32, x.shape, 1)
    front = (lane % HEAD_DIM) < HEAD_DIM // 2
    return jnp.where(
        front,
        pltpu.roll(x, width - HEAD_DIM // 2, 1),
        pltpu.roll(x, HEAD_DIM // 2, 1),
    )


def head_masks(heads, width):
    lane = lax.broadcasted_iota(jnp.int32, (QB, width), 1) // HEAD_DIM
    return [lane == h for h in range(heads)]


def stack_heads(x, masks):
    x = x.astype(F32)
    return jnp.concatenate([jnp.where(m, x, 0.0) for m in masks], axis=0).astype(BF16)


def merge_heads(x, masks):
    total = None
    for h, m in enumerate(masks):
        part = jnp.where(m, x[h * QB : (h + 1) * QB], 0.0)
        total = part if total is None else total + part
    return total


def window_bias(ids_q, ids_k):
    row = lax.broadcasted_iota(jnp.int32, (QB, QB + 2 * HALF), 0)
    col = lax.broadcasted_iota(jnp.int32, (QB, QB + 2 * HALF), 1)
    ids_q = jnp.concatenate([ids_q] * ((QB + 2 * HALF) // LANES), axis=1)
    allowed = (col >= row) & (col <= row + 2 * HALF) & (ids_q == ids_k)
    return jnp.where(allowed, 0.0, masked_score)


def block_probs(stacked_q, keys, bias, heads):
    scores = dot(stacked_q, keys, ((1,), (1,)))
    rows, cols = scores.shape
    scores = (scores.reshape(heads, QB, cols) + bias[None]).reshape(rows, cols)
    weights = jnp.exp(scores - jnp.max(scores, axis=-1, keepdims=True))
    return weights * (1.0 / jnp.sum(weights, axis=-1, keepdims=True))


def column_chunk(ref, chunk, cols):
    if cols >= LANES:
        return ref[:, pl.ds(pl.multiple_of(chunk * cols, cols), cols)]
    per = LANES // cols
    tile = ref[:, pl.ds(pl.multiple_of(chunk // per * LANES, LANES), LANES)]
    result = tile
    for k in range(1, per):
        result = jnp.where(chunk % per == k, pltpu.roll(tile, LANES - k * cols, 1), result)
    return result


def row_chunk(ref, chunk, rows, start):
    if rows % 8 == 0:
        return ref[pl.ds(pl.multiple_of(chunk * rows, rows), rows), start : start + LANES]
    per = 8 // rows
    tile = ref[pl.ds(pl.multiple_of(chunk // per * 8, 8), 8), start : start + LANES]
    result = tile[:rows]
    for k in range(1, per):
        result = jnp.where(chunk % per == k, tile[k * rows : (k + 1) * rows], result)
    return result


def take_columns(ref, offset, valid, size):
    begin = offset // LANES * LANES
    end = -(-(offset + valid) // LANES) * LANES
    x = ref[:, begin:end].astype(F32)
    if offset != begin:
        x = pltpu.roll(x, end - offset, 1)
    x = x[:, :size]
    if valid != size:
        lane = lax.broadcasted_iota(jnp.int32, x.shape, 1)
        x = jnp.where(lane < valid, x, 0.0)
    return x


def split_kernel(n, blocks, valid, size, gain_ref, w_ref, out_ref):
    gain = gain_ref[...]
    for owner in range(n):
        for b in range(blocks):
            x = take_columns(w_ref, (b * n + owner) * valid, valid, size)
            out_ref[owner, :, b * size : (b + 1) * size] = (x * gain).astype(BF16)


def split_columns(w, gain, n, blocks, valid, size):
    rows, cols = w.shape
    step = min(rows, 64)
    return pl.pallas_call(
        functools.partial(split_kernel, n, blocks, valid, size),
        grid=(rows // step,),
        in_specs=[
            pl.BlockSpec((step, 1), lambda i: (i, 0)),
            pl.BlockSpec((step, cols), lambda i: (i, 0)),
        ],
        out_specs=pl.BlockSpec((n, step, blocks * size), lambda i: (0, i, 0)),
        out_shape=jax.ShapeDtypeStruct((n, rows, blocks * size), BF16),
        compiler_params=pltpu.CompilerParams(vmem_limit_bytes=24 << 20),
        name="split_columns",
    )(gain, w)


def attention_kernel(
    tok_held, held, n, heads, place_ref, cos_ref, sin_ref, idq_ref, idk_ref, *refs
):
    tok_refs, refs = blocks_of(tok_held, refs), refs[len(tok_held) :]
    piece_refs, refs = refs[: len(held)], refs[len(held) :]
    q_ref, k_ref, v_ref, out_ref, normed_ref, w_ref, sems = refs
    seq, width = q_ref.shape
    rows = seq // n
    me, rep = place_ref[0], place_ref[1]
    copies = weight_copies(
        held, piece_refs, w_ref, me, sems, rep, True, w_ref.shape[0] // n
    )
    for c in copies:
        c.start()
    edge = jnp.zeros((HALF, width), BF16)
    for ref in (k_ref, v_ref):
        ref[0:HALF, :] = edge
        ref[seq + HALF : seq + 2 * HALF, :] = edge
    for c in copies:
        c.wait()
    for j in range(n):
        start = (me ^ j) * rows
        at = pl.ds(pl.multiple_of(start, rows), rows)
        shifted = pl.ds(pl.multiple_of(start + HALF, HALF), rows)
        hat, _ = normalise(tok_refs[j][...].astype(F32))
        normed = hat.astype(BF16)
        normed_ref[at, :] = normed
        qkv = jnp.dot(normed, w_ref[...], preferred_element_type=F32)
        cos, sin = cos_ref[at, :], sin_ref[at, :]
        q, k = qkv[:, 0:width], qkv[:, width : 2 * width]
        rotated = (q * cos + partner(q) * sin).astype(BF16)
        q_ref[at, :] = (rotated.astype(F32) * (1.0 / math.sqrt(HEAD_DIM))).astype(BF16)
        k_ref[shifted, :] = (k * cos + partner(k) * sin).astype(BF16)
        v_ref[shifted, :] = qkv[:, 2 * width : 3 * width].astype(BF16)
    masks = head_masks(heads, width)

    def attend(i, carry):
        at = pl.ds(pl.multiple_of(i * QB, QB), QB)
        window = pl.ds(pl.multiple_of(i * QB, QB), QB + 2 * HALF)
        bias = window_bias(idq_ref[at, :], idk_ref[0:1, window])
        probs = block_probs(stack_heads(q_ref[at, :], masks), k_ref[window, :], bias, heads)
        mixed = jnp.dot(probs.astype(BF16), v_ref[window, :], preferred_element_type=F32)
        out_ref[at, :] = merge_heads(mixed, masks).astype(BF16)
        return carry

    lax.fori_loop(0, seq // QB, attend, 0, unroll=2)


def up_kernel(tok_held, att_held, out_held, in_held, n, place_ref, *refs):
    tok_refs, refs = blocks_of(tok_held, refs), refs[len(tok_held) :]
    att_refs, refs = blocks_of(att_held, refs), refs[len(att_held) :]
    out_refs, refs = refs[: len(out_held)], refs[len(out_held) :]
    in_refs, refs = refs[: len(in_held)], refs[len(in_held) :]
    hidden_out, normed_out, up_out, in_out, *refs = refs
    tok, att, w_out, w_in, hidden_own, normed, up, *refs = refs
    out_sems, in_sems, att_sems, tok_sems, sems = refs
    me, rep = place_ref[0], place_ref[1]
    rows, model = tok_refs[0].shape
    copy = pltpu.make_async_copy
    att_copies = [copy(att_refs[j], att.at[j], att_sems.at[j]) for j in range(n)]
    tok_copies = [copy(tok_refs[j], tok.at[j], tok_sems.at[j]) for j in range(n)]
    part = model // n
    out_copies = weight_copies(out_held, out_refs, w_out, me, out_sems, rep, False, part)
    in_copies = weight_copies(in_held, in_refs, w_in, me, in_sems, rep, True, part)
    for c in att_copies + tok_copies[:1] + out_copies + in_copies + tok_copies[1:]:
        c.start()
    for c in att_copies + out_copies:
        c.wait()
    sent = []
    for j in range(n):
        at = pl.ds(pl.multiple_of((me ^ j) * rows, rows), rows)
        here = slice(j * rows, (j + 1) * rows)
        tok_copies[j].wait()
        hidden = tok[j].astype(F32)
        for i in range(n):
            hidden = hidden + jnp.dot(
                att[i, at, :], w_out[i * part : (i + 1) * part, :], preferred_element_type=F32
            )
        if j == 0:
            hidden_own[...] = hidden
            sent.append(copy(hidden_own, hidden_out, sems.at[2 * n]))
            sent[-1].start()
        hat, _ = normalise(hidden)
        low = hat.astype(BF16)
        normed[here, :] = low
        if j == 0:
            for c in in_copies:
                c.wait()
            sent.append(copy(w_in, in_out, sems.at[2 * n + 1]))
            sent[-1].start()
        up[here, :] = jnp.dot(low, w_in[...], preferred_element_type=F32)
        sent += [
            copy(normed.at[here, :], normed_out.at[here, :], sems.at[2 * j]),
            copy(up.at[here, :], up_out.at[here, :], sems.at[2 * j + 1]),
        ]
        for c in sent[-2:]:
            c.start()
    for c in sent:
        c.wait()


def dup_kernel(cot_held, n, up_ref, w_in_ref, down_ref, *refs):
    cot_refs, refs = blocks_of(cot_held, refs), refs[len(cot_held) :]
    act_out, dup_out, keep_out, send_out, *refs = refs
    up, cot, w_in, w_down, act, dup, dnormed, in_sem, down_sem, up_sems, cot_sems, sems = refs
    rows, model = cot_refs[0].shape
    padded = w_down.shape[0]
    given = down_ref.shape[0]
    if given != padded:
        w_down[given:padded, :] = jnp.zeros((padded - given, model), BF16)
    copy = pltpu.make_async_copy
    down_copy = copy(down_ref, w_down.at[0:given, :], down_sem)
    in_copy = copy(w_in_ref, w_in, in_sem)
    cot_copies = [copy(cot_refs[j], cot.at[j], cot_sems.at[j]) for j in range(n)]
    up_copies = []
    for j in range(n):
        here = slice(j * rows, (j + 1) * rows)
        up_copies.append(copy(up_ref.at[here, :], up.at[here, :], up_sems.at[j]))
    for c in [up_copies[0], cot_copies[0], down_copy, in_copy]:
        c.start()
    for c in up_copies[1:] + cot_copies[1:]:
        c.start()
    sent = []
    order = block_order(n)
    for j in range(n):
        here = slice(j * rows, (j + 1) * rows)
        place = order.index(j)
        target = (keep_out if place < n // 2 else send_out).at[place % (n // 2)]
        up_copies[j].wait()
        gate, lin = up[here, :padded], up[here, padded:]
        phi = 0.5 + 0.5 * lax.erf(gate * (1.0 / math.sqrt(2.0)))
        gelu = gate * phi
        slope = phi + gate * jnp.exp(gate * gate * -0.5) * (1.0 / math.sqrt(2.0 * math.pi))
        act[here, :] = (gelu * lin).astype(BF16)
        cot_copies[j].wait()
        if j == 0:
            down_copy.wait()
        dact = dot(cot[j], w_down[...], ((1,), (1,)))
        dup[here, :padded] = (dact * lin * slope).astype(BF16)
        dup[here, padded:] = (dact * gelu).astype(BF16)
        if j == 0:
            in_copy.wait()
        dnormed[j] = dot(dup[here, :], w_in[...], ((1,), (1,))).astype(BF16)
        sent += [
            copy(dnormed.at[j], target, sems.at[3 * j]),
            copy(act.at[here, :], act_out.at[here, :], sems.at[3 * j + 1]),
            copy(dup.at[here, :], dup_out.at[here, :], sems.at[3 * j + 2]),
        ]
        for c in sent[-3:]:
            c.start()
    for c in sent:
        c.wait()


def store_slots(keep_ref, send_ref, rep, order, write):
    half = keep_ref.shape[0]
    for slot in range(2 * half):
        target = keep_ref if slot < half else send_ref
        write(target, slot % half, rep ^ slot_mask(slot, order))


def up_tiles(ff):
    return 2 * (ff // LANES) + 1


def put_block(keep, send, j, value):
    half = keep.shape[0]
    place = block_order(2 * half).index(j)
    target = keep if place < half else send
    target[place % half] = value.astype(BF16)


def down_kernel(cot_held, n, ff, order, place_ref, act, w_down, *refs):
    cot_refs, refs = blocks_of(cot_held, refs), refs[len(cot_held) :]
    keep, send, mlp_keep, mlp_send, down_sum = refs
    rows, model = cot_refs[0].shape
    cols = model // (2 * keep.shape[0])
    total = None
    for j in range(n):
        term = dot(act[j * rows : (j + 1) * rows, :], cot_refs[j][...], ((0,), (0,)))
        total = term if total is None else total + term
    down_sum[...] = total

    def write(target, slot, c):
        target[slot] = column_chunk(down_sum, c, cols)[:ff].astype(BF16)

    store_slots(keep, send, place_ref[1], order, write)
    given = w_down.shape[0]
    for j in range(n):
        low = act[j * rows : (j + 1) * rows, 0:given]
        put_block(mlp_keep, mlp_send, j, jnp.dot(low, w_down[...], preferred_element_type=F32))


def write_flows(total, starts, counts, orders, flows, index, rep):
    begin = 0
    for f, (count, order) in enumerate(zip(counts, orders)):
        keep, send = flows[2 * f], flows[2 * f + 1]
        chunk = keep.shape[2]

        def write(target, slot, c):
            for t in range(count):
                value = row_chunk(total, c, chunk, starts[begin + t])
                target[slot, index * count + t] = value.astype(BF16)

        store_slots(keep, send, rep, order, write)
        begin += count


def in_kernel(n, ff, counts, orders, place_ref, normed, dup, *refs):
    flows, in_sum = refs[:-1], refs[-1]
    me, rep = place_ref[0], place_ref[1]
    part = normed.shape[1] // n
    padded = dup.shape[1] // 2
    whole, rest = ff // LANES, ff % LANES
    starts = [t * LANES for t in range(whole)] + [padded + t * LANES for t in range(whole)]
    starts.append(2 * padded)
    for owner in range(n):
        block = dot(normed[:, owner * part : (owner + 1) * part], dup[...], ((0,), (0,)))
        in_sum[:, : 2 * padded] = block
        first = block[:, whole * LANES : (whole + 1) * LANES]
        second = block[:, padded + whole * LANES : padded + (whole + 1) * LANES]
        lane = lax.broadcasted_iota(jnp.int32, first.shape, 1)
        in_sum[:, 2 * padded :] = jnp.where(lane < rest, first, pltpu.roll(second, rest, 1))
        write_flows(in_sum, starts, counts, orders, flows, me ^ owner, rep)


def add_kernel(keep_ref, got_ref, mine_ref, other_ref):
    mine_ref[...] = keep_ref[0].astype(F32) + got_ref[0].astype(F32)
    other_ref[...] = (keep_ref[1].astype(F32) + got_ref[1].astype(F32)).astype(BF16)


def near_sums(keep, send, name, gate=None):
    bits = bits_of("shard")
    for bit in range(bits - 2):
        keep, send = add_halves(keep, swap(send, "shard", bit))
    _, rows, model = keep.shape
    got = swap(send, "shard", bits - 2)
    if gate is not None:
        got = after(got, gate)
    return pl.pallas_call(
        add_kernel,
        out_shape=[
            jax.ShapeDtypeStruct((rows, model), F32),
            jax.ShapeDtypeStruct((rows, model), BF16),
        ],
        compiler_params=pltpu.CompilerParams(vmem_limit_bytes=16 << 20),
        name=name,
    )(keep, got)


def output_kernel(mine, got, hidden, out_ref):
    out_ref[...] = (hidden[...] + mine[...] + got[...].astype(F32)).astype(BF16)


def input_kernel(mine, got, tokens, dhidden, out_ref):
    hat, scale = normalise(tokens[...].astype(F32))
    e = mine[...] + got[...].astype(F32)
    out_ref[...] = dhidden[...] + norm_backward(e, hat, scale)


def norm_back_kernel(mine, got, hidden, cotangent, dhidden, dproj):
    hat, scale = normalise(hidden[...])
    e = mine[...] + got[...].astype(F32)
    value = cotangent[...].astype(F32) + norm_backward(e, hat, scale)
    dhidden[...] = value
    dproj[...] = value.astype(BF16)


def attention_back_kernel(held, n, heads, order, place_ref, *refs):
    dproj_refs, refs = blocks_of(held, refs), refs[len(held) :]
    w_out, att, q_ref, k_ref, v_ref, cos_ref, sin_ref, idq_ref, idk_ref, *refs = refs
    dqkv, out_keep, out_send, da, dk, dv, out_sum = refs
    me, rep = place_ref[0], place_ref[1]
    seq, width = q_ref.shape
    rows, model = dproj_refs[0].shape
    part = model // n
    dk[...] = jnp.zeros_like(dk)
    dv[...] = jnp.zeros_like(dv)
    head_cols = heads * HEAD_DIM
    total = None
    for j in range(n):
        at = pl.ds(pl.multiple_of((me ^ j) * rows, rows), rows)
        dproj = dproj_refs[j][...]
        da[at, 0:head_cols] = dot(dproj, w_out[...], ((1,), (1,))).astype(BF16)
        term = dot(att[at, :], dproj, ((0,), (0,)))
        total = term if total is None else total + term
    if head_cols != width:
        da[:, head_cols:] = jnp.zeros((seq, width - head_cols), BF16)
    out_sum[...] = total[0:part]
    cols = model // (2 * out_keep.shape[0])

    def write_out(target, slot, c):
        target[slot] = column_chunk(out_sum, c, cols).astype(BF16)

    store_slots(out_keep, out_send, rep, order, write_out)
    masks = head_masks(heads, width)

    def back(i, carry):
        at = pl.ds(pl.multiple_of(i * QB, QB), QB)
        window = pl.ds(pl.multiple_of(i * QB, QB), QB + 2 * HALF)
        bias = window_bias(idq_ref[at, :], idk_ref[0:1, window])
        queries = stack_heads(q_ref[at, :], masks)
        keys = k_ref[window, :]
        probs = block_probs(queries, keys, bias, heads)
        grads = stack_heads(da[at, :], masks)
        dprobs = dot(grads, v_ref[window, :], ((1,), (1,)))
        delta = jnp.sum(probs * dprobs, axis=-1, keepdims=True)
        dscores = (probs * (dprobs - delta)).astype(BF16)
        dq = merge_heads(jnp.dot(dscores, keys, preferred_element_type=F32), masks)
        dq = dq * (1.0 / math.sqrt(HEAD_DIM))
        cos, sin = cos_ref[at, :], sin_ref[at, :]
        dqkv[at, 0:width] = (dq * cos - partner(dq) * sin).astype(BF16)
        dk[window, :] += dot(dscores, queries, ((0,), (0,)))
        dv[window, :] += dot(probs.astype(BF16), grads, ((0,), (0,)))
        return carry

    lax.fori_loop(0, seq // QB, back, 0, unroll=2)

    def finish(i, carry):
        at = pl.ds(pl.multiple_of(i * QB, QB), QB)
        shifted = pl.ds(pl.multiple_of(i * QB + HALF, HALF), QB)
        cos, sin = cos_ref[at, :], sin_ref[at, :]
        g = dk[shifted, :]
        dqkv[at, width : 2 * width] = (g * cos - partner(g) * sin).astype(BF16)
        dqkv[at, 2 * width : 3 * width] = dv[shifted, :].astype(BF16)
        return carry

    lax.fori_loop(0, seq // QB, finish, 0)


def qkv_kernel(n, counts, orders, place_ref, normed, dqkv, *refs):
    flows, qkv_sum = refs[:-1], refs[-1]
    me, rep = place_ref[0], place_ref[1]
    part = normed.shape[1] // n
    starts = [t * LANES for t in range(sum(counts))]
    for owner in range(n):
        qkv_sum[...] = dot(normed[:, owner * part : (owner + 1) * part], dqkv[...], ((0,), (0,)))
        write_flows(qkv_sum, starts, counts, orders, flows, me ^ owner, rep)


def project_back_kernel(n, place_ref, dqkv, w_qkv, keep, send):
    rows = keep.shape[1]
    for j in range(n):
        at = pl.ds(pl.multiple_of((place_ref[0] ^ j) * rows, rows), rows)
        put_block(keep, send, j, dot(dqkv[at, :], w_qkv[...], ((1,), (1,))))


def place_piece(canvas, piece, offset, valid):
    shift = offset % LANES
    height, size = piece.shape
    count = -(-(shift + valid) // LANES)
    if count * LANES > size:
        piece = jnp.concatenate([piece, jnp.zeros((height, count * LANES - size), F32)], axis=1)
    if shift:
        piece = pltpu.roll(piece, shift, 1)
    lane = lax.broadcasted_iota(jnp.int32, (height, LANES), 1)
    for t in range(count):
        tile = piece[:, t * LANES : (t + 1) * LANES]
        low, high = shift - t * LANES, shift + valid - t * LANES
        if low > 0 or high < LANES:
            tile = jnp.where((lane >= low) & (lane < high), tile, 0.0)
        index = offset // LANES + t
        canvas[index] = tile if index not in canvas else canvas[index] + tile


def columns_out_kernel(n, ff, head_cols, width, counts, orders, place_ref, gain_ref, w_ref, *refs):
    me, rep = place_ref[0], place_ref[1]
    *parts, out_ref, ln_ref = refs
    half = parts[0].shape[0]
    slots = [slot_of(rep ^ pl.program_id(0), order) for order in orders]

    def read(owner, t):
        f = 0
        while t >= counts[f]:
            t -= counts[f]
            f += 1
        slot, index = slots[f], from_place(me ^ owner, n) * counts[f] + t
        at = slot & (half - 1)
        now, got = parts[2 * f][at, index], parts[2 * f + 1][at, index]
        return jnp.where(slot < half, now, got).astype(F32)

    canvas = {}
    for owner in range(n):
        tile = functools.partial(read, owner)

        if ff:
            whole, rest = ff // LANES, ff % LANES
            last = tile(2 * whole)
            gate = jnp.concatenate([tile(t) for t in range(whole)] + [last], axis=1)
            last = pltpu.roll(last, LANES - rest, 1)
            lin = jnp.concatenate([tile(whole + t) for t in range(whole)] + [last], axis=1)
            place_piece(canvas, gate, owner * ff, ff)
            place_piece(canvas, lin, (n + owner) * ff, ff)
        else:
            per = width // LANES
            for b in range(3):
                piece = jnp.concatenate([tile(b * per + t) for t in range(per)], axis=1)
                place_piece(canvas, piece, (b * n + owner) * head_cols, head_cols)
    gain = gain_ref[...]
    total = None
    for index, value in canvas.items():
        at = slice(index * LANES, (index + 1) * LANES)
        term = value * w_ref[:, at].astype(F32)
        total = term if total is None else total + term
        out_ref[:, at] = value * gain
    ln_ref[...] = jnp.sum(total, axis=1, keepdims=True)


def columns_out(place, pairs, counts, orders, weight, gain, n, ff=0, head_cols=0, width=0):
    parts = [a for pair in pairs for a in pair]
    chunk = parts[0].shape[2]
    part, cols = weight.shape
    count = part // chunk
    part_specs = [pl.BlockSpec(a.shape, lambda i: (0, 0, 0, 0)) for a in parts]
    total, ln = pl.pallas_call(
        functools.partial(columns_out_kernel, n, ff, head_cols, width, counts, orders),
        grid=(count,),
        in_specs=[
            pl.BlockSpec(memory_space=pltpu.SMEM),
            pl.BlockSpec((None, chunk, 1), lambda i: (i, 0, 0)),
            pl.BlockSpec((None, chunk, cols), lambda i: (i, 0, 0)),
            *part_specs,
        ],
        out_specs=[
            pl.BlockSpec((None, chunk, cols), lambda i: (i, 0, 0)),
            pl.BlockSpec((None, chunk, 1), lambda i: (i, 0, 0)),
        ],
        out_shape=[
            jax.ShapeDtypeStruct((count, chunk, cols), F32),
            jax.ShapeDtypeStruct((count, chunk, 1), F32),
        ],
        compiler_params=pltpu.CompilerParams(vmem_limit_bytes=32 << 20),
        name="columns_out",
    )(place, gain.reshape(count, chunk, 1), weight.reshape(count, chunk, cols), *parts)
    return total.reshape(part, cols), ln.reshape(part)


def rows_out_kernel(order, cols, skip, place_ref, *refs):
    *parts, out_ref = refs
    rep = place_ref[1]

    def chunk(c):
        half = parts[0].shape[0]
        slot = slot_of(rep ^ c, order)
        at = slot & (half - 1)
        rows = slice(skip, skip + out_ref.shape[0])
        return jnp.where(slot < half, parts[0][at, rows], parts[1][at, rows]).astype(F32)

    count = out_ref.shape[1] // cols
    if cols >= LANES:
        for c in range(count):
            out_ref[:, c * cols : (c + 1) * cols] = chunk(c)
    else:
        per = LANES // cols
        lane = lax.broadcasted_iota(jnp.int32, out_ref.shape[:1] + (LANES,), 1) // cols
        for t in range(count // per):
            value = chunk(per * t)
            for k in range(1, per):
                value = jnp.where(lane == k, pltpu.roll(chunk(per * t + k), k * cols, 1), value)
            out_ref[:, t * LANES : (t + 1) * LANES] = value


def rows_out(place, pair, skip, rows, model, order):
    return pl.pallas_call(
        functools.partial(rows_out_kernel, order, model // (2 * pair[0].shape[0]), skip),
        in_specs=[pl.BlockSpec(memory_space=pltpu.SMEM)]
        + [pl.BlockSpec(memory_space=pltpu.VMEM)] * 2,
        out_shape=jax.ShapeDtypeStruct((rows, model), F32),
        compiler_params=pltpu.CompilerParams(vmem_limit_bytes=32 << 20),
        name="rows_out",
    )(place, *pair)


def ordered(kernel, first, count):
    def body(*refs):
        kernel(*refs[:first], *refs[first + count :])

    return body


def work(flops):
    return pl.CostEstimate(flops=int(flops), bytes_accessed=1 << 22, transcendentals=0)


SMEM_SPEC = pl.BlockSpec(memory_space=pltpu.SMEM)
VMEM_SPEC = pl.BlockSpec(memory_space=pltpu.VMEM)
ANY_SPEC = pl.BlockSpec(memory_space=pl.ANY)


def norm_backward(grad_hat, normed, scale):
    return (
        grad_hat
        - jnp.mean(grad_hat, axis=-1, keepdims=True)
        - normed * jnp.mean(grad_hat * normed, axis=-1, keepdims=True)
    ) * scale


def after(value, *earlier):
    return lax.optimization_barrier((value,) + earlier)[0]


def shards(tokens, segment_ids, ln1_gain, w_qkv, w_out, ln2_gain, w_in, w_down, cotangent):
    n = lax.axis_size("shard")
    replicas = lax.axis_size("rep")
    me = lax.axis_index("shard")
    place = jnp.stack([me, lax.axis_index("rep")]).astype(jnp.int32)
    rows, model = tokens.shape
    seq = rows * n
    part = model // n
    ff = w_down.shape[0]
    heads = HEADS // n
    head_cols = heads * HEAD_DIM
    width = max(LANES, head_cols)
    padded = -(-ff // LANES) * LANES
    near = list(range(bits_of("rep")))
    far = near[1:2] + near[:1] + near[2:]
    shape = jax.ShapeDtypeStruct
    params = pltpu.CompilerParams(vmem_limit_bytes=VMEM_LIMIT)

    gain1 = ln1_gain.astype(F32)[:, None]
    gain2 = ln2_gain.astype(F32)[:, None]
    qkv_to = split_columns(w_qkv, gain1, n, 3, head_cols, width)
    in_to = split_columns(w_in, gain2, n, 2, ff, padded)
    lane = jnp.arange(width, dtype=jnp.int32) % HEAD_DIM
    half = HEAD_DIM // 2
    frequency = jnp.exp(-math.log(rope_base) * 2.0 * (lane % half).astype(F32) / HEAD_DIM)
    angles = jnp.arange(seq, dtype=F32)[:, None] * frequency[None, :]
    sign = jnp.where(lane < half, -1.0, 1.0)
    ids = segment_ids[0]
    tables = (
        jnp.cos(angles),
        jnp.sin(angles) * sign[None, :],
        jnp.broadcast_to(ids[:, None], (seq, LANES)),
        jnp.pad(ids, (HALF, HALF), constant_values=-1)[None],
    )

    qkv_groups = split_weight(qkv_to, (tables[0], tables[1], in_to), (0, 1))
    toks = gather_rows(tokens, apart=True)

    queries, keys, values, attended, normed1, qkv_w = pl.pallas_call(
        ordered(
            functools.partial(attention_kernel, held_of(toks), held_of(qkv_groups), n, heads),
            5 + len(toks) + len(qkv_groups),
            0,
        ),
        in_specs=[SMEM_SPEC]
        + [VMEM_SPEC] * (4 + len(toks))
        + [ANY_SPEC] * len(qkv_groups),
        out_shape=(
            shape((seq, width), BF16),
            shape((seq + 2 * HALF, width), BF16),
            shape((seq + 2 * HALF, width), BF16),
            shape((seq, width), BF16),
            shape((seq, model), BF16),
            shape((model, 3 * width), BF16),
        ),
        scratch_shapes=[pltpu.SemaphoreType.DMA((pieces_of(held_of(qkv_groups)),))],
        compiler_params=params,
        cost_estimate=work(40 * seq * model * width),
        name="attention",
    )(place, *tables, *arrays_of(toks + qkv_groups))

    out_groups = gather_weight(after(w_out, toks[1].array), (attended,), (2,))
    in_groups = split_weight(after(in_to, qkv_groups[1].array), (attended,), (0, 1))
    atts = gather_rows(attended[:, :head_cols])
    block_shape = shape((n // 2, rows, model), BF16)
    hidden, normed2, up, in_w = pl.pallas_call(
        functools.partial(
            up_kernel, held_of(toks), held_of(atts), held_of(out_groups), held_of(in_groups), n
        ),
        in_specs=[SMEM_SPEC] + [ANY_SPEC] * len(toks + atts + out_groups + in_groups),
        out_specs=[ANY_SPEC] * 4,
        out_shape=[
            shape((rows, model), F32),
            shape((seq, model), BF16),
            shape((seq, 2 * padded), F32),
            shape((model, 2 * padded), BF16),
        ],
        scratch_shapes=[
            pltpu.VMEM((n, rows, model), BF16),
            pltpu.VMEM((n, seq, head_cols), BF16),
            pltpu.VMEM((model, model), BF16),
            pltpu.VMEM((model, 2 * padded), BF16),
            pltpu.VMEM((rows, model), F32),
            pltpu.VMEM((seq, model), BF16),
            pltpu.VMEM((seq, 2 * padded), F32),
            pltpu.SemaphoreType.DMA((pieces_of(held_of(out_groups)),)),
            pltpu.SemaphoreType.DMA((pieces_of(held_of(in_groups)),)),
            pltpu.SemaphoreType.DMA((n,)),
            pltpu.SemaphoreType.DMA((n,)),
            pltpu.SemaphoreType.DMA((2 * n + 2,)),
        ],
        compiler_params=params,
        cost_estimate=work(12 * seq * model * padded),
        name="up_projection",
    )(place, *arrays_of(toks + atts + out_groups + in_groups))
    cots = gather_rows(after(cotangent, atts[1].array), lambda: (up,), apart=True)
    down_w = jnp.pad(w_down, ((0, -ff % 16), (0, 0)))
    act, dup, dnormed2_keep, dnormed2_send = pl.pallas_call(
        functools.partial(dup_kernel, held_of(cots), n),
        in_specs=[ANY_SPEC] * (3 + len(cots)),
        out_specs=[ANY_SPEC] * 4,
        out_shape=[shape((seq, padded), BF16), shape((seq, 2 * padded), BF16)] + [block_shape] * 2,
        scratch_shapes=[
            pltpu.VMEM((seq, 2 * padded), F32),
            pltpu.VMEM((n, rows, model), BF16),
            pltpu.VMEM((model, 2 * padded), BF16),
            pltpu.VMEM((padded, model), BF16),
            pltpu.VMEM((seq, padded), BF16),
            pltpu.VMEM((seq, 2 * padded), BF16),
            pltpu.VMEM((n, rows, model), BF16),
            pltpu.SemaphoreType.DMA,
            pltpu.SemaphoreType.DMA,
            pltpu.SemaphoreType.DMA((n,)),
            pltpu.SemaphoreType.DMA((n,)),
            pltpu.SemaphoreType.DMA((3 * n,)),
        ],
        compiler_params=params,
        cost_estimate=work(14 * seq * model * padded),
        name="dup",
    )(up, in_w, down_w, *arrays_of(cots))

    slots = replicas // 2
    chunk = part // replicas
    lanes = max(LANES, model // replicas)
    tiles = up_tiles(ff)
    orders = [near, far]
    in_counts = [tiles // 2, tiles - tiles // 2]
    in_shapes = [shape((slots, n * c, chunk, LANES), BF16) for c in in_counts for _ in range(2)]
    down_shape = shape((slots, ff, lanes), BF16)
    top = bits_of("shard") - 1

    def flow_rows(a):
        return a.reshape(a.shape[0], -1, LANES)

    mine, other = near_sums(dnormed2_keep, dnormed2_send, "near_sum_2")
    in_flows = pl.pallas_call(
        ordered(functools.partial(in_kernel, n, ff, in_counts, orders), 3, 1),
        in_specs=[SMEM_SPEC] + [VMEM_SPEC] * 2 + [ANY_SPEC],
        out_shape=in_shapes,
        scratch_shapes=[pltpu.VMEM((part, 2 * padded + LANES), F32)],
        compiler_params=params,
        cost_estimate=work(8 * seq * model * padded),
        name="in_gradient",
    )(place, normed2, dup, other)
    in_flows = [flow_rows(a) for a in in_flows]
    in_reduce = PairReduce(in_flows[:2], in_flows[2:], orders)
    dhidden, dproj = pl.pallas_call(
        ordered(norm_back_kernel, 4, 1),
        in_specs=[VMEM_SPEC] * 4 + [ANY_SPEC],
        out_shape=[shape((rows, model), F32), shape((rows, model), BF16)],
        compiler_params=pltpu.CompilerParams(vmem_limit_bytes=24 << 20),
        name="norm_back",
    )(mine, swap(other, "shard", top), hidden, cotangent, in_flows[0])
    down_keep, down_send, mlp_keep, mlp_send = pl.pallas_call(
        ordered(functools.partial(down_kernel, held_of(cots), n, ff, near), 3 + len(cots), 1),
        in_specs=[SMEM_SPEC] + [VMEM_SPEC] * (2 + len(cots)) + [ANY_SPEC],
        out_shape=[down_shape] * 2 + [block_shape] * 2,
        scratch_shapes=[pltpu.VMEM((padded, model), F32)],
        compiler_params=params,
        cost_estimate=work(8 * seq * model * padded),
        name="down_gradient",
    )(place, act, down_w, *arrays_of(cots), dproj)
    dprojs = gather_rows(dproj, lambda: (down_keep,))
    in_reduce.step(0, [dprojs[1].array])

    out_shape = shape((slots, part, lanes), BF16)
    dqkv, out_keep, out_send = pl.pallas_call(
        ordered(
            functools.partial(attention_back_kernel, held_of(dprojs), n, heads, far),
            len(dprojs) + 10,
            2,
        ),
        in_specs=[SMEM_SPEC] + [VMEM_SPEC] * (len(dprojs) + 9) + [ANY_SPEC] * 2,
        out_shape=[shape((seq, 3 * width), BF16), out_shape, out_shape],
        scratch_shapes=[
            pltpu.VMEM((seq, width), BF16),
            pltpu.VMEM((seq + 2 * HALF, width), F32),
            pltpu.VMEM((seq + 2 * HALF, width), F32),
            pltpu.VMEM((part, model), F32),
        ],
        compiler_params=params,
        cost_estimate=work(40 * seq * model * width),
        name="attention_back",
    )(
        place,
        *arrays_of(dprojs),
        w_out,
        attended,
        queries,
        keys,
        values,
        *tables,
        in_reduce.p[1],
        in_reduce.q[1],
    )

    mlp_mine, mlp_other = near_sums(mlp_keep, mlp_send, "near_sum_mlp", dqkv)
    qkv_tiles = 3 * width // LANES
    qkv_counts = [qkv_tiles - qkv_tiles // 3, qkv_tiles // 3]
    in_reduce.step(1, [dqkv])
    qkv_flows = pl.pallas_call(
        ordered(functools.partial(qkv_kernel, n, qkv_counts, orders), 3, 1),
        in_specs=[SMEM_SPEC] + [VMEM_SPEC] * 2 + [ANY_SPEC],
        out_shape=[shape((slots, n * c, chunk, LANES), BF16) for c in qkv_counts for _ in range(2)],
        scratch_shapes=[pltpu.VMEM((part, 3 * width), F32)],
        compiler_params=params,
        cost_estimate=work(12 * seq * model * width),
        name="qkv_gradient",
    )(place, normed1, dqkv, mlp_other)
    qkv_flows = [flow_rows(a) for a in qkv_flows]
    split = qkv_flows[2].shape[1]
    down_first = add_halves(down_keep, after(swap(down_send, "rep", near[0]), dqkv))
    qkv_q = [jnp.concatenate(x, axis=1) for x in zip(qkv_flows[2:], (out_keep, out_send))]
    qkv_q[1] = after(qkv_q[1], down_first[1])
    att_reduce = PairReduce(qkv_flows[:2], qkv_q, orders)
    att_reduce.step(0)
    att_first = att_reduce.p[1]
    att_reduce.step(1)
    output = pl.pallas_call(
        ordered(output_kernel, 3, 1),
        in_specs=[VMEM_SPEC] * 3 + [ANY_SPEC],
        out_shape=shape((rows, model), BF16),
        compiler_params=pltpu.CompilerParams(vmem_limit_bytes=16 << 20),
        name="output",
    )(mlp_mine, swap(mlp_other, "shard", top), hidden, qkv_flows[0])
    dnormed1_keep, dnormed1_send = pl.pallas_call(
        ordered(functools.partial(project_back_kernel, n), 3, 1),
        in_specs=[SMEM_SPEC] + [VMEM_SPEC] * 2 + [ANY_SPEC],
        out_shape=[block_shape] * 2,
        compiler_params=params,
        cost_estimate=work(6 * seq * model * width),
        name="project_back",
    )(place, dqkv, qkv_w, att_first)
    mine, other = near_sums(dnormed1_keep, dnormed1_send, "near_sum_1")
    input_grad = pl.pallas_call(
        input_kernel,
        out_shape=shape((rows, model), F32),
        compiler_params=pltpu.CompilerParams(vmem_limit_bytes=24 << 20),
        name="input_grad",
    )(mine, swap(other, "shard", top), tokens, dhidden)

    def turned(p, q, counts):
        sizes = [c * chunk for c in counts]
        whole = jnp.concatenate([p.reshape(n, sizes[0], LANES), q.reshape(n, sizes[1], LANES)], 1)
        whole = turn(whole, n)
        return whole[:, : sizes[0]].reshape(-1, LANES), whole[:, sizes[0] :].reshape(-1, LANES)

    def tiles_of(pair, count):
        size = n * count * chunk
        return [a[:, :size].reshape(a.shape[0], n * count, chunk, LANES) for a in pair]

    in_p, in_q = turned(*in_reduce.finish([[qkv_flows[0]]]), in_counts)
    down_share = replica_reduce(*down_first, near[1:], [[att_first]])

    att_p, att_q = att_reduce.finish()
    att_done = att_p[:16]
    in_p, in_q = pair_gather(in_p, in_q, orders)
    down_pair = replica_spread(after(down_share, att_done), near)
    qkv_p, qkv_q = turned(att_p, att_q[:split], qkv_counts)
    att_p, att_q = pair_gather(qkv_p, jnp.concatenate([qkv_q, att_q[split:]]), orders)

    in_total, ln2_total = columns_out(
        place,
        [tiles_of(in_p, in_counts[0]), tiles_of(in_q, in_counts[1])],
        in_counts,
        orders,
        w_in,
        gain2,
        n,
        ff=ff,
    )
    down_total = rows_out(place, down_pair, 0, ff, model, near)
    out_total = rows_out(place, att_q, split, part, model, far)
    qkv_total, ln1_total = columns_out(
        place,
        [tiles_of(att_p, qkv_counts[0]), tiles_of(att_q, qkv_counts[1])],
        qkv_counts,
        orders,
        w_qkv,
        gain1,
        n,
        head_cols=head_cols,
        width=width,
    )
    return (
        output,
        input_grad,
        ln1_total,
        qkv_total,
        out_total,
        ln2_total,
        in_total,
        down_total,
    )


def solution(mesh):
    return jax.shard_map(
        shards,
        mesh=mesh,
        in_specs=(
            P(("rep", "shard"), None),
            P("rep", None),
            P("shard"),
            P("shard", None),
            P("shard", None),
            P("shard"),
            P("shard", None),
            P("shard", None),
            P(("rep", "shard"), None),
        ),
        out_specs=(
            P(("rep", "shard"), None),
            P(("rep", "shard"), None),
            P("shard"),
            P("shard", None),
            P("shard", None),
            P("shard"),
            P("shard", None),
            P("shard", None),
        ),
        check_vma=False,
    )
```
